32 devices in a mesh: band: 4 (over z), sx: 4 (over x, core), sy: 2 (over y).
Axes of the slice: x: 2, y: 2, z: 4, core: 2. Of those that a mesh axis runs over, the one named last changes fastest.
Arguments:
- orbitals: float32 [256, 24, 12, 128], P('band', 'sx', 'sy'), may hold values from -6 to 6
- potential: float32 [24, 12, 128], P('sx', 'sy'), may hold values from -3 to 0
- projectors: float32 [32, 4, 5, 128], P(('sx', 'sy')), may hold values from -0.25 to 0.25
- energies: float32 [32, 4], P(('sx', 'sy')), may hold values from 1 to 6
- centers: int32 [32, 2], P(('sx', 'sy')), may hold values from 0 to 23, as said below
Outputs:
- filtered: float32 [256, 24, 12, 128], P('band', 'sx', 'sy')
- gram: float32 [256, 256], P('band')
The draws below stay inside these ranges and needn't reach their ends.
Inputs may be any that keep to these rules, and one draw needn't show every extreme that they name: `centers`: atom a's cell lies in the grid slab of the device numbered a // 4 along sx+sy, sy counting fastest; the first entry indexes the first grid dimension, the second the second.
All inputs are finite; a program needn't handle non-finite values.
Results may differ from the reference program's by a relative error of at most 0.0022.
Values may be sent and summed in bfloat16 or wider, within the bound.
No kernel may reach another device: no remote copies, remote signals or barrier semaphores. Data moves between devices by JAX's collectives and lax.ppermute only.
A program may use at most 64 MiB of HBM per device.

```python
import math
import jax
import jax.numpy as jnp
from jax import lax

NB = 256
NPROJ = 4
TPA = 5
NZ = 128
DEG = 2
CX = 6
CY = 6
ATOM_DEV = 4
NX = 24
NY = 12
ATOMS = 32


def draw_orbitals(key, part):
    k_noise, k_base, k_mix = jax.random.split(jax.random.fold_in(key, 3), 3)
    shape = (NB, NX, NY, NZ)
    noise = jax.random.normal(k_noise, shape, jnp.float32)
    base = jax.random.normal(k_base, (NX, NY, NZ), jnp.float32)
    mix = 0.7 * jax.random.normal(k_mix, (NB,), jnp.float32)
    value = mix[:, None, None, None] * base[None] + noise
    return jnp.clip(value, -6.0, 6.0).astype(jnp.float32)


def draw_centers(key, part):
    slabs_y = NY // CY
    count = ATOM_DEV * (NX // CX) * slabs_y
    owner = jnp.arange(count, dtype=jnp.int32) // ATOM_DEV
    index_x = owner // slabs_y
    index_y = owner % slabs_y
    key_x, key_y = jax.random.split(jax.random.fold_in(key, 7), 2)
    cell_x = index_x * CX + jax.random.randint(key_x, (count,), 0, CX, jnp.int32)
    cell_y = index_y * CY + jax.random.randint(key_y, (count,), 0, CY, jnp.int32)
    position = jnp.arange(count, dtype=jnp.int32)
    cell_x = jnp.where(position == 0, 0, cell_x)
    cell_y = jnp.where(position == 0, 0, cell_y)
    cell_x = jnp.where(position == count - 1, NX - 1, cell_x)
    cell_y = jnp.where(position == count - 1, NY - 1, cell_y)
    return jnp.stack([cell_x, cell_y], axis=1).astype(jnp.int32)


def levels(own_key, dims, pieces, smallest, high):
    gain = 1.0
    for dim, blocks in pieces:
        steps = jax.random.uniform(jax.random.fold_in(jax.random.fold_in(own_key, 6), dim), (blocks,), jnp.float32, smallest / len(pieces), high / len(pieces))
        gain = gain * jnp.repeat(jnp.exp(steps), dims[dim] // blocks).reshape((-1,) + (1,) * (len(dims) - 1 - dim))
    return gain


def scatter_about(stream_key, dims, deviation, bound, cuts=(), kind=jnp.bfloat16):
    gain = levels(stream_key, dims, cuts, -0.22, 0.18) if cuts else 1.0
    values = jax.random.normal(stream_key, dims, jnp.float32) * deviation * gain
    return jnp.minimum(jnp.maximum(values, -bound), bound).astype(kind)


def setup_inputs(seed: int = 0) -> dict:
    keys = jax.random.split(jax.random.key(seed), 6)
    return {
        "orbitals": draw_orbitals(jax.random.fold_in(keys[5], 71), 0),
        "potential": jnp.clip(-3.0 + 3.0 * jax.random.uniform(keys[1], (NX, NY, NZ), jnp.float32) ** levels(keys[1], (NX, NY, NZ), ((0, 4), (1, 2)), -0.2, 0.2), -3.0, 0.0),
        "projectors": scatter_about(keys[2], (ATOMS, NPROJ, TPA, NZ), (TPA * NZ) ** -0.5, 0.25, ((0, 8),), jnp.float32),
        "energies": jnp.clip(jnp.exp(math.log(6.0) - 1.7917595 * jax.random.uniform(keys[3], (ATOMS, NPROJ), jnp.float32) ** levels(keys[3], (ATOMS, NPROJ), ((0, 8),), -0.2, 0.2)), 1.0, 6.0),
        "centers": draw_centers(jax.random.fold_in(keys[5], 71), 0),
    }


stencil_weights = (-5369.0 / 1800.0, 12.0 / 7.0, -15.0 / 56.0, 10.0 / 189.0, -1.0 / 112.0, 2.0 / 1925.0, -1.0 / 16632.0)
filter_center = 6.5
filter_half = 6.0
offsets_x = (0, -1, 1, 0, 0)
offsets_y = (0, 0, 0, -1, 1)


def laplace_full(field):
    count_x = field.shape[1]
    count_y = field.shape[2]
    count_z = field.shape[3]
    padded = jnp.pad(field, ((0, 0), (6, 6), (6, 6), (6, 6)))
    total = (3.0 * stencil_weights[0]) * field
    for step in range(1, 7):
        weight = stencil_weights[step]
        total = total + weight * (padded[:, 6 + step:6 + step + count_x, 6:6 + count_y, 6:6 + count_z] + padded[:, 6 - step:6 - step + count_x, 6:6 + count_y, 6:6 + count_z])
        total = total + weight * (padded[:, 6:6 + count_x, 6 + step:6 + step + count_y, 6:6 + count_z] + padded[:, 6:6 + count_x, 6 - step:6 - step + count_y, 6:6 + count_z])
        total = total + weight * (padded[:, 6:6 + count_x, 6:6 + count_y, 6 + step:6 + step + count_z] + padded[:, 6:6 + count_x, 6:6 + count_y, 6 - step:6 - step + count_z])
    return total


def nonlocal_full(field, centers, projectors, energies):
    batch, count_x, count_y, count_z = field.shape
    shift_x = jnp.array(offsets_x, jnp.int32)
    shift_y = jnp.array(offsets_y, jnp.int32)
    cell_x = centers[:, 0:1].astype(jnp.int32) + shift_x[None, :]
    cell_y = centers[:, 1:2].astype(jnp.int32) + shift_y[None, :]
    inside = (cell_x >= 0) & (cell_x < count_x) & (cell_y >= 0) & (cell_y < count_y)
    flat = (jnp.clip(cell_x, 0, count_x - 1) * count_y + jnp.clip(cell_y, 0, count_y - 1)).astype(jnp.int32)
    keep = inside.astype(jnp.float32)
    columns = field.reshape(batch, count_x * count_y, count_z)
    picked = columns[:, flat, :] * keep[None, :, :, None]
    coeffs = jnp.einsum('aptz,batz->bap', projectors, picked, precision=lax.Precision.HIGHEST)
    weighted = coeffs * energies[None]
    spread = jnp.einsum('aptz,bap->batz', projectors, weighted, precision=lax.Precision.HIGHEST) * keep[None, :, :, None]
    result = jnp.zeros_like(columns).at[:, flat.reshape(-1), :].add(spread.reshape(batch, -1, count_z))
    return result.reshape(field.shape)


def reference(orbitals, potential, projectors, energies, centers):
    block = min(16, NB)

    def apply_h(vector):
        return -0.5 * laplace_full(vector) + potential[None] * vector + nonlocal_full(vector, centers, projectors, energies)

    def filter_block(vectors):
        previous = vectors
        current = (apply_h(vectors) - filter_center * vectors) / filter_half
        for degree in range(1, DEG):
            following = 2.0 * (apply_h(current) - filter_center * current) / filter_half - previous
            previous, current = current, following
        return current

    grouped = orbitals.reshape(NB // block, block, NX, NY, NZ)
    filtered = lax.map(filter_block, grouped).reshape(NB, NX, NY, NZ)
    rounded = filtered.astype(jnp.bfloat16).reshape(NB, NX * NY * NZ)
    gram = jnp.dot(rounded, rounded.T, preferred_element_type=jnp.float32) / (NX * NY * NZ)
    return filtered, gram
```

```python
import functools

import jax
import jax.numpy as jnp
from jax import lax
from jax.experimental import pallas as pl
from jax.experimental.pallas import tpu as pltpu
from jax.sharding import PartitionSpec as P

stencil_weights = (
    -5369.0 / 1800.0,
    12.0 / 7.0,
    -15.0 / 56.0,
    10.0 / 189.0,
    -1.0 / 112.0,
    2.0 / 1925.0,
    -1.0 / 16632.0,
)
filter_center = 6.5
filter_half = 6.0
offsets_x = (0, -1, 1, 0, 0)
offsets_y = (0, 0, 0, -1, 1)
width = 6
plane = ("sx", "sy")
every = ("band", "sx", "sy")


def filter_kernel(
    slabs_y,
    cells_x,
    cells_y,
    each,
    centers_ref,
    energies_ref,
    got_ref,
    field_ref,
    rounded_ref,
    first,
    second,
    partial,
    pot,
):
    group, _, nz = got_ref.shape
    count_x, count_y = pot.shape[0], pot.shape[1]
    tiles = len(offsets_x)
    atoms_here = centers_ref.shape[1] // 2
    projs = energies_ref.shape[1] // atoms_here
    slab_cells = cells_x * cells_y
    proj_row = slab_cells * each
    pot_row = proj_row + atoms_here * projs * tiles
    scale = 1.0 / filter_half
    factors = [-0.5 * scale * w for w in stencil_weights]
    span = cells_y * 2 if slabs_y % 2 == 0 else cells_y
    spans = count_y // span

    first[...] = jnp.zeros_like(first)
    second[...] = jnp.zeros_like(second)

    def take_slab(g, carry):
        x0 = (g // slabs_y) * cells_x
        y0 = (g % slabs_y) * cells_y
        for i in range(cells_x):
            for j in range(cells_y):
                cell = i * cells_y + j
                first[width + x0 + i, width + y0 + j] = got_ref[g, pl.ds(cell * each, each), :]
                pot[x0 + i, y0 + j] = got_ref[g, pl.ds(pot_row + cell, 1), :]
        return carry

    lax.fori_loop(0, group, take_slab, 0)

    distance = jnp.abs(
        lax.broadcasted_iota(jnp.int32, (nz, nz), 0) - lax.broadcasted_iota(jnp.int32, (nz, nz), 1)
    )
    along_z = jnp.zeros((nz, nz), jnp.float32)
    for step in range(1, width + 1):
        along_z = jnp.where(distance == step, factors[step], along_z)
    z_high = along_z.astype(jnp.bfloat16)
    z_low = (along_z - z_high.astype(jnp.float32)).astype(jnp.bfloat16)
    z_matrix = jnp.concatenate(
        [
            jnp.concatenate([z_high, z_low], axis=1),
            jnp.concatenate([z_high, jnp.zeros_like(z_high)], axis=1),
        ],
        axis=0,
    )

    def apply(source, target, finish, gain):
        def z_part(block, carry):
            rows = source[pl.ds(width + block * cells_x, cells_x), pl.ds(width, count_y)]
            flat = rows.reshape(cells_x * count_y * each, nz)
            high = flat.astype(jnp.bfloat16)
            low = (flat - high.astype(jnp.float32)).astype(jnp.bfloat16)
            both = jnp.dot(
                jnp.concatenate([high, low], axis=1), z_matrix, preferred_element_type=jnp.float32
            )
            partial[pl.ds(block * cells_x, cells_x)] = (both[:, :nz] + both[:, nz:]).reshape(
                rows.shape
            )
            return carry

        lax.fori_loop(0, count_x // cells_x, z_part, 0)

        def xy_part(index, carry):
            x = index // spans
            y = (index % spans) * span
            at_x = width + x
            at_y = width + y
            center = source[at_x, pl.ds(at_y, span)]
            total = partial[x, pl.ds(y, span)] + (
                (3.0 * factors[0] - filter_center * scale) + scale * pot[x, pl.ds(y, span)]
            ) * center
            for step in range(1, width + 1):
                pair_x = source[at_x + step, pl.ds(at_y, span)] + source[at_x - step, pl.ds(at_y, span)]
                pair_y = source[at_x, pl.ds(at_y + step, span)] + source[at_x, pl.ds(at_y - step, span)]
                total = total + factors[step] * (pair_x + pair_y)
            target[at_x, pl.ds(at_y, span)] = finish(total, target[at_x, pl.ds(at_y, span)])
            return carry

        lax.fori_loop(0, count_x * spans, xy_part, 0)

        def atoms_part(g, carry):
            for a in range(atoms_here):
                at_x = width + centers_ref[g, 2 * a]
                at_y = width + centers_ref[g, 2 * a + 1]
                base = proj_row + a * projs * tiles
                sums = [None] * projs
                for t in range(tiles):
                    tile = source[at_x + offsets_x[t], at_y + offsets_y[t]]
                    for p in range(projs):
                        term = tile * got_ref[g, pl.ds(base + p * tiles + t, 1), :]
                        sums[p] = term if t == 0 else sums[p] + term
                coeffs = [
                    jnp.sum(sums[p], axis=-1, keepdims=True)
                    * (energies_ref[g, a * projs + p] * gain)
                    for p in range(projs)
                ]
                for t in range(tiles):
                    spread = coeffs[0] * got_ref[g, pl.ds(base + t, 1), :]
                    for p in range(1, projs):
                        spread = spread + coeffs[p] * got_ref[g, pl.ds(base + p * tiles + t, 1), :]
                    to_x = at_x + offsets_x[t]
                    to_y = at_y + offsets_y[t]
                    target[to_x, to_y] = target[to_x, to_y] + spread
            return carry

        lax.fori_loop(0, group, atoms_part, 0)

    apply(first, second, lambda total, old: total, scale)

    for x in (width - 1, width + count_x):
        second[x] = jnp.zeros(second.shape[1:], jnp.float32)
    for y in (width - 1, width + count_y):
        second[:, y] = jnp.zeros((second.shape[0],) + second.shape[2:], jnp.float32)

    apply(second, first, lambda total, old: 2.0 * total - old, 2.0 * scale)

    shares = rounded_ref.shape[0] // group
    portion = slab_cells // shares

    def give_slab(g, carry):
        x0 = (g // slabs_y) * cells_x
        y0 = (g % slabs_y) * cells_y
        for i in range(cells_x):
            for j in range(cells_y):
                cell = i * cells_y + j
                value = first[width + x0 + i, width + y0 + j]
                field_ref[g, pl.ds(cell * each, each), :] = value
                rounded_ref[
                    (cell // portion) * group + g, :, pl.ds((cell % portion) * nz, nz)
                ] = value.astype(jnp.bfloat16)
        return carry

    lax.fori_loop(0, group, give_slab, 0)


def local(orbitals, potential, projectors, energies, centers):
    band_orbitals, cells_x, cells_y, nz = orbitals.shape
    bands = lax.axis_size("band")
    slabs_x = lax.axis_size("sx")
    slabs_y = lax.axis_size("sy")
    group = slabs_x * slabs_y
    each = band_orbitals // group
    slab_cells = cells_x * cells_y
    grid = (slabs_x * cells_x, slabs_y * cells_y)

    chunks = orbitals.transpose(1, 2, 0, 3).reshape(slab_cells, group, each, nz)
    chunks = chunks.transpose(1, 0, 2, 3).reshape(group, slab_cells * each, nz)
    atoms, projs = energies.shape
    numbers = jnp.concatenate([energies.reshape(-1), centers.reshape(-1).astype(jnp.float32)])
    numbers = jnp.pad(numbers, (0, nz - numbers.shape[0])).reshape(1, nz)
    shared = jnp.concatenate([projectors.reshape(-1, nz), potential.reshape(-1, nz), numbers])
    shared = jnp.pad(shared, ((0, -shared.shape[0] % 8), (0, 0)))
    sent = jnp.concatenate(
        [chunks, jnp.broadcast_to(shared[None], (group,) + shared.shape)], axis=1
    )
    got = lax.all_to_all(sent, plane, 0, 0)
    numbers = got[:, slab_cells * each + projectors.size // nz + slab_cells]
    all_energies = numbers[:, : atoms * projs]
    all_centers = numbers[:, atoms * projs : atoms * (projs + 2)].astype(jnp.int32)

    portion = slab_cells // bands
    padded = (grid[0] + 2 * width, grid[1] + 2 * width, each, nz)
    field, rounded = pl.pallas_call(
        functools.partial(filter_kernel, slabs_y, cells_x, cells_y, each),
        in_specs=[
            pl.BlockSpec(memory_space=pltpu.SMEM),
            pl.BlockSpec(memory_space=pltpu.SMEM),
            pl.BlockSpec(memory_space=pltpu.VMEM),
        ],
        out_specs=[pl.BlockSpec(memory_space=pltpu.VMEM)] * 2,
        out_shape=[
            jax.ShapeDtypeStruct((group, slab_cells * each, nz), jnp.float32),
            jax.ShapeDtypeStruct((bands * group, each, portion * nz), jnp.bfloat16),
        ],
        scratch_shapes=[
            pltpu.VMEM(padded, jnp.float32),
            pltpu.VMEM(padded, jnp.float32),
            pltpu.VMEM(grid + (each, nz), jnp.float32),
            pltpu.VMEM(grid + (1, nz), jnp.float32),
        ],
        compiler_params=pltpu.CompilerParams(vmem_limit_bytes=56 * 1024 * 1024),
        cost_estimate=pl.CostEstimate(
            flops=2 * 2 * 40 * grid[0] * grid[1] * each * nz,
            bytes_accessed=8 * grid[0] * grid[1] * each * nz,
            transcendentals=0,
        ),
    )(all_centers, all_energies, got)

    pieces = lax.all_to_all(rounded, every, 0, 0)
    matrix = pieces.reshape(bands * band_orbitals, portion * nz)
    sums = lax.dot_general(
        matrix, matrix, (((1,), (1,)), ((), ())), preferred_element_type=jnp.float32
    )
    parts = lax.all_to_all(sums.reshape(bands * group, each, bands * band_orbitals), every, 0, 0)
    rows = jnp.sum(parts, axis=0) / (grid[0] * grid[1] * nz)
    gram = lax.all_to_all(jnp.broadcast_to(rows[None], (group,) + rows.shape), plane, 0, 0)
    gram = gram.reshape(band_orbitals, bands * band_orbitals)

    back = lax.all_to_all(field, plane, 0, 0)
    back = back.reshape(group, slab_cells, each, nz).transpose(1, 0, 2, 3)
    filtered = back.reshape(cells_x, cells_y, band_orbitals, nz).transpose(2, 0, 1, 3)
    return (filtered, gram)


def solution(mesh):
    in_specs = (
        P("band", "sx", "sy", None),
        P("sx", "sy", None),
        P(("sx", "sy"), None, None, None),
        P(("sx", "sy"), None),
        P(("sx", "sy"), None),
    )
    out_specs = (P("band", "sx", "sy", None), P("band", None))
    return jax.shard_map(local, mesh=mesh, in_specs=in_specs, out_specs=out_specs, check_vma=False)
```

```python
import functools

import jax
import jax.numpy as jnp
from jax import lax
from jax.experimental import pallas as pl
from jax.experimental.pallas import tpu as pltpu
from jax.sharding import PartitionSpec as P

stencil_weights = (
    -5369.0 / 1800.0,
    12.0 / 7.0,
    -15.0 / 56.0,
    10.0 / 189.0,
    -1.0 / 112.0,
    2.0 / 1925.0,
    -1.0 / 16632.0,
)
filter_center = 6.5
filter_half = 6.0
offsets_x = (0, -1, 1, 0, 0)
offsets_y = (0, 0, 0, -1, 1)
reach = 6
plane = ("sx", "sy")
every = ("band", "sx", "sy")

orbital_gain = 2.0**12
projector_gain = 2.0**17
potential_gain = 2.0**13
remainder_gain = 2.0**10
top = 15
middle = 8
levels = 17

vmem = pl.BlockSpec(memory_space=pltpu.VMEM)
smem = pl.BlockSpec(memory_space=pltpu.SMEM)
params = pltpu.CompilerParams(vmem_limit_bytes=24 * 1024 * 1024)


def level_of(largest):
    level = jnp.float32(0.0)
    scale = jnp.float32(2.0 ** (top + 8 * middle))
    for j in range(levels):
        above = largest >= jnp.float32(2.0 ** (8 * (j - middle)))
        level = jnp.where(above, jnp.float32(j + 1), level)
        scale = jnp.where(above, jnp.float32(2.0 ** (top - 8 * (j + 1 - middle))), scale)
    return level, scale


def shrink_of(level):
    return jnp.exp2(8.0 * (level - middle) - top)


def pack_kernel(each, energies_ref, centers_ref, orbitals_ref, projectors_ref, potential_ref, out_ref):
    group, rows, nz = out_ref.shape
    slab_cells = orbitals_ref.shape[0]
    atoms, tiles, projs = projectors_ref.shape[:3]
    base = slab_cells * each

    def take(g, carry):
        for cell in range(slab_cells):
            out_ref[g, pl.ds(cell * each, each), :] = (
                orbitals_ref[cell, pl.ds(pl.multiple_of(g * each, each), each), :] * orbital_gain
            )
        return carry

    lax.fori_loop(0, group, take, 0)

    row = base
    for a in range(atoms):
        for t in range(tiles):
            out_ref[0, pl.ds(row, projs), :] = projectors_ref[a, t] * projector_gain
            row += projs
    for i in range(potential_ref.shape[0]):
        count = potential_ref.shape[1]
        out_ref[0, pl.ds(row, count), :] = potential_ref[i] * potential_gain
        row += count
    lane = lax.broadcasted_iota(jnp.int32, (1, nz), 1)
    numbers = jnp.zeros((1, nz), jnp.float32)
    for a in range(atoms):
        for p in range(projs):
            numbers = jnp.where(lane == a * projs + p, energies_ref[a, p], numbers)
    high = numbers.astype(jnp.bfloat16).astype(jnp.float32)
    low = (numbers - high) * remainder_gain
    count = atoms * projs
    numbers = high + pltpu.roll(low, count, 1)
    for a in range(atoms):
        for d in range(2):
            here = centers_ref[a, d].astype(jnp.float32)
            numbers = jnp.where(lane == 2 * count + 2 * a + d, here, numbers)
    out_ref[0, pl.ds(row, 1), :] = numbers
    out_ref[0, pl.ds(row + 1, rows - row - 1), :] = jnp.zeros((rows - row - 1, nz), jnp.float32)

    def repeat(g, carry):
        out_ref[g, pl.ds(base, rows - base), :] = out_ref[0, pl.ds(base, rows - base), :]
        return carry

    lax.fori_loop(1, group, repeat, 0)


def filter_kernel(
    slabs_y,
    cells_x,
    cells_y,
    each,
    atoms,
    projs,
    got_ref,
    field_ref,
    rounded_ref,
    scale_ref,
    first,
    second,
    partial,
    diagonal,
    numbers,
    arrived,
):
    group, _, nz = got_ref.shape
    count_x, count_y = diagonal.shape[0], diagonal.shape[1]
    tiles = len(offsets_x)
    slab_cells = cells_x * cells_y
    proj_row = slab_cells * each
    pot_row = proj_row + atoms * projs * tiles
    number_row = pot_row + slab_cells
    scale = 1.0 / filter_half
    factors = [-0.5 * scale * w for w in stencil_weights]
    ring = 1

    copy = pltpu.make_async_copy(got_ref.at[:, number_row, :], numbers, arrived)
    copy.start()

    for field in (first, second):
        for x in (0, ring + count_x):
            field[x] = jnp.zeros(field.shape[1:], jnp.float32)
        for y in (0, ring + count_y):
            field[:, y] = jnp.zeros((field.shape[0],) + field.shape[2:], jnp.float32)

    def take_slab(g, carry):
        x0 = (g // slabs_y) * cells_x
        y0 = (g % slabs_y) * cells_y
        for i in range(cells_x):
            for j in range(cells_y):
                cell = i * cells_y + j
                first[ring + x0 + i, ring + y0 + j] = got_ref[g, pl.ds(cell * each, each), :] * (
                    1.0 / orbital_gain
                )
                diagonal[x0 + i, y0 + j] = got_ref[g, pl.ds(pot_row + cell, 1), :] * (
                    scale / potential_gain
                ) + (3.0 * factors[0] - filter_center * scale)
        return carry

    lax.fori_loop(0, group, take_slab, 0)

    distance = jnp.abs(
        lax.broadcasted_iota(jnp.int32, (nz, nz), 0) - lax.broadcasted_iota(jnp.int32, (nz, nz), 1)
    )
    along_z = jnp.zeros((nz, nz), jnp.float32)
    for step in range(1, reach + 1):
        along_z = jnp.where(distance == step, factors[step], along_z)
    z_high = along_z.astype(jnp.bfloat16)
    z_low = (along_z - z_high.astype(jnp.float32)).astype(jnp.bfloat16)
    z_matrix = jnp.concatenate(
        [
            jnp.concatenate([z_high, z_low], axis=1),
            jnp.concatenate([z_high, jnp.zeros_like(z_high)], axis=1),
        ],
        axis=0,
    )

    def along(cells, at):
        total = None
        for step in range(1, reach + 1):
            near = [cells[n] for n in (at - step, at + step) if 0 <= n < len(cells)]
            if near:
                term = factors[step] * sum(near[1:], near[0])
                total = term if total is None else total + term
        return total

    def apply(source, target, finish, gain):
        def z_part(block, carry):
            rows = source[pl.ds(ring + block * cells_x, cells_x), pl.ds(ring, count_y)]
            flat = rows.reshape(cells_x * count_y * each, nz)
            high = flat.astype(jnp.bfloat16)
            low = (flat - high.astype(jnp.float32)).astype(jnp.bfloat16)
            both = jnp.dot(
                jnp.concatenate([high, low], axis=1), z_matrix, preferred_element_type=jnp.float32
            )
            partial[pl.ds(block * cells_x, cells_x)] = (both[:, :nz] + both[:, nz:]).reshape(
                rows.shape
            )
            return carry

        lax.fori_loop(0, count_x // cells_x, z_part, 0)

        def x_part(y, carry):
            cells = [source[ring + x, ring + y] for x in range(count_x)]
            for x in range(count_x):
                partial[x, y] = partial[x, y] + diagonal[x, y] * cells[x] + along(cells, x)
            return carry

        lax.fori_loop(0, count_y, x_part, 0)

        def y_part(x, carry):
            cells = [source[ring + x, ring + y] for y in range(count_y)]
            for y in range(count_y):
                total = partial[x, y] + along(cells, y)
                target[ring + x, ring + y] = finish(total, target, ring + x, ring + y)
            return carry

        lax.fori_loop(0, count_x, y_part, 0)

        def atoms_part(g, carry):
            places = []
            sums = []
            for a in range(atoms):
                at_x = ring + numbers[g, 2 * atoms * projs + 2 * a].astype(jnp.int32)
                at_y = ring + numbers[g, 2 * atoms * projs + 2 * a + 1].astype(jnp.int32)
                places.append((at_x, at_y))
                totals = [None] * projs
                for t in range(tiles):
                    tile = source[at_x + offsets_x[t], at_y + offsets_y[t]]
                    for p in range(projs):
                        row = proj_row + (a * tiles + t) * projs + p
                        term = tile * got_ref[g, pl.ds(row, 1), :]
                        totals[p] = term if t == 0 else totals[p] + term
                sums.append(totals)
            for a in range(atoms):
                at_x, at_y = places[a]
                coeffs = []
                for p in range(projs):
                    k = a * projs + p
                    energy = numbers[g, k] + numbers[g, atoms * projs + k] * (1.0 / remainder_gain)
                    coeffs.append(
                        jnp.sum(sums[a][p], axis=-1, keepdims=True)
                        * (energy * (gain / projector_gain / projector_gain))
                    )
                for t in range(tiles):
                    row = proj_row + (a * tiles + t) * projs
                    spread = coeffs[0] * got_ref[g, pl.ds(row, 1), :]
                    for p in range(1, projs):
                        spread = spread + coeffs[p] * got_ref[g, pl.ds(row + p, 1), :]
                    to_x = at_x + offsets_x[t]
                    to_y = at_y + offsets_y[t]
                    target[to_x, to_y] = target[to_x, to_y] + spread
            return carry

        lax.fori_loop(0, group, atoms_part, 0)

    copy.wait()
    apply(first, second, lambda total, target, x, y: total, scale)

    for x in (0, ring + count_x):
        second[x] = jnp.zeros(second.shape[1:], jnp.float32)
    for y in (0, ring + count_y):
        second[:, y] = jnp.zeros((second.shape[0],) + second.shape[2:], jnp.float32)

    apply(second, first, lambda total, target, x, y: 2.0 * total - target[x, y], 2.0 * scale)

    shares = rounded_ref.shape[0] // group
    portion = slab_cells // shares

    def give_slab(g, largest):
        x0 = (g // slabs_y) * cells_x
        y0 = (g % slabs_y) * cells_y
        for i in range(cells_x):
            for j in range(cells_y):
                cell = i * cells_y + j
                value = first[ring + x0 + i, ring + y0 + j]
                field_ref[g, pl.ds(cell * each, each), :] = value
                rounded_ref[
                    (cell // portion) * group + g, :, pl.ds((cell % portion) * nz, nz)
                ] = value.astype(jnp.bfloat16)
                largest = jnp.maximum(largest, jnp.abs(value))
        return largest

    largest = lax.fori_loop(0, group, give_slab, jnp.zeros((each, nz), jnp.float32))
    level, gain = level_of(jnp.max(largest))
    scale_ref[0:1] = jnp.full((1, nz), gain, jnp.float32)
    scale_ref[1:2] = jnp.full((1, nz), level, jnp.float32)


def rows_kernel(cells, parts_ref, scale_ref, out_ref):
    _, each, columns = parts_ref.shape
    nz = out_ref.shape[1]
    total = jnp.sum(parts_ref[...], axis=0) / cells
    level, gain = level_of(jnp.max(jnp.abs(total)))
    total = total * gain
    high = total.astype(jnp.bfloat16).astype(jnp.float32)
    low = total - high
    row = 0
    for part in (high, low):
        for column in range(0, columns, nz):
            out_ref[pl.ds(row, each), :] = part[:, column : column + nz]
            row += each
    rest = out_ref.shape[0] - row
    out_ref[pl.ds(row, rest), :] = jnp.zeros((rest, nz), jnp.float32)
    out_ref[pl.ds(row, 1), :] = scale_ref[1:2]
    out_ref[pl.ds(row + 1, 1), :] = jnp.full((1, nz), level, jnp.float32)


def local(orbitals, potential, projectors, energies, centers):
    band_orbitals, cells_x, cells_y, nz = orbitals.shape
    bands = lax.axis_size("band")
    slabs_x = lax.axis_size("sx")
    slabs_y = lax.axis_size("sy")
    group = slabs_x * slabs_y
    each = band_orbitals // group
    total_orbitals = bands * band_orbitals
    slab_cells = cells_x * cells_y
    grid = (slabs_x * cells_x, slabs_y * cells_y)
    atoms, projs, tiles, _ = projectors.shape

    rows = slab_cells * each + atoms * projs * tiles + slab_cells + 1
    rows += -rows % 16
    sent = pl.pallas_call(
        functools.partial(pack_kernel, each),
        in_specs=[smem, smem, vmem, vmem, vmem],
        out_specs=vmem,
        out_shape=jax.ShapeDtypeStruct((group, rows, nz), jnp.float32),
        compiler_params=params,
    )(
        energies,
        centers,
        orbitals.transpose(1, 2, 0, 3).reshape(slab_cells, band_orbitals, nz),
        projectors.transpose(0, 2, 1, 3),
        potential,
    )
    got = lax.all_to_all(sent.astype(jnp.float16), plane, 0, 0).astype(jnp.float32)

    portion = slab_cells // bands
    ringed = (grid[0] + 2, grid[1] + 2, each, nz)
    field, rounded, scale = pl.pallas_call(
        functools.partial(filter_kernel, slabs_y, cells_x, cells_y, each, atoms, projs),
        in_specs=[vmem],
        out_specs=[vmem] * 3,
        out_shape=[
            jax.ShapeDtypeStruct((group, slab_cells * each, nz), jnp.float32),
            jax.ShapeDtypeStruct((bands * group, each, portion * nz), jnp.bfloat16),
            jax.ShapeDtypeStruct((2, nz), jnp.float32),
        ],
        scratch_shapes=[
            pltpu.VMEM(ringed, jnp.float32),
            pltpu.VMEM(ringed, jnp.float32),
            pltpu.VMEM(grid + (each, nz), jnp.float32),
            pltpu.VMEM(grid + (1, nz), jnp.float32),
            pltpu.SMEM((group, nz), jnp.float32),
            pltpu.SemaphoreType.DMA,
        ],
        compiler_params=params,
        cost_estimate=pl.CostEstimate(
            flops=2 * 2 * 40 * grid[0] * grid[1] * each * nz,
            bytes_accessed=8 * grid[0] * grid[1] * each * nz,
            transcendentals=0,
        ),
    )(got)

    pieces = lax.all_to_all(rounded, every, 0, 0)
    matrix = pieces.reshape(total_orbitals, portion * nz)
    sums = lax.dot_general(
        matrix, matrix, (((1,), (1,)), ((), ())), preferred_element_type=jnp.float32
    )
    parts = lax.all_to_all(sums.reshape(bands * group, each, total_orbitals), every, 0, 0)

    halves = total_orbitals // nz
    gram_rows = 2 * halves * each
    block = pl.pallas_call(
        functools.partial(rows_kernel, grid[0] * grid[1] * nz),
        in_specs=[vmem, vmem],
        out_specs=vmem,
        out_shape=jax.ShapeDtypeStruct((gram_rows + 8, nz), jnp.float32),
        compiler_params=params,
    )(parts, scale)
    sent = jnp.concatenate(
        [field * scale[0, 0], jnp.broadcast_to(block[None], (group,) + block.shape)], axis=1
    ).astype(jnp.float16)
    back = lax.all_to_all(sent, plane, 0, 0)

    start = slab_cells * each
    shrink = shrink_of(back[:, start + gram_rows : start + gram_rows + 2, :1].astype(jnp.float32))
    filtered = back[:, :start].reshape(group, slab_cells, each, nz).astype(jnp.float32)
    filtered = (filtered * shrink[:, :1, :, None]).transpose(1, 0, 2, 3)
    filtered = filtered.reshape(cells_x, cells_y, band_orbitals, nz).transpose(2, 0, 1, 3)
    gram = back[:, start : start + gram_rows].reshape(group, 2, halves, each, nz).astype(jnp.float32)
    gram = (gram[:, 0] + gram[:, 1]) * shrink[:, 1][:, None, None]
    gram = gram.transpose(0, 2, 1, 3).reshape(band_orbitals, total_orbitals)
    return (filtered, gram)


def solution(mesh):
    in_specs = (
        P("band", "sx", "sy", None),
        P("sx", "sy", None),
        P(("sx", "sy"), None, None, None),
        P(("sx", "sy"), None),
        P(("sx", "sy"), None),
    )
    out_specs = (P("band", "sx", "sy", None), P("band", None))
    return jax.shard_map(local, mesh=mesh, in_specs=in_specs, out_specs=out_specs, check_vma=False)
```

```python
import functools

import jax
import jax.numpy as jnp
from jax import lax
from jax.experimental import pallas as pl
from jax.experimental.pallas import tpu as pltpu
from jax.sharding import PartitionSpec as P

stencil_weights = (
    -5369.0 / 1800.0,
    12.0 / 7.0,
    -15.0 / 56.0,
    10.0 / 189.0,
    -1.0 / 112.0,
    2.0 / 1925.0,
    -1.0 / 16632.0,
)
filter_center = 6.5
filter_half = 6.0
offsets_x = (0, -1, 1, 0, 0)
offsets_y = (0, 0, 0, -1, 1)
reach = 6
plane = ("sx", "sy")
every = ("band", "sx", "sy")

orbital_gain = 2.0**12
projector_gain = 2.0**17
potential_gain = 2.0**13
remainder_gain = 2.0**10
top = 15
middle = 8
levels = 17

vmem = pl.BlockSpec(memory_space=pltpu.VMEM)
smem = pl.BlockSpec(memory_space=pltpu.SMEM)
hbm = pl.BlockSpec(memory_space=pl.ANY)
params = pltpu.CompilerParams(vmem_limit_bytes=24 * 1024 * 1024)


def level_of(largest):
    level = jnp.float32(0.0)
    scale = jnp.float32(2.0 ** (top + 8 * middle))
    for j in range(levels):
        above = largest >= jnp.float32(2.0 ** (8 * (j - middle)))
        level = jnp.where(above, jnp.float32(j + 1), level)
        scale = jnp.where(above, jnp.float32(2.0 ** (top - 8 * (j + 1 - middle))), scale)
    return level, scale


def shrink_of(level):
    shrink = jnp.full(level.shape, 2.0 ** (-top - 8 * middle), jnp.float32)
    for j in range(levels):
        shrink = jnp.where(level > j, jnp.float32(2.0 ** (8 * (j + 1 - middle) - top)), shrink)
    return shrink


def over_group(group, each, body):
    if each % 8 == 0:

        def step(g, carry):
            body(g, pl.ds(pl.multiple_of(g * each, each), each))
            return carry

        lax.fori_loop(0, group, step, 0, unroll=min(group, 8))
    else:
        for g in range(group):
            body(g, pl.ds(g * each, each))


def share_kernel(_, energies_ref, centers_ref, projectors_ref, potential_ref, out_ref):
    rows, nz = out_ref.shape
    atoms, tiles, projs = projectors_ref.shape[:3]

    row = 0
    for a in range(atoms):
        for t in range(tiles):
            out_ref[pl.ds(row, projs), :] = projectors_ref[a, t] * projector_gain
            row += projs
    for i in range(potential_ref.shape[0]):
        count = potential_ref.shape[1]
        out_ref[pl.ds(row, count), :] = potential_ref[i] * potential_gain
        row += count
    lane = lax.broadcasted_iota(jnp.int32, (1, nz), 1)
    numbers = jnp.zeros((1, nz), jnp.float32)
    for a in range(atoms):
        for p in range(projs):
            numbers = jnp.where(lane == a * projs + p, energies_ref[a, p], numbers)
    high = numbers.astype(jnp.bfloat16).astype(jnp.float32)
    low = (numbers - high) * remainder_gain
    count = atoms * projs
    numbers = high + pltpu.roll(low, count, 1)
    for a in range(atoms):
        for d in range(2):
            here = centers_ref[d, a].astype(jnp.float32)
            numbers = jnp.where(lane == 2 * count + 2 * a + d, here, numbers)
    out_ref[pl.ds(row, 1), :] = numbers
    out_ref[pl.ds(row + 1, rows - row - 1), :] = jnp.zeros((rows - row - 1, nz), jnp.float32)


def filter_kernel(
    slabs_y,
    cells_x,
    cells_y,
    each,
    atoms,
    projs,
    got_ref,
    field_ref,
    rounded_ref,
    level_ref,
    first,
    second,
    partial,
    diagonal,
    coeffs,
    numbers,
    arrived,
):
    group, _, nz = got_ref.shape
    count_x, count_y = diagonal.shape[0], diagonal.shape[1]
    tiles = len(offsets_x)
    slab_cells = cells_x * cells_y
    proj_row = slab_cells * each
    pot_row = proj_row + atoms * projs * tiles
    number_row = pot_row + slab_cells
    scale = 1.0 / filter_half
    factors = [-0.5 * scale * w for w in stencil_weights]
    ring = 1

    copy = pltpu.make_async_copy(got_ref.at[:, number_row, :], numbers, arrived)
    copy.start()

    for field in (first, second):
        for x in (0, ring + count_x):
            field[x] = jnp.zeros(field.shape[1:], jnp.float32)
        for y in (0, ring + count_y):
            field[:, y] = jnp.zeros((field.shape[0],) + field.shape[2:], jnp.float32)

    def take_slab(g, carry):
        x0 = (g // slabs_y) * cells_x
        y0 = (g % slabs_y) * cells_y
        for i in range(cells_x):
            for j in range(cells_y):
                cell = i * cells_y + j
                first[ring + x0 + i, ring + y0 + j] = got_ref[g, pl.ds(cell * each, each), :] * (
                    1.0 / orbital_gain
                )
                diagonal[x0 + i, y0 + j] = got_ref[g, pl.ds(pot_row + cell, 1), :] * (
                    scale / potential_gain
                ) + (3.0 * factors[0] - filter_center * scale)
        return carry

    lax.fori_loop(0, group, take_slab, 0)

    distance = jnp.abs(
        lax.broadcasted_iota(jnp.int32, (nz, nz), 0) - lax.broadcasted_iota(jnp.int32, (nz, nz), 1)
    )
    along_z = jnp.zeros((nz, nz), jnp.float32)
    for step in range(1, reach + 1):
        along_z = jnp.where(distance == step, factors[step], along_z)
    z_high = along_z.astype(jnp.bfloat16)
    z_low = (along_z - z_high.astype(jnp.float32)).astype(jnp.bfloat16)
    z_matrix = jnp.concatenate(
        [
            jnp.concatenate([z_high, z_low], axis=1),
            jnp.concatenate([z_high, jnp.zeros_like(z_high)], axis=1),
        ],
        axis=0,
    )

    def along(cells, at):
        total = None
        for step in range(1, reach + 1):
            near = [cells[n] for n in (at - step, at + step) if 0 <= n < len(cells)]
            if near:
                term = factors[step] * sum(near[1:], near[0])
                total = term if total is None else total + term
        return total

    def apply(source, target, finish, gain):
        def z_part(block, carry):
            rows = source[pl.ds(ring + block * cells_x, cells_x), pl.ds(ring, count_y)]
            flat = rows.reshape(cells_x * count_y * each, nz)
            high = flat.astype(jnp.bfloat16)
            low = (flat - high.astype(jnp.float32)).astype(jnp.bfloat16)
            both = jnp.dot(
                jnp.concatenate([high, low], axis=1), z_matrix, preferred_element_type=jnp.float32
            )
            partial[pl.ds(block * cells_x, cells_x)] = (both[:, :nz] + both[:, nz:]).reshape(
                rows.shape
            )
            return carry

        lax.fori_loop(0, count_x // cells_x, z_part, 0)

        def x_part(y, carry):
            cells = [source[ring + x, ring + y] for x in range(count_x)]
            for x in range(count_x):
                partial[x, y] = partial[x, y] + diagonal[x, y] * cells[x] + along(cells, x)
            return carry

        lax.fori_loop(0, count_y, x_part, 0)

        def y_part(x, carry):
            cells = [source[ring + x, ring + y] for y in range(count_y)]
            for y in range(count_y):
                total = partial[x, y] + along(cells, y)
                target[ring + x, ring + y] = finish(total, target, ring + x, ring + y)
            return carry

        lax.fori_loop(0, count_x, y_part, 0)

        def place_of(g, a):
            at = 2 * atoms * projs + 2 * a
            return (
                ring + numbers[g, at].astype(jnp.int32),
                ring + numbers[g, at + 1].astype(jnp.int32),
            )

        def gather_part(g, carry):
            for a in range(atoms):
                at_x, at_y = place_of(g, a)
                totals = [None] * projs
                for t in range(tiles):
                    tile = source[at_x + offsets_x[t], at_y + offsets_y[t]]
                    for p in range(projs):
                        row = proj_row + (a * tiles + t) * projs + p
                        term = tile * got_ref[g, pl.ds(row, 1), :]
                        totals[p] = term if t == 0 else totals[p] + term
                for p in range(projs):
                    k = a * projs + p
                    energy = numbers[g, k] + numbers[g, atoms * projs + k] * (1.0 / remainder_gain)
                    coeffs[g, k] = jnp.broadcast_to(
                        jnp.sum(totals[p], axis=-1, keepdims=True)
                        * (energy * (gain / projector_gain / projector_gain)),
                        (each, nz),
                    )
            return carry

        lax.fori_loop(0, group, gather_part, 0, unroll=min(group, 4))

        def scatter_part(g, carry):
            for a in range(atoms):
                at_x, at_y = place_of(g, a)
                factor = [coeffs[g, a * projs + p] for p in range(projs)]
                for t in range(tiles):
                    row = proj_row + (a * tiles + t) * projs
                    spread = factor[0] * got_ref[g, pl.ds(row, 1), :]
                    for p in range(1, projs):
                        spread = spread + factor[p] * got_ref[g, pl.ds(row + p, 1), :]
                    to_x = at_x + offsets_x[t]
                    to_y = at_y + offsets_y[t]
                    target[to_x, to_y] = target[to_x, to_y] + spread
            return carry

        lax.fori_loop(0, group, scatter_part, 0, unroll=min(group, 2))

    copy.wait()
    apply(first, second, lambda total, target, x, y: total, scale)

    for x in (0, ring + count_x):
        second[x] = jnp.zeros(second.shape[1:], jnp.float32)
    for y in (0, ring + count_y):
        second[:, y] = jnp.zeros((second.shape[0],) + second.shape[2:], jnp.float32)

    apply(second, first, lambda total, target, x, y: 2.0 * total - target[x, y], 2.0 * scale)

    shares = rounded_ref.shape[0] // group
    portion = slab_cells // shares

    def largest_of(x, largest):
        row = jnp.abs(first[ring + x, pl.ds(ring, count_y)])
        return jnp.maximum(largest, jnp.max(row, axis=0))

    largest = lax.fori_loop(0, count_x, largest_of, jnp.zeros((each, nz), jnp.float32))
    level, gain = level_of(jnp.max(largest))
    level_ref[...] = jnp.full((1, nz), level, jnp.float32)

    def give_slab(g, carry):
        x0 = (g // slabs_y) * cells_x
        y0 = (g % slabs_y) * cells_y
        for i in range(cells_x):
            for j in range(cells_y):
                cell = i * cells_y + j
                value = first[ring + x0 + i, ring + y0 + j]
                field_ref[g, pl.ds(cell * each, each), :] = value * gain
                rounded_ref[
                    (cell // portion) * group + g, :, pl.ds((cell % portion) * nz, nz)
                ] = value.astype(jnp.bfloat16)
        return carry

    lax.fori_loop(0, group, give_slab, 0)


def rows_kernel(cells, parts_ref, level_ref, out_ref):
    _, each, columns = parts_ref.shape
    nz = out_ref.shape[1]
    total = jnp.sum(parts_ref[...], axis=0) / cells
    level, gain = level_of(jnp.max(jnp.abs(total)))
    total = total * gain
    high = total.astype(jnp.bfloat16).astype(jnp.float32)
    low = total - high
    row = 0
    for part in (high, low):
        for column in range(0, columns, nz):
            out_ref[pl.ds(row, each), :] = part[:, column : column + nz]
            row += each
    rest = out_ref.shape[0] - row
    out_ref[pl.ds(row, rest), :] = jnp.zeros((rest, nz), jnp.float32)
    out_ref[pl.ds(row, 1), :] = level_ref[...]
    out_ref[pl.ds(row + 1, 1), :] = jnp.full((1, nz), level, jnp.float32)


def unpack_kernel(each, back_ref, filtered_hbm, gram_hbm, filtered_ref, gram_ref, chunk_sems, sem):
    group, _, nz = back_ref.shape
    slab_cells = filtered_ref.shape[0]
    halves = gram_ref.shape[1] // nz
    chunks = chunk_sems.shape[0]
    chunk = slab_cells // chunks
    base = slab_cells * each
    number_row = base + 2 * halves * each

    def put_rows(g, rows):
        shrink = shrink_of(back_ref[g, pl.ds(number_row + 1, 1), :])
        for half in range(halves):
            row = base + half * each
            value = back_ref[g, pl.ds(row, each), :] + back_ref[g, pl.ds(row + halves * each, each), :]
            gram_ref[rows, half * nz : (half + 1) * nz] = value * shrink

    over_group(group, each, put_rows)
    copies = [pltpu.make_async_copy(gram_ref, gram_hbm, sem)]
    copies[0].start()

    for c in range(chunks):

        def put_cells(g, rows):
            shrink = shrink_of(back_ref[g, pl.ds(number_row, 1), :])
            for cell in range(c * chunk, (c + 1) * chunk):
                filtered_ref[cell, rows, :] = back_ref[g, pl.ds(cell * each, each), :] * shrink

        over_group(group, each, put_cells)
        part = pl.ds(c * chunk, chunk)
        copies.append(
            pltpu.make_async_copy(filtered_ref.at[part], filtered_hbm.at[part], chunk_sems.at[c])
        )
        copies[-1].start()
    for copy in copies:
        copy.wait()


def local(orbitals, potential, projectors, energies, centers):
    band_orbitals, cells_x, cells_y, nz = orbitals.shape
    bands = lax.axis_size("band")
    slabs_x = lax.axis_size("sx")
    slabs_y = lax.axis_size("sy")
    group = slabs_x * slabs_y
    each = band_orbitals // group
    total_orbitals = bands * band_orbitals
    slab_cells = cells_x * cells_y
    grid = (slabs_x * cells_x, slabs_y * cells_y)
    atoms, projs, tiles, _ = projectors.shape

    rows = atoms * projs * tiles + slab_cells + 1
    rows += -rows % 8
    chunks = (orbitals * orbital_gain).astype(jnp.float16)
    chunks = chunks.transpose(1, 2, 0, 3).reshape(slab_cells, group, each, nz)
    chunks = chunks.transpose(1, 0, 2, 3).reshape(group, slab_cells * each, nz)
    shared = pl.pallas_call(
        share_kernel,
        in_specs=[hbm, smem, smem, vmem, vmem],
        out_specs=vmem,
        out_shape=jax.ShapeDtypeStruct((rows, nz), jnp.float32),
        compiler_params=params,
    )(chunks[0, :8].astype(jnp.float32), energies, centers.T, projectors.transpose(0, 2, 1, 3), potential).astype(jnp.float16)
    sent = jnp.concatenate([chunks, jnp.broadcast_to(shared[None], (group, rows, nz))], axis=1)
    got = lax.all_to_all(sent, plane, 0, 0).astype(jnp.float32)

    portion = slab_cells // bands
    ringed = (grid[0] + 2, grid[1] + 2, each, nz)
    field, rounded, level = pl.pallas_call(
        functools.partial(filter_kernel, slabs_y, cells_x, cells_y, each, atoms, projs),
        in_specs=[vmem],
        out_specs=[vmem] * 3,
        out_shape=[
            jax.ShapeDtypeStruct((group, slab_cells * each, nz), jnp.float32),
            jax.ShapeDtypeStruct((bands * group, each, portion * nz), jnp.bfloat16),
            jax.ShapeDtypeStruct((1, nz), jnp.float32),
        ],
        scratch_shapes=[
            pltpu.VMEM(ringed, jnp.float32),
            pltpu.VMEM(ringed, jnp.float32),
            pltpu.VMEM(grid + (each, nz), jnp.float32),
            pltpu.VMEM(grid + (1, nz), jnp.float32),
            pltpu.VMEM((group, atoms * projs, each, nz), jnp.float32),
            pltpu.SMEM((group, nz), jnp.float32),
            pltpu.SemaphoreType.DMA,
        ],
        compiler_params=params,
        cost_estimate=pl.CostEstimate(
            flops=2 * 2 * 40 * grid[0] * grid[1] * each * nz,
            bytes_accessed=8 * grid[0] * grid[1] * each * nz,
            transcendentals=0,
        ),
    )(got)

    pieces = lax.all_to_all(rounded, every, 0, 0)
    matrix = pieces.reshape(total_orbitals, portion * nz)
    sums = lax.dot_general(
        matrix, matrix, (((1,), (1,)), ((), ())), preferred_element_type=jnp.float32
    )
    parts = lax.all_to_all(sums.reshape(bands * group, each, total_orbitals), every, 0, 0)

    halves = total_orbitals // nz
    gram_rows = 2 * halves * each
    block = pl.pallas_call(
        functools.partial(rows_kernel, grid[0] * grid[1] * nz),
        in_specs=[vmem, vmem],
        out_specs=vmem,
        out_shape=jax.ShapeDtypeStruct((gram_rows + 8, nz), jnp.float32),
        compiler_params=params,
    )(parts, level)
    sent = jnp.concatenate(
        [field, jnp.broadcast_to(block[None], (group,) + block.shape)], axis=1
    ).astype(jnp.float16)
    back = lax.all_to_all(sent, plane, 0, 0)

    filtered, gram = pl.pallas_call(
        functools.partial(unpack_kernel, each),
        in_specs=[vmem],
        out_specs=[hbm] * 2,
        out_shape=[
            jax.ShapeDtypeStruct((slab_cells, band_orbitals, nz), jnp.float32),
            jax.ShapeDtypeStruct((band_orbitals, total_orbitals), jnp.float32),
        ],
        scratch_shapes=[
            pltpu.VMEM((slab_cells, band_orbitals, nz), jnp.float32),
            pltpu.VMEM((band_orbitals, total_orbitals), jnp.float32),
            pltpu.SemaphoreType.DMA((cells_x,)),
            pltpu.SemaphoreType.DMA,
        ],
        compiler_params=params,
    )(back.astype(jnp.float32))
    filtered = filtered.reshape(cells_x, cells_y, band_orbitals, nz).transpose(2, 0, 1, 3)
    return (filtered, gram)


def solution(mesh):
    in_specs = (
        P("band", "sx", "sy", None),
        P("sx", "sy", None),
        P(("sx", "sy"), None, None, None),
        P(("sx", "sy"), None),
        P(("sx", "sy"), None),
    )
    out_specs = (P("band", "sx", "sy", None), P("band", None))
    return jax.shard_map(local, mesh=mesh, in_specs=in_specs, out_specs=out_specs, check_vma=False)
```

```python
import functools

import jax
import jax.numpy as jnp
from jax import lax
from jax.experimental import pallas as pl
from jax.experimental.pallas import tpu as pltpu
from jax.sharding import PartitionSpec as P

stencil_weights = (
    -5369.0 / 1800.0,
    12.0 / 7.0,
    -15.0 / 56.0,
    10.0 / 189.0,
    -1.0 / 112.0,
    2.0 / 1925.0,
    -1.0 / 16632.0,
)
filter_center = 6.5
filter_half = 6.0
offsets_x = (0, -1, 1, 0, 0)
offsets_y = (0, 0, 0, -1, 1)
reach = 6
plane = ("sx", "sy")
every = ("band", "sx", "sy")

orbital_gain = 2.0**12
projector_gain = 2.0**17
potential_gain = 2.0**13
remainder_gain = 2.0**10
top = 15
middle = 8
levels = 17

vmem = pl.BlockSpec(memory_space=pltpu.VMEM)
smem = pl.BlockSpec(memory_space=pltpu.SMEM)
hbm = pl.BlockSpec(memory_space=pl.ANY)
params = pltpu.CompilerParams(vmem_limit_bytes=24 * 1024 * 1024)


def level_of(largest):
    level = jnp.float32(0.0)
    scale = jnp.float32(2.0 ** (top + 8 * middle))
    for j in range(levels):
        above = largest >= jnp.float32(2.0 ** (8 * (j - middle)))
        level = jnp.where(above, jnp.float32(j + 1), level)
        scale = jnp.where(above, jnp.float32(2.0 ** (top - 8 * (j + 1 - middle))), scale)
    return level, scale


def shrink_of(level):
    shrink = jnp.full(level.shape, 2.0 ** (-top - 8 * middle), jnp.float32)
    for j in range(levels):
        shrink = jnp.where(level > j, jnp.float32(2.0 ** (8 * (j + 1 - middle) - top)), shrink)
    return shrink


def over_group(group, each, body):
    if each % 8 == 0:

        def step(g, carry):
            body(g, pl.ds(pl.multiple_of(g * each, each), each))
            return carry

        lax.fori_loop(0, group, step, 0, unroll=min(group, 8))
    else:
        for g in range(group):
            body(g, pl.ds(g * each, each))


def share_kernel(_, energies_ref, centers_ref, projectors_ref, potential_ref, out_ref):
    rows, nz = out_ref.shape
    atoms, tiles, projs = projectors_ref.shape[:3]

    row = 0
    for a in range(atoms):
        for t in range(tiles):
            out_ref[pl.ds(row, projs), :] = projectors_ref[a, t] * projector_gain
            row += projs
    for i in range(potential_ref.shape[0]):
        count = potential_ref.shape[1]
        out_ref[pl.ds(row, count), :] = potential_ref[i] * potential_gain
        row += count
    lane = lax.broadcasted_iota(jnp.int32, (1, nz), 1)
    numbers = jnp.zeros((1, nz), jnp.float32)
    for a in range(atoms):
        for p in range(projs):
            numbers = jnp.where(lane == a * projs + p, energies_ref[a, p], numbers)
    high = numbers.astype(jnp.bfloat16).astype(jnp.float32)
    low = (numbers - high) * remainder_gain
    count = atoms * projs
    numbers = high + pltpu.roll(low, count, 1)
    for a in range(atoms):
        for d in range(2):
            here = centers_ref[d, a].astype(jnp.float32)
            numbers = jnp.where(lane == 2 * count + 2 * a + d, here, numbers)
    out_ref[pl.ds(row, 1), :] = numbers
    out_ref[pl.ds(row + 1, rows - row - 1), :] = jnp.zeros((rows - row - 1, nz), jnp.float32)


def filter_kernel(
    slabs_y,
    cells_x,
    cells_y,
    each,
    atoms,
    projs,
    got_ref,
    field_ref,
    rounded_ref,
    level_ref,
    first,
    second,
    partial,
    diagonal,
    coeffs,
    numbers,
    arrived,
):
    group, _, nz = got_ref.shape
    count_x, count_y = diagonal.shape[0], diagonal.shape[1]
    tiles = len(offsets_x)
    slab_cells = cells_x * cells_y
    proj_row = slab_cells * each
    pot_row = proj_row + atoms * projs * tiles
    number_row = pot_row + slab_cells
    scale = 1.0 / filter_half
    factors = [-0.5 * scale * w for w in stencil_weights]
    ring = 1

    copy = pltpu.make_async_copy(got_ref.at[:, number_row, :], numbers, arrived)
    copy.start()

    for field in (first, second):
        for x in (0, ring + count_x):
            field[x] = jnp.zeros(field.shape[1:], jnp.float32)
        for y in (0, ring + count_y):
            field[:, y] = jnp.zeros((field.shape[0],) + field.shape[2:], jnp.float32)

    def take_slab(g, carry):
        x0 = (g // slabs_y) * cells_x
        y0 = (g % slabs_y) * cells_y
        for i in range(cells_x):
            for j in range(cells_y):
                cell = i * cells_y + j
                first[ring + x0 + i, ring + y0 + j] = got_ref[g, pl.ds(cell * each, each), :] * (
                    1.0 / orbital_gain
                )
                diagonal[x0 + i, y0 + j] = got_ref[g, pl.ds(pot_row + cell, 1), :] * (
                    scale / potential_gain
                ) + (3.0 * factors[0] - filter_center * scale)
        return carry

    lax.fori_loop(0, group, take_slab, 0)

    distance = jnp.abs(
        lax.broadcasted_iota(jnp.int32, (nz, nz), 0) - lax.broadcasted_iota(jnp.int32, (nz, nz), 1)
    )
    along_z = jnp.zeros((nz, nz), jnp.float32)
    for step in range(1, reach + 1):
        along_z = jnp.where(distance == step, factors[step], along_z)
    z_high = along_z.astype(jnp.bfloat16)
    z_low = (along_z - z_high.astype(jnp.float32)).astype(jnp.bfloat16)
    z_matrix = jnp.concatenate(
        [
            jnp.concatenate([z_high, z_low], axis=1),
            jnp.concatenate([z_high, jnp.zeros_like(z_high)], axis=1),
        ],
        axis=0,
    )

    def along(cells, at):
        total = None
        for step in range(1, reach + 1):
            near = [cells[n] for n in (at - step, at + step) if 0 <= n < len(cells)]
            if near:
                term = factors[step] * sum(near[1:], near[0])
                total = term if total is None else total + term
        return total

    def apply(source, target, finish, gain):
        def xz_part(y, carry):
            column = source[pl.ds(ring, count_x), ring + y]
            flat = column.reshape(count_x * each, nz)
            high = flat.astype(jnp.bfloat16)
            low = (flat - high.astype(jnp.float32)).astype(jnp.bfloat16)
            both = jnp.dot(
                jnp.concatenate([high, low], axis=1), z_matrix, preferred_element_type=jnp.float32
            )
            along_z = (both[:, :nz] + both[:, nz:]).reshape(column.shape)
            cells = [column[x] for x in range(count_x)]
            for x in range(count_x):
                partial[x, y] = along_z[x] + diagonal[x, y] * cells[x] + along(cells, x)
            return carry

        lax.fori_loop(0, count_y, xz_part, 0, unroll=2)

        def y_part(x, carry):
            cells = [source[ring + x, ring + y] for y in range(count_y)]
            for y in range(count_y):
                total = partial[x, y] + along(cells, y)
                target[ring + x, ring + y] = finish(total, target, ring + x, ring + y)
            return carry

        lax.fori_loop(0, count_x, y_part, 0, unroll=2)

        def place_of(g, a):
            at = 2 * atoms * projs + 2 * a
            return (
                ring + numbers[g, at].astype(jnp.int32),
                ring + numbers[g, at + 1].astype(jnp.int32),
            )

        def gather_part(g, carry):
            for a in range(atoms):
                at_x, at_y = place_of(g, a)
                totals = [None] * projs
                for t in range(tiles):
                    tile = source[at_x + offsets_x[t], at_y + offsets_y[t]]
                    for p in range(projs):
                        row = proj_row + (a * tiles + t) * projs + p
                        term = tile * got_ref[g, pl.ds(row, 1), :]
                        totals[p] = term if t == 0 else totals[p] + term
                for p in range(projs):
                    k = a * projs + p
                    energy = numbers[g, k] + numbers[g, atoms * projs + k] * (1.0 / remainder_gain)
                    coeffs[g, k] = jnp.broadcast_to(
                        jnp.sum(totals[p], axis=-1, keepdims=True)
                        * (energy * (gain / projector_gain / projector_gain)),
                        (each, nz),
                    )
            return carry

        lax.fori_loop(0, group, gather_part, 0, unroll=min(group, 4))

        def scatter_part(g, carry):
            for a in range(atoms):
                at_x, at_y = place_of(g, a)
                factor = [coeffs[g, a * projs + p] for p in range(projs)]
                for t in range(tiles):
                    row = proj_row + (a * tiles + t) * projs
                    spread = factor[0] * got_ref[g, pl.ds(row, 1), :]
                    for p in range(1, projs):
                        spread = spread + factor[p] * got_ref[g, pl.ds(row + p, 1), :]
                    to_x = at_x + offsets_x[t]
                    to_y = at_y + offsets_y[t]
                    target[to_x, to_y] = target[to_x, to_y] + spread
            return carry

        lax.fori_loop(0, group, scatter_part, 0, unroll=min(group, 2))

    copy.wait()
    apply(first, second, lambda total, target, x, y: total, scale)

    for x in (0, ring + count_x):
        second[x] = jnp.zeros(second.shape[1:], jnp.float32)
    for y in (0, ring + count_y):
        second[:, y] = jnp.zeros((second.shape[0],) + second.shape[2:], jnp.float32)

    apply(second, first, lambda total, target, x, y: 2.0 * total - target[x, y], 2.0 * scale)

    shares = rounded_ref.shape[0] // group
    portion = slab_cells // shares

    def largest_of(x, largest):
        row = jnp.abs(first[ring + x, pl.ds(ring, count_y)])
        return jnp.maximum(largest, jnp.max(row, axis=0))

    largest = lax.fori_loop(0, count_x, largest_of, jnp.zeros((each, nz), jnp.float32))
    level, gain = level_of(jnp.max(largest))
    level_ref[...] = jnp.full((1, nz), level, jnp.float32)

    def give_slab(g, carry):
        x0 = (g // slabs_y) * cells_x
        y0 = (g % slabs_y) * cells_y
        for i in range(cells_x):
            for j in range(cells_y):
                cell = i * cells_y + j
                value = first[ring + x0 + i, ring + y0 + j]
                field_ref[g, pl.ds(cell * each, each), :] = value * gain
                rounded_ref[
                    (cell // portion) * group + g, :, pl.ds((cell % portion) * nz, nz)
                ] = value.astype(jnp.bfloat16)
        return carry

    lax.fori_loop(0, group, give_slab, 0)


def gram_kernel(each, matrix_ref, out_ref):
    matrix = matrix_ref[...]
    sums = lax.dot_general(
        matrix, matrix, (((1,), (1,)), ((), ())), preferred_element_type=jnp.float32
    )
    level, gain = level_of(jnp.max(jnp.abs(sums)))
    row = lax.broadcasted_iota(jnp.int32, sums.shape, 0)
    column = lax.broadcasted_iota(jnp.int32, sums.shape, 1)
    spare = (column == row - 1) & (row % each == 1)
    out_ref[...] = jnp.where(spare, level, sums * gain)


def rows_kernel(cells, first_ref, parts_ref, level_ref, out_ref):
    count, each, columns = parts_ref.shape
    nz = out_ref.shape[1]
    if each > 1:
        row = lax.broadcasted_iota(jnp.int32, (each, columns), 0)
        column = lax.broadcasted_iota(jnp.int32, (each, columns), 1)
        spare = (row == 1) & (column == first_ref[0])
        twin = (row == 0) & (column == first_ref[0] + 1)

        def entry(block, place):
            picked = jnp.where(place, block, 0.0)
            return jnp.sum(jnp.sum(picked, axis=0, keepdims=True), axis=1, keepdims=True)

        total = jnp.zeros((each, columns), jnp.float32)
        for source in range(count):
            block = parts_ref[source]
            total = total + block * shrink_of(entry(block, spare))
        total = jnp.where(spare, entry(total, twin), total)
    else:
        total = jnp.sum(parts_ref[...], axis=0)
    total = total / cells
    level, gain = level_of(jnp.max(jnp.abs(total)))
    total = total * gain
    high = total.astype(jnp.bfloat16).astype(jnp.float32)
    low = total - high
    row = 0
    for part in (high, low):
        for column in range(0, columns, nz):
            out_ref[pl.ds(row, each), :] = part[:, column : column + nz]
            row += each
    rest = out_ref.shape[0] - row
    out_ref[pl.ds(row, rest), :] = jnp.zeros((rest, nz), jnp.float32)
    out_ref[pl.ds(row, 1), :] = level_ref[...]
    out_ref[pl.ds(row + 1, 1), :] = jnp.full((1, nz), level, jnp.float32)


def unpack_kernel(each, back_ref, filtered_hbm, gram_hbm, filtered_ref, gram_ref, chunk_sems, sem):
    group, _, nz = back_ref.shape
    slab_cells = filtered_ref.shape[0]
    halves = gram_ref.shape[1] // nz
    chunks = chunk_sems.shape[0]
    chunk = slab_cells // chunks
    base = slab_cells * each
    number_row = base + 2 * halves * each

    def put_rows(g, rows):
        shrink = shrink_of(back_ref[g, pl.ds(number_row + 1, 1), :])
        for half in range(halves):
            row = base + half * each
            value = back_ref[g, pl.ds(row, each), :] + back_ref[g, pl.ds(row + halves * each, each), :]
            gram_ref[rows, half * nz : (half + 1) * nz] = value * shrink

    over_group(group, each, put_rows)
    copies = [pltpu.make_async_copy(gram_ref, gram_hbm, sem)]
    copies[0].start()

    for c in range(chunks):

        def put_cells(g, rows):
            shrink = shrink_of(back_ref[g, pl.ds(number_row, 1), :])
            for cell in range(c * chunk, (c + 1) * chunk):
                filtered_ref[cell, rows, :] = back_ref[g, pl.ds(cell * each, each), :] * shrink

        over_group(group, each, put_cells)
        part = pl.ds(c * chunk, chunk)
        copies.append(
            pltpu.make_async_copy(filtered_ref.at[part], filtered_hbm.at[part], chunk_sems.at[c])
        )
        copies[-1].start()
    for copy in copies:
        copy.wait()


def local(orbitals, potential, projectors, energies, centers):
    band_orbitals, cells_x, cells_y, nz = orbitals.shape
    bands = lax.axis_size("band")
    slabs_x = lax.axis_size("sx")
    slabs_y = lax.axis_size("sy")
    group = slabs_x * slabs_y
    each = band_orbitals // group
    total_orbitals = bands * band_orbitals
    slab_cells = cells_x * cells_y
    grid = (slabs_x * cells_x, slabs_y * cells_y)
    atoms, projs, tiles, _ = projectors.shape

    rows = atoms * projs * tiles + slab_cells + 1
    rows += -rows % 8
    chunks = (orbitals * orbital_gain).astype(jnp.float16)
    chunks = chunks.transpose(1, 2, 0, 3).reshape(slab_cells, group, each, nz)
    chunks = chunks.transpose(1, 0, 2, 3).reshape(group, slab_cells * each, nz)
    shared = pl.pallas_call(
        share_kernel,
        in_specs=[hbm, smem, smem, vmem, vmem],
        out_specs=vmem,
        out_shape=jax.ShapeDtypeStruct((rows, nz), jnp.float32),
        compiler_params=params,
    )(chunks[0, :8].astype(jnp.float32), energies, centers.T, projectors.transpose(0, 2, 1, 3), potential).astype(jnp.float16)
    sent = jnp.concatenate([chunks, jnp.broadcast_to(shared[None], (group, rows, nz))], axis=1)
    got = lax.all_to_all(sent, plane, 0, 0).astype(jnp.float32)

    portion = slab_cells // bands
    ringed = (grid[0] + 2, grid[1] + 2, each, nz)
    field, rounded, level = pl.pallas_call(
        functools.partial(filter_kernel, slabs_y, cells_x, cells_y, each, atoms, projs),
        in_specs=[vmem],
        out_specs=[vmem] * 3,
        out_shape=[
            jax.ShapeDtypeStruct((group, slab_cells * each, nz), jnp.float32),
            jax.ShapeDtypeStruct((bands * group, each, portion * nz), jnp.bfloat16),
            jax.ShapeDtypeStruct((1, nz), jnp.float32),
        ],
        scratch_shapes=[
            pltpu.VMEM(ringed, jnp.float32),
            pltpu.VMEM(ringed, jnp.float32),
            pltpu.VMEM(grid + (each, nz), jnp.float32),
            pltpu.VMEM(grid + (1, nz), jnp.float32),
            pltpu.VMEM((group, atoms * projs, each, nz), jnp.float32),
            pltpu.SMEM((group, nz), jnp.float32),
            pltpu.SemaphoreType.DMA,
        ],
        compiler_params=params,
        cost_estimate=pl.CostEstimate(
            flops=2 * 2 * 40 * grid[0] * grid[1] * each * nz,
            bytes_accessed=8 * grid[0] * grid[1] * each * nz,
            transcendentals=0,
        ),
    )(got)

    pieces = lax.all_to_all(rounded, every, 0, 0)
    matrix = pieces.reshape(total_orbitals, portion * nz)
    spread = (bands * group, each, total_orbitals)
    if each > 1:
        sums = pl.pallas_call(
            functools.partial(gram_kernel, each),
            in_specs=[vmem],
            out_specs=vmem,
            out_shape=jax.ShapeDtypeStruct((total_orbitals, total_orbitals), jnp.float32),
            compiler_params=params,
        )(matrix)
        sums = sums.astype(jnp.float16).reshape(spread)
    else:
        sums = lax.dot_general(
            matrix, matrix, (((1,), (1,)), ((), ())), preferred_element_type=jnp.float32
        ).reshape(spread)
    parts = lax.all_to_all(sums, every, 0, 0).astype(jnp.float32)
    field, parts = lax.optimization_barrier((field, parts))
    first_row = lax.axis_index(every).astype(jnp.int32).reshape(1) * each

    halves = total_orbitals // nz
    gram_rows = 2 * halves * each
    block = pl.pallas_call(
        functools.partial(rows_kernel, grid[0] * grid[1] * nz),
        in_specs=[smem, vmem, vmem],
        out_specs=vmem,
        out_shape=jax.ShapeDtypeStruct((gram_rows + 8, nz), jnp.float32),
        compiler_params=params,
    )(first_row, parts, level)
    sent = jnp.concatenate(
        [field, jnp.broadcast_to(block[None], (group,) + block.shape)], axis=1
    ).astype(jnp.float16)
    back = lax.all_to_all(sent, plane, 0, 0)

    filtered, gram = pl.pallas_call(
        functools.partial(unpack_kernel, each),
        in_specs=[vmem],
        out_specs=[hbm] * 2,
        out_shape=[
            jax.ShapeDtypeStruct((slab_cells, band_orbitals, nz), jnp.float32),
            jax.ShapeDtypeStruct((band_orbitals, total_orbitals), jnp.float32),
        ],
        scratch_shapes=[
            pltpu.VMEM((slab_cells, band_orbitals, nz), jnp.float32),
            pltpu.VMEM((band_orbitals, total_orbitals), jnp.float32),
            pltpu.SemaphoreType.DMA((cells_x,)),
            pltpu.SemaphoreType.DMA,
        ],
        compiler_params=params,
    )(back.astype(jnp.float32))
    filtered = filtered.reshape(cells_x, cells_y, band_orbitals, nz).transpose(2, 0, 1, 3)
    return (filtered, gram)


def solution(mesh):
    in_specs = (
        P("band", "sx", "sy", None),
        P("sx", "sy", None),
        P(("sx", "sy"), None, None, None),
        P(("sx", "sy"), None),
        P(("sx", "sy"), None),
    )
    out_specs = (P("band", "sx", "sy", None), P("band", None))
    return jax.shard_map(local, mesh=mesh, in_specs=in_specs, out_specs=out_specs, check_vma=False)
```

```python
import functools

import jax
import jax.numpy as jnp
from jax import lax
from jax.experimental import pallas as pl
from jax.experimental.pallas import tpu as pltpu
from jax.sharding import PartitionSpec as P

stencil_weights = (
    -5369.0 / 1800.0,
    12.0 / 7.0,
    -15.0 / 56.0,
    10.0 / 189.0,
    -1.0 / 112.0,
    2.0 / 1925.0,
    -1.0 / 16632.0,
)
filter_center = 6.5
filter_half = 6.0
offsets_x = (0, -1, 1, 0, 0)
offsets_y = (0, 0, 0, -1, 1)
reach = 6
plane = ("sx", "sy")
every = ("band", "sx", "sy")

orbital_gain = 2.0**12
projector_gain = 2.0**17
potential_gain = 2.0**13
remainder_gain = 2.0**10
top = 15
middle = 8
levels = 17

vmem = pl.BlockSpec(memory_space=pltpu.VMEM)
smem = pl.BlockSpec(memory_space=pltpu.SMEM)
hbm = pl.BlockSpec(memory_space=pl.ANY)
params = pltpu.CompilerParams(vmem_limit_bytes=24 * 1024 * 1024)


def level_of(largest):
    level = jnp.float32(0.0)
    scale = jnp.float32(2.0 ** (top + 8 * middle))
    for j in range(levels):
        above = largest >= jnp.float32(2.0 ** (8 * (j - middle)))
        level = jnp.where(above, jnp.float32(j + 1), level)
        scale = jnp.where(above, jnp.float32(2.0 ** (top - 8 * (j + 1 - middle))), scale)
    return level, scale


def shrink_of(level):
    shrink = jnp.full(level.shape, 2.0 ** (-top - 8 * middle), jnp.float32)
    for j in range(levels):
        shrink = jnp.where(level > j, jnp.float32(2.0 ** (8 * (j + 1 - middle) - top)), shrink)
    return shrink


def share_kernel(_, energies_ref, centers_ref, projectors_ref, potential_ref, out_ref):
    rows, nz = out_ref.shape
    atoms, tiles, projs = projectors_ref.shape[:3]

    row = 0
    for a in range(atoms):
        for t in range(tiles):
            out_ref[pl.ds(row, projs), :] = projectors_ref[a, t] * projector_gain
            row += projs
    for i in range(potential_ref.shape[0]):
        count = potential_ref.shape[1]
        out_ref[pl.ds(row, count), :] = potential_ref[i] * potential_gain
        row += count
    lane = lax.broadcasted_iota(jnp.int32, (1, nz), 1)
    numbers = jnp.zeros((1, nz), jnp.float32)
    for a in range(atoms):
        for p in range(projs):
            numbers = jnp.where(lane == a * projs + p, energies_ref[a, p], numbers)
    high = numbers.astype(jnp.bfloat16).astype(jnp.float32)
    low = (numbers - high) * remainder_gain
    count = atoms * projs
    numbers = high + pltpu.roll(low, count, 1)
    for a in range(atoms):
        for d in range(2):
            here = centers_ref[d, a].astype(jnp.float32)
            numbers = jnp.where(lane == 2 * count + 2 * a + d, here, numbers)
    out_ref[pl.ds(row, 1), :] = numbers
    out_ref[pl.ds(row + 1, rows - row - 1), :] = jnp.zeros((rows - row - 1, nz), jnp.float32)


def filter_kernel(
    slabs_y,
    cells_x,
    cells_y,
    each,
    atoms,
    projs,
    me_ref,
    got_ref,
    field_ref,
    rounded_ref,
    first,
    second,
    partial,
    diagonal,
    coeffs,
    numbers,
    arrived,
):
    group, _, nz = got_ref.shape
    count_x, count_y = diagonal.shape[0], diagonal.shape[1]
    tiles = len(offsets_x)
    slab_cells = cells_x * cells_y
    proj_row = slab_cells * each
    pot_row = proj_row + atoms * projs * tiles
    number_row = pot_row + slab_cells
    scale = 1.0 / filter_half
    factors = [-0.5 * scale * w for w in stencil_weights]
    ring = 1

    copy = pltpu.make_async_copy(got_ref.at[:, number_row, :], numbers, arrived)
    copy.start()

    for field in (first, second):
        for x in (0, ring + count_x):
            field[x] = jnp.zeros(field.shape[1:], jnp.float32)
        for y in (0, ring + count_y):
            field[:, y] = jnp.zeros((field.shape[0],) + field.shape[2:], jnp.float32)

    def take_slab(g, carry):
        x0 = (g // slabs_y) * cells_x
        y0 = (g % slabs_y) * cells_y
        for i in range(cells_x):
            for j in range(cells_y):
                cell = i * cells_y + j
                first[ring + x0 + i, ring + y0 + j] = got_ref[g, pl.ds(cell * each, each), :] * (
                    1.0 / orbital_gain
                )
                diagonal[x0 + i, y0 + j] = got_ref[g, pl.ds(pot_row + cell, 1), :] * (
                    scale / potential_gain
                ) + (3.0 * factors[0] - filter_center * scale)
        return carry

    lax.fori_loop(0, group, take_slab, 0)

    distance = jnp.abs(
        lax.broadcasted_iota(jnp.int32, (nz, nz), 0) - lax.broadcasted_iota(jnp.int32, (nz, nz), 1)
    )
    along_z = jnp.zeros((nz, nz), jnp.float32)
    for step in range(1, reach + 1):
        along_z = jnp.where(distance == step, factors[step], along_z)
    z_high = along_z.astype(jnp.bfloat16)
    z_low = (along_z - z_high.astype(jnp.float32)).astype(jnp.bfloat16)
    z_matrix = jnp.concatenate(
        [
            jnp.concatenate([z_high, z_low], axis=1),
            jnp.concatenate([z_high, jnp.zeros_like(z_high)], axis=1),
        ],
        axis=0,
    )

    def along(cells, at):
        total = None
        for step in range(1, reach + 1):
            near = [cells[n] for n in (at - step, at + step) if 0 <= n < len(cells)]
            if near:
                term = factors[step] * sum(near[1:], near[0])
                total = term if total is None else total + term
        return total

    def apply(source, target, finish, gain):
        def xz_part(y, carry):
            column = source[pl.ds(ring, count_x), ring + y]
            flat = column.reshape(count_x * each, nz)
            high = flat.astype(jnp.bfloat16)
            low = (flat - high.astype(jnp.float32)).astype(jnp.bfloat16)
            both = jnp.dot(
                jnp.concatenate([high, low], axis=1), z_matrix, preferred_element_type=jnp.float32
            )
            along_z = (both[:, :nz] + both[:, nz:]).reshape(column.shape)
            cells = [column[x] for x in range(count_x)]
            for x in range(count_x):
                partial[x, y] = along_z[x] + diagonal[x, y] * cells[x] + along(cells, x)
            return carry

        lax.fori_loop(0, count_y, xz_part, 0, unroll=2)

        def y_part(x, carry):
            cells = [source[ring + x, ring + y] for y in range(count_y)]
            for y in range(count_y):
                total = partial[x, y] + along(cells, y)
                target[ring + x, ring + y] = finish(total, target, ring + x, ring + y)
            return carry

        lax.fori_loop(0, count_x, y_part, 0, unroll=2)

        def place_of(g, a):
            at = 2 * atoms * projs + 2 * a
            return (
                ring + numbers[g, at].astype(jnp.int32),
                ring + numbers[g, at + 1].astype(jnp.int32),
            )

        def gather_part(g, carry):
            for a in range(atoms):
                at_x, at_y = place_of(g, a)
                totals = [None] * projs
                for t in range(tiles):
                    tile = source[at_x + offsets_x[t], at_y + offsets_y[t]]
                    for p in range(projs):
                        row = proj_row + (a * tiles + t) * projs + p
                        term = tile * got_ref[g, pl.ds(row, 1), :]
                        totals[p] = term if t == 0 else totals[p] + term
                for p in range(projs):
                    k = a * projs + p
                    energy = numbers[g, k] + numbers[g, atoms * projs + k] * (1.0 / remainder_gain)
                    coeffs[g, k] = jnp.broadcast_to(
                        jnp.sum(totals[p], axis=-1, keepdims=True)
                        * (energy * (gain / projector_gain / projector_gain)),
                        (each, nz),
                    )
            return carry

        lax.fori_loop(0, group, gather_part, 0, unroll=min(group, 4))

        def scatter_part(g, carry):
            for a in range(atoms):
                at_x, at_y = place_of(g, a)
                factor = [coeffs[g, a * projs + p] for p in range(projs)]
                for t in range(tiles):
                    row = proj_row + (a * tiles + t) * projs
                    spread = factor[0] * got_ref[g, pl.ds(row, 1), :]
                    for p in range(1, projs):
                        spread = spread + factor[p] * got_ref[g, pl.ds(row + p, 1), :]
                    to_x = at_x + offsets_x[t]
                    to_y = at_y + offsets_y[t]
                    target[to_x, to_y] = target[to_x, to_y] + spread
            return carry

        lax.fori_loop(0, group, scatter_part, 0, unroll=min(group, 2))

    copy.wait()
    apply(first, second, lambda total, target, x, y: total, scale)

    for x in (0, ring + count_x):
        second[x] = jnp.zeros(second.shape[1:], jnp.float32)
    for y in (0, ring + count_y):
        second[:, y] = jnp.zeros((second.shape[0],) + second.shape[2:], jnp.float32)

    apply(second, first, lambda total, target, x, y: 2.0 * total - target[x, y], 2.0 * scale)

    shares = rounded_ref.shape[0] // group
    portion = slab_cells // shares

    def largest_of(x, largest):
        row = jnp.abs(first[ring + x, pl.ds(ring, count_y)])
        return jnp.maximum(largest, jnp.max(row, axis=0))

    largest = lax.fori_loop(0, count_x, largest_of, jnp.zeros((each, nz), jnp.float32))
    level, gain = level_of(jnp.max(largest))
    level_rows = jnp.full((8, nz), level, jnp.float32)

    def give_slab(g, carry):
        slot = jnp.bitwise_xor(g, me_ref[0])
        field_ref[slot, pl.ds(slab_cells * each, 8), :] = level_rows
        x0 = (g // slabs_y) * cells_x
        y0 = (g % slabs_y) * cells_y
        for i in range(cells_x):
            for j in range(cells_y):
                cell = i * cells_y + j
                value = first[ring + x0 + i, ring + y0 + j]
                field_ref[slot, pl.ds(cell * each, each), :] = value * gain
                rounded_ref[
                    (cell // portion) * group + g, :, pl.ds((cell % portion) * nz, nz)
                ] = value.astype(jnp.bfloat16)
        return carry

    lax.fori_loop(0, group, give_slab, 0)


def gram_kernel(each, matrix_ref, out_ref):
    matrix = matrix_ref[...]
    sums = lax.dot_general(
        matrix, matrix, (((1,), (1,)), ((), ())), preferred_element_type=jnp.float32
    )
    level, gain = level_of(jnp.max(jnp.abs(sums)))
    row = lax.broadcasted_iota(jnp.int32, sums.shape, 0)
    column = lax.broadcasted_iota(jnp.int32, sums.shape, 1)
    spare = (column == row - 1) & (row % each == 1)
    out_ref[...] = jnp.where(spare, level, sums * gain)


def rows_kernel(cells, first_ref, parts_ref, out_ref):
    count, each, columns = parts_ref.shape
    if each > 1:
        row = lax.broadcasted_iota(jnp.int32, (each, columns), 0)
        column = lax.broadcasted_iota(jnp.int32, (each, columns), 1)
        spare = (row == 1) & (column == first_ref[0])
        twin = (row == 0) & (column == first_ref[0] + 1)

        def entry(block, place):
            picked = jnp.where(place, block, 0.0)
            return jnp.sum(jnp.sum(picked, axis=0, keepdims=True), axis=1, keepdims=True)

        total = jnp.zeros((each, columns), jnp.float32)
        for source in range(count):
            block = parts_ref[source]
            total = total + block * shrink_of(entry(block, spare))
        total = jnp.where(spare, entry(total, twin), total)
    else:
        total = jnp.sum(parts_ref[...], axis=0)
    out_ref[...] = total / cells


def unpack_kernel(each, me_ref, pieces_ref, filtered_hbm, filtered_ref, chunk_sems):
    group, _, nz = pieces_ref.shape
    slab_cells = filtered_ref.shape[0]
    chunks = chunk_sems.shape[0]
    chunk = slab_cells // chunks
    copies = []
    for c in range(chunks):
        for slot in range(group):
            shrink = shrink_of(pieces_ref[slot, pl.ds(slab_cells * each, 1), :])
            if each % 8 == 0:
                source = jnp.bitwise_xor(me_ref[0], slot)
                rows = pl.ds(pl.multiple_of(source * each, each), each)
            else:
                rows = pl.ds(slot * each, each)
            for cell in range(c * chunk, (c + 1) * chunk):
                filtered_ref[cell, rows, :] = pieces_ref[slot, pl.ds(cell * each, each), :] * shrink
        part = pl.ds(c * chunk, chunk)
        copies.append(
            pltpu.make_async_copy(filtered_ref.at[part], filtered_hbm.at[part], chunk_sems.at[c])
        )
        copies[-1].start()
    for copy in copies:
        copy.wait()


def swap_stages(slabs_x, slabs_y):
    stages = [("sx", 1 << k) for k in range(slabs_x.bit_length() - 1)]
    stages = stages[1:] + [("sy", 1 << k) for k in range(slabs_y.bit_length() - 1)] + stages[:1]
    return [(axis, bit, bit * (slabs_y if axis == "sx" else 1)) for axis, bit in stages]


def swap_pieces(field, stages):
    group = field.shape[0]
    held = {(r, 0): field[r] for r in range(group)}
    for axis, bit, value in stages:
        leaving = sorted(key for key in held if key[0] & value)
        pairs = [(i, i ^ bit) for i in range(lax.axis_size(axis))]
        sent = jnp.stack([held[key].astype(jnp.float16) for key in leaving])
        came = lax.ppermute(sent, axis, pairs)
        held = {key: piece for key, piece in held.items() if not key[0] & value}
        for i, (to, origin) in enumerate(leaving):
            held[(to ^ value, origin ^ value)] = came[i]
    return jnp.stack([held[(0, r)].astype(jnp.float32) for r in range(group)])


def local(orbitals, potential, projectors, energies, centers):
    band_orbitals, cells_x, cells_y, nz = orbitals.shape
    bands = lax.axis_size("band")
    slabs_x = lax.axis_size("sx")
    slabs_y = lax.axis_size("sy")
    group = slabs_x * slabs_y
    each = band_orbitals // group
    total_orbitals = bands * band_orbitals
    slab_cells = cells_x * cells_y
    grid = (slabs_x * cells_x, slabs_y * cells_y)
    atoms, projs, tiles, _ = projectors.shape

    rows = atoms * projs * tiles + slab_cells + 1
    rows += -rows % 8
    chunks = (orbitals * orbital_gain).astype(jnp.float16)
    chunks = chunks.transpose(1, 2, 0, 3).reshape(slab_cells, group, each, nz)
    chunks = chunks.transpose(1, 0, 2, 3).reshape(group, slab_cells * each, nz)
    shared = pl.pallas_call(
        share_kernel,
        in_specs=[hbm, smem, smem, vmem, vmem],
        out_specs=vmem,
        out_shape=jax.ShapeDtypeStruct((rows, nz), jnp.float32),
        compiler_params=params,
    )(chunks[0, :8].astype(jnp.float32), energies, centers.T, projectors.transpose(0, 2, 1, 3), potential).astype(jnp.float16)
    sent = jnp.concatenate([chunks, jnp.broadcast_to(shared[None], (group, rows, nz))], axis=1)
    got = lax.all_to_all(sent, plane, 0, 0).astype(jnp.float32)

    stages = swap_stages(slabs_x, slabs_y)
    by_swaps = group <= 8 and each % 8 == 0 and group == 1 << len(stages)
    place = lax.axis_index(plane).astype(jnp.int32).reshape(1)
    me = place if by_swaps else jnp.zeros((1,), jnp.int32)

    portion = slab_cells // bands
    ringed = (grid[0] + 2, grid[1] + 2, each, nz)
    field, rounded = pl.pallas_call(
        functools.partial(filter_kernel, slabs_y, cells_x, cells_y, each, atoms, projs),
        in_specs=[smem, vmem],
        out_specs=[vmem] * 2,
        out_shape=[
            jax.ShapeDtypeStruct((group, slab_cells * each + 8, nz), jnp.float32),
            jax.ShapeDtypeStruct((bands * group, each, portion * nz), jnp.bfloat16),
        ],
        scratch_shapes=[
            pltpu.VMEM(ringed, jnp.float32),
            pltpu.VMEM(ringed, jnp.float32),
            pltpu.VMEM(grid + (each, nz), jnp.float32),
            pltpu.VMEM(grid + (1, nz), jnp.float32),
            pltpu.VMEM((group, atoms * projs, each, nz), jnp.float32),
            pltpu.SMEM((group, nz), jnp.float32),
            pltpu.SemaphoreType.DMA,
        ],
        compiler_params=params,
        cost_estimate=pl.CostEstimate(
            flops=2 * 2 * 40 * grid[0] * grid[1] * each * nz,
            bytes_accessed=8 * grid[0] * grid[1] * each * nz,
            transcendentals=0,
        ),
    )(me, got)

    if by_swaps:
        pieces = swap_pieces(field, stages)
    else:
        pieces = lax.all_to_all(field.astype(jnp.float16), plane, 0, 0).astype(jnp.float32)

    matrix = lax.all_to_all(rounded, every, 0, 0).reshape(total_orbitals, portion * nz)
    spread = (bands * group, each, total_orbitals)
    if each > 1:
        sums = pl.pallas_call(
            functools.partial(gram_kernel, each),
            in_specs=[vmem],
            out_specs=vmem,
            out_shape=jax.ShapeDtypeStruct((total_orbitals, total_orbitals), jnp.float32),
            compiler_params=params,
        )(matrix)
        sums = sums.astype(jnp.float16).reshape(spread)
    else:
        sums = lax.dot_general(
            matrix, matrix, (((1,), (1,)), ((), ())), preferred_element_type=jnp.float32
        ).reshape(spread)
    parts = lax.all_to_all(sums, every, 0, 0).astype(jnp.float32)
    first_row = (lax.axis_index("band").astype(jnp.int32) * group + place) * each
    rows = pl.pallas_call(
        functools.partial(rows_kernel, grid[0] * grid[1] * nz),
        in_specs=[smem, vmem],
        out_specs=vmem,
        out_shape=jax.ShapeDtypeStruct((each, total_orbitals), jnp.float32),
        compiler_params=params,
    )(first_row, parts)
    gram = lax.all_to_all(jnp.broadcast_to(rows[None], (group,) + rows.shape), plane, 0, 0)
    gram = gram.reshape(band_orbitals, total_orbitals)

    filtered = pl.pallas_call(
        functools.partial(unpack_kernel, each),
        in_specs=[smem, vmem],
        out_specs=hbm,
        out_shape=jax.ShapeDtypeStruct((slab_cells, band_orbitals, nz), jnp.float32),
        scratch_shapes=[
            pltpu.VMEM((slab_cells, band_orbitals, nz), jnp.float32),
            pltpu.SemaphoreType.DMA((cells_x,)),
        ],
        compiler_params=params,
    )(me, pieces)
    filtered = filtered.reshape(cells_x, cells_y, band_orbitals, nz).transpose(2, 0, 1, 3)
    return (filtered, gram)


def solution(mesh):
    in_specs = (
        P("band", "sx", "sy", None),
        P("sx", "sy", None),
        P(("sx", "sy"), None, None, None),
        P(("sx", "sy"), None),
        P(("sx", "sy"), None),
    )
    out_specs = (P("band", "sx", "sy", None), P("band", None))
    return jax.shard_map(local, mesh=mesh, in_specs=in_specs, out_specs=out_specs, check_vma=False)
```

```python
import functools

import jax
import jax.numpy as jnp
from jax import lax
from jax.experimental import pallas as pl
from jax.experimental.pallas import tpu as pltpu
from jax.sharding import PartitionSpec as P

stencil_weights = (
    -5369.0 / 1800.0,
    12.0 / 7.0,
    -15.0 / 56.0,
    10.0 / 189.0,
    -1.0 / 112.0,
    2.0 / 1925.0,
    -1.0 / 16632.0,
)
filter_center = 6.5
filter_half = 6.0
offsets_x = (0, -1, 1, 0, 0)
offsets_y = (0, 0, 0, -1, 1)
reach = 6
plane = ("sx", "sy")
every = ("band", "sx", "sy")

orbital_gain = 2.0**12
projector_gain = 2.0**17
potential_gain = 2.0**13
remainder_gain = 2.0**10
top = 15
middle = 8
levels = 17

vmem = pl.BlockSpec(memory_space=pltpu.VMEM)
smem = pl.BlockSpec(memory_space=pltpu.SMEM)
hbm = pl.BlockSpec(memory_space=pl.ANY)
params = pltpu.CompilerParams(vmem_limit_bytes=24 * 1024 * 1024)


def level_of(largest):
    level = jnp.float32(0.0)
    scale = jnp.float32(2.0 ** (top + 8 * middle))
    for j in range(levels):
        above = largest >= jnp.float32(2.0 ** (8 * (j - middle)))
        level = jnp.where(above, jnp.float32(j + 1), level)
        scale = jnp.where(above, jnp.float32(2.0 ** (top - 8 * (j + 1 - middle))), scale)
    return level, scale


def shrink_of(level):
    shrink = jnp.full(level.shape, 2.0 ** (-top - 8 * middle), jnp.float32)
    for j in range(levels):
        shrink = jnp.where(level > j, jnp.float32(2.0 ** (8 * (j + 1 - middle) - top)), shrink)
    return shrink


def share_kernel(_, energies_ref, centers_ref, projectors_ref, potential_ref, out_ref):
    rows, nz = out_ref.shape
    atoms, tiles, projs = projectors_ref.shape[:3]

    row = 0
    for a in range(atoms):
        for t in range(tiles):
            out_ref[pl.ds(row, projs), :] = projectors_ref[a, t] * projector_gain
            row += projs
    for i in range(potential_ref.shape[0]):
        count = potential_ref.shape[1]
        out_ref[pl.ds(row, count), :] = potential_ref[i] * potential_gain
        row += count
    lane = lax.broadcasted_iota(jnp.int32, (1, nz), 1)
    numbers = jnp.zeros((1, nz), jnp.float32)
    for a in range(atoms):
        for p in range(projs):
            numbers = jnp.where(lane == a * projs + p, energies_ref[a, p], numbers)
    high = numbers.astype(jnp.bfloat16).astype(jnp.float32)
    low = (numbers - high) * remainder_gain
    count = atoms * projs
    numbers = high + pltpu.roll(low, count, 1)
    for a in range(atoms):
        for d in range(2):
            here = centers_ref[d, a].astype(jnp.float32)
            numbers = jnp.where(lane == 2 * count + 2 * a + d, here, numbers)
    out_ref[pl.ds(row, 1), :] = numbers
    out_ref[pl.ds(row + 1, rows - row - 1), :] = jnp.zeros((rows - row - 1, nz), jnp.float32)


def filter_kernel(
    slabs_y,
    cells_x,
    cells_y,
    each,
    atoms,
    projs,
    by_swaps,
    got_ref,
    field_ref,
    rounded_ref,
    first,
    second,
    partial,
    diagonal,
    coeffs,
    numbers,
    arrived,
):
    group, _, nz = got_ref.shape
    count_x, count_y = diagonal.shape[0], diagonal.shape[1]
    tiles = len(offsets_x)
    slab_cells = cells_x * cells_y
    proj_row = slab_cells * each
    pot_row = proj_row + atoms * projs * tiles
    number_row = pot_row + slab_cells
    scale = 1.0 / filter_half
    factors = [-0.5 * scale * w for w in stencil_weights]
    ring = 1

    copy = pltpu.make_async_copy(got_ref.at[:, number_row, :], numbers, arrived)
    copy.start()

    for field in (first, second):
        for x in (0, ring + count_x):
            field[x] = jnp.zeros(field.shape[1:], jnp.float32)
        for y in (0, ring + count_y):
            field[:, y] = jnp.zeros((field.shape[0],) + field.shape[2:], jnp.float32)

    def take_slab(g, carry):
        x0 = (g // slabs_y) * cells_x
        y0 = (g % slabs_y) * cells_y
        for i in range(cells_x):
            for j in range(cells_y):
                cell = i * cells_y + j
                first[ring + x0 + i, ring + y0 + j] = got_ref[g, pl.ds(cell * each, each), :] * (
                    1.0 / orbital_gain
                )
                diagonal[x0 + i, y0 + j] = got_ref[g, pl.ds(pot_row + cell, 1), :] * (
                    scale / potential_gain
                ) + (3.0 * factors[0] - filter_center * scale)
        return carry

    lax.fori_loop(0, group, take_slab, 0)

    distance = jnp.abs(
        lax.broadcasted_iota(jnp.int32, (nz, nz), 0) - lax.broadcasted_iota(jnp.int32, (nz, nz), 1)
    )
    along_z = jnp.zeros((nz, nz), jnp.float32)
    for step in range(1, reach + 1):
        along_z = jnp.where(distance == step, factors[step], along_z)
    z_high = along_z.astype(jnp.bfloat16)
    z_low = (along_z - z_high.astype(jnp.float32)).astype(jnp.bfloat16)
    z_matrix = jnp.concatenate(
        [
            jnp.concatenate([z_high, z_low], axis=1),
            jnp.concatenate([z_high, jnp.zeros_like(z_high)], axis=1),
        ],
        axis=0,
    )

    def along(cells, at):
        total = None
        for step in range(1, reach + 1):
            near = [cells[n] for n in (at - step, at + step) if 0 <= n < len(cells)]
            if near:
                term = factors[step] * sum(near[1:], near[0])
                total = term if total is None else total + term
        return total

    def apply(source, target, finish, gain):
        def xz_part(y, carry):
            column = source[pl.ds(ring, count_x), ring + y]
            flat = column.reshape(count_x * each, nz)
            high = flat.astype(jnp.bfloat16)
            low = (flat - high.astype(jnp.float32)).astype(jnp.bfloat16)
            both = jnp.dot(
                jnp.concatenate([high, low], axis=1), z_matrix, preferred_element_type=jnp.float32
            )
            along_z = (both[:, :nz] + both[:, nz:]).reshape(column.shape)
            cells = [column[x] for x in range(count_x)]
            for x in range(count_x):
                partial[x, y] = along_z[x] + diagonal[x, y] * cells[x] + along(cells, x)
            return carry

        lax.fori_loop(0, count_y, xz_part, 0, unroll=2)

        def y_part(x, carry):
            cells = [source[ring + x, ring + y] for y in range(count_y)]
            for y in range(count_y):
                total = partial[x, y] + along(cells, y)
                target[ring + x, ring + y] = finish(total, target, ring + x, ring + y)
            return carry

        lax.fori_loop(0, count_x, y_part, 0, unroll=2)

        def place_of(g, a):
            at = 2 * atoms * projs + 2 * a
            return (
                ring + numbers[g, at].astype(jnp.int32),
                ring + numbers[g, at + 1].astype(jnp.int32),
            )

        def gather_part(g, carry):
            for a in range(atoms):
                at_x, at_y = place_of(g, a)
                totals = [None] * projs
                for t in range(tiles):
                    tile = source[at_x + offsets_x[t], at_y + offsets_y[t]]
                    for p in range(projs):
                        row = proj_row + (a * tiles + t) * projs + p
                        term = tile * got_ref[g, pl.ds(row, 1), :]
                        totals[p] = term if t == 0 else totals[p] + term
                for p in range(projs):
                    k = a * projs + p
                    energy = numbers[g, k] + numbers[g, atoms * projs + k] * (1.0 / remainder_gain)
                    coeffs[g, k] = jnp.broadcast_to(
                        jnp.sum(totals[p], axis=-1, keepdims=True)
                        * (energy * (gain / projector_gain / projector_gain)),
                        (each, nz),
                    )
            return carry

        lax.fori_loop(0, group, gather_part, 0, unroll=min(group, 4))

        def scatter_part(g, carry):
            for a in range(atoms):
                at_x, at_y = place_of(g, a)
                factor = [coeffs[g, a * projs + p] for p in range(projs)]
                for t in range(tiles):
                    row = proj_row + (a * tiles + t) * projs
                    spread = factor[0] * got_ref[g, pl.ds(row, 1), :]
                    for p in range(1, projs):
                        spread = spread + factor[p] * got_ref[g, pl.ds(row + p, 1), :]
                    to_x = at_x + offsets_x[t]
                    to_y = at_y + offsets_y[t]
                    target[to_x, to_y] = target[to_x, to_y] + spread
            return carry

        lax.fori_loop(0, group, scatter_part, 0, unroll=min(group, 2))

    copy.wait()
    apply(first, second, lambda total, target, x, y: total, scale)

    for x in (0, ring + count_x):
        second[x] = jnp.zeros(second.shape[1:], jnp.float32)
    for y in (0, ring + count_y):
        second[:, y] = jnp.zeros((second.shape[0],) + second.shape[2:], jnp.float32)

    apply(second, first, lambda total, target, x, y: 2.0 * total - target[x, y], 2.0 * scale)

    shares = rounded_ref.shape[0] // group
    portion = slab_cells // shares

    def largest_of(x, largest):
        row = jnp.abs(first[ring + x, pl.ds(ring, count_y)])
        return jnp.maximum(largest, jnp.max(row, axis=0))

    largest = lax.fori_loop(0, count_x, largest_of, jnp.zeros((each, nz), jnp.float32))
    level, gain = level_of(jnp.max(largest))
    level_rows = jnp.full((8, nz), level, jnp.float32)
    me = lax.axis_index("sx") * slabs_y + lax.axis_index("sy") if by_swaps else 0

    def give_slab(g, carry):
        slot = jnp.bitwise_xor(g, me) if by_swaps else g
        field_ref[slot, pl.ds(slab_cells * each, 8), :] = level_rows
        x0 = (g // slabs_y) * cells_x
        y0 = (g % slabs_y) * cells_y
        for i in range(cells_x):
            for j in range(cells_y):
                cell = i * cells_y + j
                value = first[ring + x0 + i, ring + y0 + j]
                field_ref[slot, pl.ds(cell * each, each), :] = value * gain
                rounded_ref[
                    (cell // portion) * group + g, :, pl.ds((cell % portion) * nz, nz)
                ] = value.astype(jnp.bfloat16)
        return carry

    lax.fori_loop(0, group, give_slab, 0)


def gram_kernel(each, matrix_ref, out_ref):
    matrix = matrix_ref[...]
    sums = lax.dot_general(
        matrix, matrix, (((1,), (1,)), ((), ())), preferred_element_type=jnp.float32
    )
    level, gain = level_of(jnp.max(jnp.abs(sums)))
    row = lax.broadcasted_iota(jnp.int32, sums.shape, 0)
    column = lax.broadcasted_iota(jnp.int32, sums.shape, 1)
    spare = (column == row - 1) & (row % each == 1)
    out_ref[...] = jnp.where(spare, level, sums * gain)


def rows_kernel(cells, plane_shape, parts_ref, out_ref):
    count, each, columns = parts_ref.shape
    if each > 1:
        band = lax.axis_index("band") * plane_shape[0] + lax.axis_index("sx")
        first = (band * plane_shape[1] + lax.axis_index("sy")) * each
        row = lax.broadcasted_iota(jnp.int32, (each, columns), 0)
        column = lax.broadcasted_iota(jnp.int32, (each, columns), 1)
        spare = (row == 1) & (column == first)
        twin = (row == 0) & (column == first + 1)

        def entry(block, place):
            picked = jnp.where(place, block, 0.0)
            return jnp.sum(jnp.sum(picked, axis=0, keepdims=True), axis=1, keepdims=True)

        total = jnp.zeros((each, columns), jnp.float32)
        for source in range(count):
            block = parts_ref[source]
            total = total + block * shrink_of(entry(block, spare))
        total = jnp.where(spare, entry(total, twin), total)
    else:
        total = jnp.sum(parts_ref[...], axis=0)
    out_ref[...] = total / cells


def unpack_kernel(each, slabs_y, places, *refs):
    pieces = refs[:-3]
    filtered_hbm, filtered_ref, chunk_sems = refs[-3:]
    slab_cells, _, nz = filtered_ref.shape
    chunks = chunk_sems.shape[0]
    chunk = slab_cells // chunks
    me = lax.axis_index("sx") * slabs_y + lax.axis_index("sy") if len(pieces) > 1 else 0
    copies = []
    for c in range(chunks):
        for which, entry, other in places:
            piece = pieces[which]
            shrink = shrink_of(piece[entry, pl.ds(slab_cells * each, 1), :])
            if len(pieces) > 1:
                rows = pl.ds(pl.multiple_of(jnp.bitwise_xor(me, other) * each, each), each)
            else:
                rows = pl.ds(other * each, each)
            for cell in range(c * chunk, (c + 1) * chunk):
                filtered_ref[cell, rows, :] = piece[entry, pl.ds(cell * each, each), :] * shrink
        part = pl.ds(c * chunk, chunk)
        copies.append(
            pltpu.make_async_copy(filtered_ref.at[part], filtered_hbm.at[part], chunk_sems.at[c])
        )
        copies[-1].start()
    for copy in copies:
        copy.wait()


def swap(pieces, value):
    group = lax.axis_size(plane)
    return lax.ppermute(
        jnp.stack(pieces).astype(jnp.float16), plane, [(i, i ^ value) for i in range(group)]
    )


def local(orbitals, potential, projectors, energies, centers):
    band_orbitals, cells_x, cells_y, nz = orbitals.shape
    bands = lax.axis_size("band")
    slabs_x = lax.axis_size("sx")
    slabs_y = lax.axis_size("sy")
    group = slabs_x * slabs_y
    each = band_orbitals // group
    total_orbitals = bands * band_orbitals
    slab_cells = cells_x * cells_y
    grid = (slabs_x * cells_x, slabs_y * cells_y)
    atoms, projs, tiles, _ = projectors.shape

    rows = atoms * projs * tiles + slab_cells + 1
    rows += -rows % 8
    chunks = (orbitals * orbital_gain).astype(jnp.float16)
    chunks = chunks.transpose(1, 2, 0, 3).reshape(slab_cells, group, each, nz)
    chunks = chunks.transpose(1, 0, 2, 3).reshape(group, slab_cells * each, nz)
    shared = pl.pallas_call(
        share_kernel,
        in_specs=[hbm, smem, smem, vmem, vmem],
        out_specs=vmem,
        out_shape=jax.ShapeDtypeStruct((rows, nz), jnp.float32),
        compiler_params=params,
    )(chunks[0, :8].astype(jnp.float32), energies, centers.T, projectors.transpose(0, 2, 1, 3), potential).astype(jnp.float16)
    sent = jnp.concatenate([chunks, jnp.broadcast_to(shared[None], (group, rows, nz))], axis=1)
    got = lax.all_to_all(sent, plane, 0, 0).astype(jnp.float32)

    near = slabs_y
    far = [v for v in range(1, group) if not v & near]
    by_swaps = group <= 8 and each % 8 == 0 and slabs_x > 1 and group & (group - 1) == 0

    portion = slab_cells // bands
    ringed = (grid[0] + 2, grid[1] + 2, each, nz)
    field, rounded = pl.pallas_call(
        functools.partial(filter_kernel, slabs_y, cells_x, cells_y, each, atoms, projs, by_swaps),
        in_specs=[vmem],
        out_specs=[vmem] * 2,
        out_shape=[
            jax.ShapeDtypeStruct((group, slab_cells * each + 8, nz), jnp.float32),
            jax.ShapeDtypeStruct((bands * group, each, portion * nz), jnp.bfloat16),
        ],
        scratch_shapes=[
            pltpu.VMEM(ringed, jnp.float32),
            pltpu.VMEM(ringed, jnp.float32),
            pltpu.VMEM(grid + (each, nz), jnp.float32),
            pltpu.VMEM(grid + (1, nz), jnp.float32),
            pltpu.VMEM((group, atoms * projs, each, nz), jnp.float32),
            pltpu.SMEM((group, nz), jnp.float32),
            pltpu.SemaphoreType.DMA,
        ],
        compiler_params=params,
        cost_estimate=pl.CostEstimate(
            flops=2 * 2 * 40 * grid[0] * grid[1] * each * nz,
            bytes_accessed=8 * grid[0] * grid[1] * each * nz,
            transcendentals=0,
        ),
    )(got)

    matrix = lax.all_to_all(rounded, every, 0, 0).reshape(total_orbitals, portion * nz)
    if by_swaps:
        came = [swap([field[v], field[v | near]], v) for v in far]
        came, matrix = lax.optimization_barrier((came, matrix))
        came.append(swap([field[near]] + [block[1] for block in came], near))
        pieces = [field] + [block.astype(jnp.float32) for block in came]
        places = [(0, 0, 0), (len(pieces) - 1, 0, near)]
        for i, v in enumerate(far):
            places += [(i + 1, 0, v), (len(pieces) - 1, i + 1, v | near)]
    else:
        pieces = [lax.all_to_all(field.astype(jnp.float16), plane, 0, 0).astype(jnp.float32)]
        places = [(0, g, g) for g in range(group)]

    spread = (bands * group, each, total_orbitals)
    if each > 1:
        sums = pl.pallas_call(
            functools.partial(gram_kernel, each),
            in_specs=[vmem],
            out_specs=vmem,
            out_shape=jax.ShapeDtypeStruct((total_orbitals, total_orbitals), jnp.float32),
            compiler_params=params,
        )(matrix)
        sums = sums.astype(jnp.float16).reshape(spread)
    else:
        sums = lax.dot_general(
            matrix, matrix, (((1,), (1,)), ((), ())), preferred_element_type=jnp.float32
        ).reshape(spread)
    parts = lax.all_to_all(sums, every, 0, 0).astype(jnp.float32)
    rows = pl.pallas_call(
        functools.partial(rows_kernel, grid[0] * grid[1] * nz, (slabs_x, slabs_y)),
        in_specs=[vmem],
        out_specs=vmem,
        out_shape=jax.ShapeDtypeStruct((each, total_orbitals), jnp.float32),
        compiler_params=params,
    )(parts)
    gram = lax.all_to_all(jnp.broadcast_to(rows[None], (group,) + rows.shape), plane, 0, 0)
    gram = gram.reshape(band_orbitals, total_orbitals)

    filtered = pl.pallas_call(
        functools.partial(unpack_kernel, each, slabs_y, places),
        in_specs=[vmem] * len(pieces),
        out_specs=hbm,
        out_shape=jax.ShapeDtypeStruct((slab_cells, band_orbitals, nz), jnp.float32),
        scratch_shapes=[
            pltpu.VMEM((slab_cells, band_orbitals, nz), jnp.float32),
            pltpu.SemaphoreType.DMA((cells_x,)),
        ],
        compiler_params=params,
    )(*pieces)
    filtered = filtered.reshape(cells_x, cells_y, band_orbitals, nz).transpose(2, 0, 1, 3)
    return (filtered, gram)


def solution(mesh):
    in_specs = (
        P("band", "sx", "sy", None),
        P("sx", "sy", None),
        P(("sx", "sy"), None, None, None),
        P(("sx", "sy"), None),
        P(("sx", "sy"), None),
    )
    out_specs = (P("band", "sx", "sy", None), P("band", None))
    return jax.shard_map(local, mesh=mesh, in_specs=in_specs, out_specs=out_specs, check_vma=False)
```

```python
import functools

import jax
import jax.numpy as jnp
from jax import lax
from jax.experimental import pallas as pl
from jax.experimental.pallas import tpu as pltpu
from jax.sharding import PartitionSpec as P

stencil_weights = (
    -5369.0 / 1800.0,
    12.0 / 7.0,
    -15.0 / 56.0,
    10.0 / 189.0,
    -1.0 / 112.0,
    2.0 / 1925.0,
    -1.0 / 16632.0,
)
filter_center = 6.5
filter_half = 6.0
offsets_x = (0, -1, 1, 0, 0)
offsets_y = (0, 0, 0, -1, 1)
reach = 6
plane = ("sx", "sy")
every = ("band", "sx", "sy")

orbital_gain = 2.0**12
projector_gain = 2.0**17
potential_gain = 2.0**13
remainder_gain = 2.0**10
top = 15
middle = 8
levels = 17

vmem = pl.BlockSpec(memory_space=pltpu.VMEM)
smem = pl.BlockSpec(memory_space=pltpu.SMEM)
hbm = pl.BlockSpec(memory_space=pl.ANY)
params = pltpu.CompilerParams(vmem_limit_bytes=24 * 1024 * 1024)


def level_of(largest):
    level = jnp.float32(0.0)
    scale = jnp.float32(2.0 ** (top + 8 * middle))
    for j in range(levels):
        above = largest >= jnp.float32(2.0 ** (8 * (j - middle)))
        level = jnp.where(above, jnp.float32(j + 1), level)
        scale = jnp.where(above, jnp.float32(2.0 ** (top - 8 * (j + 1 - middle))), scale)
    return level, scale


def shrink_of(level):
    shrink = jnp.full(level.shape, 2.0 ** (-top - 8 * middle), jnp.float32)
    for j in range(levels):
        shrink = jnp.where(level > j, jnp.float32(2.0 ** (8 * (j + 1 - middle) - top)), shrink)
    return shrink


def share_kernel(_, energies_ref, centers_ref, projectors_ref, potential_ref, out_ref):
    rows, nz = out_ref.shape
    atoms, tiles, projs = projectors_ref.shape[:3]

    row = 0
    for a in range(atoms):
        for t in range(tiles):
            out_ref[pl.ds(row, projs), :] = projectors_ref[a, t] * projector_gain
            row += projs
    for i in range(potential_ref.shape[0]):
        count = potential_ref.shape[1]
        out_ref[pl.ds(row, count), :] = potential_ref[i] * potential_gain
        row += count
    lane = lax.broadcasted_iota(jnp.int32, (1, nz), 1)
    numbers = jnp.zeros((1, nz), jnp.float32)
    for a in range(atoms):
        for p in range(projs):
            numbers = jnp.where(lane == a * projs + p, energies_ref[a, p], numbers)
    high = numbers.astype(jnp.bfloat16).astype(jnp.float32)
    low = (numbers - high) * remainder_gain
    count = atoms * projs
    numbers = high + pltpu.roll(low, count, 1)
    for a in range(atoms):
        for d in range(2):
            here = centers_ref[d, a].astype(jnp.float32)
            numbers = jnp.where(lane == 2 * count + 2 * a + d, here, numbers)
    out_ref[pl.ds(row, 1), :] = numbers
    out_ref[pl.ds(row + 1, rows - row - 1), :] = jnp.zeros((rows - row - 1, nz), jnp.float32)


def filter_kernel(
    slabs_y,
    cells_x,
    cells_y,
    each,
    atoms,
    projs,
    by_swaps,
    got_ref,
    field_ref,
    rounded_ref,
    first,
    second,
    partial,
    diagonal,
    coeffs,
    numbers,
    arrived,
):
    group, _, nz = got_ref.shape
    count_x, count_y = diagonal.shape[0], diagonal.shape[1]
    tiles = len(offsets_x)
    slab_cells = cells_x * cells_y
    proj_row = slab_cells * each
    pot_row = proj_row + atoms * projs * tiles
    number_row = pot_row + slab_cells
    scale = 1.0 / filter_half
    factors = [-0.5 * scale * w for w in stencil_weights]
    ring = 1

    copy = pltpu.make_async_copy(got_ref.at[:, number_row, :], numbers, arrived)
    copy.start()

    for field in (first, second):
        for x in (0, ring + count_x):
            field[x] = jnp.zeros(field.shape[1:], jnp.float32)
        for y in (0, ring + count_y):
            field[:, y] = jnp.zeros((field.shape[0],) + field.shape[2:], jnp.float32)

    def take_slab(g, carry):
        x0 = (g // slabs_y) * cells_x
        y0 = (g % slabs_y) * cells_y
        for i in range(cells_x):
            for j in range(cells_y):
                cell = i * cells_y + j
                first[ring + x0 + i, ring + y0 + j] = got_ref[g, pl.ds(cell * each, each), :] * (
                    1.0 / orbital_gain
                )
                diagonal[x0 + i, y0 + j] = got_ref[g, pl.ds(pot_row + cell, 1), :] * (
                    scale / potential_gain
                ) + (3.0 * factors[0] - filter_center * scale)
        return carry

    lax.fori_loop(0, group, take_slab, 0)

    distance = jnp.abs(
        lax.broadcasted_iota(jnp.int32, (nz, nz), 0) - lax.broadcasted_iota(jnp.int32, (nz, nz), 1)
    )
    along_z = jnp.zeros((nz, nz), jnp.float32)
    for step in range(1, reach + 1):
        along_z = jnp.where(distance == step, factors[step], along_z)
    z_high = along_z.astype(jnp.bfloat16)
    z_low = (along_z - z_high.astype(jnp.float32)).astype(jnp.bfloat16)
    z_matrix = jnp.concatenate(
        [
            jnp.concatenate([z_high, z_low], axis=1),
            jnp.concatenate([z_high, jnp.zeros_like(z_high)], axis=1),
        ],
        axis=0,
    )

    def along(cells, at):
        total = None
        for step in range(1, reach + 1):
            near = [cells[n] for n in (at - step, at + step) if 0 <= n < len(cells)]
            if near:
                term = factors[step] * sum(near[1:], near[0])
                total = term if total is None else total + term
        return total

    def apply(source, target, finish, gain):
        def xz_part(y, carry):
            column = source[pl.ds(ring, count_x), ring + y]
            flat = column.reshape(count_x * each, nz)
            high = flat.astype(jnp.bfloat16)
            low = (flat - high.astype(jnp.float32)).astype(jnp.bfloat16)
            both = jnp.dot(
                jnp.concatenate([high, low], axis=1), z_matrix, preferred_element_type=jnp.float32
            )
            along_z = (both[:, :nz] + both[:, nz:]).reshape(column.shape)
            cells = [column[x] for x in range(count_x)]
            for x in range(count_x):
                partial[x, y] = along_z[x] + diagonal[x, y] * cells[x] + along(cells, x)
            return carry

        lax.fori_loop(0, count_y, xz_part, 0, unroll=2)

        def y_part(x, carry):
            cells = [source[ring + x, ring + y] for y in range(count_y)]
            for y in range(count_y):
                total = partial[x, y] + along(cells, y)
                target[ring + x, ring + y] = finish(total, target, ring + x, ring + y)
            return carry

        lax.fori_loop(0, count_x, y_part, 0, unroll=2)

        def place_of(g, a):
            at = 2 * atoms * projs + 2 * a
            return (
                ring + numbers[g, at].astype(jnp.int32),
                ring + numbers[g, at + 1].astype(jnp.int32),
            )

        def gather_part(g, carry):
            for a in range(atoms):
                at_x, at_y = place_of(g, a)
                totals = [None] * projs
                for t in range(tiles):
                    tile = source[at_x + offsets_x[t], at_y + offsets_y[t]]
                    for p in range(projs):
                        row = proj_row + (a * tiles + t) * projs + p
                        term = tile * got_ref[g, pl.ds(row, 1), :]
                        totals[p] = term if t == 0 else totals[p] + term
                for p in range(projs):
                    k = a * projs + p
                    energy = numbers[g, k] + numbers[g, atoms * projs + k] * (1.0 / remainder_gain)
                    coeffs[g, k] = jnp.broadcast_to(
                        jnp.sum(totals[p], axis=-1, keepdims=True)
                        * (energy * (gain / projector_gain / projector_gain)),
                        (each, nz),
                    )
            return carry

        lax.fori_loop(0, group, gather_part, 0, unroll=min(group, 4))

        def scatter_part(g, carry):
            for a in range(atoms):
                at_x, at_y = place_of(g, a)
                factor = [coeffs[g, a * projs + p] for p in range(projs)]
                for t in range(tiles):
                    row = proj_row + (a * tiles + t) * projs
                    spread = factor[0] * got_ref[g, pl.ds(row, 1), :]
                    for p in range(1, projs):
                        spread = spread + factor[p] * got_ref[g, pl.ds(row + p, 1), :]
                    to_x = at_x + offsets_x[t]
                    to_y = at_y + offsets_y[t]
                    target[to_x, to_y] = target[to_x, to_y] + spread
            return carry

        lax.fori_loop(0, group, scatter_part, 0, unroll=min(group, 2))

    copy.wait()
    apply(first, second, lambda total, target, x, y: total, scale)

    for x in (0, ring + count_x):
        second[x] = jnp.zeros(second.shape[1:], jnp.float32)
    for y in (0, ring + count_y):
        second[:, y] = jnp.zeros((second.shape[0],) + second.shape[2:], jnp.float32)

    apply(second, first, lambda total, target, x, y: 2.0 * total - target[x, y], 2.0 * scale)

    shares = rounded_ref.shape[0] // group
    portion = slab_cells // shares

    def largest_of(x, largest):
        row = jnp.abs(first[ring + x, pl.ds(ring, count_y)])
        return jnp.maximum(largest, jnp.max(row, axis=0))

    largest = lax.fori_loop(0, count_x, largest_of, jnp.zeros((each, nz), jnp.float32))
    level, gain = level_of(jnp.max(largest))
    level_rows = jnp.full((8, nz), level, jnp.float32)
    me = lax.axis_index("sx") * slabs_y + lax.axis_index("sy") if by_swaps else 0

    def give_slab(g, carry):
        slot = jnp.bitwise_xor(g, me) if by_swaps else g
        field_ref[slot, pl.ds(slab_cells * each, 8), :] = level_rows
        x0 = (g // slabs_y) * cells_x
        y0 = (g % slabs_y) * cells_y
        for i in range(cells_x):
            for j in range(cells_y):
                cell = i * cells_y + j
                value = first[ring + x0 + i, ring + y0 + j]
                field_ref[slot, pl.ds(cell * each, each), :] = value * gain
                rounded_ref[
                    (cell // portion) * group + g, :, pl.ds((cell % portion) * nz, nz)
                ] = value.astype(jnp.bfloat16)
        return carry

    lax.fori_loop(0, group, give_slab, 0)


def entry(block, place):
    picked = jnp.where(place, block, 0.0)
    return jnp.sum(jnp.sum(picked, axis=0, keepdims=True), axis=1, keepdims=True)


def band_corner(shape, band):
    row = lax.broadcasted_iota(jnp.int32, shape, 0)
    column = lax.broadcasted_iota(jnp.int32, shape, 1)
    return (
        (row == 1) & (column == band * shape[0]),
        (row == 0) & (column == band * shape[0] + 1),
    )


def gram_kernel(matrix_ref, out_ref, sums_ref):
    bands, rows, columns = out_ref.shape
    matrix = matrix_ref[...]
    sums = lax.dot_general(
        matrix, matrix, (((1,), (1,)), ((), ())), preferred_element_type=jnp.float32
    )
    level, gain = level_of(jnp.max(jnp.abs(sums)))
    sums_ref[...] = sums * gain
    me = lax.axis_index("band")
    for k in range(bands):
        band = jnp.bitwise_xor(me, k)
        spare, _ = band_corner((rows, columns), band)
        block = sums_ref[pl.ds(pl.multiple_of(band * rows, rows), rows), :]
        out_ref[k] = jnp.where(spare, level, block)


def rows_kernel(cells, own_ref, *refs):
    out_ref = refs[-1]
    spare, twin = band_corner(out_ref.shape, lax.axis_index("band"))
    total = None
    for block in [own_ref[0]] + [ref[...] for ref in refs[:-1]]:
        block = block * shrink_of(entry(block, spare))
        total = block if total is None else total + block
    out_ref[...] = jnp.where(spare, entry(total, twin), total) / cells


def unpack_kernel(each, slabs_y, places, *refs):
    pieces = refs[:-3]
    filtered_hbm, filtered_ref, chunk_sems = refs[-3:]
    slab_cells, _, nz = filtered_ref.shape
    chunks = chunk_sems.shape[0]
    chunk = slab_cells // chunks
    me = lax.axis_index("sx") * slabs_y + lax.axis_index("sy") if len(pieces) > 1 else 0
    copies = []
    for c in range(chunks):
        for which, entry, other in places:
            piece = pieces[which]
            shrink = shrink_of(piece[entry, pl.ds(slab_cells * each, 1), :])
            if len(pieces) > 1:
                rows = pl.ds(pl.multiple_of(jnp.bitwise_xor(me, other) * each, each), each)
            else:
                rows = pl.ds(other * each, each)
            for cell in range(c * chunk, (c + 1) * chunk):
                filtered_ref[cell, rows, :] = piece[entry, pl.ds(cell * each, each), :] * shrink
        part = pl.ds(c * chunk, chunk)
        copies.append(
            pltpu.make_async_copy(filtered_ref.at[part], filtered_hbm.at[part], chunk_sems.at[c])
        )
        copies[-1].start()
    for copy in copies:
        copy.wait()


def swap(pieces, value):
    group = lax.axis_size(plane)
    return lax.ppermute(
        jnp.stack(pieces).astype(jnp.float16), plane, [(i, i ^ value) for i in range(group)]
    )


def local(orbitals, potential, projectors, energies, centers):
    band_orbitals, cells_x, cells_y, nz = orbitals.shape
    bands = lax.axis_size("band")
    slabs_x = lax.axis_size("sx")
    slabs_y = lax.axis_size("sy")
    group = slabs_x * slabs_y
    each = band_orbitals // group
    total_orbitals = bands * band_orbitals
    slab_cells = cells_x * cells_y
    grid = (slabs_x * cells_x, slabs_y * cells_y)
    atoms, projs, tiles, _ = projectors.shape

    rows = atoms * projs * tiles + slab_cells + 1
    rows += -rows % 8
    chunks = (orbitals * orbital_gain).astype(jnp.float16)
    chunks = chunks.transpose(1, 2, 0, 3).reshape(slab_cells, group, each, nz)
    chunks = chunks.transpose(1, 0, 2, 3).reshape(group, slab_cells * each, nz)
    shared = pl.pallas_call(
        share_kernel,
        in_specs=[hbm, smem, smem, vmem, vmem],
        out_specs=vmem,
        out_shape=jax.ShapeDtypeStruct((rows, nz), jnp.float32),
        compiler_params=params,
    )(chunks[0, :8].astype(jnp.float32), energies, centers.T, projectors.transpose(0, 2, 1, 3), potential).astype(jnp.float16)
    sent = jnp.concatenate([chunks, jnp.broadcast_to(shared[None], (group, rows, nz))], axis=1)
    got = lax.all_to_all(sent, plane, 0, 0).astype(jnp.float32)

    near = slabs_y
    far = [v for v in range(1, group) if not v & near]
    by_swaps = group <= 8 and each % 8 == 0 and slabs_x > 1
    by_swaps = by_swaps and group & (group - 1) == 0 and bands & (bands - 1) == 0

    portion = slab_cells // bands
    ringed = (grid[0] + 2, grid[1] + 2, each, nz)
    field, rounded = pl.pallas_call(
        functools.partial(filter_kernel, slabs_y, cells_x, cells_y, each, atoms, projs, by_swaps),
        in_specs=[vmem],
        out_specs=[vmem] * 2,
        out_shape=[
            jax.ShapeDtypeStruct((group, slab_cells * each + 8, nz), jnp.float32),
            jax.ShapeDtypeStruct((bands * group, each, portion * nz), jnp.bfloat16),
        ],
        scratch_shapes=[
            pltpu.VMEM(ringed, jnp.float32),
            pltpu.VMEM(ringed, jnp.float32),
            pltpu.VMEM(grid + (each, nz), jnp.float32),
            pltpu.VMEM(grid + (1, nz), jnp.float32),
            pltpu.VMEM((group, atoms * projs, each, nz), jnp.float32),
            pltpu.SMEM((group, nz), jnp.float32),
            pltpu.SemaphoreType.DMA,
        ],
        compiler_params=params,
        cost_estimate=pl.CostEstimate(
            flops=2 * 2 * 40 * grid[0] * grid[1] * each * nz,
            bytes_accessed=8 * grid[0] * grid[1] * each * nz,
            transcendentals=0,
        ),
    )(got)

    matrix = lax.all_to_all(rounded, every, 0, 0).reshape(total_orbitals, portion * nz)
    if by_swaps:
        came = [swap([field[v], field[v | near]], v) for v in far]
        came, matrix = lax.optimization_barrier((came, matrix))
        came.append(swap([field[near]] + [block[1] for block in came], near))
        pieces = [field] + [block.astype(jnp.float32) for block in came]
        places = [(0, 0, 0), (len(pieces) - 1, 0, near)]
        for i, v in enumerate(far):
            places += [(i + 1, 0, v), (len(pieces) - 1, i + 1, v | near)]
    else:
        pieces = [lax.all_to_all(field.astype(jnp.float16), plane, 0, 0).astype(jnp.float32)]
        places = [(0, g, g) for g in range(group)]

    cells = grid[0] * grid[1] * nz
    if by_swaps:
        sums = pl.pallas_call(
            gram_kernel,
            in_specs=[vmem],
            out_specs=vmem,
            out_shape=jax.ShapeDtypeStruct((bands, band_orbitals, total_orbitals), jnp.float32),
            scratch_shapes=[pltpu.VMEM((total_orbitals, total_orbitals), jnp.float32)],
            compiler_params=params,
        )(matrix)
        parts = [
            lax.ppermute(
                sums[k].astype(jnp.float16), "band", [(i, i ^ k) for i in range(bands)]
            ).astype(jnp.float32)
            for k in range(1, bands)
        ]
        gram = pl.pallas_call(
            functools.partial(rows_kernel, cells),
            in_specs=[vmem] * bands,
            out_specs=vmem,
            out_shape=jax.ShapeDtypeStruct((band_orbitals, total_orbitals), jnp.float32),
            compiler_params=params,
        )(sums, *parts)
        terms = {v: lax.ppermute(gram, plane, [(i, i ^ v) for i in range(group)]) for v in far}
        terms[0] = gram
        bit = 1
        while len(terms) > 1:
            terms = {v: terms[v] + terms[v ^ bit] for v in terms if not v & bit and v ^ bit in terms} or terms
            bit *= 2
        gram = terms[0]
        gram = gram + lax.ppermute(gram, plane, [(i, i ^ near) for i in range(group)])
    else:
        sums = lax.dot_general(
            matrix, matrix, (((1,), (1,)), ((), ())), preferred_element_type=jnp.float32
        )
        parts = lax.all_to_all(sums.reshape(bands * group, each, total_orbitals), every, 0, 0)
        rows = jnp.sum(parts, axis=0) / cells
        gram = lax.all_to_all(jnp.broadcast_to(rows[None], (group,) + rows.shape), plane, 0, 0)
        gram = gram.reshape(band_orbitals, total_orbitals)

    filtered = pl.pallas_call(
        functools.partial(unpack_kernel, each, slabs_y, places),
        in_specs=[vmem] * len(pieces),
        out_specs=hbm,
        out_shape=jax.ShapeDtypeStruct((slab_cells, band_orbitals, nz), jnp.float32),
        scratch_shapes=[
            pltpu.VMEM((slab_cells, band_orbitals, nz), jnp.float32),
            pltpu.SemaphoreType.DMA((cells_x,)),
        ],
        compiler_params=params,
    )(*pieces)
    filtered = filtered.reshape(cells_x, cells_y, band_orbitals, nz).transpose(2, 0, 1, 3)
    return (filtered, gram)


def solution(mesh):
    in_specs = (
        P("band", "sx", "sy", None),
        P("sx", "sy", None),
        P(("sx", "sy"), None, None, None),
        P(("sx", "sy"), None),
        P(("sx", "sy"), None),
    )
    out_specs = (P("band", "sx", "sy", None), P("band", None))
    return jax.shard_map(local, mesh=mesh, in_specs=in_specs, out_specs=out_specs, check_vma=False)
```

```python
import functools

import jax
import jax.numpy as jnp
from jax import lax
from jax.experimental import pallas as pl
from jax.experimental.pallas import tpu as pltpu
from jax.sharding import PartitionSpec as P

stencil_weights = (
    -5369.0 / 1800.0,
    12.0 / 7.0,
    -15.0 / 56.0,
    10.0 / 189.0,
    -1.0 / 112.0,
    2.0 / 1925.0,
    -1.0 / 16632.0,
)
filter_center = 6.5
filter_half = 6.0
offsets_x = (0, -1, 1, 0, 0)
offsets_y = (0, 0, 0, -1, 1)
reach = 6
plane = ("sx", "sy")
every = ("band", "sx", "sy")

orbital_gain = 2.0**12
projector_gain = 2.0**17
potential_gain = 2.0**13
remainder_gain = 2.0**10
top = 15
middle = 8
levels = 17

vmem = pl.BlockSpec(memory_space=pltpu.VMEM)
smem = pl.BlockSpec(memory_space=pltpu.SMEM)
hbm = pl.BlockSpec(memory_space=pl.ANY)
params = pltpu.CompilerParams(vmem_limit_bytes=24 * 1024 * 1024)


def level_of(largest):
    level = jnp.float32(0.0)
    scale = jnp.float32(2.0 ** (top + 8 * middle))
    for j in range(levels):
        above = largest >= jnp.float32(2.0 ** (8 * (j - middle)))
        level = jnp.where(above, jnp.float32(j + 1), level)
        scale = jnp.where(above, jnp.float32(2.0 ** (top - 8 * (j + 1 - middle))), scale)
    return level, scale


def shrink_of(level):
    shrink = jnp.full(level.shape, 2.0 ** (-top - 8 * middle), jnp.float32)
    for j in range(levels):
        shrink = jnp.where(level > j, jnp.float32(2.0 ** (8 * (j + 1 - middle) - top)), shrink)
    return shrink


def share_kernel(_, energies_ref, centers_ref, projectors_ref, potential_ref, out_ref):
    rows, nz = out_ref.shape
    atoms, tiles, projs = projectors_ref.shape[:3]

    row = 0
    for a in range(atoms):
        for t in range(tiles):
            out_ref[pl.ds(row, projs), :] = projectors_ref[a, t] * projector_gain
            row += projs
    for i in range(potential_ref.shape[0]):
        count = potential_ref.shape[1]
        out_ref[pl.ds(row, count), :] = potential_ref[i] * potential_gain
        row += count
    lane = lax.broadcasted_iota(jnp.int32, (1, nz), 1)
    numbers = jnp.zeros((1, nz), jnp.float32)
    for a in range(atoms):
        for p in range(projs):
            numbers = jnp.where(lane == a * projs + p, energies_ref[a, p], numbers)
    high = numbers.astype(jnp.bfloat16).astype(jnp.float32)
    low = (numbers - high) * remainder_gain
    count = atoms * projs
    numbers = high + pltpu.roll(low, count, 1)
    for a in range(atoms):
        for d in range(2):
            here = centers_ref[d, a].astype(jnp.float32)
            numbers = jnp.where(lane == 2 * count + 2 * a + d, here, numbers)
    out_ref[pl.ds(row, 1), :] = numbers
    out_ref[pl.ds(row + 1, rows - row - 1), :] = jnp.zeros((rows - row - 1, nz), jnp.float32)


def filter_kernel(slabs_y, cells_x, cells_y, each, atoms, projs, slabs, *refs):
    inputs, (field_ref, rounded_out) = refs[:-11], refs[-11:-9]
    first, second, partial, diagonal, coeffs, numbers, rounded_ref, arrived, sent = refs[-9:]
    group = numbers.shape[0]
    nz = first.shape[-1]
    count_x, count_y = diagonal.shape[0], diagonal.shape[1]
    tiles = len(offsets_x)
    slab_cells = cells_x * cells_y
    pot_row = atoms * projs * tiles
    number_row = pot_row + slab_cells
    scale = 1.0 / filter_half
    factors = [-0.5 * scale * w for w in stencil_weights]
    ring = 1
    me = 0 if slabs is None else lax.axis_index("sx") * slabs_y + lax.axis_index("sy")

    def rows_of(g, shared, row, count):
        if slabs is None:
            return inputs[0].at[g, pl.ds(row + (slab_cells * each if shared else 0), count), :]
        which, at, start = slabs[g][1 if shared else 0]
        return inputs[which].at[at, pl.ds(start + row, count), :]

    def shared_row(g, row):
        return rows_of(g, True, row, 1)[...]

    def over_slabs(body, unroll):
        if slabs is None:
            lax.fori_loop(0, group, lambda g, carry: body(g) or carry, 0, unroll=min(group, unroll))
        else:
            for g in range(group):
                body(g)

    def corner(g):
        place = g if slabs is None else jnp.bitwise_xor(me, g)
        return place, (place // slabs_y) * cells_x, (place % slabs_y) * cells_y

    if slabs is None:
        copies = [
            pltpu.make_async_copy(
                inputs[0].at[:, slab_cells * each + number_row, :], numbers, arrived.at[0]
            )
        ]
    else:
        copies = [
            pltpu.make_async_copy(
                rows_of(g, True, number_row, 1), numbers.at[pl.ds(g, 1), :], arrived.at[g]
            )
            for g in range(group)
        ]
    for copy in copies:
        copy.start()

    for field in (first, second):
        for x in (0, ring + count_x):
            field[x] = jnp.zeros(field.shape[1:], jnp.float32)
        for y in (0, ring + count_y):
            field[:, y] = jnp.zeros((field.shape[0],) + field.shape[2:], jnp.float32)

    def take_slab(g):
        _, x0, y0 = corner(g)
        for i in range(cells_x):
            for j in range(cells_y):
                cell = i * cells_y + j
                first[ring + x0 + i, ring + y0 + j] = rows_of(g, False, cell * each, each)[...] * (
                    1.0 / orbital_gain
                )
                diagonal[x0 + i, y0 + j] = shared_row(g, pot_row + cell) * (
                    scale / potential_gain
                ) + (3.0 * factors[0] - filter_center * scale)

    over_slabs(take_slab, 1)

    distance = jnp.abs(
        lax.broadcasted_iota(jnp.int32, (nz, nz), 0) - lax.broadcasted_iota(jnp.int32, (nz, nz), 1)
    )
    along_z = jnp.zeros((nz, nz), jnp.float32)
    for step in range(1, reach + 1):
        along_z = jnp.where(distance == step, factors[step], along_z)
    z_high = along_z.astype(jnp.bfloat16)
    z_low = (along_z - z_high.astype(jnp.float32)).astype(jnp.bfloat16)
    z_matrix = jnp.concatenate(
        [
            jnp.concatenate([z_high, z_low], axis=1),
            jnp.concatenate([z_high, jnp.zeros_like(z_high)], axis=1),
        ],
        axis=0,
    )

    def along(cells, at):
        total = None
        for step in range(1, reach + 1):
            near = [cells[n] for n in (at - step, at + step) if 0 <= n < len(cells)]
            if near:
                term = factors[step] * sum(near[1:], near[0])
                total = term if total is None else total + term
        return total

    def apply(source, target, finish, gain):
        def xz_part(y, carry):
            column = source[pl.ds(ring, count_x), ring + y]
            flat = column.reshape(count_x * each, nz)
            high = flat.astype(jnp.bfloat16)
            low = (flat - high.astype(jnp.float32)).astype(jnp.bfloat16)
            both = jnp.dot(
                jnp.concatenate([high, low], axis=1), z_matrix, preferred_element_type=jnp.float32
            )
            along_z = (both[:, :nz] + both[:, nz:]).reshape(column.shape)
            cells = [column[x] for x in range(count_x)]
            for x in range(count_x):
                partial[x, y] = along_z[x] + diagonal[x, y] * cells[x] + along(cells, x)
            return carry

        lax.fori_loop(0, count_y, xz_part, 0, unroll=2)

        def y_part(x, carry):
            cells = [source[ring + x, ring + y] for y in range(count_y)]
            for y in range(count_y):
                total = partial[x, y] + along(cells, y)
                target[ring + x, ring + y] = finish(total, target, ring + x, ring + y)
            return carry

        lax.fori_loop(0, count_x, y_part, 0, unroll=2)

        def place_of(g, a):
            at = 2 * atoms * projs + 2 * a
            return (
                ring + numbers[g, at].astype(jnp.int32),
                ring + numbers[g, at + 1].astype(jnp.int32),
            )

        def gather_part(g):
            for a in range(atoms):
                at_x, at_y = place_of(g, a)
                totals = [None] * projs
                for t in range(tiles):
                    tile = source[at_x + offsets_x[t], at_y + offsets_y[t]]
                    for p in range(projs):
                        term = tile * shared_row(g, (a * tiles + t) * projs + p)
                        totals[p] = term if t == 0 else totals[p] + term
                for p in range(projs):
                    k = a * projs + p
                    energy = numbers[g, k] + numbers[g, atoms * projs + k] * (1.0 / remainder_gain)
                    coeffs[g, k] = jnp.broadcast_to(
                        jnp.sum(totals[p], axis=-1, keepdims=True)
                        * (energy * (gain / projector_gain / projector_gain)),
                        (each, nz),
                    )

        over_slabs(gather_part, 4)

        def scatter_part(g):
            for a in range(atoms):
                at_x, at_y = place_of(g, a)
                factor = [coeffs[g, a * projs + p] for p in range(projs)]
                for t in range(tiles):
                    row = (a * tiles + t) * projs
                    spread = factor[0] * shared_row(g, row)
                    for p in range(1, projs):
                        spread = spread + factor[p] * shared_row(g, row + p)
                    to_x = at_x + offsets_x[t]
                    to_y = at_y + offsets_y[t]
                    target[to_x, to_y] = target[to_x, to_y] + spread

        over_slabs(scatter_part, 2)

    for copy in copies:
        copy.wait()
    apply(first, second, lambda total, target, x, y: total, scale)

    for x in (0, ring + count_x):
        second[x] = jnp.zeros(second.shape[1:], jnp.float32)
    for y in (0, ring + count_y):
        second[:, y] = jnp.zeros((second.shape[0],) + second.shape[2:], jnp.float32)

    apply(second, first, lambda total, target, x, y: 2.0 * total - target[x, y], 2.0 * scale)

    portion = rounded_ref.shape[-1] // nz

    def round_slab(g):
        place, x0, y0 = corner(g)
        for i in range(cells_x):
            for j in range(cells_y):
                cell = i * cells_y + j
                share = (cell // portion) * group + place
                lanes = pl.ds((cell % portion) * nz, nz)
                value = first[ring + x0 + i, ring + y0 + j].astype(jnp.bfloat16)
                rounded_ref[share, :, lanes] = value

    over_slabs(round_slab, 1)
    copy_out = pltpu.make_async_copy(rounded_ref, rounded_out, sent)
    copy_out.start()

    def largest_of(x, largest):
        row = jnp.abs(first[ring + x, pl.ds(ring, count_y)])
        return jnp.maximum(largest, jnp.max(row, axis=0))

    largest = lax.fori_loop(0, count_x, largest_of, jnp.zeros((each, nz), jnp.float32), unroll=2)
    level, gain = level_of(jnp.max(largest))
    level_rows = jnp.full((8, nz), level, jnp.float32)

    def give_slab(g):
        _, x0, y0 = corner(g)
        field_ref[g, pl.ds(slab_cells * each, 8), :] = level_rows
        for i in range(cells_x):
            for j in range(cells_y):
                cell = i * cells_y + j
                field_ref[g, pl.ds(cell * each, each), :] = first[ring + x0 + i, ring + y0 + j] * gain

    over_slabs(give_slab, 1)
    copy_out.wait()


def entry(block, place):
    picked = jnp.where(place, block, 0.0)
    return jnp.sum(jnp.sum(picked, axis=0, keepdims=True), axis=1, keepdims=True)


def band_corner(shape, band):
    row = lax.broadcasted_iota(jnp.int32, shape, 0)
    column = lax.broadcasted_iota(jnp.int32, shape, 1)
    return (
        (row == 1) & (column == band * shape[0]),
        (row == 0) & (column == band * shape[0] + 1),
    )


def gram_kernel(matrix_ref, out_ref, sums_ref):
    bands, rows, columns = out_ref.shape
    matrix = matrix_ref[...]
    sums = lax.dot_general(
        matrix, matrix, (((1,), (1,)), ((), ())), preferred_element_type=jnp.float32
    )
    level, gain = level_of(jnp.max(jnp.abs(sums)))
    sums_ref[...] = sums * gain
    me = lax.axis_index("band")
    for k in range(bands):
        band = jnp.bitwise_xor(me, k)
        spare, _ = band_corner((rows, columns), band)
        block = sums_ref[pl.ds(pl.multiple_of(band * rows, rows), rows), :]
        out_ref[k] = jnp.where(spare, level, block)


def rows_kernel(cells, own_ref, *refs):
    out_ref = refs[-1]
    spare, twin = band_corner(out_ref.shape, lax.axis_index("band"))
    total = None
    for block in [own_ref[0]] + [ref[...] for ref in refs[:-1]]:
        block = block * shrink_of(entry(block, spare))
        total = block if total is None else total + block
    out_ref[...] = jnp.where(spare, entry(total, twin), total) / cells


def unpack_kernel(each, slabs_y, places, *refs):
    pieces = refs[:-3]
    filtered_hbm, filtered_ref, chunk_sems = refs[-3:]
    slab_cells, _, nz = filtered_ref.shape
    chunks = chunk_sems.shape[0]
    chunk = slab_cells // chunks
    me = lax.axis_index("sx") * slabs_y + lax.axis_index("sy") if len(pieces) > 1 else 0
    copies = []
    for c in range(chunks):
        for which, entry, other in places:
            piece = pieces[which]
            shrink = shrink_of(piece[entry, pl.ds(slab_cells * each, 1), :])
            if len(pieces) > 1:
                rows = pl.ds(pl.multiple_of(jnp.bitwise_xor(me, other) * each, each), each)
            else:
                rows = pl.ds(other * each, each)
            for cell in range(c * chunk, (c + 1) * chunk):
                filtered_ref[cell, rows, :] = piece[entry, pl.ds(cell * each, each), :] * shrink
        part = pl.ds(c * chunk, chunk)
        copies.append(
            pltpu.make_async_copy(filtered_ref.at[part], filtered_hbm.at[part], chunk_sems.at[c])
        )
        copies[-1].start()
    for copy in copies:
        copy.wait()


def swap(block, value):
    group = lax.axis_size(plane)
    return lax.ppermute(block, plane, [(i, i ^ value) for i in range(group)])


def local(orbitals, potential, projectors, energies, centers):
    band_orbitals, cells_x, cells_y, nz = orbitals.shape
    bands = lax.axis_size("band")
    slabs_x = lax.axis_size("sx")
    slabs_y = lax.axis_size("sy")
    group = slabs_x * slabs_y
    each = band_orbitals // group
    total_orbitals = bands * band_orbitals
    slab_cells = cells_x * cells_y
    grid = (slabs_x * cells_x, slabs_y * cells_y)
    atoms, projs, tiles, _ = projectors.shape

    near = slabs_y
    far = [v for v in range(1, group) if not v & near]
    by_swaps = group <= 8 and each % 8 == 0 and slabs_x > 1
    by_swaps = by_swaps and group & (group - 1) == 0 and bands & (bands - 1) == 0

    rows = atoms * projs * tiles + slab_cells + 1
    rows += -rows % 8
    piece_rows = slab_cells * each
    chunks = (orbitals * orbital_gain).astype(jnp.float16)
    chunks = chunks.transpose(1, 2, 0, 3).reshape(slab_cells, group, each, nz)
    chunks = chunks.transpose(1, 0, 2, 3).reshape(group, piece_rows, nz)
    shared = pl.pallas_call(
        share_kernel,
        in_specs=[hbm, smem, smem, vmem, vmem],
        out_specs=vmem,
        out_shape=jax.ShapeDtypeStruct((rows, nz), jnp.float32),
        compiler_params=params,
    )(chunks[0, :8].astype(jnp.float32), energies, centers.T, projectors.transpose(0, 2, 1, 3), potential)
    narrow = shared.astype(jnp.float16)
    if by_swaps:
        me = lax.axis_index(plane)

        def chunk_for(value):
            return lax.dynamic_index_in_dim(chunks, me ^ value, 0, keepdims=False)

        passed = [swap(jnp.concatenate([chunk_for(v ^ near), narrow]), v) for v in far]
        direct = [swap(chunk_for(v), v) for v in far]
        mine = jnp.concatenate([chunk_for(near), narrow])
        crossed = swap(jnp.stack([mine] + passed), near)
        operands = [chunk_for(0)[None], narrow[None]] + [b[None] for b in direct + passed] + [crossed]
        operands = [block.astype(jnp.float32) for block in operands]
        operands[1] = shared[None]
        slabs = {0: ((0, 0, 0), (1, 0, 0))}
        last = len(operands) - 1
        slabs[near] = ((last, 0, 0), (last, 0, piece_rows))
        for i, v in enumerate(far):
            slabs[v] = ((2 + i, 0, 0), (2 + len(far) + i, 0, piece_rows))
            slabs[v ^ near] = ((last, 1 + i, 0), (last, 1 + i, piece_rows))
    else:
        sent = jnp.concatenate([chunks, jnp.broadcast_to(narrow[None], (group, rows, nz))], axis=1)
        operands = [lax.all_to_all(sent, plane, 0, 0).astype(jnp.float32)]
        slabs = None

    portion = slab_cells // bands
    ringed = (grid[0] + 2, grid[1] + 2, each, nz)
    shares = bands * group
    rounded_shape = (shares, each, portion * nz)
    field, rounded = pl.pallas_call(
        functools.partial(filter_kernel, slabs_y, cells_x, cells_y, each, atoms, projs, slabs),
        in_specs=[vmem] * len(operands),
        out_specs=[vmem, hbm],
        out_shape=[
            jax.ShapeDtypeStruct((group, piece_rows + 8, nz), jnp.float32),
            jax.ShapeDtypeStruct(rounded_shape, jnp.bfloat16),
        ],
        scratch_shapes=[
            pltpu.VMEM(ringed, jnp.float32),
            pltpu.VMEM(ringed, jnp.float32),
            pltpu.VMEM(grid + (each, nz), jnp.float32),
            pltpu.VMEM(grid + (1, nz), jnp.float32),
            pltpu.VMEM((group, atoms * projs, each, nz), jnp.float32),
            pltpu.SMEM((group, nz), jnp.float32),
            pltpu.VMEM(rounded_shape, jnp.bfloat16),
            pltpu.SemaphoreType.DMA((group,)),
            pltpu.SemaphoreType.DMA,
        ],
        compiler_params=params,
        cost_estimate=pl.CostEstimate(
            flops=2 * 2 * 40 * grid[0] * grid[1] * each * nz,
            bytes_accessed=8 * grid[0] * grid[1] * each * nz,
            transcendentals=0,
        ),
    )(*operands)

    matrix = lax.all_to_all(rounded, every, 0, 0)
    matrix = matrix.reshape(total_orbitals, portion * nz)
    if by_swaps:
        narrow = field.astype(jnp.float16)
        came = [swap(jnp.stack([narrow[v], narrow[v | near]]), v) for v in far]
        came, matrix = lax.optimization_barrier((came, matrix))
        came.append(swap(jnp.stack([narrow[near]] + [block[1] for block in came]), near))
        pieces = [field] + [block.astype(jnp.float32) for block in came]
        places = [(0, 0, 0), (len(pieces) - 1, 0, near)]
        for i, v in enumerate(far):
            places += [(i + 1, 0, v), (len(pieces) - 1, i + 1, v | near)]
    else:
        pieces = [lax.all_to_all(field.astype(jnp.float16), plane, 0, 0).astype(jnp.float32)]
        places = [(0, g, g) for g in range(group)]

    def unpack(pieces):
        return pl.pallas_call(
            functools.partial(unpack_kernel, each, slabs_y, places),
            in_specs=[vmem] * len(pieces),
            out_specs=hbm,
            out_shape=jax.ShapeDtypeStruct((slab_cells, band_orbitals, nz), jnp.float32),
            scratch_shapes=[
                pltpu.VMEM((slab_cells, band_orbitals, nz), jnp.float32),
                pltpu.SemaphoreType.DMA((cells_x,)),
            ],
            compiler_params=params,
        )(*pieces)

    cells = grid[0] * grid[1] * nz
    if by_swaps:
        sums = pl.pallas_call(
            gram_kernel,
            in_specs=[vmem],
            out_specs=vmem,
            out_shape=jax.ShapeDtypeStruct((bands, band_orbitals, total_orbitals), jnp.float32),
            scratch_shapes=[pltpu.VMEM((total_orbitals, total_orbitals), jnp.float32)],
            compiler_params=params,
        )(matrix)
        parts = [
            lax.ppermute(
                sums[k].astype(jnp.float16), "band", [(i, i ^ k) for i in range(bands)]
            ).astype(jnp.float32)
            for k in range(1, bands)
        ]
        parts, pieces = lax.optimization_barrier((parts, pieces))
        gram = pl.pallas_call(
            functools.partial(rows_kernel, cells),
            in_specs=[vmem] * bands,
            out_specs=vmem,
            out_shape=jax.ShapeDtypeStruct((band_orbitals, total_orbitals), jnp.float32),
            compiler_params=params,
        )(sums, *parts)
        terms = {v: swap(gram, v) for v in far}
        terms[0] = gram
        bit = 1
        while len(terms) > 1:
            terms = {v: terms[v] + terms[v ^ bit] for v in terms if not v & bit and v ^ bit in terms} or terms
            bit *= 2
        gram, filtered = lax.optimization_barrier((terms[0], unpack(pieces)))
        gram = gram + swap(gram, near)
    else:
        sums = lax.dot_general(
            matrix, matrix, (((1,), (1,)), ((), ())), preferred_element_type=jnp.float32
        )
        parts = lax.all_to_all(sums.reshape(shares, each, total_orbitals), every, 0, 0)
        rows = jnp.sum(parts, axis=0) / cells
        gram = lax.all_to_all(jnp.broadcast_to(rows[None], (group,) + rows.shape), plane, 0, 0)
        gram = gram.reshape(band_orbitals, total_orbitals)
        filtered = unpack(pieces)

    filtered = filtered.reshape(cells_x, cells_y, band_orbitals, nz).transpose(2, 0, 1, 3)
    return (filtered, gram)


def solution(mesh):
    in_specs = (
        P("band", "sx", "sy", None),
        P("sx", "sy", None),
        P(("sx", "sy"), None, None, None),
        P(("sx", "sy"), None),
        P(("sx", "sy"), None),
    )
    out_specs = (P("band", "sx", "sy", None), P("band", None))
    return jax.shard_map(local, mesh=mesh, in_specs=in_specs, out_specs=out_specs, check_vma=False)
```

```python
import functools

import jax
import jax.numpy as jnp
from jax import lax
from jax.experimental import pallas as pl
from jax.experimental.pallas import tpu as pltpu
from jax.sharding import PartitionSpec as P

stencil_weights = (
    -5369.0 / 1800.0,
    12.0 / 7.0,
    -15.0 / 56.0,
    10.0 / 189.0,
    -1.0 / 112.0,
    2.0 / 1925.0,
    -1.0 / 16632.0,
)
filter_center = 6.5
filter_half = 6.0
offsets_x = (0, -1, 1, 0, 0)
offsets_y = (0, 0, 0, -1, 1)
reach = 6
plane = ("sx", "sy")
every = ("band", "sx", "sy")

orbital_gain = 2.0**12
projector_gain = 2.0**17
potential_gain = 2.0**13
remainder_gain = 2.0**10
top = 15
middle = 8
levels = 17

vmem = pl.BlockSpec(memory_space=pltpu.VMEM)
smem = pl.BlockSpec(memory_space=pltpu.SMEM)
hbm = pl.BlockSpec(memory_space=pl.ANY)
params = pltpu.CompilerParams(vmem_limit_bytes=24 * 1024 * 1024)


def level_of(largest):
    level = jnp.float32(0.0)
    scale = jnp.float32(2.0 ** (top + 8 * middle))
    for j in range(levels):
        above = largest >= jnp.float32(2.0 ** (8 * (j - middle)))
        level = jnp.where(above, jnp.float32(j + 1), level)
        scale = jnp.where(above, jnp.float32(2.0 ** (top - 8 * (j + 1 - middle))), scale)
    return level, scale


def shrink_of(level):
    shrink = jnp.full(level.shape, 2.0 ** (-top - 8 * middle), jnp.float32)
    for j in range(levels):
        shrink = jnp.where(level > j, jnp.float32(2.0 ** (8 * (j + 1 - middle) - top)), shrink)
    return shrink


def share_kernel(_, energies_ref, centers_ref, projectors_ref, potential_ref, out_ref):
    rows, nz = out_ref.shape
    atoms, tiles, projs = projectors_ref.shape[:3]

    row = 0
    for a in range(atoms):
        for t in range(tiles):
            out_ref[pl.ds(row, projs), :] = projectors_ref[a, t] * projector_gain
            row += projs
    for i in range(potential_ref.shape[0]):
        count = potential_ref.shape[1]
        out_ref[pl.ds(row, count), :] = potential_ref[i] * potential_gain
        row += count
    lane = lax.broadcasted_iota(jnp.int32, (1, nz), 1)
    numbers = jnp.zeros((1, nz), jnp.float32)
    for a in range(atoms):
        for p in range(projs):
            numbers = jnp.where(lane == a * projs + p, energies_ref[a, p], numbers)
    high = numbers.astype(jnp.bfloat16).astype(jnp.float32)
    low = (numbers - high) * remainder_gain
    count = atoms * projs
    numbers = high + pltpu.roll(low, count, 1)
    for a in range(atoms):
        for d in range(2):
            here = centers_ref[d, a].astype(jnp.float32)
            numbers = jnp.where(lane == 2 * count + 2 * a + d, here, numbers)
    out_ref[pl.ds(row, 1), :] = numbers
    out_ref[pl.ds(row + 1, rows - row - 1), :] = jnp.zeros((rows - row - 1, nz), jnp.float32)


def filter_kernel(slabs_y, cells_x, cells_y, each, atoms, projs, slabs, *refs):
    inputs, (first, rounded_out) = refs[:-10], refs[-10:-8]
    second, partial, diagonal, coeffs, numbers, rounded_ref, arrived, sent = refs[-8:]
    group = numbers.shape[0]
    nz = first.shape[-1]
    count_x, count_y = diagonal.shape[0], diagonal.shape[1]
    tiles = len(offsets_x)
    slab_cells = cells_x * cells_y
    pot_row = atoms * projs * tiles
    number_row = pot_row + slab_cells
    scale = 1.0 / filter_half
    factors = [-0.5 * scale * w for w in stencil_weights]
    ring = 1
    me = 0 if slabs is None else lax.axis_index("sx") * slabs_y + lax.axis_index("sy")

    def rows_of(g, shared, row, count):
        if slabs is None:
            return inputs[0].at[g, pl.ds(row + (slab_cells * each if shared else 0), count), :]
        which, at, start = slabs[g][1 if shared else 0]
        return inputs[which].at[at, pl.ds(start + row, count), :]

    def shared_row(g, row):
        return rows_of(g, True, row, 1)[...]

    def over_slabs(body, unroll):
        if slabs is None:
            lax.fori_loop(0, group, lambda g, carry: body(g) or carry, 0, unroll=min(group, unroll))
        else:
            for g in range(group):
                body(g)

    def corner(g):
        place = g if slabs is None else jnp.bitwise_xor(me, g)
        return place, (place // slabs_y) * cells_x, (place % slabs_y) * cells_y

    if slabs is None:
        copies = [
            pltpu.make_async_copy(
                inputs[0].at[:, slab_cells * each + number_row, :], numbers, arrived.at[0]
            )
        ]
    else:
        copies = [
            pltpu.make_async_copy(
                rows_of(g, True, number_row, 1), numbers.at[pl.ds(g, 1), :], arrived.at[g]
            )
            for g in range(group)
        ]
    for copy in copies:
        copy.start()

    for field in (first, second):
        for x in (0, ring + count_x):
            field[x] = jnp.zeros(field.shape[1:], jnp.float32)
        for y in (0, ring + count_y):
            field[:, y] = jnp.zeros((field.shape[0],) + field.shape[2:], jnp.float32)

    def take_slab(g):
        _, x0, y0 = corner(g)
        for i in range(cells_x):
            for j in range(cells_y):
                cell = i * cells_y + j
                first[ring + x0 + i, ring + y0 + j] = rows_of(g, False, cell * each, each)[...] * (
                    1.0 / orbital_gain
                )
                diagonal[x0 + i, y0 + j] = shared_row(g, pot_row + cell) * (
                    scale / potential_gain
                ) + (3.0 * factors[0] - filter_center * scale)

    over_slabs(take_slab, 1)

    distance = jnp.abs(
        lax.broadcasted_iota(jnp.int32, (nz, nz), 0) - lax.broadcasted_iota(jnp.int32, (nz, nz), 1)
    )
    along_z = jnp.zeros((nz, nz), jnp.float32)
    for step in range(1, reach + 1):
        along_z = jnp.where(distance == step, factors[step], along_z)
    z_high = along_z.astype(jnp.bfloat16)
    z_low = (along_z - z_high.astype(jnp.float32)).astype(jnp.bfloat16)
    z_matrix = jnp.concatenate(
        [
            jnp.concatenate([z_high, z_low], axis=1),
            jnp.concatenate([z_high, jnp.zeros_like(z_high)], axis=1),
        ],
        axis=0,
    )

    def along(cells, at):
        total = None
        for step in range(1, reach + 1):
            near = [cells[n] for n in (at - step, at + step) if 0 <= n < len(cells)]
            if near:
                term = factors[step] * sum(near[1:], near[0])
                total = term if total is None else total + term
        return total

    def apply(source, target, finish, gain):
        def xz_part(y, carry):
            column = source[pl.ds(ring, count_x), ring + y]
            flat = column.reshape(count_x * each, nz)
            high = flat.astype(jnp.bfloat16)
            low = (flat - high.astype(jnp.float32)).astype(jnp.bfloat16)
            both = jnp.dot(
                jnp.concatenate([high, low], axis=1), z_matrix, preferred_element_type=jnp.float32
            )
            along_z = (both[:, :nz] + both[:, nz:]).reshape(column.shape)
            cells = [column[x] for x in range(count_x)]
            for x in range(count_x):
                partial[x, y] = along_z[x] + diagonal[x, y] * cells[x] + along(cells, x)
            return carry

        lax.fori_loop(0, count_y, xz_part, 0, unroll=2)

        def y_part(x, carry):
            cells = [source[ring + x, ring + y] for y in range(count_y)]
            for y in range(count_y):
                total = partial[x, y] + along(cells, y)
                target[ring + x, ring + y] = finish(total, target, ring + x, ring + y)
            return carry

        lax.fori_loop(0, count_x, y_part, 0, unroll=2)

        def place_of(g, a):
            at = 2 * atoms * projs + 2 * a
            return (
                ring + numbers[g, at].astype(jnp.int32),
                ring + numbers[g, at + 1].astype(jnp.int32),
            )

        def gather_part(g):
            for a in range(atoms):
                at_x, at_y = place_of(g, a)
                totals = [None] * projs
                for t in range(tiles):
                    tile = source[at_x + offsets_x[t], at_y + offsets_y[t]]
                    for p in range(projs):
                        term = tile * shared_row(g, (a * tiles + t) * projs + p)
                        totals[p] = term if t == 0 else totals[p] + term
                for p in range(projs):
                    k = a * projs + p
                    energy = numbers[g, k] + numbers[g, atoms * projs + k] * (1.0 / remainder_gain)
                    coeffs[g, k] = jnp.broadcast_to(
                        jnp.sum(totals[p], axis=-1, keepdims=True)
                        * (energy * (gain / projector_gain / projector_gain)),
                        (each, nz),
                    )

        over_slabs(gather_part, 4)

        def scatter_part(g):
            for a in range(atoms):
                at_x, at_y = place_of(g, a)
                factor = [coeffs[g, a * projs + p] for p in range(projs)]
                for t in range(tiles):
                    row = (a * tiles + t) * projs
                    spread = factor[0] * shared_row(g, row)
                    for p in range(1, projs):
                        spread = spread + factor[p] * shared_row(g, row + p)
                    to_x = at_x + offsets_x[t]
                    to_y = at_y + offsets_y[t]
                    target[to_x, to_y] = target[to_x, to_y] + spread

        over_slabs(scatter_part, 2)

    for copy in copies:
        copy.wait()
    apply(first, second, lambda total, target, x, y: total, scale)

    for x in (0, ring + count_x):
        second[x] = jnp.zeros(second.shape[1:], jnp.float32)
    for y in (0, ring + count_y):
        second[:, y] = jnp.zeros((second.shape[0],) + second.shape[2:], jnp.float32)

    apply(second, first, lambda total, target, x, y: 2.0 * total - target[x, y], 2.0 * scale)

    portion = rounded_ref.shape[-1] // nz

    parts = slab_cells // portion
    leaving = []
    for part in range(parts):

        def round_slab(g):
            place, x0, y0 = corner(g)
            for within in range(portion):
                i, j = divmod(part * portion + within, cells_y)
                rounded_ref[part * group + place, :, pl.ds(within * nz, nz)] = first[
                    ring + x0 + i, ring + y0 + j
                ].astype(jnp.bfloat16)

        over_slabs(round_slab, 1)
        shares = pl.ds(part * group, group)
        leaving.append(
            pltpu.make_async_copy(rounded_ref.at[shares], rounded_out.at[shares], sent.at[part])
        )
        leaving[-1].start()
    for copy in leaving:
        copy.wait()


def scale_kernel(slabs_y, cells_x, cells_y, by_swaps, values_ref, field_ref):
    group, rows, nz = field_ref.shape
    each = values_ref.shape[2]
    ring = 1
    count_x, count_y = values_ref.shape[0] - 2 * ring, values_ref.shape[1] - 2 * ring
    me = lax.axis_index("sx") * slabs_y + lax.axis_index("sy") if by_swaps else 0

    def largest_of(x, largest):
        row = jnp.abs(values_ref[ring + x, pl.ds(ring, count_y)])
        return jnp.maximum(largest, jnp.max(row, axis=0))

    largest = lax.fori_loop(0, count_x, largest_of, jnp.zeros((each, nz), jnp.float32), unroll=2)
    level, gain = level_of(jnp.max(largest))
    level_rows = jnp.full((8, nz), level, jnp.float32)

    def give_slab(g, carry):
        place = jnp.bitwise_xor(me, g) if by_swaps else g
        x0 = (place // slabs_y) * cells_x
        y0 = (place % slabs_y) * cells_y
        field_ref[g, pl.ds(rows - 8, 8), :] = level_rows
        for i in range(cells_x):
            for j in range(cells_y):
                field_ref[g, pl.ds((i * cells_y + j) * each, each), :] = (
                    values_ref[ring + x0 + i, ring + y0 + j] * gain
                )
        return carry

    lax.fori_loop(0, group, give_slab, 0)


def entry(block, place):
    picked = jnp.where(place, block, 0.0)
    return jnp.sum(jnp.sum(picked, axis=0, keepdims=True), axis=1, keepdims=True)


def band_corner(shape, band):
    row = lax.broadcasted_iota(jnp.int32, shape, 0)
    column = lax.broadcasted_iota(jnp.int32, shape, 1)
    return (
        (row == 1) & (column == band * shape[0]),
        (row == 0) & (column == band * shape[0] + 1),
    )


def gram_kernel(matrix_ref, out_ref, sums_ref):
    bands, rows, columns = out_ref.shape
    matrix = matrix_ref[...]
    sums = lax.dot_general(
        matrix, matrix, (((1,), (1,)), ((), ())), preferred_element_type=jnp.float32
    )
    level, gain = level_of(jnp.max(jnp.abs(sums)))
    sums_ref[...] = sums * gain
    me = lax.axis_index("band")
    for k in range(bands):
        band = jnp.bitwise_xor(me, k)
        spare, _ = band_corner((rows, columns), band)
        block = sums_ref[pl.ds(pl.multiple_of(band * rows, rows), rows), :]
        out_ref[k] = jnp.where(spare, level, block)


def rows_kernel(cells, own_ref, *refs):
    out_ref = refs[-1]
    spare, twin = band_corner(out_ref.shape, lax.axis_index("band"))
    total = None
    for block in [own_ref[0]] + [ref[...] for ref in refs[:-1]]:
        block = block * shrink_of(entry(block, spare))
        total = block if total is None else total + block
    total = jnp.where(spare, entry(total, twin), total) / cells
    level, gain = level_of(jnp.max(jnp.abs(total)))
    out_ref[...] = jnp.where(spare, level, total * gain)


def plane_kernel(far, *refs):
    out_ref = refs[-1]
    spare, twin = band_corner(out_ref.shape, lax.axis_index("band"))
    terms = {}
    for v, ref in zip([0] + far, refs[:-1]):
        block = ref[...]
        terms[v] = block * shrink_of(entry(block, spare))
    bit = 1
    while len(terms) > 1:
        if any(v ^ bit in terms for v in terms):
            terms = {v: terms[v] + terms[v ^ bit] for v in terms if not v & bit}
        bit *= 2
    total = terms[0]
    out_ref[...] = jnp.where(spare, entry(total, twin), total)


def unpack_kernel(each, slabs_y, places, *refs):
    pieces = refs[:-3]
    filtered_hbm, filtered_ref, chunk_sems = refs[-3:]
    slab_cells, _, nz = filtered_ref.shape
    chunks = chunk_sems.shape[0]
    chunk = slab_cells // chunks
    me = lax.axis_index("sx") * slabs_y + lax.axis_index("sy") if len(pieces) > 1 else 0
    copies = []
    for c in range(chunks):
        for which, entry, other in places:
            piece = pieces[which]
            shrink = shrink_of(piece[entry, pl.ds(slab_cells * each, 1), :])
            if len(pieces) > 1:
                rows = pl.ds(pl.multiple_of(jnp.bitwise_xor(me, other) * each, each), each)
            else:
                rows = pl.ds(other * each, each)
            for cell in range(c * chunk, (c + 1) * chunk):
                filtered_ref[cell, rows, :] = piece[entry, pl.ds(cell * each, each), :] * shrink
        part = pl.ds(c * chunk, chunk)
        copies.append(
            pltpu.make_async_copy(filtered_ref.at[part], filtered_hbm.at[part], chunk_sems.at[c])
        )
        copies[-1].start()
    for copy in copies:
        copy.wait()


def swap(block, value):
    group = lax.axis_size(plane)
    return lax.ppermute(block, plane, [(i, i ^ value) for i in range(group)])


def local(orbitals, potential, projectors, energies, centers):
    band_orbitals, cells_x, cells_y, nz = orbitals.shape
    bands = lax.axis_size("band")
    slabs_x = lax.axis_size("sx")
    slabs_y = lax.axis_size("sy")
    group = slabs_x * slabs_y
    each = band_orbitals // group
    total_orbitals = bands * band_orbitals
    slab_cells = cells_x * cells_y
    grid = (slabs_x * cells_x, slabs_y * cells_y)
    atoms, projs, tiles, _ = projectors.shape

    near = slabs_y
    far = [v for v in range(1, group) if not v & near]
    by_swaps = group <= 8 and each % 8 == 0 and slabs_x > 1
    by_swaps = by_swaps and group & (group - 1) == 0 and bands & (bands - 1) == 0

    rows = atoms * projs * tiles + slab_cells + 1
    rows += -rows % 8
    piece_rows = slab_cells * each
    chunks = (orbitals * orbital_gain).astype(jnp.float16)
    chunks = chunks.transpose(1, 2, 0, 3).reshape(slab_cells, group, each, nz)
    chunks = chunks.transpose(1, 0, 2, 3).reshape(group, piece_rows, nz)
    shared = pl.pallas_call(
        share_kernel,
        in_specs=[hbm, smem, smem, vmem, vmem],
        out_specs=vmem,
        out_shape=jax.ShapeDtypeStruct((rows, nz), jnp.float32),
        compiler_params=params,
    )(chunks[0, :8].astype(jnp.float32), energies, centers.T, projectors.transpose(0, 2, 1, 3), potential)
    narrow = shared.astype(jnp.float16)
    if by_swaps:
        me = lax.axis_index(plane)

        def chunk_for(value):
            return lax.dynamic_index_in_dim(chunks, me ^ value, 0, keepdims=False)

        passed = [swap(jnp.concatenate([chunk_for(v ^ near), narrow]), v) for v in far]
        direct = [swap(chunk_for(v), v) for v in far]
        mine = jnp.concatenate([chunk_for(near), narrow])
        crossed = swap(jnp.stack([mine] + passed), near)
        operands = [chunk_for(0)[None], narrow[None]] + [b[None] for b in direct + passed] + [crossed]
        operands = [block.astype(jnp.float32) for block in operands]
        operands[1] = shared[None]
        slabs = {0: ((0, 0, 0), (1, 0, 0))}
        last = len(operands) - 1
        slabs[near] = ((last, 0, 0), (last, 0, piece_rows))
        for i, v in enumerate(far):
            slabs[v] = ((2 + i, 0, 0), (2 + len(far) + i, 0, piece_rows))
            slabs[v ^ near] = ((last, 1 + i, 0), (last, 1 + i, piece_rows))
    else:
        sent = jnp.concatenate([chunks, jnp.broadcast_to(narrow[None], (group, rows, nz))], axis=1)
        operands = [lax.all_to_all(sent, plane, 0, 0).astype(jnp.float32)]
        slabs = None

    portion = slab_cells // bands
    ringed = (grid[0] + 2, grid[1] + 2, each, nz)
    shares = bands * group
    rounded_shape = (shares, each, portion * nz)
    values, rounded = pl.pallas_call(
        functools.partial(filter_kernel, slabs_y, cells_x, cells_y, each, atoms, projs, slabs),
        in_specs=[vmem] * len(operands),
        out_specs=[vmem, hbm],
        out_shape=[
            jax.ShapeDtypeStruct(ringed, jnp.float32),
            jax.ShapeDtypeStruct(rounded_shape, jnp.bfloat16),
        ],
        scratch_shapes=[
            pltpu.VMEM(ringed, jnp.float32),
            pltpu.VMEM(grid + (each, nz), jnp.float32),
            pltpu.VMEM(grid + (1, nz), jnp.float32),
            pltpu.VMEM((group, atoms * projs, each, nz), jnp.float32),
            pltpu.SMEM((group, nz), jnp.float32),
            pltpu.VMEM(rounded_shape, jnp.bfloat16),
            pltpu.SemaphoreType.DMA((group,)),
            pltpu.SemaphoreType.DMA((bands,)),
        ],
        compiler_params=params,
        cost_estimate=pl.CostEstimate(
            flops=2 * 2 * 40 * grid[0] * grid[1] * each * nz,
            bytes_accessed=8 * grid[0] * grid[1] * each * nz,
            transcendentals=0,
        ),
    )(*operands)

    matrix = lax.all_to_all(rounded, every, 0, 0)
    matrix = matrix.reshape(total_orbitals, portion * nz)
    field = pl.pallas_call(
        functools.partial(scale_kernel, slabs_y, cells_x, cells_y, by_swaps),
        in_specs=[vmem],
        out_specs=vmem,
        out_shape=jax.ShapeDtypeStruct((group, piece_rows + 8, nz), jnp.float32),
        compiler_params=params,
    )(values)
    narrow = field.astype(jnp.float16)
    if by_swaps:
        came = [swap(narrow[v], v) for v in range(1, group)]
        came, matrix = lax.optimization_barrier((came, matrix))
        pieces = [field] + [block.astype(jnp.float32)[None] for block in came]
        places = [(v, 0, v) for v in range(group)]
    else:
        pieces = [lax.all_to_all(narrow, plane, 0, 0).astype(jnp.float32)]
        places = [(0, g, g) for g in range(group)]

    def unpack(pieces):
        return pl.pallas_call(
            functools.partial(unpack_kernel, each, slabs_y, places),
            in_specs=[vmem] * len(pieces),
            out_specs=hbm,
            out_shape=jax.ShapeDtypeStruct((slab_cells, band_orbitals, nz), jnp.float32),
            scratch_shapes=[
                pltpu.VMEM((slab_cells, band_orbitals, nz), jnp.float32),
                pltpu.SemaphoreType.DMA((cells_x,)),
            ],
            compiler_params=params,
        )(*pieces)

    cells = grid[0] * grid[1] * nz
    if by_swaps:
        sums = pl.pallas_call(
            gram_kernel,
            in_specs=[vmem],
            out_specs=vmem,
            out_shape=jax.ShapeDtypeStruct((bands, band_orbitals, total_orbitals), jnp.float32),
            scratch_shapes=[pltpu.VMEM((total_orbitals, total_orbitals), jnp.float32)],
            compiler_params=params,
        )(matrix)
        parts = [
            lax.ppermute(
                sums[k].astype(jnp.float16), "band", [(i, i ^ k) for i in range(bands)]
            ).astype(jnp.float32)
            for k in range(1, bands)
        ]
        parts, filtered = lax.optimization_barrier((parts, unpack(pieces)))
        block = jax.ShapeDtypeStruct((band_orbitals, total_orbitals), jnp.float32)
        own = pl.pallas_call(
            functools.partial(rows_kernel, cells),
            in_specs=[vmem] * bands,
            out_specs=vmem,
            out_shape=block,
            compiler_params=params,
        )(sums, *parts)
        own = lax.reduce_precision(own, 5, 10)
        terms = [own] + [swap(own.astype(jnp.float16), v) for v in far]
        gram = pl.pallas_call(
            functools.partial(plane_kernel, far),
            in_specs=[vmem] * len(terms),
            out_specs=vmem,
            out_shape=block,
            compiler_params=params,
        )(*[term.astype(jnp.float32) for term in terms])
        gram = gram + swap(gram, near)
    else:
        sums = lax.dot_general(
            matrix, matrix, (((1,), (1,)), ((), ())), preferred_element_type=jnp.float32
        )
        parts = lax.all_to_all(sums.reshape(shares, each, total_orbitals), every, 0, 0)
        rows = jnp.sum(parts, axis=0) / cells
        gram = lax.all_to_all(jnp.broadcast_to(rows[None], (group,) + rows.shape), plane, 0, 0)
        gram = gram.reshape(band_orbitals, total_orbitals)
        filtered = unpack(pieces)

    filtered = filtered.reshape(cells_x, cells_y, band_orbitals, nz).transpose(2, 0, 1, 3)
    return (filtered, gram)


def solution(mesh):
    in_specs = (
        P("band", "sx", "sy", None),
        P("sx", "sy", None),
        P(("sx", "sy"), None, None, None),
        P(("sx", "sy"), None),
        P(("sx", "sy"), None),
    )
    out_specs = (P("band", "sx", "sy", None), P("band", None))
    return jax.shard_map(local, mesh=mesh, in_specs=in_specs, out_specs=out_specs, check_vma=False)
```

```python
import functools

import jax
import jax.numpy as jnp
from jax import lax
from jax.experimental import pallas as pl
from jax.experimental.pallas import tpu as pltpu
from jax.sharding import PartitionSpec as P

stencil_weights = (
    -5369.0 / 1800.0,
    12.0 / 7.0,
    -15.0 / 56.0,
    10.0 / 189.0,
    -1.0 / 112.0,
    2.0 / 1925.0,
    -1.0 / 16632.0,
)
filter_center = 6.5
filter_half = 6.0
offsets_x = (0, -1, 1, 0, 0)
offsets_y = (0, 0, 0, -1, 1)
reach = 6
plane = ("sx", "sy")
every = ("band", "sx", "sy")

orbital_gain = 2.0**12
projector_gain = 2.0**17
potential_gain = 2.0**13
remainder_gain = 2.0**10
top = 15
middle = 8
levels = 17

vmem = pl.BlockSpec(memory_space=pltpu.VMEM)
smem = pl.BlockSpec(memory_space=pltpu.SMEM)
hbm = pl.BlockSpec(memory_space=pl.ANY)
params = pltpu.CompilerParams(vmem_limit_bytes=24 * 1024 * 1024)


def level_of(largest):
    level = jnp.float32(0.0)
    scale = jnp.float32(2.0 ** (top + 8 * middle))
    for j in range(levels):
        above = largest >= jnp.float32(2.0 ** (8 * (j - middle)))
        level = jnp.where(above, jnp.float32(j + 1), level)
        scale = jnp.where(above, jnp.float32(2.0 ** (top - 8 * (j + 1 - middle))), scale)
    return level, scale


def shrink_of(level):
    shrink = jnp.full(level.shape, 2.0 ** (-top - 8 * middle), jnp.float32)
    for j in range(levels):
        shrink = jnp.where(level > j, jnp.float32(2.0 ** (8 * (j + 1 - middle) - top)), shrink)
    return shrink


def share_kernel(_, energies_ref, centers_ref, projectors_ref, potential_ref, out_ref):
    rows, nz = out_ref.shape
    atoms, tiles, projs = projectors_ref.shape[:3]

    row = 0
    for a in range(atoms):
        for t in range(tiles):
            out_ref[pl.ds(row, projs), :] = projectors_ref[a, t] * projector_gain
            row += projs
    for i in range(potential_ref.shape[0]):
        count = potential_ref.shape[1]
        out_ref[pl.ds(row, count), :] = potential_ref[i] * potential_gain
        row += count
    lane = lax.broadcasted_iota(jnp.int32, (1, nz), 1)
    numbers = jnp.zeros((1, nz), jnp.float32)
    for a in range(atoms):
        for p in range(projs):
            numbers = jnp.where(lane == a * projs + p, energies_ref[a, p], numbers)
    high = numbers.astype(jnp.bfloat16).astype(jnp.float32)
    low = (numbers - high) * remainder_gain
    count = atoms * projs
    numbers = high + pltpu.roll(low, count, 1)
    for a in range(atoms):
        for d in range(2):
            here = centers_ref[d, a].astype(jnp.float32)
            numbers = jnp.where(lane == 2 * count + 2 * a + d, here, numbers)
    out_ref[pl.ds(row, 1), :] = numbers
    out_ref[pl.ds(row + 1, rows - row - 1), :] = jnp.zeros((rows - row - 1, nz), jnp.float32)


def filter_kernel(slabs_y, cells_x, cells_y, each, atoms, projs, slabs, *refs):
    inputs, (first, rounded_out) = refs[:-10], refs[-10:-8]
    second, partial, diagonal, coeffs, numbers, rounded_ref, arrived, sent = refs[-8:]
    group = numbers.shape[0]
    nz = first.shape[-1]
    count_x, count_y = diagonal.shape[0], diagonal.shape[1]
    tiles = len(offsets_x)
    slab_cells = cells_x * cells_y
    pot_row = atoms * projs * tiles
    number_row = pot_row + slab_cells
    scale = 1.0 / filter_half
    factors = [-0.5 * scale * w for w in stencil_weights]
    ring = 1
    me = 0 if slabs is None else lax.axis_index("sx") * slabs_y + lax.axis_index("sy")

    def rows_of(g, shared, row, count):
        if slabs is None:
            return inputs[0].at[g, pl.ds(row + (slab_cells * each if shared else 0), count), :]
        which, at, start = slabs[g][1 if shared else 0]
        return inputs[which].at[at, pl.ds(start + row, count), :]

    def shared_row(g, row):
        return rows_of(g, True, row, 1)[...]

    def over_slabs(body, unroll):
        if slabs is None:
            lax.fori_loop(0, group, lambda g, carry: body(g) or carry, 0, unroll=min(group, unroll))
        else:
            for g in range(group):
                body(g)

    def corner(g):
        place = g if slabs is None else jnp.bitwise_xor(me, g)
        return place, (place // slabs_y) * cells_x, (place % slabs_y) * cells_y

    if slabs is None:
        copies = [
            pltpu.make_async_copy(
                inputs[0].at[:, slab_cells * each + number_row, :], numbers, arrived.at[0]
            )
        ]
    else:
        copies = [
            pltpu.make_async_copy(
                rows_of(g, True, number_row, 1), numbers.at[pl.ds(g, 1), :], arrived.at[g]
            )
            for g in range(group)
        ]
    for copy in copies:
        copy.start()

    for field in (first, second):
        for x in (0, ring + count_x):
            field[x] = jnp.zeros(field.shape[1:], jnp.float32)
        for y in (0, ring + count_y):
            field[:, y] = jnp.zeros((field.shape[0],) + field.shape[2:], jnp.float32)

    def take_slab(g):
        _, x0, y0 = corner(g)
        for i in range(cells_x):
            for j in range(cells_y):
                cell = i * cells_y + j
                first[ring + x0 + i, ring + y0 + j] = rows_of(g, False, cell * each, each)[...] * (
                    1.0 / orbital_gain
                )
                diagonal[x0 + i, y0 + j] = shared_row(g, pot_row + cell) * (
                    scale / potential_gain
                ) + (3.0 * factors[0] - filter_center * scale)

    over_slabs(take_slab, 1)

    distance = jnp.abs(
        lax.broadcasted_iota(jnp.int32, (nz, nz), 0) - lax.broadcasted_iota(jnp.int32, (nz, nz), 1)
    )
    along_z = jnp.zeros((nz, nz), jnp.float32)
    for step in range(1, reach + 1):
        along_z = jnp.where(distance == step, factors[step], along_z)
    z_high = along_z.astype(jnp.bfloat16)
    z_low = (along_z - z_high.astype(jnp.float32)).astype(jnp.bfloat16)
    z_matrix = jnp.concatenate(
        [
            jnp.concatenate([z_high, z_low], axis=1),
            jnp.concatenate([z_high, jnp.zeros_like(z_high)], axis=1),
        ],
        axis=0,
    )

    def along(cells, at):
        total = None
        for step in range(1, reach + 1):
            near = [cells[n] for n in (at - step, at + step) if 0 <= n < len(cells)]
            if near:
                term = factors[step] * sum(near[1:], near[0])
                total = term if total is None else total + term
        return total

    def apply(source, target, finish, gain):
        def xz_part(y, carry):
            column = source[pl.ds(ring, count_x), ring + y]
            flat = column.reshape(count_x * each, nz)
            high = flat.astype(jnp.bfloat16)
            low = (flat - high.astype(jnp.float32)).astype(jnp.bfloat16)
            both = jnp.dot(
                jnp.concatenate([high, low], axis=1), z_matrix, preferred_element_type=jnp.float32
            )
            along_z = (both[:, :nz] + both[:, nz:]).reshape(column.shape)
            cells = [column[x] for x in range(count_x)]
            for x in range(count_x):
                partial[x, y] = along_z[x] + diagonal[x, y] * cells[x] + along(cells, x)
            return carry

        lax.fori_loop(0, count_y, xz_part, 0, unroll=2)

        def y_part(x, carry):
            cells = [source[ring + x, ring + y] for y in range(count_y)]
            for y in range(count_y):
                total = partial[x, y] + along(cells, y)
                target[ring + x, ring + y] = finish(total, target, ring + x, ring + y)
            return carry

        lax.fori_loop(0, count_x, y_part, 0, unroll=2)

        def place_of(g, a):
            at = 2 * atoms * projs + 2 * a
            return (
                ring + numbers[g, at].astype(jnp.int32),
                ring + numbers[g, at + 1].astype(jnp.int32),
            )

        def gather_part(g):
            for a in range(atoms):
                at_x, at_y = place_of(g, a)
                totals = [None] * projs
                for t in range(tiles):
                    tile = source[at_x + offsets_x[t], at_y + offsets_y[t]]
                    for p in range(projs):
                        term = tile * shared_row(g, (a * tiles + t) * projs + p)
                        totals[p] = term if t == 0 else totals[p] + term
                for p in range(projs):
                    k = a * projs + p
                    energy = numbers[g, k] + numbers[g, atoms * projs + k] * (1.0 / remainder_gain)
                    coeffs[g, k] = jnp.broadcast_to(
                        jnp.sum(totals[p], axis=-1, keepdims=True)
                        * (energy * (gain / projector_gain / projector_gain)),
                        (each, nz),
                    )

        over_slabs(gather_part, 4)

        def scatter_part(g):
            for a in range(atoms):
                at_x, at_y = place_of(g, a)
                factor = [coeffs[g, a * projs + p] for p in range(projs)]
                for t in range(tiles):
                    row = (a * tiles + t) * projs
                    spread = factor[0] * shared_row(g, row)
                    for p in range(1, projs):
                        spread = spread + factor[p] * shared_row(g, row + p)
                    to_x = at_x + offsets_x[t]
                    to_y = at_y + offsets_y[t]
                    target[to_x, to_y] = target[to_x, to_y] + spread

        over_slabs(scatter_part, 2)

    for copy in copies:
        copy.wait()
    apply(first, second, lambda total, target, x, y: total, scale)

    for x in (0, ring + count_x):
        second[x] = jnp.zeros(second.shape[1:], jnp.float32)
    for y in (0, ring + count_y):
        second[:, y] = jnp.zeros((second.shape[0],) + second.shape[2:], jnp.float32)

    apply(second, first, lambda total, target, x, y: 2.0 * total - target[x, y], 2.0 * scale)

    portion = rounded_ref.shape[-1] // nz

    parts = slab_cells // portion
    leaving = []
    for part in range(parts):

        def round_slab(g):
            place, x0, y0 = corner(g)
            for within in range(portion):
                i, j = divmod(part * portion + within, cells_y)
                rounded_ref[part * group + place, :, pl.ds(within * nz, nz)] = first[
                    ring + x0 + i, ring + y0 + j
                ].astype(jnp.bfloat16)

        over_slabs(round_slab, 1)
        shares = pl.ds(part * group, group)
        leaving.append(
            pltpu.make_async_copy(rounded_ref.at[shares], rounded_out.at[shares], sent.at[part])
        )
        leaving[-1].start()
    for copy in leaving:
        copy.wait()


def scale_kernel(slabs_y, cells_x, cells_y, by_swaps, values_ref, field_ref):
    group, rows, nz = field_ref.shape
    each = values_ref.shape[2]
    ring = 1
    count_x, count_y = values_ref.shape[0] - 2 * ring, values_ref.shape[1] - 2 * ring
    me = lax.axis_index("sx") * slabs_y + lax.axis_index("sy") if by_swaps else 0

    def largest_of(x, largest):
        row = jnp.abs(values_ref[ring + x, pl.ds(ring, count_y)])
        return jnp.maximum(largest, jnp.max(row, axis=0))

    largest = lax.fori_loop(0, count_x, largest_of, jnp.zeros((each, nz), jnp.float32), unroll=2)
    level, gain = level_of(jnp.max(largest))
    level_rows = jnp.full((8, nz), level, jnp.float32)

    def give_slab(g, carry):
        place = jnp.bitwise_xor(me, g) if by_swaps else g
        x0 = (place // slabs_y) * cells_x
        y0 = (place % slabs_y) * cells_y
        field_ref[g, pl.ds(rows - 8, 8), :] = level_rows
        for i in range(cells_x):
            for j in range(cells_y):
                field_ref[g, pl.ds((i * cells_y + j) * each, each), :] = (
                    values_ref[ring + x0 + i, ring + y0 + j] * gain
                )
        return carry

    lax.fori_loop(0, group, give_slab, 0)


def entry(block, place):
    picked = jnp.where(place, block, 0.0)
    return jnp.sum(jnp.sum(picked, axis=0, keepdims=True), axis=1, keepdims=True)


def band_corner(shape, band):
    row = lax.broadcasted_iota(jnp.int32, shape, 0)
    column = lax.broadcasted_iota(jnp.int32, shape, 1)
    return (
        (row == 1) & (column == band * shape[0]),
        (row == 0) & (column == band * shape[0] + 1),
    )


def gram_kernel(matrix_ref, out_ref, sums_ref):
    bands, rows, columns = out_ref.shape
    matrix = matrix_ref[...]
    sums = lax.dot_general(
        matrix, matrix, (((1,), (1,)), ((), ())), preferred_element_type=jnp.float32
    )
    level, gain = level_of(jnp.max(jnp.abs(sums)))
    sums_ref[...] = sums * gain
    me = lax.axis_index("band")
    for k in range(bands):
        band = jnp.bitwise_xor(me, k)
        spare, _ = band_corner((rows, columns), band)
        block = sums_ref[pl.ds(pl.multiple_of(band * rows, rows), rows), :]
        out_ref[k] = jnp.where(spare, level, block)


def rows_kernel(cells, own_ref, *refs):
    out_ref = refs[-1]
    spare, twin = band_corner(out_ref.shape, lax.axis_index("band"))
    total = None
    for block in [own_ref[0]] + [ref[...] for ref in refs[:-1]]:
        block = block * shrink_of(entry(block, spare))
        total = block if total is None else total + block
    out_ref[...] = jnp.where(spare, entry(total, twin), total) / cells


def unpack_kernel(each, slabs_y, places, *refs):
    pieces = refs[:-3]
    filtered_hbm, filtered_ref, chunk_sems = refs[-3:]
    slab_cells, _, nz = filtered_ref.shape
    chunks = chunk_sems.shape[0]
    chunk = slab_cells // chunks
    me = lax.axis_index("sx") * slabs_y + lax.axis_index("sy") if len(pieces) > 1 else 0
    copies = []
    for c in range(chunks):
        for which, entry, other in places:
            piece = pieces[which]
            shrink = shrink_of(piece[entry, pl.ds(slab_cells * each, 1), :])
            if len(pieces) > 1:
                rows = pl.ds(pl.multiple_of(jnp.bitwise_xor(me, other) * each, each), each)
            else:
                rows = pl.ds(other * each, each)
            for cell in range(c * chunk, (c + 1) * chunk):
                filtered_ref[cell, rows, :] = piece[entry, pl.ds(cell * each, each), :] * shrink
        part = pl.ds(c * chunk, chunk)
        copies.append(
            pltpu.make_async_copy(filtered_ref.at[part], filtered_hbm.at[part], chunk_sems.at[c])
        )
        copies[-1].start()
    for copy in copies:
        copy.wait()


def swap(block, value):
    group = lax.axis_size(plane)
    return lax.ppermute(block, plane, [(i, i ^ value) for i in range(group)])


def local(orbitals, potential, projectors, energies, centers):
    band_orbitals, cells_x, cells_y, nz = orbitals.shape
    bands = lax.axis_size("band")
    slabs_x = lax.axis_size("sx")
    slabs_y = lax.axis_size("sy")
    group = slabs_x * slabs_y
    each = band_orbitals // group
    total_orbitals = bands * band_orbitals
    slab_cells = cells_x * cells_y
    grid = (slabs_x * cells_x, slabs_y * cells_y)
    atoms, projs, tiles, _ = projectors.shape

    near = slabs_y
    far = [v for v in range(1, group) if not v & near]
    by_swaps = group <= 8 and each % 8 == 0 and slabs_x > 1
    by_swaps = by_swaps and group & (group - 1) == 0 and bands & (bands - 1) == 0

    rows = atoms * projs * tiles + slab_cells + 1
    rows += -rows % 8
    piece_rows = slab_cells * each
    chunks = (orbitals * orbital_gain).astype(jnp.float16)
    chunks = chunks.transpose(1, 2, 0, 3).reshape(slab_cells, group, each, nz)
    chunks = chunks.transpose(1, 0, 2, 3).reshape(group, piece_rows, nz)
    shared = pl.pallas_call(
        share_kernel,
        in_specs=[hbm, smem, smem, vmem, vmem],
        out_specs=vmem,
        out_shape=jax.ShapeDtypeStruct((rows, nz), jnp.float32),
        compiler_params=params,
    )(chunks[0, :8].astype(jnp.float32), energies, centers.T, projectors.transpose(0, 2, 1, 3), potential)
    narrow = shared.astype(jnp.float16)
    if by_swaps:
        me = lax.axis_index(plane)

        def chunk_for(value):
            return lax.dynamic_index_in_dim(chunks, me ^ value, 0, keepdims=False)

        came = [swap(jnp.concatenate([chunk_for(v), narrow]), v) for v in range(1, group)]
        operands = [chunk_for(0).astype(jnp.float32)[None], shared[None]]
        operands += [block.astype(jnp.float32)[None] for block in came]
        slabs = {v: ((1 + v, 0, 0), (1 + v, 0, piece_rows)) for v in range(1, group)}
        slabs[0] = ((0, 0, 0), (1, 0, 0))
    else:
        sent = jnp.concatenate([chunks, jnp.broadcast_to(narrow[None], (group, rows, nz))], axis=1)
        operands = [lax.all_to_all(sent, plane, 0, 0).astype(jnp.float32)]
        slabs = None

    portion = slab_cells // bands
    ringed = (grid[0] + 2, grid[1] + 2, each, nz)
    shares = bands * group
    rounded_shape = (shares, each, portion * nz)
    values, rounded = pl.pallas_call(
        functools.partial(filter_kernel, slabs_y, cells_x, cells_y, each, atoms, projs, slabs),
        in_specs=[vmem] * len(operands),
        out_specs=[vmem, hbm],
        out_shape=[
            jax.ShapeDtypeStruct(ringed, jnp.float32),
            jax.ShapeDtypeStruct(rounded_shape, jnp.bfloat16),
        ],
        scratch_shapes=[
            pltpu.VMEM(ringed, jnp.float32),
            pltpu.VMEM(grid + (each, nz), jnp.float32),
            pltpu.VMEM(grid + (1, nz), jnp.float32),
            pltpu.VMEM((group, atoms * projs, each, nz), jnp.float32),
            pltpu.SMEM((group, nz), jnp.float32),
            pltpu.VMEM(rounded_shape, jnp.bfloat16),
            pltpu.SemaphoreType.DMA((group,)),
            pltpu.SemaphoreType.DMA((bands,)),
        ],
        compiler_params=params,
        cost_estimate=pl.CostEstimate(
            flops=2 * 2 * 40 * grid[0] * grid[1] * each * nz,
            bytes_accessed=8 * grid[0] * grid[1] * each * nz,
            transcendentals=0,
        ),
    )(*operands)

    matrix = lax.all_to_all(rounded, every, 0, 0)
    matrix = matrix.reshape(total_orbitals, portion * nz)
    field = pl.pallas_call(
        functools.partial(scale_kernel, slabs_y, cells_x, cells_y, by_swaps),
        in_specs=[vmem],
        out_specs=vmem,
        out_shape=jax.ShapeDtypeStruct((group, piece_rows + 8, nz), jnp.float32),
        compiler_params=params,
    )(values)
    narrow = field.astype(jnp.float16)
    if by_swaps:
        came = [swap(narrow[v], v) for v in range(1, group)]
        came, matrix = lax.optimization_barrier((came, matrix))
        pieces = [field] + [block.astype(jnp.float32)[None] for block in came]
        places = [(v, 0, v) for v in range(group)]
    else:
        pieces = [lax.all_to_all(narrow, plane, 0, 0).astype(jnp.float32)]
        places = [(0, g, g) for g in range(group)]

    def unpack(pieces):
        return pl.pallas_call(
            functools.partial(unpack_kernel, each, slabs_y, places),
            in_specs=[vmem] * len(pieces),
            out_specs=hbm,
            out_shape=jax.ShapeDtypeStruct((slab_cells, band_orbitals, nz), jnp.float32),
            scratch_shapes=[
                pltpu.VMEM((slab_cells, band_orbitals, nz), jnp.float32),
                pltpu.SemaphoreType.DMA((cells_x,)),
            ],
            compiler_params=params,
        )(*pieces)

    cells = grid[0] * grid[1] * nz
    if by_swaps:
        sums = pl.pallas_call(
            gram_kernel,
            in_specs=[vmem],
            out_specs=vmem,
            out_shape=jax.ShapeDtypeStruct((bands, band_orbitals, total_orbitals), jnp.float32),
            scratch_shapes=[pltpu.VMEM((total_orbitals, total_orbitals), jnp.float32)],
            compiler_params=params,
        )(matrix)
        parts = [
            lax.ppermute(
                sums[k].astype(jnp.float16), "band", [(i, i ^ k) for i in range(bands)]
            ).astype(jnp.float32)
            for k in range(1, bands)
        ]
        gram = pl.pallas_call(
            functools.partial(rows_kernel, cells),
            in_specs=[vmem] * bands,
            out_specs=vmem,
            out_shape=jax.ShapeDtypeStruct((band_orbitals, total_orbitals), jnp.float32),
            compiler_params=params,
        )(sums, *parts)
        terms = {v: swap(gram, v) for v in far}
        terms[0] = gram
        bit = 1
        while len(terms) > 1:
            if any(v ^ bit in terms for v in terms):
                terms = {v: terms[v] + terms[v ^ bit] for v in terms if not v & bit}
            bit *= 2
        gram, filtered = lax.optimization_barrier((terms[0], unpack(pieces)))
        gram = gram + swap(gram, near)
    else:
        sums = lax.dot_general(
            matrix, matrix, (((1,), (1,)), ((), ())), preferred_element_type=jnp.float32
        )
        parts = lax.all_to_all(sums.reshape(shares, each, total_orbitals), every, 0, 0)
        rows = jnp.sum(parts, axis=0) / cells
        gram = lax.all_to_all(jnp.broadcast_to(rows[None], (group,) + rows.shape), plane, 0, 0)
        gram = gram.reshape(band_orbitals, total_orbitals)
        filtered = unpack(pieces)

    filtered = filtered.reshape(cells_x, cells_y, band_orbitals, nz).transpose(2, 0, 1, 3)
    return (filtered, gram)


def solution(mesh):
    in_specs = (
        P("band", "sx", "sy", None),
        P("sx", "sy", None),
        P(("sx", "sy"), None, None, None),
        P(("sx", "sy"), None),
        P(("sx", "sy"), None),
    )
    out_specs = (P("band", "sx", "sy", None), P("band", None))
    return jax.shard_map(local, mesh=mesh, in_specs=in_specs, out_specs=out_specs, check_vma=False)
```

```python
import functools

import jax
import jax.numpy as jnp
from jax import lax
from jax.experimental import pallas as pl
from jax.experimental.pallas import tpu as pltpu
from jax.sharding import PartitionSpec as P

stencil_weights = (
    -5369.0 / 1800.0,
    12.0 / 7.0,
    -15.0 / 56.0,
    10.0 / 189.0,
    -1.0 / 112.0,
    2.0 / 1925.0,
    -1.0 / 16632.0,
)
filter_center = 6.5
filter_half = 6.0
offsets_x = (0, -1, 1, 0, 0)
offsets_y = (0, 0, 0, -1, 1)
reach = 6
plane = ("sx", "sy")
every = ("band", "sx", "sy")

orbital_gain = 2.0**12
projector_gain = 2.0**17
potential_gain = 2.0**13
remainder_gain = 2.0**10
top = 15
middle = 8
levels = 17

vmem = pl.BlockSpec(memory_space=pltpu.VMEM)
smem = pl.BlockSpec(memory_space=pltpu.SMEM)
hbm = pl.BlockSpec(memory_space=pl.ANY)
params = pltpu.CompilerParams(vmem_limit_bytes=24 * 1024 * 1024)


def level_of(largest):
    level = jnp.float32(0.0)
    scale = jnp.float32(2.0 ** (top + 8 * middle))
    for j in range(levels):
        above = largest >= jnp.float32(2.0 ** (8 * (j - middle)))
        level = jnp.where(above, jnp.float32(j + 1), level)
        scale = jnp.where(above, jnp.float32(2.0 ** (top - 8 * (j + 1 - middle))), scale)
    return level, scale


def shrink_of(level):
    shrink = jnp.full(level.shape, 2.0 ** (-top - 8 * middle), jnp.float32)
    for j in range(levels):
        shrink = jnp.where(level > j, jnp.float32(2.0 ** (8 * (j + 1 - middle) - top)), shrink)
    return shrink


def share_kernel(_, energies_ref, centers_ref, projectors_ref, potential_ref, out_ref):
    rows, nz = out_ref.shape
    atoms, tiles, projs = projectors_ref.shape[:3]

    row = 0
    for a in range(atoms):
        for t in range(tiles):
            out_ref[pl.ds(row, projs), :] = projectors_ref[a, t] * projector_gain
            row += projs
    for i in range(potential_ref.shape[0]):
        count = potential_ref.shape[1]
        out_ref[pl.ds(row, count), :] = potential_ref[i] * potential_gain
        row += count
    lane = lax.broadcasted_iota(jnp.int32, (1, nz), 1)
    numbers = jnp.zeros((1, nz), jnp.float32)
    for a in range(atoms):
        for p in range(projs):
            numbers = jnp.where(lane == a * projs + p, energies_ref[a, p], numbers)
    high = numbers.astype(jnp.bfloat16).astype(jnp.float32)
    low = (numbers - high) * remainder_gain
    count = atoms * projs
    numbers = high + pltpu.roll(low, count, 1)
    for a in range(atoms):
        for d in range(2):
            here = centers_ref[d, a].astype(jnp.float32)
            numbers = jnp.where(lane == 2 * count + 2 * a + d, here, numbers)
    out_ref[pl.ds(row, 1), :] = numbers
    out_ref[pl.ds(row + 1, rows - row - 1), :] = jnp.zeros((rows - row - 1, nz), jnp.float32)


def filter_kernel(slabs_y, cells_x, cells_y, each, atoms, projs, slabs, *refs):
    inputs, (first, rounded_out) = refs[:-10], refs[-10:-8]
    second, partial, diagonal, coeffs, numbers, rounded_ref, arrived, sent = refs[-8:]
    group = numbers.shape[0]
    nz = first.shape[-1]
    count_x, count_y = diagonal.shape[0], diagonal.shape[1]
    tiles = len(offsets_x)
    slab_cells = cells_x * cells_y
    pot_row = atoms * projs * tiles
    number_row = pot_row + slab_cells
    scale = 1.0 / filter_half
    factors = [-0.5 * scale * w for w in stencil_weights]
    ring = 1
    me = 0 if slabs is None else lax.axis_index("sx") * slabs_y + lax.axis_index("sy")

    def rows_of(g, shared, row, count):
        if slabs is None:
            return inputs[0].at[g, pl.ds(row + (slab_cells * each if shared else 0), count), :]
        which, at, start = slabs[g][1 if shared else 0]
        return inputs[which].at[at, pl.ds(start + row, count), :]

    def shared_row(g, row):
        return rows_of(g, True, row, 1)[...]

    def over_slabs(body, unroll):
        if slabs is None:
            lax.fori_loop(0, group, lambda g, carry: body(g) or carry, 0, unroll=min(group, unroll))
        else:
            for g in range(group):
                body(g)

    def corner(g):
        place = g if slabs is None else jnp.bitwise_xor(me, g)
        return place, (place // slabs_y) * cells_x, (place % slabs_y) * cells_y

    if slabs is None:
        copies = [
            pltpu.make_async_copy(
                inputs[0].at[:, slab_cells * each + number_row, :], numbers, arrived.at[0]
            )
        ]
    else:
        copies = [
            pltpu.make_async_copy(
                rows_of(g, True, number_row, 1), numbers.at[pl.ds(g, 1), :], arrived.at[g]
            )
            for g in range(group)
        ]
    for copy in copies:
        copy.start()

    for field in (first, second):
        for x in (0, ring + count_x):
            field[x] = jnp.zeros(field.shape[1:], jnp.float32)
        for y in (0, ring + count_y):
            field[:, y] = jnp.zeros((field.shape[0],) + field.shape[2:], jnp.float32)

    def take_slab(g):
        _, x0, y0 = corner(g)
        for i in range(cells_x):
            for j in range(cells_y):
                cell = i * cells_y + j
                first[ring + x0 + i, ring + y0 + j] = rows_of(g, False, cell * each, each)[...] * (
                    1.0 / orbital_gain
                )
                diagonal[x0 + i, y0 + j] = shared_row(g, pot_row + cell) * (
                    scale / potential_gain
                ) + (3.0 * factors[0] - filter_center * scale)

    over_slabs(take_slab, 1)

    distance = jnp.abs(
        lax.broadcasted_iota(jnp.int32, (nz, nz), 0) - lax.broadcasted_iota(jnp.int32, (nz, nz), 1)
    )
    along_z = jnp.zeros((nz, nz), jnp.float32)
    for step in range(1, reach + 1):
        along_z = jnp.where(distance == step, factors[step], along_z)
    z_high = along_z.astype(jnp.bfloat16)
    z_low = (along_z - z_high.astype(jnp.float32)).astype(jnp.bfloat16)
    z_matrix = jnp.concatenate(
        [
            jnp.concatenate([z_high, z_low], axis=1),
            jnp.concatenate([z_high, jnp.zeros_like(z_high)], axis=1),
        ],
        axis=0,
    )

    def along(cells, at):
        total = None
        for step in range(1, reach + 1):
            near = [cells[n] for n in (at - step, at + step) if 0 <= n < len(cells)]
            if near:
                term = factors[step] * sum(near[1:], near[0])
                total = term if total is None else total + term
        return total

    def apply(source, target, finish, gain):
        def xz_part(y, carry):
            column = source[pl.ds(ring, count_x), ring + y]
            flat = column.reshape(count_x * each, nz)
            high = flat.astype(jnp.bfloat16)
            low = (flat - high.astype(jnp.float32)).astype(jnp.bfloat16)
            both = jnp.dot(
                jnp.concatenate([high, low], axis=1), z_matrix, preferred_element_type=jnp.float32
            )
            along_z = (both[:, :nz] + both[:, nz:]).reshape(column.shape)
            cells = [column[x] for x in range(count_x)]
            for x in range(count_x):
                partial[x, y] = along_z[x] + diagonal[x, y] * cells[x] + along(cells, x)
            return carry

        lax.fori_loop(0, count_y, xz_part, 0, unroll=2)

        def y_part(x, carry):
            cells = [source[ring + x, ring + y] for y in range(count_y)]
            for y in range(count_y):
                total = partial[x, y] + along(cells, y)
                target[ring + x, ring + y] = finish(total, target, ring + x, ring + y)
            return carry

        lax.fori_loop(0, count_x, y_part, 0, unroll=2)

        def place_of(g, a):
            at = 2 * atoms * projs + 2 * a
            return (
                ring + numbers[g, at].astype(jnp.int32),
                ring + numbers[g, at + 1].astype(jnp.int32),
            )

        def gather_part(g):
            for a in range(atoms):
                at_x, at_y = place_of(g, a)
                totals = [None] * projs
                for t in range(tiles):
                    tile = source[at_x + offsets_x[t], at_y + offsets_y[t]]
                    for p in range(projs):
                        term = tile * shared_row(g, (a * tiles + t) * projs + p)
                        totals[p] = term if t == 0 else totals[p] + term
                for p in range(projs):
                    k = a * projs + p
                    energy = numbers[g, k] + numbers[g, atoms * projs + k] * (1.0 / remainder_gain)
                    coeffs[g, k] = jnp.broadcast_to(
                        jnp.sum(totals[p], axis=-1, keepdims=True)
                        * (energy * (gain / projector_gain / projector_gain)),
                        (each, nz),
                    )

        over_slabs(gather_part, 4)

        def scatter_part(g):
            for a in range(atoms):
                at_x, at_y = place_of(g, a)
                factor = [coeffs[g, a * projs + p] for p in range(projs)]
                cells = [(at_x + offsets_x[t], at_y + offsets_y[t]) for t in range(tiles)]
                values = [target[cell] for cell in cells]
                for t in range(tiles):
                    row = (a * tiles + t) * projs
                    for p in range(projs):
                        values[t] = values[t] + factor[p] * shared_row(g, row + p)
                for t in range(tiles):
                    target[cells[t]] = values[t]

        over_slabs(scatter_part, 2)

    for copy in copies:
        copy.wait()
    apply(first, second, lambda total, target, x, y: total, scale)

    for x in (0, ring + count_x):
        second[x] = jnp.zeros(second.shape[1:], jnp.float32)
    for y in (0, ring + count_y):
        second[:, y] = jnp.zeros((second.shape[0],) + second.shape[2:], jnp.float32)

    apply(second, first, lambda total, target, x, y: 2.0 * total - target[x, y], 2.0 * scale)

    portion = rounded_ref.shape[-1] // nz

    parts = slab_cells // portion
    leaving = []
    for part in range(parts):

        def round_slab(g):
            place, x0, y0 = corner(g)
            for within in range(portion):
                i, j = divmod(part * portion + within, cells_y)
                rounded_ref[part * group + place, :, pl.ds(within * nz, nz)] = first[
                    ring + x0 + i, ring + y0 + j
                ].astype(jnp.bfloat16)

        over_slabs(round_slab, 1)
        shares = pl.ds(part * group, group)
        leaving.append(
            pltpu.make_async_copy(rounded_ref.at[shares], rounded_out.at[shares], sent.at[part])
        )
        leaving[-1].start()
    for copy in leaving:
        copy.wait()


def scale_kernel(slabs_y, cells_x, cells_y, by_swaps, values_ref, field_ref):
    group, rows, nz = field_ref.shape
    each = values_ref.shape[2]
    ring = 1
    count_x, count_y = values_ref.shape[0] - 2 * ring, values_ref.shape[1] - 2 * ring
    me = lax.axis_index("sx") * slabs_y + lax.axis_index("sy") if by_swaps else 0

    def largest_of(x, largest):
        row = jnp.abs(values_ref[ring + x, pl.ds(ring, count_y)])
        return jnp.maximum(largest, jnp.max(row, axis=0))

    largest = lax.fori_loop(0, count_x, largest_of, jnp.zeros((each, nz), jnp.float32), unroll=2)
    level, gain = level_of(jnp.max(largest))
    level_rows = jnp.full((8, nz), level, jnp.float32)

    def give_slab(g, carry):
        place = jnp.bitwise_xor(me, g) if by_swaps else g
        x0 = (place // slabs_y) * cells_x
        y0 = (place % slabs_y) * cells_y
        field_ref[g, pl.ds(rows - 8, 8), :] = level_rows
        for i in range(cells_x):
            for j in range(cells_y):
                field_ref[g, pl.ds((i * cells_y + j) * each, each), :] = (
                    values_ref[ring + x0 + i, ring + y0 + j] * gain
                )
        return carry

    lax.fori_loop(0, group, give_slab, 0)


def entry(block, place):
    picked = jnp.where(place, block, 0.0)
    return jnp.sum(jnp.sum(picked, axis=0, keepdims=True), axis=1, keepdims=True)


def band_corner(shape, band):
    row = lax.broadcasted_iota(jnp.int32, shape, 0)
    column = lax.broadcasted_iota(jnp.int32, shape, 1)
    return (
        (row == 1) & (column == band * shape[0]),
        (row == 0) & (column == band * shape[0] + 1),
    )


def gram_kernel(matrix_ref, out_ref):
    bands, rows, columns = out_ref.shape
    matrix = matrix_ref[...]
    sums = lax.dot_general(
        matrix, matrix, (((1,), (1,)), ((), ())), preferred_element_type=jnp.float32
    )
    level, gain = level_of(jnp.max(jnp.abs(sums)))
    for band in range(bands):
        spare, _ = band_corner((rows, columns), band)
        block = sums[band * rows : (band + 1) * rows]
        out_ref[band] = jnp.where(spare, level, block * gain)


def rows_kernel(cells, parts_ref, out_ref):
    spare, twin = band_corner(out_ref.shape, lax.axis_index("band"))
    total = None
    for source in range(parts_ref.shape[0]):
        block = parts_ref[source]
        block = block * shrink_of(entry(block, spare))
        total = block if total is None else total + block
    out_ref[...] = jnp.where(spare, entry(total, twin), total) / cells


def unpack_kernel(each, slabs_y, places, *refs):
    pieces = refs[:-3]
    filtered_hbm, filtered_ref, chunk_sems = refs[-3:]
    slab_cells, _, nz = filtered_ref.shape
    chunks = chunk_sems.shape[0]
    chunk = slab_cells // chunks
    me = lax.axis_index("sx") * slabs_y + lax.axis_index("sy") if len(pieces) > 1 else 0
    copies = []
    for c in range(chunks):
        for which, entry, other in places:
            piece = pieces[which]
            shrink = shrink_of(piece[entry, pl.ds(slab_cells * each, 1), :])
            if len(pieces) > 1:
                rows = pl.ds(pl.multiple_of(jnp.bitwise_xor(me, other) * each, each), each)
            else:
                rows = pl.ds(other * each, each)
            for cell in range(c * chunk, (c + 1) * chunk):
                filtered_ref[cell, rows, :] = piece[entry, pl.ds(cell * each, each), :] * shrink
        part = pl.ds(c * chunk, chunk)
        copies.append(
            pltpu.make_async_copy(filtered_ref.at[part], filtered_hbm.at[part], chunk_sems.at[c])
        )
        copies[-1].start()
    for copy in copies:
        copy.wait()


def swap(block, value):
    group = lax.axis_size(plane)
    return lax.ppermute(block, plane, [(i, i ^ value) for i in range(group)])


def local(orbitals, potential, projectors, energies, centers):
    band_orbitals, cells_x, cells_y, nz = orbitals.shape
    bands = lax.axis_size("band")
    slabs_x = lax.axis_size("sx")
    slabs_y = lax.axis_size("sy")
    group = slabs_x * slabs_y
    each = band_orbitals // group
    total_orbitals = bands * band_orbitals
    slab_cells = cells_x * cells_y
    grid = (slabs_x * cells_x, slabs_y * cells_y)
    atoms, projs, tiles, _ = projectors.shape

    near = slabs_y
    far = [v for v in range(1, group) if not v & near]
    by_swaps = group <= 8 and each % 8 == 0 and slabs_x > 1
    by_swaps = by_swaps and group & (group - 1) == 0 and bands & (bands - 1) == 0

    rows = atoms * projs * tiles + slab_cells + 1
    rows += -rows % 8
    piece_rows = slab_cells * each
    chunks = (orbitals * orbital_gain).astype(jnp.float16)
    chunks = chunks.transpose(1, 2, 0, 3).reshape(slab_cells, group, each, nz)
    chunks = chunks.transpose(1, 0, 2, 3).reshape(group, piece_rows, nz)
    shared = pl.pallas_call(
        share_kernel,
        in_specs=[hbm, smem, smem, vmem, vmem],
        out_specs=vmem,
        out_shape=jax.ShapeDtypeStruct((rows, nz), jnp.float32),
        compiler_params=params,
    )(chunks[0, :8].astype(jnp.float32), energies, centers.T, projectors.transpose(0, 2, 1, 3), potential)
    narrow = shared.astype(jnp.float16)
    if by_swaps:
        me = lax.axis_index(plane)

        def chunk_for(value):
            return lax.dynamic_index_in_dim(chunks, me ^ value, 0, keepdims=False)

        came = [swap(jnp.concatenate([chunk_for(v), narrow]), v) for v in range(1, group)]
        operands = [chunk_for(0).astype(jnp.float32)[None], shared[None]]
        operands += [block.astype(jnp.float32)[None] for block in came]
        slabs = {v: ((1 + v, 0, 0), (1 + v, 0, piece_rows)) for v in range(1, group)}
        slabs[0] = ((0, 0, 0), (1, 0, 0))
    else:
        sent = jnp.concatenate([chunks, jnp.broadcast_to(narrow[None], (group, rows, nz))], axis=1)
        operands = [lax.all_to_all(sent, plane, 0, 0).astype(jnp.float32)]
        slabs = None

    portion = slab_cells // bands
    ringed = (grid[0] + 2, grid[1] + 2, each, nz)
    shares = bands * group
    rounded_shape = (shares, each, portion * nz)
    values, rounded = pl.pallas_call(
        functools.partial(filter_kernel, slabs_y, cells_x, cells_y, each, atoms, projs, slabs),
        in_specs=[vmem] * len(operands),
        out_specs=[vmem, hbm],
        out_shape=[
            jax.ShapeDtypeStruct(ringed, jnp.float32),
            jax.ShapeDtypeStruct(rounded_shape, jnp.bfloat16),
        ],
        scratch_shapes=[
            pltpu.VMEM(ringed, jnp.float32),
            pltpu.VMEM(grid + (each, nz), jnp.float32),
            pltpu.VMEM(grid + (1, nz), jnp.float32),
            pltpu.VMEM((group, atoms * projs, each, nz), jnp.float32),
            pltpu.SMEM((group, nz), jnp.float32),
            pltpu.VMEM(rounded_shape, jnp.bfloat16),
            pltpu.SemaphoreType.DMA((group,)),
            pltpu.SemaphoreType.DMA((bands,)),
        ],
        compiler_params=params,
        cost_estimate=pl.CostEstimate(
            flops=2 * 2 * 40 * grid[0] * grid[1] * each * nz,
            bytes_accessed=8 * grid[0] * grid[1] * each * nz,
            transcendentals=0,
        ),
    )(*operands)

    matrix = lax.all_to_all(rounded, every, 0, 0)
    matrix = matrix.reshape(total_orbitals, portion * nz)
    field = pl.pallas_call(
        functools.partial(scale_kernel, slabs_y, cells_x, cells_y, by_swaps),
        in_specs=[vmem],
        out_specs=vmem,
        out_shape=jax.ShapeDtypeStruct((group, piece_rows + 8, nz), jnp.float32),
        compiler_params=params,
    )(values)
    narrow = field.astype(jnp.float16)
    if by_swaps:
        came = [swap(narrow[v], v) for v in range(1, group)]
        came, matrix = lax.optimization_barrier((came, matrix))
        pieces = [field] + [block.astype(jnp.float32)[None] for block in came]
        places = [(v, 0, v) for v in range(group)]
    else:
        pieces = [lax.all_to_all(narrow, plane, 0, 0).astype(jnp.float32)]
        places = [(0, g, g) for g in range(group)]

    def unpack(pieces):
        return pl.pallas_call(
            functools.partial(unpack_kernel, each, slabs_y, places),
            in_specs=[vmem] * len(pieces),
            out_specs=hbm,
            out_shape=jax.ShapeDtypeStruct((slab_cells, band_orbitals, nz), jnp.float32),
            scratch_shapes=[
                pltpu.VMEM((slab_cells, band_orbitals, nz), jnp.float32),
                pltpu.SemaphoreType.DMA((cells_x,)),
            ],
            compiler_params=params,
        )(*pieces)

    cells = grid[0] * grid[1] * nz
    if by_swaps:
        sums = pl.pallas_call(
            gram_kernel,
            in_specs=[vmem],
            out_specs=vmem,
            out_shape=jax.ShapeDtypeStruct((bands, band_orbitals, total_orbitals), jnp.float32),
            compiler_params=params,
        )(matrix)
        parts = lax.all_to_all(sums.astype(jnp.float16), "band", 0, 0).astype(jnp.float32)
        gram = pl.pallas_call(
            functools.partial(rows_kernel, cells),
            in_specs=[vmem],
            out_specs=vmem,
            out_shape=jax.ShapeDtypeStruct((band_orbitals, total_orbitals), jnp.float32),
            compiler_params=params,
        )(parts)
        terms = {v: swap(gram, v) for v in far}
        terms[0] = gram
        bit = 1
        while len(terms) > 1:
            if any(v ^ bit in terms for v in terms):
                terms = {v: terms[v] + terms[v ^ bit] for v in terms if not v & bit}
            bit *= 2
        gram, filtered = lax.optimization_barrier((terms[0], unpack(pieces)))
        gram = gram + swap(gram, near)
    else:
        sums = lax.dot_general(
            matrix, matrix, (((1,), (1,)), ((), ())), preferred_element_type=jnp.float32
        )
        parts = lax.all_to_all(sums.reshape(shares, each, total_orbitals), every, 0, 0)
        rows = jnp.sum(parts, axis=0) / cells
        gram = lax.all_to_all(jnp.broadcast_to(rows[None], (group,) + rows.shape), plane, 0, 0)
        gram = gram.reshape(band_orbitals, total_orbitals)
        filtered = unpack(pieces)

    filtered = filtered.reshape(cells_x, cells_y, band_orbitals, nz).transpose(2, 0, 1, 3)
    return (filtered, gram)


def solution(mesh):
    in_specs = (
        P("band", "sx", "sy", None),
        P("sx", "sy", None),
        P(("sx", "sy"), None, None, None),
        P(("sx", "sy"), None),
        P(("sx", "sy"), None),
    )
    out_specs = (P("band", "sx", "sy", None), P("band", None))
    return jax.shard_map(local, mesh=mesh, in_specs=in_specs, out_specs=out_specs, check_vma=False)
```

```python
import functools

import jax
import jax.numpy as jnp
from jax import lax
from jax.experimental import pallas as pl
from jax.experimental.pallas import tpu as pltpu
from jax.sharding import PartitionSpec as P

stencil_weights = (
    -5369.0 / 1800.0,
    12.0 / 7.0,
    -15.0 / 56.0,
    10.0 / 189.0,
    -1.0 / 112.0,
    2.0 / 1925.0,
    -1.0 / 16632.0,
)
filter_center = 6.5
filter_half = 6.0
offsets_x = (0, -1, 1, 0, 0)
offsets_y = (0, 0, 0, -1, 1)
reach = 6
plane = ("sx", "sy")
every = ("band", "sx", "sy")

orbital_gain = 2.0**12
projector_gain = 2.0**17
potential_gain = 2.0**13
remainder_gain = 2.0**10
top = 15
middle = 8
levels = 17

vmem = pl.BlockSpec(memory_space=pltpu.VMEM)
smem = pl.BlockSpec(memory_space=pltpu.SMEM)
hbm = pl.BlockSpec(memory_space=pl.ANY)
params = pltpu.CompilerParams(vmem_limit_bytes=24 * 1024 * 1024)


def level_of(largest):
    level = jnp.float32(0.0)
    scale = jnp.float32(2.0 ** (top + 8 * middle))
    for j in range(levels):
        above = largest >= jnp.float32(2.0 ** (8 * (j - middle)))
        level = jnp.where(above, jnp.float32(j + 1), level)
        scale = jnp.where(above, jnp.float32(2.0 ** (top - 8 * (j + 1 - middle))), scale)
    return level, scale


def shrink_of(level):
    shrink = jnp.full(level.shape, 2.0 ** (-top - 8 * middle), jnp.float32)
    for j in range(levels):
        shrink = jnp.where(level > j, jnp.float32(2.0 ** (8 * (j + 1 - middle) - top)), shrink)
    return shrink


def share_kernel(_, energies_ref, centers_ref, projectors_ref, potential_ref, out_ref):
    rows, nz = out_ref.shape
    atoms, tiles, projs = projectors_ref.shape[:3]

    row = 0
    for a in range(atoms):
        for t in range(tiles):
            out_ref[pl.ds(row, projs), :] = projectors_ref[a, t] * projector_gain
            row += projs
    for i in range(potential_ref.shape[0]):
        count = potential_ref.shape[1]
        out_ref[pl.ds(row, count), :] = potential_ref[i] * potential_gain
        row += count
    lane = lax.broadcasted_iota(jnp.int32, (1, nz), 1)
    numbers = jnp.zeros((1, nz), jnp.float32)
    for a in range(atoms):
        for p in range(projs):
            numbers = jnp.where(lane == a * projs + p, energies_ref[a, p], numbers)
    high = numbers.astype(jnp.bfloat16).astype(jnp.float32)
    low = (numbers - high) * remainder_gain
    count = atoms * projs
    numbers = high + pltpu.roll(low, count, 1)
    for a in range(atoms):
        for d in range(2):
            here = centers_ref[d, a].astype(jnp.float32)
            numbers = jnp.where(lane == 2 * count + 2 * a + d, here, numbers)
    out_ref[pl.ds(row, 1), :] = numbers
    out_ref[pl.ds(row + 1, rows - row - 1), :] = jnp.zeros((rows - row - 1, nz), jnp.float32)


def filter_kernel(slabs_y, cells_x, cells_y, each, atoms, projs, slabs, *refs):
    inputs, (first, rounded_out) = refs[:-10], refs[-10:-8]
    second, partial, diagonal, coeffs, numbers, rounded_ref, arrived, sent = refs[-8:]
    group = numbers.shape[0]
    nz = first.shape[-1]
    count_x, count_y = diagonal.shape[0], diagonal.shape[1]
    tiles = len(offsets_x)
    slab_cells = cells_x * cells_y
    pot_row = atoms * projs * tiles
    number_row = pot_row + slab_cells
    scale = 1.0 / filter_half
    factors = [-0.5 * scale * w for w in stencil_weights]
    ring = 1
    me = 0 if slabs is None else lax.axis_index("sx") * slabs_y + lax.axis_index("sy")

    def rows_of(g, shared, row, count):
        if slabs is None:
            return inputs[0].at[g, pl.ds(row + (slab_cells * each if shared else 0), count), :]
        which, at, start = slabs[g][1 if shared else 0]
        return inputs[which].at[at, pl.ds(start + row, count), :]

    def shared_row(g, row):
        return rows_of(g, True, row, 1)[...]

    def over_slabs(body, unroll):
        if slabs is None:
            lax.fori_loop(0, group, lambda g, carry: body(g) or carry, 0, unroll=min(group, unroll))
        else:
            for g in range(group):
                body(g)

    def corner(g):
        place = g if slabs is None else jnp.bitwise_xor(me, g)
        return place, (place // slabs_y) * cells_x, (place % slabs_y) * cells_y

    if slabs is None:
        copies = [
            pltpu.make_async_copy(
                inputs[0].at[:, slab_cells * each + number_row, :], numbers, arrived.at[0]
            )
        ]
    else:
        copies = [
            pltpu.make_async_copy(
                rows_of(g, True, number_row, 1), numbers.at[pl.ds(g, 1), :], arrived.at[g]
            )
            for g in range(group)
        ]
    for copy in copies:
        copy.start()

    for field in (first, second):
        for x in (0, ring + count_x):
            field[x] = jnp.zeros(field.shape[1:], jnp.float32)
        for y in (0, ring + count_y):
            field[:, y] = jnp.zeros((field.shape[0],) + field.shape[2:], jnp.float32)

    def take_slab(g):
        _, x0, y0 = corner(g)
        for i in range(cells_x):
            for j in range(cells_y):
                cell = i * cells_y + j
                first[ring + x0 + i, ring + y0 + j] = rows_of(g, False, cell * each, each)[...] * (
                    1.0 / orbital_gain
                )
                diagonal[x0 + i, y0 + j] = shared_row(g, pot_row + cell) * (
                    scale / potential_gain
                ) + (3.0 * factors[0] - filter_center * scale)

    over_slabs(take_slab, 1)

    distance = jnp.abs(
        lax.broadcasted_iota(jnp.int32, (nz, nz), 0) - lax.broadcasted_iota(jnp.int32, (nz, nz), 1)
    )
    along_z = jnp.zeros((nz, nz), jnp.float32)
    for step in range(1, reach + 1):
        along_z = jnp.where(distance == step, factors[step], along_z)
    z_high = along_z.astype(jnp.bfloat16)
    z_low = (along_z - z_high.astype(jnp.float32)).astype(jnp.bfloat16)
    z_matrix = jnp.concatenate(
        [
            jnp.concatenate([z_high, z_low], axis=1),
            jnp.concatenate([z_high, jnp.zeros_like(z_high)], axis=1),
        ],
        axis=0,
    )

    def along(cells, at):
        total = None
        for step in range(1, reach + 1):
            near = [cells[n] for n in (at - step, at + step) if 0 <= n < len(cells)]
            if near:
                term = factors[step] * sum(near[1:], near[0])
                total = term if total is None else total + term
        return total

    def apply(source, target, finish, gain):
        def xz_part(y, carry):
            column = source[pl.ds(ring, count_x), ring + y]
            flat = column.reshape(count_x * each, nz)
            high = flat.astype(jnp.bfloat16)
            low = (flat - high.astype(jnp.float32)).astype(jnp.bfloat16)
            both = jnp.dot(
                jnp.concatenate([high, low], axis=1), z_matrix, preferred_element_type=jnp.float32
            )
            along_z = (both[:, :nz] + both[:, nz:]).reshape(column.shape)
            cells = [column[x] for x in range(count_x)]
            for x in range(count_x):
                partial[x, y] = along_z[x] + diagonal[x, y] * cells[x] + along(cells, x)
            return carry

        lax.fori_loop(0, count_y, xz_part, 0)

        def y_part(x, carry):
            cells = [source[ring + x, ring + y] for y in range(count_y)]
            for y in range(count_y):
                total = partial[x, y] + along(cells, y)
                target[ring + x, ring + y] = finish(total, target, ring + x, ring + y)
            return carry

        lax.fori_loop(0, count_x, y_part, 0, unroll=4)

        def place_of(g, a):
            at = 2 * atoms * projs + 2 * a
            return (
                ring + numbers[g, at].astype(jnp.int32),
                ring + numbers[g, at + 1].astype(jnp.int32),
            )

        def gather_part(g):
            for a in range(atoms):
                at_x, at_y = place_of(g, a)
                totals = [None] * projs
                for t in range(tiles):
                    tile = source[at_x + offsets_x[t], at_y + offsets_y[t]]
                    for p in range(projs):
                        term = tile * shared_row(g, (a * tiles + t) * projs + p)
                        totals[p] = term if t == 0 else totals[p] + term
                for p in range(projs):
                    k = a * projs + p
                    energy = numbers[g, k] + numbers[g, atoms * projs + k] * (1.0 / remainder_gain)
                    coeffs[g, k] = jnp.broadcast_to(
                        jnp.sum(totals[p], axis=-1, keepdims=True)
                        * (energy * (gain / projector_gain / projector_gain)),
                        (each, nz),
                    )

        over_slabs(gather_part, 4)

        def scatter_part(g):
            for a in range(atoms):
                at_x, at_y = place_of(g, a)
                factor = [coeffs[g, a * projs + p] for p in range(projs)]
                for t in range(tiles):
                    row = (a * tiles + t) * projs
                    spread = factor[0] * shared_row(g, row)
                    for p in range(1, projs):
                        spread = spread + factor[p] * shared_row(g, row + p)
                    to_x = at_x + offsets_x[t]
                    to_y = at_y + offsets_y[t]
                    target[to_x, to_y] = target[to_x, to_y] + spread

        over_slabs(scatter_part, 2)

    for copy in copies:
        copy.wait()
    apply(first, second, lambda total, target, x, y: total, scale)

    for x in (0, ring + count_x):
        second[x] = jnp.zeros(second.shape[1:], jnp.float32)
    for y in (0, ring + count_y):
        second[:, y] = jnp.zeros((second.shape[0],) + second.shape[2:], jnp.float32)

    apply(second, first, lambda total, target, x, y: 2.0 * total - target[x, y], 2.0 * scale)

    portion = rounded_ref.shape[-1] // nz

    parts = slab_cells // portion
    leaving = []
    for part in range(parts):

        def round_slab(g):
            place, x0, y0 = corner(g)
            for within in range(portion):
                i, j = divmod(part * portion + within, cells_y)
                rounded_ref[part * group + place, :, pl.ds(within * nz, nz)] = first[
                    ring + x0 + i, ring + y0 + j
                ].astype(jnp.bfloat16)

        over_slabs(round_slab, 1)
        shares = pl.ds(part * group, group)
        leaving.append(
            pltpu.make_async_copy(rounded_ref.at[shares], rounded_out.at[shares], sent.at[part])
        )
        leaving[-1].start()
    for copy in leaving:
        copy.wait()


def scale_kernel(slabs_y, cells_x, cells_y, by_swaps, values_ref, field_ref):
    group, rows, nz = field_ref.shape
    each = values_ref.shape[2]
    ring = 1
    count_x, count_y = values_ref.shape[0] - 2 * ring, values_ref.shape[1] - 2 * ring
    me = lax.axis_index("sx") * slabs_y + lax.axis_index("sy") if by_swaps else 0

    def largest_of(x, largest):
        row = jnp.abs(values_ref[ring + x, pl.ds(ring, count_y)])
        return jnp.maximum(largest, jnp.max(row, axis=0))

    largest = lax.fori_loop(0, count_x, largest_of, jnp.zeros((each, nz), jnp.float32), unroll=2)
    level, gain = level_of(jnp.max(largest))
    level_rows = jnp.full((8, nz), level, jnp.float32)

    def give_slab(g, carry):
        place = jnp.bitwise_xor(me, g) if by_swaps else g
        x0 = (place // slabs_y) * cells_x
        y0 = (place % slabs_y) * cells_y
        field_ref[g, pl.ds(rows - 8, 8), :] = level_rows
        for i in range(cells_x):
            for j in range(cells_y):
                field_ref[g, pl.ds((i * cells_y + j) * each, each), :] = (
                    values_ref[ring + x0 + i, ring + y0 + j] * gain
                )
        return carry

    lax.fori_loop(0, group, give_slab, 0)


def entry(block, place):
    picked = jnp.where(place, block, 0.0)
    return jnp.sum(jnp.sum(picked, axis=0, keepdims=True), axis=1, keepdims=True)


def band_corner(shape, band):
    row = lax.broadcasted_iota(jnp.int32, shape, 0)
    column = lax.broadcasted_iota(jnp.int32, shape, 1)
    return (
        (row == 1) & (column == band * shape[0]),
        (row == 0) & (column == band * shape[0] + 1),
    )


def gram_kernel(matrix_ref, out_ref, sums_ref):
    bands, rows, columns = out_ref.shape
    matrix = matrix_ref[...]
    sums = lax.dot_general(
        matrix, matrix, (((1,), (1,)), ((), ())), preferred_element_type=jnp.float32
    )
    level, gain = level_of(jnp.max(jnp.abs(sums)))
    sums_ref[...] = sums * gain
    me = lax.axis_index("band")
    for k in range(bands):
        band = jnp.bitwise_xor(me, k)
        spare, _ = band_corner((rows, columns), band)
        block = sums_ref[pl.ds(pl.multiple_of(band * rows, rows), rows), :]
        out_ref[k] = jnp.where(spare, level, block)


def rows_kernel(cells, own_ref, *refs):
    out_ref = refs[-1]
    spare, twin = band_corner(out_ref.shape, lax.axis_index("band"))
    total = None
    for block in [own_ref[0]] + [ref[...] for ref in refs[:-1]]:
        block = block * shrink_of(entry(block, spare))
        total = block if total is None else total + block
    out_ref[...] = jnp.where(spare, entry(total, twin), total) / cells


def unpack_kernel(each, slabs_y, places, *refs):
    pieces = refs[:-3]
    filtered_hbm, filtered_ref, chunk_sems = refs[-3:]
    slab_cells, _, nz = filtered_ref.shape
    chunks = chunk_sems.shape[0]
    chunk = slab_cells // chunks
    me = lax.axis_index("sx") * slabs_y + lax.axis_index("sy") if len(pieces) > 1 else 0
    copies = []
    for c in range(chunks):
        for which, entry, other in places:
            piece = pieces[which]
            shrink = shrink_of(piece[entry, pl.ds(slab_cells * each, 1), :])
            if len(pieces) > 1:
                rows = pl.ds(pl.multiple_of(jnp.bitwise_xor(me, other) * each, each), each)
            else:
                rows = pl.ds(other * each, each)
            for cell in range(c * chunk, (c + 1) * chunk):
                filtered_ref[cell, rows, :] = piece[entry, pl.ds(cell * each, each), :] * shrink
        part = pl.ds(c * chunk, chunk)
        copies.append(
            pltpu.make_async_copy(filtered_ref.at[part], filtered_hbm.at[part], chunk_sems.at[c])
        )
        copies[-1].start()
    for copy in copies:
        copy.wait()


def swap(block, value):
    group = lax.axis_size(plane)
    return lax.ppermute(block, plane, [(i, i ^ value) for i in range(group)])


def local(orbitals, potential, projectors, energies, centers):
    band_orbitals, cells_x, cells_y, nz = orbitals.shape
    bands = lax.axis_size("band")
    slabs_x = lax.axis_size("sx")
    slabs_y = lax.axis_size("sy")
    group = slabs_x * slabs_y
    each = band_orbitals // group
    total_orbitals = bands * band_orbitals
    slab_cells = cells_x * cells_y
    grid = (slabs_x * cells_x, slabs_y * cells_y)
    atoms, projs, tiles, _ = projectors.shape

    near = slabs_y
    far = [v for v in range(1, group) if not v & near]
    by_swaps = group <= 8 and each % 8 == 0 and slabs_x > 1
    by_swaps = by_swaps and group & (group - 1) == 0 and bands & (bands - 1) == 0

    rows = atoms * projs * tiles + slab_cells + 1
    rows += -rows % 8
    piece_rows = slab_cells * each
    chunks = (orbitals * orbital_gain).astype(jnp.float16)
    chunks = chunks.transpose(1, 2, 0, 3).reshape(slab_cells, group, each, nz)
    chunks = chunks.transpose(1, 0, 2, 3).reshape(group, piece_rows, nz)
    shared = pl.pallas_call(
        share_kernel,
        in_specs=[hbm, smem, smem, vmem, vmem],
        out_specs=vmem,
        out_shape=jax.ShapeDtypeStruct((rows, nz), jnp.float32),
        compiler_params=params,
    )(chunks[0, :8].astype(jnp.float32), energies, centers.T, projectors.transpose(0, 2, 1, 3), potential)
    narrow = shared.astype(jnp.float16)
    if by_swaps:
        me = lax.axis_index(plane)

        def chunk_for(value):
            return lax.dynamic_index_in_dim(chunks, me ^ value, 0, keepdims=False)

        pieces = [swap(jnp.stack([chunk_for(v), chunk_for(v ^ near)]), v) for v in far]
        common = [swap(narrow, v) for v in far]
        for_core = [chunk_for(near)] + [block[1] for block in pieces]
        crossed = swap(
            jnp.stack([jnp.concatenate(pair) for pair in zip(for_core, [narrow] + common)]), near
        )
        operands = [chunk_for(0)[None], narrow[None]] + pieces + [block[None] for block in common]
        operands = [block.astype(jnp.float32) for block in operands + [crossed]]
        operands[1] = shared[None]
        last = len(operands) - 1
        slabs = {0: ((0, 0, 0), (1, 0, 0)), near: ((last, 0, 0), (last, 0, piece_rows))}
        for i, v in enumerate(far):
            slabs[v] = ((2 + i, 0, 0), (2 + len(far) + i, 0, 0))
            slabs[v ^ near] = ((last, 1 + i, 0), (last, 1 + i, piece_rows))
    else:
        sent = jnp.concatenate([chunks, jnp.broadcast_to(narrow[None], (group, rows, nz))], axis=1)
        operands = [lax.all_to_all(sent, plane, 0, 0).astype(jnp.float32)]
        slabs = None

    portion = slab_cells // bands
    ringed = (grid[0] + 2, grid[1] + 2, each, nz)
    shares = bands * group
    rounded_shape = (shares, each, portion * nz)
    values, rounded = pl.pallas_call(
        functools.partial(filter_kernel, slabs_y, cells_x, cells_y, each, atoms, projs, slabs),
        in_specs=[vmem] * len(operands),
        out_specs=[vmem, hbm],
        out_shape=[
            jax.ShapeDtypeStruct(ringed, jnp.float32),
            jax.ShapeDtypeStruct(rounded_shape, jnp.bfloat16),
        ],
        scratch_shapes=[
            pltpu.VMEM(ringed, jnp.float32),
            pltpu.VMEM(grid + (each, nz), jnp.float32),
            pltpu.VMEM(grid + (1, nz), jnp.float32),
            pltpu.VMEM((group, atoms * projs, each, nz), jnp.float32),
            pltpu.SMEM((group, nz), jnp.float32),
            pltpu.VMEM(rounded_shape, jnp.bfloat16),
            pltpu.SemaphoreType.DMA((group,)),
            pltpu.SemaphoreType.DMA((bands,)),
        ],
        compiler_params=params,
        cost_estimate=pl.CostEstimate(
            flops=2 * 2 * 40 * grid[0] * grid[1] * each * nz,
            bytes_accessed=8 * grid[0] * grid[1] * each * nz,
            transcendentals=0,
        ),
    )(*operands)

    matrix = lax.all_to_all(rounded, every, 0, 0)
    matrix = matrix.reshape(total_orbitals, portion * nz)
    field = pl.pallas_call(
        functools.partial(scale_kernel, slabs_y, cells_x, cells_y, by_swaps),
        in_specs=[vmem],
        out_specs=vmem,
        out_shape=jax.ShapeDtypeStruct((group, piece_rows + 8, nz), jnp.float32),
        compiler_params=params,
    )(values)
    narrow = field.astype(jnp.float16)
    if by_swaps:
        came = [swap(narrow[v], v) for v in range(1, group)]
        came, matrix = lax.optimization_barrier((came, matrix))
        pieces = [field] + [block.astype(jnp.float32)[None] for block in came]
        places = [(v, 0, v) for v in range(group)]
    else:
        pieces = [lax.all_to_all(narrow, plane, 0, 0).astype(jnp.float32)]
        places = [(0, g, g) for g in range(group)]

    def unpack(pieces):
        return pl.pallas_call(
            functools.partial(unpack_kernel, each, slabs_y, places),
            in_specs=[vmem] * len(pieces),
            out_specs=hbm,
            out_shape=jax.ShapeDtypeStruct((slab_cells, band_orbitals, nz), jnp.float32),
            scratch_shapes=[
                pltpu.VMEM((slab_cells, band_orbitals, nz), jnp.float32),
                pltpu.SemaphoreType.DMA((cells_x,)),
            ],
            compiler_params=params,
        )(*pieces)

    cells = grid[0] * grid[1] * nz
    if by_swaps:
        sums = pl.pallas_call(
            gram_kernel,
            in_specs=[vmem],
            out_specs=vmem,
            out_shape=jax.ShapeDtypeStruct((bands, band_orbitals, total_orbitals), jnp.float32),
            scratch_shapes=[pltpu.VMEM((total_orbitals, total_orbitals), jnp.float32)],
            compiler_params=params,
        )(matrix)
        parts = [
            lax.ppermute(
                sums[k].astype(jnp.float16), "band", [(i, i ^ k) for i in range(bands)]
            ).astype(jnp.float32)
            for k in range(1, bands)
        ]
        gram = pl.pallas_call(
            functools.partial(rows_kernel, cells),
            in_specs=[vmem] * bands,
            out_specs=vmem,
            out_shape=jax.ShapeDtypeStruct((band_orbitals, total_orbitals), jnp.float32),
            compiler_params=params,
        )(sums, *parts)
        terms = {v: swap(gram, v) for v in far}
        terms[0] = gram
        bit = 1
        while len(terms) > 1:
            if any(v ^ bit in terms for v in terms):
                terms = {v: terms[v] + terms[v ^ bit] for v in terms if not v & bit}
            bit *= 2
        gram, filtered = lax.optimization_barrier((terms[0], unpack(pieces)))
        gram = gram + swap(gram, near)
    else:
        sums = lax.dot_general(
            matrix, matrix, (((1,), (1,)), ((), ())), preferred_element_type=jnp.float32
        )
        parts = lax.all_to_all(sums.reshape(shares, each, total_orbitals), every, 0, 0)
        rows = jnp.sum(parts, axis=0) / cells
        gram = lax.all_to_all(jnp.broadcast_to(rows[None], (group,) + rows.shape), plane, 0, 0)
        gram = gram.reshape(band_orbitals, total_orbitals)
        filtered = unpack(pieces)

    filtered = filtered.reshape(cells_x, cells_y, band_orbitals, nz).transpose(2, 0, 1, 3)
    return (filtered, gram)


def solution(mesh):
    in_specs = (
        P("band", "sx", "sy", None),
        P("sx", "sy", None),
        P(("sx", "sy"), None, None, None),
        P(("sx", "sy"), None),
        P(("sx", "sy"), None),
    )
    out_specs = (P("band", "sx", "sy", None), P("band", None))
    return jax.shard_map(local, mesh=mesh, in_specs=in_specs, out_specs=out_specs, check_vma=False)
```

```python
import functools

import jax
import jax.numpy as jnp
from jax import lax
from jax.experimental import pallas as pl
from jax.experimental.pallas import tpu as pltpu
from jax.sharding import PartitionSpec as P

stencil_weights = (
    -5369.0 / 1800.0,
    12.0 / 7.0,
    -15.0 / 56.0,
    10.0 / 189.0,
    -1.0 / 112.0,
    2.0 / 1925.0,
    -1.0 / 16632.0,
)
filter_center = 6.5
filter_half = 6.0
offsets_x = (0, -1, 1, 0, 0)
offsets_y = (0, 0, 0, -1, 1)
reach = 6
plane = ("sx", "sy")
every = ("band", "sx", "sy")

orbital_gain = 2.0**12
projector_gain = 2.0**17
potential_gain = 2.0**13
remainder_gain = 2.0**10
top = 15
middle = 8
levels = 17

vmem = pl.BlockSpec(memory_space=pltpu.VMEM)
smem = pl.BlockSpec(memory_space=pltpu.SMEM)
hbm = pl.BlockSpec(memory_space=pl.ANY)
params = pltpu.CompilerParams(vmem_limit_bytes=24 * 1024 * 1024)


def level_of(largest):
    level = jnp.float32(0.0)
    scale = jnp.float32(2.0 ** (top + 8 * middle))
    for j in range(levels):
        above = largest >= jnp.float32(2.0 ** (8 * (j - middle)))
        level = jnp.where(above, jnp.float32(j + 1), level)
        scale = jnp.where(above, jnp.float32(2.0 ** (top - 8 * (j + 1 - middle))), scale)
    return level, scale


def shrink_of(level):
    shrink = jnp.full(level.shape, 2.0 ** (-top - 8 * middle), jnp.float32)
    for j in range(levels):
        shrink = jnp.where(level > j, jnp.float32(2.0 ** (8 * (j + 1 - middle) - top)), shrink)
    return shrink


def share_kernel(_, energies_ref, centers_ref, projectors_ref, potential_ref, out_ref):
    rows, nz = out_ref.shape
    atoms, tiles, projs = projectors_ref.shape[:3]

    row = 0
    for a in range(atoms):
        for t in range(tiles):
            out_ref[pl.ds(row, projs), :] = projectors_ref[a, t] * projector_gain
            row += projs
    for i in range(potential_ref.shape[0]):
        count = potential_ref.shape[1]
        out_ref[pl.ds(row, count), :] = potential_ref[i] * potential_gain
        row += count
    lane = lax.broadcasted_iota(jnp.int32, (1, nz), 1)
    numbers = jnp.zeros((1, nz), jnp.float32)
    for a in range(atoms):
        for p in range(projs):
            numbers = jnp.where(lane == a * projs + p, energies_ref[a, p], numbers)
    high = numbers.astype(jnp.bfloat16).astype(jnp.float32)
    low = (numbers - high) * remainder_gain
    count = atoms * projs
    numbers = high + pltpu.roll(low, count, 1)
    for a in range(atoms):
        for d in range(2):
            here = centers_ref[d, a].astype(jnp.float32)
            numbers = jnp.where(lane == 2 * count + 2 * a + d, here, numbers)
    out_ref[pl.ds(row, 1), :] = numbers
    out_ref[pl.ds(row + 1, rows - row - 1), :] = jnp.zeros((rows - row - 1, nz), jnp.float32)


def filter_kernel(slabs_y, cells_x, cells_y, each, atoms, projs, slabs, *refs):
    inputs, (first, rounded_out) = refs[:-10], refs[-10:-8]
    second, partial, diagonal, coeffs, numbers, rounded_ref, arrived, sent = refs[-8:]
    group = numbers.shape[0]
    nz = first.shape[-1]
    count_x, count_y = diagonal.shape[0], diagonal.shape[1]
    tiles = len(offsets_x)
    slab_cells = cells_x * cells_y
    pot_row = atoms * projs * tiles
    number_row = pot_row + slab_cells
    scale = 1.0 / filter_half
    factors = [-0.5 * scale * w for w in stencil_weights]
    ring = 1
    me = 0 if slabs is None else lax.axis_index("sx") * slabs_y + lax.axis_index("sy")

    def rows_of(g, shared, row, count):
        if slabs is None:
            return inputs[0].at[g, pl.ds(row + (slab_cells * each if shared else 0), count), :]
        which, at, start = slabs[g][1 if shared else 0]
        return inputs[which].at[at, pl.ds(start + row, count), :]

    def shared_row(g, row):
        return rows_of(g, True, row, 1)[...]

    def over_slabs(body, unroll):
        if slabs is None:
            lax.fori_loop(0, group, lambda g, carry: body(g) or carry, 0, unroll=min(group, unroll))
        else:
            for g in range(group):
                body(g)

    def corner(g):
        place = g if slabs is None else jnp.bitwise_xor(me, g)
        return place, (place // slabs_y) * cells_x, (place % slabs_y) * cells_y

    if slabs is None:
        copies = [
            pltpu.make_async_copy(
                inputs[0].at[:, slab_cells * each + number_row, :], numbers, arrived.at[0]
            )
        ]
    else:
        copies = [
            pltpu.make_async_copy(
                rows_of(g, True, number_row, 1), numbers.at[pl.ds(g, 1), :], arrived.at[g]
            )
            for g in range(group)
        ]
    for copy in copies:
        copy.start()

    for field in (first, second):
        for x in (0, ring + count_x):
            field[x] = jnp.zeros(field.shape[1:], jnp.float32)
        for y in (0, ring + count_y):
            field[:, y] = jnp.zeros((field.shape[0],) + field.shape[2:], jnp.float32)

    def take_slab(g):
        _, x0, y0 = corner(g)
        for i in range(cells_x):
            for j in range(cells_y):
                cell = i * cells_y + j
                first[ring + x0 + i, ring + y0 + j] = rows_of(g, False, cell * each, each)[...] * (
                    1.0 / orbital_gain
                )
                diagonal[x0 + i, y0 + j] = shared_row(g, pot_row + cell) * (
                    scale / potential_gain
                ) + (3.0 * factors[0] - filter_center * scale)

    over_slabs(take_slab, 1)

    distance = jnp.abs(
        lax.broadcasted_iota(jnp.int32, (nz, nz), 0) - lax.broadcasted_iota(jnp.int32, (nz, nz), 1)
    )
    along_z = jnp.zeros((nz, nz), jnp.float32)
    for step in range(1, reach + 1):
        along_z = jnp.where(distance == step, factors[step], along_z)
    z_high = along_z.astype(jnp.bfloat16)
    z_low = (along_z - z_high.astype(jnp.float32)).astype(jnp.bfloat16)
    z_matrix = jnp.concatenate(
        [
            jnp.concatenate([z_high, z_low], axis=1),
            jnp.concatenate([z_high, jnp.zeros_like(z_high)], axis=1),
        ],
        axis=0,
    )

    def along(cells, at):
        total = None
        for step in range(1, reach + 1):
            near = [cells[n] for n in (at - step, at + step) if 0 <= n < len(cells)]
            if near:
                term = factors[step] * sum(near[1:], near[0])
                total = term if total is None else total + term
        return total

    def apply(source, target, finish, gain):
        def xz_part(y, carry):
            column = source[pl.ds(ring, count_x), ring + y]
            flat = column.reshape(count_x * each, nz)
            high = flat.astype(jnp.bfloat16)
            low = (flat - high.astype(jnp.float32)).astype(jnp.bfloat16)
            both = jnp.dot(
                jnp.concatenate([high, low], axis=1), z_matrix, preferred_element_type=jnp.float32
            )
            along_z = (both[:, :nz] + both[:, nz:]).reshape(column.shape)
            cells = [column[x] for x in range(count_x)]
            for x in range(count_x):
                partial[x, y] = along_z[x] + diagonal[x, y] * cells[x] + along(cells, x)
            return carry

        lax.fori_loop(0, count_y, xz_part, 0, unroll=4)

        def y_part(x, carry):
            cells = [source[ring + x, ring + y] for y in range(count_y)]
            for y in range(count_y):
                total = partial[x, y] + along(cells, y)
                target[ring + x, ring + y] = finish(total, target, ring + x, ring + y)
            return carry

        lax.fori_loop(0, count_x, y_part, 0, unroll=2)

        def place_of(g, a):
            at = 2 * atoms * projs + 2 * a
            return (
                ring + numbers[g, at].astype(jnp.int32),
                ring + numbers[g, at + 1].astype(jnp.int32),
            )

        def gather_part(g):
            for a in range(atoms):
                at_x, at_y = place_of(g, a)
                totals = [None] * projs
                for t in range(tiles):
                    tile = source[at_x + offsets_x[t], at_y + offsets_y[t]]
                    for p in range(projs):
                        term = tile * shared_row(g, (a * tiles + t) * projs + p)
                        totals[p] = term if t == 0 else totals[p] + term
                for p in range(projs):
                    k = a * projs + p
                    energy = numbers[g, k] + numbers[g, atoms * projs + k] * (1.0 / remainder_gain)
                    coeffs[g, k] = jnp.broadcast_to(
                        jnp.sum(totals[p], axis=-1, keepdims=True)
                        * (energy * (gain / projector_gain / projector_gain)),
                        (each, nz),
                    )

        over_slabs(gather_part, 4)

        def scatter_part(g):
            for a in range(atoms):
                at_x, at_y = place_of(g, a)
                factor = [coeffs[g, a * projs + p] for p in range(projs)]
                for t in range(tiles):
                    row = (a * tiles + t) * projs
                    spread = factor[0] * shared_row(g, row)
                    for p in range(1, projs):
                        spread = spread + factor[p] * shared_row(g, row + p)
                    to_x = at_x + offsets_x[t]
                    to_y = at_y + offsets_y[t]
                    target[to_x, to_y] = target[to_x, to_y] + spread

        over_slabs(scatter_part, 2)

    for copy in copies:
        copy.wait()
    apply(first, second, lambda total, target, x, y: total, scale)

    for x in (0, ring + count_x):
        second[x] = jnp.zeros(second.shape[1:], jnp.float32)
    for y in (0, ring + count_y):
        second[:, y] = jnp.zeros((second.shape[0],) + second.shape[2:], jnp.float32)

    apply(second, first, lambda total, target, x, y: 2.0 * total - target[x, y], 2.0 * scale)

    portion = rounded_ref.shape[-1] // nz

    parts = slab_cells // portion
    leaving = []
    for part in range(parts):

        def round_slab(g):
            place, x0, y0 = corner(g)
            for within in range(portion):
                i, j = divmod(part * portion + within, cells_y)
                rounded_ref[part * group + place, :, pl.ds(within * nz, nz)] = first[
                    ring + x0 + i, ring + y0 + j
                ].astype(jnp.bfloat16)

        over_slabs(round_slab, 1)
        shares = pl.ds(part * group, group)
        leaving.append(
            pltpu.make_async_copy(rounded_ref.at[shares], rounded_out.at[shares], sent.at[part])
        )
        leaving[-1].start()
    for copy in leaving:
        copy.wait()


def scale_kernel(slabs_y, cells_x, cells_y, by_swaps, values_ref, field_ref):
    group, rows, nz = field_ref.shape
    each = values_ref.shape[2]
    ring = 1
    count_x, count_y = values_ref.shape[0] - 2 * ring, values_ref.shape[1] - 2 * ring
    me = lax.axis_index("sx") * slabs_y + lax.axis_index("sy") if by_swaps else 0

    def largest_of(x, largest):
        row = jnp.abs(values_ref[ring + x, pl.ds(ring, count_y)])
        return jnp.maximum(largest, jnp.max(row, axis=0))

    largest = lax.fori_loop(0, count_x, largest_of, jnp.zeros((each, nz), jnp.float32), unroll=2)
    level, gain = level_of(jnp.max(largest))
    level_rows = jnp.full((8, nz), level, jnp.float32)

    def give_slab(g, carry):
        place = jnp.bitwise_xor(me, g) if by_swaps else g
        x0 = (place // slabs_y) * cells_x
        y0 = (place % slabs_y) * cells_y
        field_ref[g, pl.ds(rows - 8, 8), :] = level_rows
        for i in range(cells_x):
            for j in range(cells_y):
                field_ref[g, pl.ds((i * cells_y + j) * each, each), :] = (
                    values_ref[ring + x0 + i, ring + y0 + j] * gain
                )
        return carry

    lax.fori_loop(0, group, give_slab, 0)


def entry(block, place):
    picked = jnp.where(place, block, 0.0)
    return jnp.sum(jnp.sum(picked, axis=0, keepdims=True), axis=1, keepdims=True)


def band_corner(shape, band):
    row = lax.broadcasted_iota(jnp.int32, shape, 0)
    column = lax.broadcasted_iota(jnp.int32, shape, 1)
    return (
        (row == 1) & (column == band * shape[0]),
        (row == 0) & (column == band * shape[0] + 1),
    )


def gram_kernel(matrix_ref, out_ref, sums_ref):
    bands, rows, columns = out_ref.shape
    matrix = matrix_ref[...]
    sums = lax.dot_general(
        matrix, matrix, (((1,), (1,)), ((), ())), preferred_element_type=jnp.float32
    )
    level, gain = level_of(jnp.max(jnp.abs(sums)))
    sums_ref[...] = sums * gain
    me = lax.axis_index("band")
    for k in range(bands):
        band = jnp.bitwise_xor(me, k)
        spare, _ = band_corner((rows, columns), band)
        block = sums_ref[pl.ds(pl.multiple_of(band * rows, rows), rows), :]
        out_ref[k] = jnp.where(spare, level, block)


def rows_kernel(cells, own_ref, *refs):
    out_ref = refs[-1]
    spare, twin = band_corner(out_ref.shape, lax.axis_index("band"))
    total = None
    for block in [own_ref[0]] + [ref[...] for ref in refs[:-1]]:
        block = block * shrink_of(entry(block, spare))
        total = block if total is None else total + block
    out_ref[...] = jnp.where(spare, entry(total, twin), total) / cells


def unpack_kernel(each, slabs_y, places, *refs):
    pieces = refs[:-3]
    filtered_hbm, filtered_ref, chunk_sems = refs[-3:]
    slab_cells, _, nz = filtered_ref.shape
    chunks = chunk_sems.shape[0]
    chunk = slab_cells // chunks
    me = lax.axis_index("sx") * slabs_y + lax.axis_index("sy") if len(pieces) > 1 else 0
    copies = []
    for c in range(chunks):
        for which, entry, other in places:
            piece = pieces[which]
            shrink = shrink_of(piece[entry, pl.ds(slab_cells * each, 1), :])
            if len(pieces) > 1:
                rows = pl.ds(pl.multiple_of(jnp.bitwise_xor(me, other) * each, each), each)
            else:
                rows = pl.ds(other * each, each)
            for cell in range(c * chunk, (c + 1) * chunk):
                filtered_ref[cell, rows, :] = piece[entry, pl.ds(cell * each, each), :] * shrink
        part = pl.ds(c * chunk, chunk)
        copies.append(
            pltpu.make_async_copy(filtered_ref.at[part], filtered_hbm.at[part], chunk_sems.at[c])
        )
        copies[-1].start()
    for copy in copies:
        copy.wait()


def swap(block, value):
    group = lax.axis_size(plane)
    return lax.ppermute(block, plane, [(i, i ^ value) for i in range(group)])


def local(orbitals, potential, projectors, energies, centers):
    band_orbitals, cells_x, cells_y, nz = orbitals.shape
    bands = lax.axis_size("band")
    slabs_x = lax.axis_size("sx")
    slabs_y = lax.axis_size("sy")
    group = slabs_x * slabs_y
    each = band_orbitals // group
    total_orbitals = bands * band_orbitals
    slab_cells = cells_x * cells_y
    grid = (slabs_x * cells_x, slabs_y * cells_y)
    atoms, projs, tiles, _ = projectors.shape

    near = slabs_y
    far = [v for v in range(1, group) if not v & near]
    by_swaps = group <= 8 and each % 8 == 0 and slabs_x > 1
    by_swaps = by_swaps and group & (group - 1) == 0 and bands & (bands - 1) == 0

    rows = atoms * projs * tiles + slab_cells + 1
    rows += -rows % 8
    piece_rows = slab_cells * each
    chunks = (orbitals * orbital_gain).astype(jnp.float16)
    chunks = chunks.transpose(1, 2, 0, 3).reshape(slab_cells, group, each, nz)
    chunks = chunks.transpose(1, 0, 2, 3).reshape(group, piece_rows, nz)
    shared = pl.pallas_call(
        share_kernel,
        in_specs=[hbm, smem, smem, vmem, vmem],
        out_specs=vmem,
        out_shape=jax.ShapeDtypeStruct((rows, nz), jnp.float32),
        compiler_params=params,
    )(chunks[0, :8].astype(jnp.float32), energies, centers.T, projectors.transpose(0, 2, 1, 3), potential)
    narrow = shared.astype(jnp.float16)
    if by_swaps:
        me = lax.axis_index(plane)

        def chunk_for(value):
            return lax.dynamic_index_in_dim(chunks, me ^ value, 0, keepdims=False)

        came = [swap(jnp.concatenate([chunk_for(v), narrow, chunk_for(v ^ near)]), v) for v in far]
        mine = jnp.concatenate([narrow, chunk_for(near)])
        crossed = swap(jnp.stack([mine] + [block[piece_rows:] for block in came]), near)
        operands = [chunk_for(0)[None], narrow[None]] + [block[None] for block in came] + [crossed]
        operands = [block.astype(jnp.float32) for block in operands]
        operands[1] = shared[None]
        last = len(operands) - 1
        slabs = {0: ((0, 0, 0), (1, 0, 0)), near: ((last, 0, rows), (last, 0, 0))}
        for i, v in enumerate(far):
            slabs[v] = ((2 + i, 0, 0), (2 + i, 0, piece_rows))
            slabs[v ^ near] = ((last, 1 + i, rows), (last, 1 + i, 0))
    else:
        sent = jnp.concatenate([chunks, jnp.broadcast_to(narrow[None], (group, rows, nz))], axis=1)
        operands = [lax.all_to_all(sent, plane, 0, 0).astype(jnp.float32)]
        slabs = None

    portion = slab_cells // bands
    ringed = (grid[0] + 2, grid[1] + 2, each, nz)
    shares = bands * group
    rounded_shape = (shares, each, portion * nz)
    values, rounded = pl.pallas_call(
        functools.partial(filter_kernel, slabs_y, cells_x, cells_y, each, atoms, projs, slabs),
        in_specs=[vmem] * len(operands),
        out_specs=[vmem, hbm],
        out_shape=[
            jax.ShapeDtypeStruct(ringed, jnp.float32),
            jax.ShapeDtypeStruct(rounded_shape, jnp.bfloat16),
        ],
        scratch_shapes=[
            pltpu.VMEM(ringed, jnp.float32),
            pltpu.VMEM(grid + (each, nz), jnp.float32),
            pltpu.VMEM(grid + (1, nz), jnp.float32),
            pltpu.VMEM((group, atoms * projs, each, nz), jnp.float32),
            pltpu.SMEM((group, nz), jnp.float32),
            pltpu.VMEM(rounded_shape, jnp.bfloat16),
            pltpu.SemaphoreType.DMA((group,)),
            pltpu.SemaphoreType.DMA((bands,)),
        ],
        compiler_params=params,
        cost_estimate=pl.CostEstimate(
            flops=2 * 2 * 40 * grid[0] * grid[1] * each * nz,
            bytes_accessed=8 * grid[0] * grid[1] * each * nz,
            transcendentals=0,
        ),
    )(*operands)

    matrix = lax.all_to_all(rounded, every, 0, 0)
    matrix = matrix.reshape(total_orbitals, portion * nz)
    field = pl.pallas_call(
        functools.partial(scale_kernel, slabs_y, cells_x, cells_y, by_swaps),
        in_specs=[vmem],
        out_specs=vmem,
        out_shape=jax.ShapeDtypeStruct((group, piece_rows + 8, nz), jnp.float32),
        compiler_params=params,
    )(values)
    narrow = field.astype(jnp.float16)
    if by_swaps:
        came = [swap(narrow[v], v) for v in range(1, group)]
        came, matrix = lax.optimization_barrier((came, matrix))
        pieces = [field] + [block.astype(jnp.float32)[None] for block in came]
        places = [(v, 0, v) for v in range(group)]
    else:
        pieces = [lax.all_to_all(narrow, plane, 0, 0).astype(jnp.float32)]
        places = [(0, g, g) for g in range(group)]

    def unpack(pieces):
        return pl.pallas_call(
            functools.partial(unpack_kernel, each, slabs_y, places),
            in_specs=[vmem] * len(pieces),
            out_specs=hbm,
            out_shape=jax.ShapeDtypeStruct((slab_cells, band_orbitals, nz), jnp.float32),
            scratch_shapes=[
                pltpu.VMEM((slab_cells, band_orbitals, nz), jnp.float32),
                pltpu.SemaphoreType.DMA((cells_x,)),
            ],
            compiler_params=params,
        )(*pieces)

    cells = grid[0] * grid[1] * nz
    if by_swaps:
        sums = pl.pallas_call(
            gram_kernel,
            in_specs=[vmem],
            out_specs=vmem,
            out_shape=jax.ShapeDtypeStruct((bands, band_orbitals, total_orbitals), jnp.float32),
            scratch_shapes=[pltpu.VMEM((total_orbitals, total_orbitals), jnp.float32)],
            compiler_params=params,
        )(matrix)
        parts = [
            lax.ppermute(
                sums[k].astype(jnp.float16), "band", [(i, i ^ k) for i in range(bands)]
            ).astype(jnp.float32)
            for k in range(1, bands)
        ]
        gram = pl.pallas_call(
            functools.partial(rows_kernel, cells),
            in_specs=[vmem] * bands,
            out_specs=vmem,
            out_shape=jax.ShapeDtypeStruct((band_orbitals, total_orbitals), jnp.float32),
            compiler_params=params,
        )(sums, *parts)
        terms = {v: swap(gram, v) for v in far}
        terms[0] = gram
        bit = 1
        while len(terms) > 1:
            if any(v ^ bit in terms for v in terms):
                terms = {v: terms[v] + terms[v ^ bit] for v in terms if not v & bit}
            bit *= 2
        gram, filtered = lax.optimization_barrier((terms[0], unpack(pieces)))
        gram = gram + swap(gram, near)
    else:
        sums = lax.dot_general(
            matrix, matrix, (((1,), (1,)), ((), ())), preferred_element_type=jnp.float32
        )
        parts = lax.all_to_all(sums.reshape(shares, each, total_orbitals), every, 0, 0)
        rows = jnp.sum(parts, axis=0) / cells
        gram = lax.all_to_all(jnp.broadcast_to(rows[None], (group,) + rows.shape), plane, 0, 0)
        gram = gram.reshape(band_orbitals, total_orbitals)
        filtered = unpack(pieces)

    filtered = filtered.reshape(cells_x, cells_y, band_orbitals, nz).transpose(2, 0, 1, 3)
    return (filtered, gram)


def solution(mesh):
    in_specs = (
        P("band", "sx", "sy", None),
        P("sx", "sy", None),
        P(("sx", "sy"), None, None, None),
        P(("sx", "sy"), None),
        P(("sx", "sy"), None),
    )
    out_specs = (P("band", "sx", "sy", None), P("band", None))
    return jax.shard_map(local, mesh=mesh, in_specs=in_specs, out_specs=out_specs, check_vma=False)
```

```python
import functools

import jax
import jax.numpy as jnp
from jax import lax
from jax.experimental import pallas as pl
from jax.experimental.pallas import tpu as pltpu
from jax.sharding import PartitionSpec as P

stencil_weights = (
    -5369.0 / 1800.0,
    12.0 / 7.0,
    -15.0 / 56.0,
    10.0 / 189.0,
    -1.0 / 112.0,
    2.0 / 1925.0,
    -1.0 / 16632.0,
)
filter_center = 6.5
filter_half = 6.0
offsets_x = (0, -1, 1, 0, 0)
offsets_y = (0, 0, 0, -1, 1)
reach = 6
plane = ("sx", "sy")
every = ("band", "sx", "sy")

orbital_gain = 2.0**12
projector_gain = 2.0**17
potential_gain = 2.0**13
remainder_gain = 2.0**10
top = 15
middle = 8
levels = 17

vmem = pl.BlockSpec(memory_space=pltpu.VMEM)
hbm = pl.BlockSpec(memory_space=pl.ANY)
params = pltpu.CompilerParams(vmem_limit_bytes=24 * 1024 * 1024)


def level_of(largest):
    level = jnp.float32(0.0)
    scale = jnp.float32(2.0 ** (top + 8 * middle))
    for j in range(levels):
        above = largest >= jnp.float32(2.0 ** (8 * (j - middle)))
        level = jnp.where(above, jnp.float32(j + 1), level)
        scale = jnp.where(above, jnp.float32(2.0 ** (top - 8 * (j + 1 - middle))), scale)
    return level, scale


def shrink_of(level):
    shrink = jnp.full(level.shape, 2.0 ** (-top - 8 * middle), jnp.float32)
    for j in range(levels):
        shrink = jnp.where(level > j, jnp.float32(2.0 ** (8 * (j + 1 - middle) - top)), shrink)
    return shrink


def share_kernel(_, energies_ref, centers_ref, projectors_ref, potential_ref, out_ref):
    rows, nz = out_ref.shape
    atoms, tiles, projs = projectors_ref.shape[:3]

    row = 0
    for a in range(atoms):
        for t in range(tiles):
            out_ref[pl.ds(row, projs), :] = projectors_ref[a, t] * projector_gain
            row += projs
    for i in range(potential_ref.shape[0]):
        count = potential_ref.shape[1]
        out_ref[pl.ds(row, count), :] = potential_ref[i] * potential_gain
        row += count
    out_ref[pl.ds(row, rows - row), :] = jnp.zeros((rows - row, nz), jnp.float32)
    energies = energies_ref[...]
    high = energies.astype(jnp.bfloat16).astype(jnp.float32)
    out_ref[pl.ds(row, atoms), :projs] = high
    out_ref[pl.ds(row + atoms, atoms), :projs] = (energies - high) * remainder_gain
    out_ref[pl.ds(row + 2 * atoms, 2), :atoms] = centers_ref[...].astype(jnp.float32)


def filter_kernel(slabs_y, cells_x, cells_y, each, atoms, projs, slabs, *refs):
    inputs, (first, rounded_out) = refs[:-10], refs[-10:-8]
    second, partial, diagonal, coeffs, numbers, rounded_ref, arrived, sent = refs[-8:]
    group, number_rows, _ = numbers.shape
    nz = first.shape[-1]
    count_x, count_y = diagonal.shape[0], diagonal.shape[1]
    tiles = len(offsets_x)
    slab_cells = cells_x * cells_y
    pot_row = atoms * projs * tiles
    number_row = pot_row + slab_cells
    scale = 1.0 / filter_half
    factors = [-0.5 * scale * w for w in stencil_weights]
    ring = 1
    me = 0 if slabs is None else lax.axis_index("sx") * slabs_y + lax.axis_index("sy")

    def rows_of(g, shared, row, count):
        if slabs is None:
            return inputs[0].at[g, pl.ds(row + (slab_cells * each if shared else 0), count), :]
        which, at, start = slabs[g][1 if shared else 0]
        return inputs[which].at[at, pl.ds(start + row, count), :]

    def shared_row(g, row):
        return rows_of(g, True, row, 1)[...]

    def over_slabs(body, unroll):
        if slabs is None:
            lax.fori_loop(0, group, lambda g, carry: body(g) or carry, 0, unroll=min(group, unroll))
        else:
            for g in range(group):
                body(g)

    def corner(g):
        place = g if slabs is None else jnp.bitwise_xor(me, g)
        return place, (place // slabs_y) * cells_x, (place % slabs_y) * cells_y

    if slabs is None:
        copies = [
            pltpu.make_async_copy(
                inputs[0].at[:, pl.ds(slab_cells * each + number_row, number_rows), :],
                numbers,
                arrived.at[0],
            )
        ]
    else:
        copies = [
            pltpu.make_async_copy(
                rows_of(g, True, number_row, number_rows), numbers.at[g], arrived.at[g]
            )
            for g in range(group)
        ]
    for copy in copies:
        copy.start()

    for field in (first, second):
        for x in (0, ring + count_x):
            field[x] = jnp.zeros(field.shape[1:], jnp.float32)
        for y in (0, ring + count_y):
            field[:, y] = jnp.zeros((field.shape[0],) + field.shape[2:], jnp.float32)

    def take_slab(g):
        _, x0, y0 = corner(g)
        for i in range(cells_x):
            for j in range(cells_y):
                cell = i * cells_y + j
                first[ring + x0 + i, ring + y0 + j] = rows_of(g, False, cell * each, each)[...] * (
                    1.0 / orbital_gain
                )
                diagonal[x0 + i, y0 + j] = shared_row(g, pot_row + cell) * (
                    scale / potential_gain
                ) + (3.0 * factors[0] - filter_center * scale)

    over_slabs(take_slab, 1)

    distance = jnp.abs(
        lax.broadcasted_iota(jnp.int32, (nz, nz), 0) - lax.broadcasted_iota(jnp.int32, (nz, nz), 1)
    )
    along_z = jnp.zeros((nz, nz), jnp.float32)
    for step in range(1, reach + 1):
        along_z = jnp.where(distance == step, factors[step], along_z)
    z_high = along_z.astype(jnp.bfloat16)
    z_low = (along_z - z_high.astype(jnp.float32)).astype(jnp.bfloat16)
    z_matrix = jnp.concatenate(
        [
            jnp.concatenate([z_high, z_low], axis=1),
            jnp.concatenate([z_high, jnp.zeros_like(z_high)], axis=1),
        ],
        axis=0,
    )

    def along(cells, at):
        total = None
        for step in range(1, reach + 1):
            near = [cells[n] for n in (at - step, at + step) if 0 <= n < len(cells)]
            if near:
                term = factors[step] * sum(near[1:], near[0])
                total = term if total is None else total + term
        return total

    def apply(source, target, finish, gain):
        def xz_part(y, carry):
            column = source[pl.ds(ring, count_x), ring + y]
            flat = column.reshape(count_x * each, nz)
            high = flat.astype(jnp.bfloat16)
            low = (flat - high.astype(jnp.float32)).astype(jnp.bfloat16)
            both = jnp.dot(
                jnp.concatenate([high, low], axis=1), z_matrix, preferred_element_type=jnp.float32
            )
            along_z = (both[:, :nz] + both[:, nz:]).reshape(column.shape)
            cells = [column[x] for x in range(count_x)]
            for x in range(count_x):
                partial[x, y] = along_z[x] + diagonal[x, y] * cells[x] + along(cells, x)
            return carry

        lax.fori_loop(0, count_y, xz_part, 0, unroll=6)

        def y_part(x, carry):
            cells = [source[ring + x, ring + y] for y in range(count_y)]
            for y in range(count_y):
                total = partial[x, y] + along(cells, y)
                target[ring + x, ring + y] = finish(total, target, ring + x, ring + y)
            return carry

        lax.fori_loop(0, count_x, y_part, 0, unroll=4)

        def place_of(g, a):
            return (
                ring + numbers[g, 2 * atoms, a].astype(jnp.int32),
                ring + numbers[g, 2 * atoms + 1, a].astype(jnp.int32),
            )

        def gather_part(g):
            for a in range(atoms):
                at_x, at_y = place_of(g, a)
                totals = [None] * projs
                for t in range(tiles):
                    tile = source[at_x + offsets_x[t], at_y + offsets_y[t]]
                    for p in range(projs):
                        term = tile * shared_row(g, (a * tiles + t) * projs + p)
                        totals[p] = term if t == 0 else totals[p] + term
                for p in range(projs):
                    energy = numbers[g, a, p] + numbers[g, atoms + a, p] * (1.0 / remainder_gain)
                    coeffs[g, a * projs + p] = jnp.broadcast_to(
                        jnp.sum(totals[p], axis=-1, keepdims=True)
                        * (energy * (gain / projector_gain / projector_gain)),
                        (each, nz),
                    )

        over_slabs(gather_part, 4)

        def scatter_part(g):
            for a in range(atoms):
                at_x, at_y = place_of(g, a)
                factor = [coeffs[g, a * projs + p] for p in range(projs)]
                for t in range(tiles):
                    row = (a * tiles + t) * projs
                    spread = factor[0] * shared_row(g, row)
                    for p in range(1, projs):
                        spread = spread + factor[p] * shared_row(g, row + p)
                    to_x = at_x + offsets_x[t]
                    to_y = at_y + offsets_y[t]
                    target[to_x, to_y] = target[to_x, to_y] + spread

        over_slabs(scatter_part, 2)

    for copy in copies:
        copy.wait()
    apply(first, second, lambda total, target, x, y: total, scale)

    for x in (0, ring + count_x):
        second[x] = jnp.zeros(second.shape[1:], jnp.float32)
    for y in (0, ring + count_y):
        second[:, y] = jnp.zeros((second.shape[0],) + second.shape[2:], jnp.float32)

    apply(second, first, lambda total, target, x, y: 2.0 * total - target[x, y], 2.0 * scale)

    portion = rounded_ref.shape[-1] // nz

    parts = slab_cells // portion
    leaving = []
    for part in range(parts):

        def round_slab(g):
            place, x0, y0 = corner(g)
            for within in range(portion):
                i, j = divmod(part * portion + within, cells_y)
                rounded_ref[part * group + place, :, pl.ds(within * nz, nz)] = first[
                    ring + x0 + i, ring + y0 + j
                ].astype(jnp.bfloat16)

        over_slabs(round_slab, 1)
        shares = pl.ds(part * group, group)
        leaving.append(
            pltpu.make_async_copy(rounded_ref.at[shares], rounded_out.at[shares], sent.at[part])
        )
        leaving[-1].start()
    for copy in leaving:
        copy.wait()


def scale_kernel(slabs_y, cells_x, cells_y, by_swaps, values_ref, field_ref):
    group, rows, nz = field_ref.shape
    each = values_ref.shape[2]
    ring = 1
    count_x, count_y = values_ref.shape[0] - 2 * ring, values_ref.shape[1] - 2 * ring
    me = lax.axis_index("sx") * slabs_y + lax.axis_index("sy") if by_swaps else 0

    def largest_of(x, largest):
        row = jnp.abs(values_ref[ring + x, pl.ds(ring, count_y)])
        return jnp.maximum(largest, jnp.max(row, axis=0))

    largest = lax.fori_loop(0, count_x, largest_of, jnp.zeros((each, nz), jnp.float32), unroll=2)
    level, gain = level_of(jnp.max(largest))
    level_rows = jnp.full((8, nz), level, jnp.float32)

    def give_slab(g, carry):
        place = jnp.bitwise_xor(me, g) if by_swaps else g
        x0 = (place // slabs_y) * cells_x
        y0 = (place % slabs_y) * cells_y
        field_ref[g, pl.ds(rows - 8, 8), :] = level_rows
        for i in range(cells_x):
            for j in range(cells_y):
                field_ref[g, pl.ds((i * cells_y + j) * each, each), :] = (
                    values_ref[ring + x0 + i, ring + y0 + j] * gain
                )
        return carry

    lax.fori_loop(0, group, give_slab, 0)


def entry(block, place):
    picked = jnp.where(place, block, 0.0)
    return jnp.sum(jnp.sum(picked, axis=0, keepdims=True), axis=1, keepdims=True)


def band_corner(shape, band):
    row = lax.broadcasted_iota(jnp.int32, shape, 0)
    column = lax.broadcasted_iota(jnp.int32, shape, 1)
    return (
        (row == 1) & (column == band * shape[0]),
        (row == 0) & (column == band * shape[0] + 1),
    )


def gram_kernel(matrix_ref, out_ref, sums_ref):
    bands, rows, columns = out_ref.shape
    matrix = matrix_ref[...]
    sums = lax.dot_general(
        matrix, matrix, (((1,), (1,)), ((), ())), preferred_element_type=jnp.float32
    )
    level, gain = level_of(jnp.max(jnp.abs(sums)))
    sums_ref[...] = sums * gain
    me = lax.axis_index("band")
    for k in range(bands):
        band = jnp.bitwise_xor(me, k)
        spare, _ = band_corner((rows, columns), band)
        block = sums_ref[pl.ds(pl.multiple_of(band * rows, rows), rows), :]
        out_ref[k] = jnp.where(spare, level, block)


def rows_kernel(cells, own_ref, *refs):
    out_ref = refs[-1]
    spare, twin = band_corner(out_ref.shape, lax.axis_index("band"))
    total = None
    for block in [own_ref[0]] + [ref[...] for ref in refs[:-1]]:
        block = block * shrink_of(entry(block, spare))
        total = block if total is None else total + block
    out_ref[...] = jnp.where(spare, entry(total, twin), total) / cells


def unpack_kernel(each, slabs_y, places, *refs):
    pieces = refs[:-3]
    filtered_hbm, filtered_ref, chunk_sems = refs[-3:]
    slab_cells, _, nz = filtered_ref.shape
    chunks = chunk_sems.shape[0]
    chunk = slab_cells // chunks
    me = lax.axis_index("sx") * slabs_y + lax.axis_index("sy") if len(pieces) > 1 else 0
    copies = []
    for c in range(chunks):
        for which, entry, other in places:
            piece = pieces[which]
            shrink = shrink_of(piece[entry, pl.ds(slab_cells * each, 1), :])
            if len(pieces) > 1:
                rows = pl.ds(pl.multiple_of(jnp.bitwise_xor(me, other) * each, each), each)
            else:
                rows = pl.ds(other * each, each)
            for cell in range(c * chunk, (c + 1) * chunk):
                filtered_ref[cell, rows, :] = piece[entry, pl.ds(cell * each, each), :] * shrink
        part = pl.ds(c * chunk, chunk)
        copies.append(
            pltpu.make_async_copy(filtered_ref.at[part], filtered_hbm.at[part], chunk_sems.at[c])
        )
        copies[-1].start()
    for copy in copies:
        copy.wait()


def swap(block, value):
    group = lax.axis_size(plane)
    return lax.ppermute(block, plane, [(i, i ^ value) for i in range(group)])


def local(orbitals, potential, projectors, energies, centers):
    band_orbitals, cells_x, cells_y, nz = orbitals.shape
    bands = lax.axis_size("band")
    slabs_x = lax.axis_size("sx")
    slabs_y = lax.axis_size("sy")
    group = slabs_x * slabs_y
    each = band_orbitals // group
    total_orbitals = bands * band_orbitals
    slab_cells = cells_x * cells_y
    grid = (slabs_x * cells_x, slabs_y * cells_y)
    atoms, projs, tiles, _ = projectors.shape

    near = slabs_y
    far = [v for v in range(1, group) if not v & near]
    by_swaps = group <= 8 and each % 8 == 0 and slabs_x > 1
    by_swaps = by_swaps and group & (group - 1) == 0 and bands & (bands - 1) == 0

    number_rows = 2 * atoms + 2
    rows = atoms * projs * tiles + slab_cells + number_rows
    rows += -rows % 8
    piece_rows = slab_cells * each
    chunks = (orbitals * orbital_gain).astype(jnp.float16)
    chunks = chunks.transpose(1, 2, 0, 3).reshape(slab_cells, group, each, nz)
    chunks = chunks.transpose(1, 0, 2, 3).reshape(group, piece_rows, nz)
    shared = pl.pallas_call(
        share_kernel,
        in_specs=[hbm, vmem, vmem, vmem, vmem],
        out_specs=vmem,
        out_shape=jax.ShapeDtypeStruct((rows, nz), jnp.float32),
        compiler_params=params,
    )(chunks[0, :8].astype(jnp.float32), energies, centers.T, projectors.transpose(0, 2, 1, 3), potential)
    narrow = shared.astype(jnp.float16)
    if by_swaps:
        me = lax.axis_index(plane)

        def chunk_for(value):
            return lax.dynamic_index_in_dim(chunks, me ^ value, 0, keepdims=False)

        came = [swap(jnp.concatenate([chunk_for(v), narrow, chunk_for(v ^ near)]), v) for v in far]
        mine = jnp.concatenate([narrow, chunk_for(near)])
        crossed = swap(jnp.stack([mine] + [block[piece_rows:] for block in came]), near)
        operands = [chunk_for(0)[None], narrow[None]] + [block[None] for block in came] + [crossed]
        operands = [block.astype(jnp.float32) for block in operands]
        operands[1] = shared[None]
        last = len(operands) - 1
        slabs = {0: ((0, 0, 0), (1, 0, 0)), near: ((last, 0, rows), (last, 0, 0))}
        for i, v in enumerate(far):
            slabs[v] = ((2 + i, 0, 0), (2 + i, 0, piece_rows))
            slabs[v ^ near] = ((last, 1 + i, rows), (last, 1 + i, 0))
    else:
        sent = jnp.concatenate([chunks, jnp.broadcast_to(narrow[None], (group, rows, nz))], axis=1)
        operands = [lax.all_to_all(sent, plane, 0, 0).astype(jnp.float32)]
        slabs = None

    portion = slab_cells // bands
    ringed = (grid[0] + 2, grid[1] + 2, each, nz)
    shares = bands * group
    rounded_shape = (shares, each, portion * nz)
    values, rounded = pl.pallas_call(
        functools.partial(filter_kernel, slabs_y, cells_x, cells_y, each, atoms, projs, slabs),
        in_specs=[vmem] * len(operands),
        out_specs=[vmem, hbm],
        out_shape=[
            jax.ShapeDtypeStruct(ringed, jnp.float32),
            jax.ShapeDtypeStruct(rounded_shape, jnp.bfloat16),
        ],
        scratch_shapes=[
            pltpu.VMEM(ringed, jnp.float32),
            pltpu.VMEM(grid + (each, nz), jnp.float32),
            pltpu.VMEM(grid + (1, nz), jnp.float32),
            pltpu.VMEM((group, atoms * projs, each, nz), jnp.float32),
            pltpu.SMEM((group, number_rows, nz), jnp.float32),
            pltpu.VMEM(rounded_shape, jnp.bfloat16),
            pltpu.SemaphoreType.DMA((group,)),
            pltpu.SemaphoreType.DMA((bands,)),
        ],
        compiler_params=params,
        cost_estimate=pl.CostEstimate(
            flops=2 * 2 * 40 * grid[0] * grid[1] * each * nz,
            bytes_accessed=8 * grid[0] * grid[1] * each * nz,
            transcendentals=0,
        ),
    )(*operands)

    matrix = lax.all_to_all(rounded, every, 0, 0)
    matrix = matrix.reshape(total_orbitals, portion * nz)
    field = pl.pallas_call(
        functools.partial(scale_kernel, slabs_y, cells_x, cells_y, by_swaps),
        in_specs=[vmem],
        out_specs=vmem,
        out_shape=jax.ShapeDtypeStruct((group, piece_rows + 8, nz), jnp.float32),
        compiler_params=params,
    )(values)
    narrow = field.astype(jnp.float16)
    if by_swaps:
        came = [swap(narrow[v], v) for v in range(1, group)]
        came, matrix = lax.optimization_barrier((came, matrix))
        pieces = [field] + [block.astype(jnp.float32)[None] for block in came]
        places = [(v, 0, v) for v in range(group)]
    else:
        pieces = [lax.all_to_all(narrow, plane, 0, 0).astype(jnp.float32)]
        places = [(0, g, g) for g in range(group)]

    def unpack(pieces):
        return pl.pallas_call(
            functools.partial(unpack_kernel, each, slabs_y, places),
            in_specs=[vmem] * len(pieces),
            out_specs=hbm,
            out_shape=jax.ShapeDtypeStruct((slab_cells, band_orbitals, nz), jnp.float32),
            scratch_shapes=[
                pltpu.VMEM((slab_cells, band_orbitals, nz), jnp.float32),
                pltpu.SemaphoreType.DMA((cells_x,)),
            ],
            compiler_params=params,
        )(*pieces)

    cells = grid[0] * grid[1] * nz
    if by_swaps:
        sums = pl.pallas_call(
            gram_kernel,
            in_specs=[vmem],
            out_specs=vmem,
            out_shape=jax.ShapeDtypeStruct((bands, band_orbitals, total_orbitals), jnp.float32),
            scratch_shapes=[pltpu.VMEM((total_orbitals, total_orbitals), jnp.float32)],
            compiler_params=params,
        )(matrix)
        parts = [
            lax.ppermute(
                sums[k].astype(jnp.float16), "band", [(i, i ^ k) for i in range(bands)]
            ).astype(jnp.float32)
            for k in range(1, bands)
        ]
        gram = pl.pallas_call(
            functools.partial(rows_kernel, cells),
            in_specs=[vmem] * bands,
            out_specs=vmem,
            out_shape=jax.ShapeDtypeStruct((band_orbitals, total_orbitals), jnp.float32),
            compiler_params=params,
        )(sums, *parts)
        terms = {v: swap(gram, v) for v in far}
        terms[0] = gram
        bit = 1
        while len(terms) > 1:
            if any(v ^ bit in terms for v in terms):
                terms = {v: terms[v] + terms[v ^ bit] for v in terms if not v & bit}
            bit *= 2
        gram, filtered = lax.optimization_barrier((terms[0], unpack(pieces)))
        gram = gram + swap(gram, near)
    else:
        sums = lax.dot_general(
            matrix, matrix, (((1,), (1,)), ((), ())), preferred_element_type=jnp.float32
        )
        parts = lax.all_to_all(sums.reshape(shares, each, total_orbitals), every, 0, 0)
        rows = jnp.sum(parts, axis=0) / cells
        gram = lax.all_to_all(jnp.broadcast_to(rows[None], (group,) + rows.shape), plane, 0, 0)
        gram = gram.reshape(band_orbitals, total_orbitals)
        filtered = unpack(pieces)

    filtered = filtered.reshape(cells_x, cells_y, band_orbitals, nz).transpose(2, 0, 1, 3)
    return (filtered, gram)


def solution(mesh):
    in_specs = (
        P("band", "sx", "sy", None),
        P("sx", "sy", None),
        P(("sx", "sy"), None, None, None),
        P(("sx", "sy"), None),
        P(("sx", "sy"), None),
    )
    out_specs = (P("band", "sx", "sy", None), P("band", None))
    return jax.shard_map(local, mesh=mesh, in_specs=in_specs, out_specs=out_specs, check_vma=False)
```

```python
import functools

import jax
import jax.numpy as jnp
from jax import lax
from jax.experimental import pallas as pl
from jax.experimental.pallas import tpu as pltpu
from jax.sharding import PartitionSpec as P

stencil_weights = (
    -5369.0 / 1800.0,
    12.0 / 7.0,
    -15.0 / 56.0,
    10.0 / 189.0,
    -1.0 / 112.0,
    2.0 / 1925.0,
    -1.0 / 16632.0,
)
filter_center = 6.5
filter_half = 6.0
offsets_x = (0, -1, 1, 0, 0)
offsets_y = (0, 0, 0, -1, 1)
reach = 6
plane = ("sx", "sy")
every = ("band", "sx", "sy")

orbital_gain = 2.0**12
projector_gain = 2.0**17
potential_gain = 2.0**13
remainder_gain = 2.0**10
top = 15
middle = 8
levels = 17

vmem = pl.BlockSpec(memory_space=pltpu.VMEM)
hbm = pl.BlockSpec(memory_space=pl.ANY)
params = pltpu.CompilerParams(vmem_limit_bytes=24 * 1024 * 1024)


def level_of(largest):
    level = jnp.float32(0.0)
    scale = jnp.float32(2.0 ** (top + 8 * middle))
    for j in range(levels):
        above = largest >= jnp.float32(2.0 ** (8 * (j - middle)))
        level = jnp.where(above, jnp.float32(j + 1), level)
        scale = jnp.where(above, jnp.float32(2.0 ** (top - 8 * (j + 1 - middle))), scale)
    return level, scale


def shrink_of(level):
    shrink = jnp.full(level.shape, 2.0 ** (-top - 8 * middle), jnp.float32)
    for j in range(levels):
        shrink = jnp.where(level > j, jnp.float32(2.0 ** (8 * (j + 1 - middle) - top)), shrink)
    return shrink


def share_kernel(_, energies_ref, centers_ref, projectors_ref, potential_ref, out_ref):
    rows, nz = out_ref.shape
    atoms, tiles, projs = projectors_ref.shape[:3]

    row = 0
    for a in range(atoms):
        for t in range(tiles):
            out_ref[pl.ds(row, projs), :] = projectors_ref[a, t] * projector_gain
            row += projs
    for i in range(potential_ref.shape[0]):
        count = potential_ref.shape[1]
        out_ref[pl.ds(row, count), :] = potential_ref[i] * potential_gain
        row += count
    out_ref[pl.ds(row, rows - row), :] = jnp.zeros((rows - row, nz), jnp.float32)
    energies = energies_ref[...]
    high = energies.astype(jnp.bfloat16).astype(jnp.float32)
    out_ref[pl.ds(row, atoms), :projs] = high
    out_ref[pl.ds(row + atoms, atoms), :projs] = (energies - high) * remainder_gain
    out_ref[pl.ds(row + 2 * atoms, 2), :atoms] = centers_ref[...].astype(jnp.float32)


def filter_kernel(slabs_y, cells_x, cells_y, each, atoms, projs, slabs, *refs):
    inputs, (first, rounded_out) = refs[:-10], refs[-10:-8]
    second, partial, diagonal, coeffs, numbers, rounded_ref, arrived, sent = refs[-8:]
    group, number_rows, _ = numbers.shape
    nz = first.shape[-1]
    count_x, count_y = diagonal.shape[0], diagonal.shape[1]
    tiles = len(offsets_x)
    slab_cells = cells_x * cells_y
    pot_row = atoms * projs * tiles
    number_row = pot_row + slab_cells
    scale = 1.0 / filter_half
    factors = [-0.5 * scale * w for w in stencil_weights]
    ring = 1
    me = 0 if slabs is None else lax.axis_index("sx") * slabs_y + lax.axis_index("sy")

    def rows_of(g, shared, row, count):
        if slabs is None:
            return inputs[0].at[g, pl.ds(row + (slab_cells * each if shared else 0), count), :]
        which, at, start = slabs[g][1 if shared else 0]
        return inputs[which].at[at, pl.ds(start + row, count), :]

    def shared_row(g, row):
        return rows_of(g, True, row, 1)[...]

    def over_slabs(body, unroll):
        if slabs is None:
            lax.fori_loop(0, group, lambda g, carry: body(g) or carry, 0, unroll=min(group, unroll))
        else:
            for g in range(group):
                body(g)

    def corner(g):
        place = g if slabs is None else jnp.bitwise_xor(me, g)
        return place, (place // slabs_y) * cells_x, (place % slabs_y) * cells_y

    if slabs is None:
        copies = [
            pltpu.make_async_copy(
                inputs[0].at[:, pl.ds(slab_cells * each + number_row, number_rows), :],
                numbers,
                arrived.at[0],
            )
        ]
    else:
        copies = [
            pltpu.make_async_copy(
                rows_of(g, True, number_row, number_rows), numbers.at[g], arrived.at[g]
            )
            for g in range(group)
        ]
    for copy in copies:
        copy.start()

    for field in (first, second):
        for x in (0, ring + count_x):
            field[x] = jnp.zeros(field.shape[1:], jnp.float32)
        for y in (0, ring + count_y):
            field[:, y] = jnp.zeros((field.shape[0],) + field.shape[2:], jnp.float32)

    def take_slab(g):
        _, x0, y0 = corner(g)
        for i in range(cells_x):
            for j in range(cells_y):
                cell = i * cells_y + j
                first[ring + x0 + i, ring + y0 + j] = rows_of(g, False, cell * each, each)[...] * (
                    1.0 / orbital_gain
                )
                diagonal[x0 + i, y0 + j] = shared_row(g, pot_row + cell) * (
                    scale / potential_gain
                ) + (3.0 * factors[0] - filter_center * scale)

    over_slabs(take_slab, 1)

    distance = jnp.abs(
        lax.broadcasted_iota(jnp.int32, (nz, nz), 0) - lax.broadcasted_iota(jnp.int32, (nz, nz), 1)
    )
    along_z = jnp.zeros((nz, nz), jnp.float32)
    for step in range(1, reach + 1):
        along_z = jnp.where(distance == step, factors[step], along_z)
    z_high = along_z.astype(jnp.bfloat16)
    z_low = (along_z - z_high.astype(jnp.float32)).astype(jnp.bfloat16)
    z_matrix = jnp.concatenate(
        [
            jnp.concatenate([z_high, z_low], axis=1),
            jnp.concatenate([z_high, jnp.zeros_like(z_high)], axis=1),
        ],
        axis=0,
    )

    def along(cells, at):
        total = None
        for step in range(1, reach + 1):
            near = [cells[n] for n in (at - step, at + step) if 0 <= n < len(cells)]
            if near:
                term = factors[step] * sum(near[1:], near[0])
                total = term if total is None else total + term
        return total

    def apply(source, target, finish, gain):
        def xz_part(y, carry):
            column = source[pl.ds(ring, count_x), ring + y]
            flat = column.reshape(count_x * each, nz)
            high = flat.astype(jnp.bfloat16)
            low = (flat - high.astype(jnp.float32)).astype(jnp.bfloat16)
            both = jnp.dot(
                jnp.concatenate([high, low], axis=1), z_matrix, preferred_element_type=jnp.float32
            )
            along_z = (both[:, :nz] + both[:, nz:]).reshape(column.shape)
            cells = [column[x] for x in range(count_x)]
            for x in range(count_x):
                partial[x, y] = along_z[x] + diagonal[x, y] * cells[x] + along(cells, x)
            return carry

        lax.fori_loop(0, count_y, xz_part, 0, unroll=6)

        def y_part(x, carry):
            cells = [source[ring + x, ring + y] for y in range(count_y)]
            for y in range(count_y):
                total = partial[x, y] + along(cells, y)
                target[ring + x, ring + y] = finish(total, target, ring + x, ring + y)
            return carry

        lax.fori_loop(0, count_x, y_part, 0, unroll=4)

        def place_of(g, a):
            return (
                ring + numbers[g, 2 * atoms, a].astype(jnp.int32),
                ring + numbers[g, 2 * atoms + 1, a].astype(jnp.int32),
            )

        def gather_part(g):
            for a in range(atoms):
                at_x, at_y = place_of(g, a)
                totals = [None] * projs
                for t in range(tiles):
                    tile = source[at_x + offsets_x[t], at_y + offsets_y[t]]
                    for p in range(projs):
                        term = tile * shared_row(g, (a * tiles + t) * projs + p)
                        totals[p] = term if t == 0 else totals[p] + term
                for p in range(projs):
                    energy = numbers[g, a, p] + numbers[g, atoms + a, p] * (1.0 / remainder_gain)
                    coeffs[g, a * projs + p] = jnp.broadcast_to(
                        jnp.sum(totals[p], axis=-1, keepdims=True)
                        * (energy * (gain / projector_gain / projector_gain)),
                        (each, nz),
                    )

        over_slabs(gather_part, 4)

        def scatter_part(g):
            for a in range(atoms):
                at_x, at_y = place_of(g, a)
                factor = [coeffs[g, a * projs + p] for p in range(projs)]
                for t in range(tiles):
                    row = (a * tiles + t) * projs
                    spread = factor[0] * shared_row(g, row)
                    for p in range(1, projs):
                        spread = spread + factor[p] * shared_row(g, row + p)
                    to_x = at_x + offsets_x[t]
                    to_y = at_y + offsets_y[t]
                    target[to_x, to_y] = target[to_x, to_y] + spread

        over_slabs(scatter_part, 2)

    for copy in copies:
        copy.wait()
    apply(first, second, lambda total, target, x, y: total, scale)

    for x in (0, ring + count_x):
        second[x] = jnp.zeros(second.shape[1:], jnp.float32)
    for y in (0, ring + count_y):
        second[:, y] = jnp.zeros((second.shape[0],) + second.shape[2:], jnp.float32)

    apply(second, first, lambda total, target, x, y: 2.0 * total - target[x, y], 2.0 * scale)

    portion = rounded_ref.shape[-1] // nz

    parts = slab_cells // portion
    leaving = []
    for part in range(parts):

        def round_slab(g):
            place, x0, y0 = corner(g)
            for within in range(portion):
                i, j = divmod(part * portion + within, cells_y)
                rounded_ref[part * group + place, :, pl.ds(within * nz, nz)] = first[
                    ring + x0 + i, ring + y0 + j
                ].astype(jnp.bfloat16)

        over_slabs(round_slab, 1)
        shares = pl.ds(part * group, group)
        leaving.append(
            pltpu.make_async_copy(rounded_ref.at[shares], rounded_out.at[shares], sent.at[part])
        )
        leaving[-1].start()
    for copy in leaving:
        copy.wait()


def scale_kernel(slabs_y, cells_x, cells_y, by_swaps, values_ref, field_ref):
    group, rows, nz = field_ref.shape
    each = values_ref.shape[2]
    ring = 1
    count_x, count_y = values_ref.shape[0] - 2 * ring, values_ref.shape[1] - 2 * ring
    me = lax.axis_index("sx") * slabs_y + lax.axis_index("sy") if by_swaps else 0

    def largest_of(x, largest):
        row = jnp.abs(values_ref[ring + x, pl.ds(ring, count_y)])
        return jnp.maximum(largest, jnp.max(row, axis=0))

    largest = lax.fori_loop(0, count_x, largest_of, jnp.zeros((each, nz), jnp.float32), unroll=2)
    level, gain = level_of(jnp.max(largest))
    level_rows = jnp.full((8, nz), level, jnp.float32)

    def give_slab(g, carry):
        place = jnp.bitwise_xor(me, g) if by_swaps else g
        x0 = (place // slabs_y) * cells_x
        y0 = (place % slabs_y) * cells_y
        field_ref[g, pl.ds(rows - 8, 8), :] = level_rows
        for i in range(cells_x):
            for j in range(cells_y):
                field_ref[g, pl.ds((i * cells_y + j) * each, each), :] = (
                    values_ref[ring + x0 + i, ring + y0 + j] * gain
                )
        return carry

    lax.fori_loop(0, group, give_slab, 0)


def entry(block, place):
    picked = jnp.where(place, block, 0.0)
    return jnp.sum(jnp.sum(picked, axis=0, keepdims=True), axis=1, keepdims=True)


def band_corner(shape, band):
    row = lax.broadcasted_iota(jnp.int32, shape, 0)
    column = lax.broadcasted_iota(jnp.int32, shape, 1)
    return (
        (row == 1) & (column == band * shape[0]),
        (row == 0) & (column == band * shape[0] + 1),
    )


def gram_kernel(matrix_ref, out_ref, sums_ref):
    bands, rows, columns = out_ref.shape
    matrix = matrix_ref[...]
    sums = lax.dot_general(
        matrix, matrix, (((1,), (1,)), ((), ())), preferred_element_type=jnp.float32
    )
    level, gain = level_of(jnp.max(jnp.abs(sums)))
    sums_ref[...] = sums * gain
    me = lax.axis_index("band")
    for k in range(bands):
        band = jnp.bitwise_xor(me, k)
        spare, _ = band_corner((rows, columns), band)
        block = sums_ref[pl.ds(pl.multiple_of(band * rows, rows), rows), :]
        out_ref[k] = jnp.where(spare, level, block)


def rows_kernel(cells, own_ref, *refs):
    out_ref = refs[-1]
    spare, twin = band_corner(out_ref.shape, lax.axis_index("band"))
    total = None
    for block in [own_ref[0]] + [ref[...] for ref in refs[:-1]]:
        block = block * shrink_of(entry(block, spare))
        total = block if total is None else total + block
    out_ref[...] = jnp.where(spare, entry(total, twin), total) / cells


def unpack_kernel(each, slabs_y, places, *refs):
    pieces = refs[:-3]
    filtered_hbm, filtered_ref, chunk_sems = refs[-3:]
    slab_cells, _, nz = filtered_ref.shape
    chunks = chunk_sems.shape[0]
    chunk = slab_cells // chunks
    me = lax.axis_index("sx") * slabs_y + lax.axis_index("sy") if len(pieces) > 1 else 0
    copies = []
    for c in range(chunks):
        for which, entry, other in places:
            piece = pieces[which]
            shrink = shrink_of(piece[entry, pl.ds(slab_cells * each, 1), :])
            if len(pieces) > 1:
                rows = pl.ds(pl.multiple_of(jnp.bitwise_xor(me, other) * each, each), each)
            else:
                rows = pl.ds(other * each, each)
            for cell in range(c * chunk, (c + 1) * chunk):
                filtered_ref[cell, rows, :] = piece[entry, pl.ds(cell * each, each), :] * shrink
        part = pl.ds(c * chunk, chunk)
        copies.append(
            pltpu.make_async_copy(filtered_ref.at[part], filtered_hbm.at[part], chunk_sems.at[c])
        )
        copies[-1].start()
    for copy in copies:
        copy.wait()


def swap(block, value):
    group = lax.axis_size(plane)
    return lax.ppermute(block, plane, [(i, i ^ value) for i in range(group)])


def local(orbitals, potential, projectors, energies, centers):
    band_orbitals, cells_x, cells_y, nz = orbitals.shape
    bands = lax.axis_size("band")
    slabs_x = lax.axis_size("sx")
    slabs_y = lax.axis_size("sy")
    group = slabs_x * slabs_y
    each = band_orbitals // group
    total_orbitals = bands * band_orbitals
    slab_cells = cells_x * cells_y
    grid = (slabs_x * cells_x, slabs_y * cells_y)
    atoms, projs, tiles, _ = projectors.shape

    near = slabs_y
    far = [v for v in range(1, group) if not v & near]
    by_swaps = group <= 8 and each % 8 == 0 and slabs_x > 1
    by_swaps = by_swaps and group & (group - 1) == 0 and bands & (bands - 1) == 0

    number_rows = 2 * atoms + 2
    rows = atoms * projs * tiles + slab_cells + number_rows
    rows += -rows % 8
    piece_rows = slab_cells * each
    chunks = (orbitals * orbital_gain).astype(jnp.float16)
    chunks = chunks.transpose(1, 2, 0, 3).reshape(slab_cells, group, each, nz)
    chunks = chunks.transpose(1, 0, 2, 3).reshape(group, piece_rows, nz)
    shared = pl.pallas_call(
        share_kernel,
        in_specs=[hbm, vmem, vmem, vmem, vmem],
        out_specs=vmem,
        out_shape=jax.ShapeDtypeStruct((rows, nz), jnp.float32),
        compiler_params=params,
    )(chunks[0, :8].astype(jnp.float32), energies, centers.T, projectors.transpose(0, 2, 1, 3), potential)
    narrow = shared.astype(jnp.float16)
    if by_swaps:
        me = lax.axis_index(plane)

        def chunk_for(value):
            return lax.dynamic_index_in_dim(chunks, me ^ value, 0, keepdims=False)

        came = [swap(jnp.concatenate([chunk_for(v), narrow, chunk_for(v ^ near)]), v) for v in far]
        mine = jnp.concatenate([narrow, chunk_for(near)])
        crossed = swap(jnp.stack([mine] + [block[piece_rows:] for block in came]), near)
        operands = [chunk_for(0)[None], narrow[None]] + [block[None] for block in came] + [crossed]
        operands = [block.astype(jnp.float32) for block in operands]
        operands[1] = shared[None]
        last = len(operands) - 1
        slabs = {0: ((0, 0, 0), (1, 0, 0)), near: ((last, 0, rows), (last, 0, 0))}
        for i, v in enumerate(far):
            slabs[v] = ((2 + i, 0, 0), (2 + i, 0, piece_rows))
            slabs[v ^ near] = ((last, 1 + i, rows), (last, 1 + i, 0))
    else:
        sent = jnp.concatenate([chunks, jnp.broadcast_to(narrow[None], (group, rows, nz))], axis=1)
        operands = [lax.all_to_all(sent, plane, 0, 0).astype(jnp.float32)]
        slabs = None

    portion = slab_cells // bands
    ringed = (grid[0] + 2, grid[1] + 2, each, nz)
    shares = bands * group
    rounded_shape = (shares, each, portion * nz)
    values, rounded = pl.pallas_call(
        functools.partial(filter_kernel, slabs_y, cells_x, cells_y, each, atoms, projs, slabs),
        in_specs=[vmem] * len(operands),
        out_specs=[vmem, hbm],
        out_shape=[
            jax.ShapeDtypeStruct(ringed, jnp.float32),
            jax.ShapeDtypeStruct(rounded_shape, jnp.bfloat16),
        ],
        scratch_shapes=[
            pltpu.VMEM(ringed, jnp.float32),
            pltpu.VMEM(grid + (each, nz), jnp.float32),
            pltpu.VMEM(grid + (1, nz), jnp.float32),
            pltpu.VMEM((group, atoms * projs, each, nz), jnp.float32),
            pltpu.SMEM((group, number_rows, nz), jnp.float32),
            pltpu.VMEM(rounded_shape, jnp.bfloat16),
            pltpu.SemaphoreType.DMA((group,)),
            pltpu.SemaphoreType.DMA((bands,)),
        ],
        compiler_params=params,
        cost_estimate=pl.CostEstimate(
            flops=2 * 2 * 40 * grid[0] * grid[1] * each * nz,
            bytes_accessed=8 * grid[0] * grid[1] * each * nz,
            transcendentals=0,
        ),
    )(*operands)

    matrix = lax.all_to_all(rounded, every, 0, 0)
    matrix = matrix.reshape(total_orbitals, portion * nz)
    field = pl.pallas_call(
        functools.partial(scale_kernel, slabs_y, cells_x, cells_y, by_swaps),
        in_specs=[vmem],
        out_specs=vmem,
        out_shape=jax.ShapeDtypeStruct((group, piece_rows + 8, nz), jnp.float32),
        compiler_params=params,
    )(values)
    narrow = field.astype(jnp.float16)
    if by_swaps:
        came = [swap(jnp.stack([narrow[v], narrow[v | near]]), v) for v in far]
        first, matrix = lax.optimization_barrier((came[:-1], matrix))
        came = first + came[-1:]
        came.append(swap(jnp.stack([narrow[near]] + [block[1] for block in came]), near))
        pieces = [field] + [block.astype(jnp.float32) for block in came]
        places = [(0, 0, 0), (len(pieces) - 1, 0, near)]
        for i, v in enumerate(far):
            places += [(i + 1, 0, v), (len(pieces) - 1, i + 1, v | near)]
    else:
        pieces = [lax.all_to_all(narrow, plane, 0, 0).astype(jnp.float32)]
        places = [(0, g, g) for g in range(group)]

    def unpack(pieces):
        return pl.pallas_call(
            functools.partial(unpack_kernel, each, slabs_y, places),
            in_specs=[vmem] * len(pieces),
            out_specs=hbm,
            out_shape=jax.ShapeDtypeStruct((slab_cells, band_orbitals, nz), jnp.float32),
            scratch_shapes=[
                pltpu.VMEM((slab_cells, band_orbitals, nz), jnp.float32),
                pltpu.SemaphoreType.DMA((cells_x,)),
            ],
            compiler_params=params,
        )(*pieces)

    cells = grid[0] * grid[1] * nz
    if by_swaps:
        sums = pl.pallas_call(
            gram_kernel,
            in_specs=[vmem],
            out_specs=vmem,
            out_shape=jax.ShapeDtypeStruct((bands, band_orbitals, total_orbitals), jnp.float32),
            scratch_shapes=[pltpu.VMEM((total_orbitals, total_orbitals), jnp.float32)],
            compiler_params=params,
        )(matrix)
        parts = [
            lax.ppermute(
                sums[k].astype(jnp.float16), "band", [(i, i ^ k) for i in range(bands)]
            ).astype(jnp.float32)
            for k in range(1, bands)
        ]
        parts, pieces = lax.optimization_barrier((parts, pieces))
        gram = pl.pallas_call(
            functools.partial(rows_kernel, cells),
            in_specs=[vmem] * bands,
            out_specs=vmem,
            out_shape=jax.ShapeDtypeStruct((band_orbitals, total_orbitals), jnp.float32),
            compiler_params=params,
        )(sums, *parts)
        terms = {v: swap(gram, v) for v in far}
        terms[0] = gram
        bit = 1
        while len(terms) > 1:
            if any(v ^ bit in terms for v in terms):
                terms = {v: terms[v] + terms[v ^ bit] for v in terms if not v & bit}
            bit *= 2
        gram, filtered = lax.optimization_barrier((terms[0], unpack(pieces)))
        gram = gram + swap(gram, near)
    else:
        sums = lax.dot_general(
            matrix, matrix, (((1,), (1,)), ((), ())), preferred_element_type=jnp.float32
        )
        parts = lax.all_to_all(sums.reshape(shares, each, total_orbitals), every, 0, 0)
        rows = jnp.sum(parts, axis=0) / cells
        gram = lax.all_to_all(jnp.broadcast_to(rows[None], (group,) + rows.shape), plane, 0, 0)
        gram = gram.reshape(band_orbitals, total_orbitals)
        filtered = unpack(pieces)

    filtered = filtered.reshape(cells_x, cells_y, band_orbitals, nz).transpose(2, 0, 1, 3)
    return (filtered, gram)


def solution(mesh):
    in_specs = (
        P("band", "sx", "sy", None),
        P("sx", "sy", None),
        P(("sx", "sy"), None, None, None),
        P(("sx", "sy"), None),
        P(("sx", "sy"), None),
    )
    out_specs = (P("band", "sx", "sy", None), P("band", None))
    return jax.shard_map(local, mesh=mesh, in_specs=in_specs, out_specs=out_specs, check_vma=False)
```

```python
import functools

import jax
import jax.numpy as jnp
from jax import lax
from jax.experimental import pallas as pl
from jax.experimental.pallas import tpu as pltpu
from jax.sharding import PartitionSpec as P

stencil_weights = (
    -5369.0 / 1800.0,
    12.0 / 7.0,
    -15.0 / 56.0,
    10.0 / 189.0,
    -1.0 / 112.0,
    2.0 / 1925.0,
    -1.0 / 16632.0,
)
filter_center = 6.5
filter_half = 6.0
offsets_x = (0, -1, 1, 0, 0)
offsets_y = (0, 0, 0, -1, 1)
reach = 6
plane = ("sx", "sy")
every = ("band", "sx", "sy")

orbital_gain = 2.0**12
projector_gain = 2.0**17
potential_gain = 2.0**13
remainder_gain = 2.0**10
top = 15
middle = 8
levels = 17

vmem = pl.BlockSpec(memory_space=pltpu.VMEM)
hbm = pl.BlockSpec(memory_space=pl.ANY)
params = pltpu.CompilerParams(vmem_limit_bytes=24 * 1024 * 1024)


def level_of(largest):
    level = jnp.float32(0.0)
    scale = jnp.float32(2.0 ** (top + 8 * middle))
    for j in range(levels):
        above = largest >= jnp.float32(2.0 ** (8 * (j - middle)))
        level = jnp.where(above, jnp.float32(j + 1), level)
        scale = jnp.where(above, jnp.float32(2.0 ** (top - 8 * (j + 1 - middle))), scale)
    return level, scale


def shrink_of(level):
    shrink = jnp.full(level.shape, 2.0 ** (-top - 8 * middle), jnp.float32)
    for j in range(levels):
        shrink = jnp.where(level > j, jnp.float32(2.0 ** (8 * (j + 1 - middle) - top)), shrink)
    return shrink


def share_kernel(_, energies_ref, centers_ref, projectors_ref, potential_ref, out_ref):
    rows, nz = out_ref.shape
    atoms, tiles, projs = projectors_ref.shape[:3]

    row = 0
    for a in range(atoms):
        for t in range(tiles):
            out_ref[pl.ds(row, projs), :] = projectors_ref[a, t] * projector_gain
            row += projs
    for i in range(potential_ref.shape[0]):
        count = potential_ref.shape[1]
        out_ref[pl.ds(row, count), :] = potential_ref[i] * potential_gain
        row += count
    out_ref[pl.ds(row, rows - row), :] = jnp.zeros((rows - row, nz), jnp.float32)
    energies = energies_ref[...]
    high = energies.astype(jnp.bfloat16).astype(jnp.float32)
    out_ref[pl.ds(row, atoms), :projs] = high
    out_ref[pl.ds(row + atoms, atoms), :projs] = (energies - high) * remainder_gain
    out_ref[pl.ds(row + 2 * atoms, 2), :atoms] = centers_ref[...].astype(jnp.float32)


def filter_kernel(slabs_y, cells_x, cells_y, each, atoms, projs, slabs, *refs):
    inputs, (first, rounded_out) = refs[:-10], refs[-10:-8]
    second, partial, diagonal, coeffs, numbers, rounded_ref, arrived, sent = refs[-8:]
    group, number_rows, _ = numbers.shape
    nz = first.shape[-1]
    count_x, count_y = diagonal.shape[0], diagonal.shape[1]
    tiles = len(offsets_x)
    slab_cells = cells_x * cells_y
    pot_row = atoms * projs * tiles
    number_row = pot_row + slab_cells
    scale = 1.0 / filter_half
    factors = [-0.5 * scale * w for w in stencil_weights]
    ring = 1
    me = 0 if slabs is None else lax.axis_index("sx") * slabs_y + lax.axis_index("sy")

    def rows_of(g, shared, row, count):
        if slabs is None:
            return inputs[0].at[g, pl.ds(row + (slab_cells * each if shared else 0), count), :]
        which, at, start = slabs[g][1 if shared else 0]
        return inputs[which].at[at, pl.ds(start + row, count), :]

    def shared_row(g, row):
        return rows_of(g, True, row, 1)[...]

    def over_slabs(body, unroll):
        if slabs is None:
            lax.fori_loop(0, group, lambda g, carry: body(g) or carry, 0, unroll=min(group, unroll))
        else:
            for g in range(group):
                body(g)

    def corner(g):
        place = g if slabs is None else jnp.bitwise_xor(me, g)
        return place, (place // slabs_y) * cells_x, (place % slabs_y) * cells_y

    if slabs is None:
        copies = [
            pltpu.make_async_copy(
                inputs[0].at[:, pl.ds(slab_cells * each + number_row, number_rows), :],
                numbers,
                arrived.at[0],
            )
        ]
    else:
        copies = [
            pltpu.make_async_copy(
                rows_of(g, True, number_row, number_rows), numbers.at[g], arrived.at[g]
            )
            for g in range(group)
        ]
    for copy in copies:
        copy.start()

    for field in (first, second):
        for x in (0, ring + count_x):
            field[x] = jnp.zeros(field.shape[1:], jnp.float32)
        for y in (0, ring + count_y):
            field[:, y] = jnp.zeros((field.shape[0],) + field.shape[2:], jnp.float32)

    def take_slab(g):
        _, x0, y0 = corner(g)
        for i in range(cells_x):
            for j in range(cells_y):
                cell = i * cells_y + j
                first[ring + x0 + i, ring + y0 + j] = rows_of(g, False, cell * each, each)[...] * (
                    1.0 / orbital_gain
                )
                diagonal[x0 + i, y0 + j] = shared_row(g, pot_row + cell) * (
                    scale / potential_gain
                ) + (3.0 * factors[0] - filter_center * scale)

    over_slabs(take_slab, 1)

    distance = jnp.abs(
        lax.broadcasted_iota(jnp.int32, (nz, nz), 0) - lax.broadcasted_iota(jnp.int32, (nz, nz), 1)
    )
    along_z = jnp.zeros((nz, nz), jnp.float32)
    for step in range(1, reach + 1):
        along_z = jnp.where(distance == step, factors[step], along_z)
    z_high = along_z.astype(jnp.bfloat16)
    z_low = (along_z - z_high.astype(jnp.float32)).astype(jnp.bfloat16)
    z_matrix = jnp.concatenate(
        [
            jnp.concatenate([z_high, z_low], axis=1),
            jnp.concatenate([z_high, jnp.zeros_like(z_high)], axis=1),
        ],
        axis=0,
    )

    def along(cells, at):
        total = None
        for step in range(1, reach + 1):
            near = [cells[n] for n in (at - step, at + step) if 0 <= n < len(cells)]
            if near:
                term = factors[step] * sum(near[1:], near[0])
                total = term if total is None else total + term
        return total

    def apply(source, target, finish, gain):
        def xz_part(y, carry):
            column = source[pl.ds(ring, count_x), ring + y]
            flat = column.reshape(count_x * each, nz)
            high = flat.astype(jnp.bfloat16)
            low = (flat - high.astype(jnp.float32)).astype(jnp.bfloat16)
            both = jnp.dot(
                jnp.concatenate([high, low], axis=1), z_matrix, preferred_element_type=jnp.float32
            )
            along_z = (both[:, :nz] + both[:, nz:]).reshape(column.shape)
            cells = [column[x] for x in range(count_x)]
            for x in range(count_x):
                partial[x, y] = along_z[x] + diagonal[x, y] * cells[x] + along(cells, x)
            return carry

        lax.fori_loop(0, count_y, xz_part, 0, unroll=6)

        def y_part(x, carry):
            cells = [source[ring + x, ring + y] for y in range(count_y)]
            for y in range(count_y):
                total = partial[x, y] + along(cells, y)
                target[ring + x, ring + y] = finish(total, target, ring + x, ring + y)
            return carry

        lax.fori_loop(0, count_x, y_part, 0, unroll=4)

        def place_of(g, a):
            return (
                ring + numbers[g, 2 * atoms, a].astype(jnp.int32),
                ring + numbers[g, 2 * atoms + 1, a].astype(jnp.int32),
            )

        def gather_part(g):
            for a in range(atoms):
                at_x, at_y = place_of(g, a)
                totals = [None] * projs
                for t in range(tiles):
                    tile = source[at_x + offsets_x[t], at_y + offsets_y[t]]
                    for p in range(projs):
                        term = tile * shared_row(g, (a * tiles + t) * projs + p)
                        totals[p] = term if t == 0 else totals[p] + term
                for p in range(projs):
                    energy = numbers[g, a, p] + numbers[g, atoms + a, p] * (1.0 / remainder_gain)
                    coeffs[g, a * projs + p] = jnp.broadcast_to(
                        jnp.sum(totals[p], axis=-1, keepdims=True)
                        * (energy * (gain / projector_gain / projector_gain)),
                        (each, nz),
                    )

        over_slabs(gather_part, 4)

        def scatter_part(g):
            for a in range(atoms):
                at_x, at_y = place_of(g, a)
                factor = [coeffs[g, a * projs + p] for p in range(projs)]
                for t in range(tiles):
                    row = (a * tiles + t) * projs
                    spread = factor[0] * shared_row(g, row)
                    for p in range(1, projs):
                        spread = spread + factor[p] * shared_row(g, row + p)
                    to_x = at_x + offsets_x[t]
                    to_y = at_y + offsets_y[t]
                    target[to_x, to_y] = target[to_x, to_y] + spread

        over_slabs(scatter_part, 2)

    for copy in copies:
        copy.wait()
    apply(first, second, lambda total, target, x, y: total, scale)

    for x in (0, ring + count_x):
        second[x] = jnp.zeros(second.shape[1:], jnp.float32)
    for y in (0, ring + count_y):
        second[:, y] = jnp.zeros((second.shape[0],) + second.shape[2:], jnp.float32)

    apply(second, first, lambda total, target, x, y: 2.0 * total - target[x, y], 2.0 * scale)

    portion = rounded_ref.shape[-1] // nz

    parts = slab_cells // portion
    leaving = []
    for part in range(parts):

        def round_slab(g):
            place, x0, y0 = corner(g)
            for within in range(portion):
                i, j = divmod(part * portion + within, cells_y)
                rounded_ref[part * group + place, :, pl.ds(within * nz, nz)] = first[
                    ring + x0 + i, ring + y0 + j
                ].astype(jnp.bfloat16)

        over_slabs(round_slab, 1)
        shares = pl.ds(part * group, group)
        leaving.append(
            pltpu.make_async_copy(rounded_ref.at[shares], rounded_out.at[shares], sent.at[part])
        )
        leaving[-1].start()
    for copy in leaving:
        copy.wait()


def scale_kernel(slabs_y, cells_x, cells_y, by_swaps, values_ref, field_ref):
    group, rows, nz = field_ref.shape
    each = values_ref.shape[2]
    ring = 1
    count_x, count_y = values_ref.shape[0] - 2 * ring, values_ref.shape[1] - 2 * ring
    me = lax.axis_index("sx") * slabs_y + lax.axis_index("sy") if by_swaps else 0

    def largest_of(x, largest):
        row = jnp.abs(values_ref[ring + x, pl.ds(ring, count_y)])
        return jnp.maximum(largest, jnp.max(row, axis=0))

    largest = lax.fori_loop(0, count_x, largest_of, jnp.zeros((each, nz), jnp.float32), unroll=2)
    level, gain = level_of(jnp.max(largest))
    level_rows = jnp.full((8, nz), level, jnp.float32)

    def give_slab(g, carry):
        place = jnp.bitwise_xor(me, g) if by_swaps else g
        x0 = (place // slabs_y) * cells_x
        y0 = (place % slabs_y) * cells_y
        field_ref[g, pl.ds(rows - 8, 8), :] = level_rows
        for i in range(cells_x):
            for j in range(cells_y):
                field_ref[g, pl.ds((i * cells_y + j) * each, each), :] = (
                    values_ref[ring + x0 + i, ring + y0 + j] * gain
                )
        return carry

    lax.fori_loop(0, group, give_slab, 0)


def entry(block, place):
    picked = jnp.where(place, block, 0.0)
    return jnp.sum(jnp.sum(picked, axis=0, keepdims=True), axis=1, keepdims=True)


def band_corner(shape, band):
    row = lax.broadcasted_iota(jnp.int32, shape, 0)
    column = lax.broadcasted_iota(jnp.int32, shape, 1)
    return (
        (row == 1) & (column == band * shape[0]),
        (row == 0) & (column == band * shape[0] + 1),
    )


def gram_kernel(matrix_ref, out_ref, sums_ref):
    bands, rows, columns = out_ref.shape
    matrix = matrix_ref[...]
    sums = lax.dot_general(
        matrix, matrix, (((1,), (1,)), ((), ())), preferred_element_type=jnp.float32
    )
    level, gain = level_of(jnp.max(jnp.abs(sums)))
    sums_ref[...] = sums * gain
    me = lax.axis_index("band")
    for k in range(bands):
        band = jnp.bitwise_xor(me, k)
        spare, _ = band_corner((rows, columns), band)
        block = sums_ref[pl.ds(pl.multiple_of(band * rows, rows), rows), :]
        out_ref[k] = jnp.where(spare, level, block)


def rows_kernel(cells, own_ref, *refs):
    out_ref = refs[-1]
    spare, twin = band_corner(out_ref.shape, lax.axis_index("band"))
    total = None
    for block in [own_ref[0]] + [ref[...] for ref in refs[:-1]]:
        block = block * shrink_of(entry(block, spare))
        total = block if total is None else total + block
    out_ref[...] = jnp.where(spare, entry(total, twin), total) / cells


def unpack_kernel(each, slabs_y, places, *refs):
    pieces = refs[:-3]
    filtered_hbm, filtered_ref, chunk_sems = refs[-3:]
    slab_cells, _, nz = filtered_ref.shape
    chunks = chunk_sems.shape[0]
    chunk = slab_cells // chunks
    me = lax.axis_index("sx") * slabs_y + lax.axis_index("sy") if len(pieces) > 1 else 0
    copies = []
    for c in range(chunks):
        for which, entry, other in places:
            piece = pieces[which]
            shrink = shrink_of(piece[entry, pl.ds(slab_cells * each, 1), :])
            if len(pieces) > 1:
                rows = pl.ds(pl.multiple_of(jnp.bitwise_xor(me, other) * each, each), each)
            else:
                rows = pl.ds(other * each, each)
            for cell in range(c * chunk, (c + 1) * chunk):
                filtered_ref[cell, rows, :] = piece[entry, pl.ds(cell * each, each), :] * shrink
        part = pl.ds(c * chunk, chunk)
        copies.append(
            pltpu.make_async_copy(filtered_ref.at[part], filtered_hbm.at[part], chunk_sems.at[c])
        )
        copies[-1].start()
    for copy in copies:
        copy.wait()


def swap(block, value):
    group = lax.axis_size(plane)
    return lax.ppermute(block, plane, [(i, i ^ value) for i in range(group)])


def local(orbitals, potential, projectors, energies, centers):
    band_orbitals, cells_x, cells_y, nz = orbitals.shape
    bands = lax.axis_size("band")
    slabs_x = lax.axis_size("sx")
    slabs_y = lax.axis_size("sy")
    group = slabs_x * slabs_y
    each = band_orbitals // group
    total_orbitals = bands * band_orbitals
    slab_cells = cells_x * cells_y
    grid = (slabs_x * cells_x, slabs_y * cells_y)
    atoms, projs, tiles, _ = projectors.shape

    near = slabs_y
    far = [v for v in range(1, group) if not v & near]
    by_swaps = group <= 8 and each % 8 == 0 and slabs_x > 1
    by_swaps = by_swaps and group & (group - 1) == 0 and bands & (bands - 1) == 0

    number_rows = 2 * atoms + 2
    rows = atoms * projs * tiles + slab_cells + number_rows
    rows += -rows % 8
    piece_rows = slab_cells * each
    chunks = (orbitals * orbital_gain).astype(jnp.float16)
    chunks = chunks.transpose(1, 2, 0, 3).reshape(slab_cells, group, each, nz)
    chunks = chunks.transpose(1, 0, 2, 3).reshape(group, piece_rows, nz)
    shared = pl.pallas_call(
        share_kernel,
        in_specs=[hbm, vmem, vmem, vmem, vmem],
        out_specs=vmem,
        out_shape=jax.ShapeDtypeStruct((rows, nz), jnp.float32),
        compiler_params=params,
    )(chunks[0, :8].astype(jnp.float32), energies, centers.T, projectors.transpose(0, 2, 1, 3), potential)
    narrow = shared.astype(jnp.float16)
    if by_swaps:
        me = lax.axis_index(plane)

        def chunk_for(value):
            return lax.dynamic_index_in_dim(chunks, me ^ value, 0, keepdims=False)

        came = [swap(jnp.concatenate([chunk_for(v), narrow, chunk_for(v ^ near)]), v) for v in far]
        mine = jnp.concatenate([narrow, chunk_for(near)])
        crossed = swap(jnp.stack([mine] + [block[piece_rows:] for block in came]), near)
        operands = [chunk_for(0)[None], narrow[None]] + [block[None] for block in came] + [crossed]
        operands = [block.astype(jnp.float32) for block in operands]
        operands[1] = shared[None]
        last = len(operands) - 1
        slabs = {0: ((0, 0, 0), (1, 0, 0)), near: ((last, 0, rows), (last, 0, 0))}
        for i, v in enumerate(far):
            slabs[v] = ((2 + i, 0, 0), (2 + i, 0, piece_rows))
            slabs[v ^ near] = ((last, 1 + i, rows), (last, 1 + i, 0))
    else:
        sent = jnp.concatenate([chunks, jnp.broadcast_to(narrow[None], (group, rows, nz))], axis=1)
        operands = [lax.all_to_all(sent, plane, 0, 0).astype(jnp.float32)]
        slabs = None

    portion = slab_cells // bands
    ringed = (grid[0] + 2, grid[1] + 2, each, nz)
    shares = bands * group
    rounded_shape = (shares, each, portion * nz)
    values, rounded = pl.pallas_call(
        functools.partial(filter_kernel, slabs_y, cells_x, cells_y, each, atoms, projs, slabs),
        in_specs=[vmem] * len(operands),
        out_specs=[vmem, hbm],
        out_shape=[
            jax.ShapeDtypeStruct(ringed, jnp.float32),
            jax.ShapeDtypeStruct(rounded_shape, jnp.bfloat16),
        ],
        scratch_shapes=[
            pltpu.VMEM(ringed, jnp.float32),
            pltpu.VMEM(grid + (each, nz), jnp.float32),
            pltpu.VMEM(grid + (1, nz), jnp.float32),
            pltpu.VMEM((group, atoms * projs, each, nz), jnp.float32),
            pltpu.SMEM((group, number_rows, nz), jnp.float32),
            pltpu.VMEM(rounded_shape, jnp.bfloat16),
            pltpu.SemaphoreType.DMA((group,)),
            pltpu.SemaphoreType.DMA((bands,)),
        ],
        compiler_params=params,
        cost_estimate=pl.CostEstimate(
            flops=2 * 2 * 40 * grid[0] * grid[1] * each * nz,
            bytes_accessed=8 * grid[0] * grid[1] * each * nz,
            transcendentals=0,
        ),
    )(*operands)

    matrix = lax.all_to_all(rounded, every, 0, 0)
    matrix = matrix.reshape(total_orbitals, portion * nz)
    field = pl.pallas_call(
        functools.partial(scale_kernel, slabs_y, cells_x, cells_y, by_swaps),
        in_specs=[vmem],
        out_specs=vmem,
        out_shape=jax.ShapeDtypeStruct((group, piece_rows + 8, nz), jnp.float32),
        compiler_params=params,
    )(values)
    narrow = field.astype(jnp.float16)
    if by_swaps:
        came = [swap(jnp.stack([narrow[v], narrow[v | near]]), v) for v in far]
        others, matrix = lax.optimization_barrier((came[1:], matrix))
        came = came[:1] + others
        came.append(swap(jnp.stack([narrow[near]] + [block[1] for block in came]), near))
        pieces = [field] + [block.astype(jnp.float32) for block in came]
        places = [(0, 0, 0), (len(pieces) - 1, 0, near)]
        for i, v in enumerate(far):
            places += [(i + 1, 0, v), (len(pieces) - 1, i + 1, v | near)]
    else:
        pieces = [lax.all_to_all(narrow, plane, 0, 0).astype(jnp.float32)]
        places = [(0, g, g) for g in range(group)]

    def unpack(pieces):
        return pl.pallas_call(
            functools.partial(unpack_kernel, each, slabs_y, places),
            in_specs=[vmem] * len(pieces),
            out_specs=hbm,
            out_shape=jax.ShapeDtypeStruct((slab_cells, band_orbitals, nz), jnp.float32),
            scratch_shapes=[
                pltpu.VMEM((slab_cells, band_orbitals, nz), jnp.float32),
                pltpu.SemaphoreType.DMA((cells_x,)),
            ],
            compiler_params=params,
        )(*pieces)

    cells = grid[0] * grid[1] * nz
    if by_swaps:
        sums = pl.pallas_call(
            gram_kernel,
            in_specs=[vmem],
            out_specs=vmem,
            out_shape=jax.ShapeDtypeStruct((bands, band_orbitals, total_orbitals), jnp.float32),
            scratch_shapes=[pltpu.VMEM((total_orbitals, total_orbitals), jnp.float32)],
            compiler_params=params,
        )(matrix)
        parts = [
            lax.ppermute(
                sums[k].astype(jnp.float16), "band", [(i, i ^ k) for i in range(bands)]
            ).astype(jnp.float32)
            for k in range(1, bands)
        ]
        parts, pieces = lax.optimization_barrier((parts, pieces))
        gram = pl.pallas_call(
            functools.partial(rows_kernel, cells),
            in_specs=[vmem] * bands,
            out_specs=vmem,
            out_shape=jax.ShapeDtypeStruct((band_orbitals, total_orbitals), jnp.float32),
            compiler_params=params,
        )(sums, *parts)
        terms = {v: swap(gram, v) for v in far}
        terms[0] = gram
        bit = 1
        while len(terms) > 1:
            if any(v ^ bit in terms for v in terms):
                terms = {v: terms[v] + terms[v ^ bit] for v in terms if not v & bit}
            bit *= 2
        gram, filtered = lax.optimization_barrier((terms[0], unpack(pieces)))
        gram = gram + swap(gram, near)
    else:
        sums = lax.dot_general(
            matrix, matrix, (((1,), (1,)), ((), ())), preferred_element_type=jnp.float32
        )
        parts = lax.all_to_all(sums.reshape(shares, each, total_orbitals), every, 0, 0)
        rows = jnp.sum(parts, axis=0) / cells
        gram = lax.all_to_all(jnp.broadcast_to(rows[None], (group,) + rows.shape), plane, 0, 0)
        gram = gram.reshape(band_orbitals, total_orbitals)
        filtered = unpack(pieces)

    filtered = filtered.reshape(cells_x, cells_y, band_orbitals, nz).transpose(2, 0, 1, 3)
    return (filtered, gram)


def solution(mesh):
    in_specs = (
        P("band", "sx", "sy", None),
        P("sx", "sy", None),
        P(("sx", "sy"), None, None, None),
        P(("sx", "sy"), None),
        P(("sx", "sy"), None),
    )
    out_specs = (P("band", "sx", "sy", None), P("band", None))
    return jax.shard_map(local, mesh=mesh, in_specs=in_specs, out_specs=out_specs, check_vma=False)
```

```python
import functools

import jax
import jax.numpy as jnp
from jax import lax
from jax.experimental import pallas as pl
from jax.experimental.pallas import tpu as pltpu
from jax.sharding import PartitionSpec as P

stencil_weights = (
    -5369.0 / 1800.0,
    12.0 / 7.0,
    -15.0 / 56.0,
    10.0 / 189.0,
    -1.0 / 112.0,
    2.0 / 1925.0,
    -1.0 / 16632.0,
)
filter_center = 6.5
filter_half = 6.0
offsets_x = (0, -1, 1, 0, 0)
offsets_y = (0, 0, 0, -1, 1)
reach = 6
plane = ("sx", "sy")
every = ("band", "sx", "sy")

orbital_gain = 2.0**12
projector_gain = 2.0**17
potential_gain = 2.0**13
remainder_gain = 2.0**10
top = 15
middle = 8
levels = 17

vmem = pl.BlockSpec(memory_space=pltpu.VMEM)
hbm = pl.BlockSpec(memory_space=pl.ANY)
params = pltpu.CompilerParams(vmem_limit_bytes=24 * 1024 * 1024)


def level_of(largest):
    level = jnp.float32(0.0)
    scale = jnp.float32(2.0 ** (top + 8 * middle))
    for j in range(levels):
        above = largest >= jnp.float32(2.0 ** (8 * (j - middle)))
        level = jnp.where(above, jnp.float32(j + 1), level)
        scale = jnp.where(above, jnp.float32(2.0 ** (top - 8 * (j + 1 - middle))), scale)
    return level, scale


def shrink_of(level):
    shrink = jnp.full(level.shape, 2.0 ** (-top - 8 * middle), jnp.float32)
    for j in range(levels):
        shrink = jnp.where(level > j, jnp.float32(2.0 ** (8 * (j + 1 - middle) - top)), shrink)
    return shrink


def share_kernel(_, energies_ref, centers_ref, projectors_ref, potential_ref, out_ref):
    rows, nz = out_ref.shape
    atoms, tiles, projs = projectors_ref.shape[:3]

    row = 0
    for a in range(atoms):
        for t in range(tiles):
            out_ref[pl.ds(row, projs), :] = projectors_ref[a, t] * projector_gain
            row += projs
    for i in range(potential_ref.shape[0]):
        count = potential_ref.shape[1]
        out_ref[pl.ds(row, count), :] = potential_ref[i] * potential_gain
        row += count
    out_ref[pl.ds(row, rows - row), :] = jnp.zeros((rows - row, nz), jnp.float32)
    energies = energies_ref[...]
    high = energies.astype(jnp.bfloat16).astype(jnp.float32)
    out_ref[pl.ds(row, atoms), :projs] = high
    out_ref[pl.ds(row + atoms, atoms), :projs] = (energies - high) * remainder_gain
    out_ref[pl.ds(row + 2 * atoms, 2), :atoms] = centers_ref[...].astype(jnp.float32)


def filter_kernel(slabs_y, cells_x, cells_y, each, atoms, projs, slabs, *refs):
    inputs, (first, rounded_out) = refs[:-10], refs[-10:-8]
    second, partial, diagonal, coeffs, numbers, rounded_ref, arrived, sent = refs[-8:]
    group, number_rows, _ = numbers.shape
    nz = first.shape[-1]
    count_x, count_y = diagonal.shape[0], diagonal.shape[1]
    tiles = len(offsets_x)
    slab_cells = cells_x * cells_y
    pot_row = atoms * projs * tiles
    number_row = pot_row + slab_cells
    scale = 1.0 / filter_half
    factors = [-0.5 * scale * w for w in stencil_weights]
    ring = 1
    me = 0 if slabs is None else lax.axis_index("sx") * slabs_y + lax.axis_index("sy")

    def rows_of(g, shared, row, count):
        if slabs is None:
            return inputs[0].at[g, pl.ds(row + (slab_cells * each if shared else 0), count), :]
        which, at, start = slabs[g][1 if shared else 0]
        return inputs[which].at[at, pl.ds(start + row, count), :]

    def shared_row(g, row):
        return rows_of(g, True, row, 1)[...]

    def over_slabs(body, unroll):
        if slabs is None:
            lax.fori_loop(0, group, lambda g, carry: body(g) or carry, 0, unroll=min(group, unroll))
        else:
            for g in range(group):
                body(g)

    def corner(g):
        place = g if slabs is None else jnp.bitwise_xor(me, g)
        return place, (place // slabs_y) * cells_x, (place % slabs_y) * cells_y

    if slabs is None:
        copies = [
            pltpu.make_async_copy(
                inputs[0].at[:, pl.ds(slab_cells * each + number_row, number_rows), :],
                numbers,
                arrived.at[0],
            )
        ]
    else:
        copies = [
            pltpu.make_async_copy(
                rows_of(g, True, number_row, number_rows), numbers.at[g], arrived.at[g]
            )
            for g in range(group)
        ]
    for copy in copies:
        copy.start()

    for field in (first, second):
        for x in (0, ring + count_x):
            field[x] = jnp.zeros(field.shape[1:], jnp.float32)
        for y in (0, ring + count_y):
            field[:, y] = jnp.zeros((field.shape[0],) + field.shape[2:], jnp.float32)

    def take_slab(g):
        _, x0, y0 = corner(g)
        for i in range(cells_x):
            for j in range(cells_y):
                cell = i * cells_y + j
                first[ring + x0 + i, ring + y0 + j] = rows_of(g, False, cell * each, each)[...] * (
                    1.0 / orbital_gain
                )
                diagonal[x0 + i, y0 + j] = shared_row(g, pot_row + cell) * (
                    scale / potential_gain
                ) + (3.0 * factors[0] - filter_center * scale)

    over_slabs(take_slab, 1)

    distance = jnp.abs(
        lax.broadcasted_iota(jnp.int32, (nz, nz), 0) - lax.broadcasted_iota(jnp.int32, (nz, nz), 1)
    )
    along_z = jnp.zeros((nz, nz), jnp.float32)
    for step in range(1, reach + 1):
        along_z = jnp.where(distance == step, factors[step], along_z)
    z_high = along_z.astype(jnp.bfloat16)
    z_low = (along_z - z_high.astype(jnp.float32)).astype(jnp.bfloat16)
    z_matrix = jnp.concatenate(
        [
            jnp.concatenate([z_high, z_low], axis=1),
            jnp.concatenate([z_high, jnp.zeros_like(z_high)], axis=1),
        ],
        axis=0,
    )

    def along(cells, at):
        total = None
        for step in range(1, reach + 1):
            near = [cells[n] for n in (at - step, at + step) if 0 <= n < len(cells)]
            if near:
                term = factors[step] * sum(near[1:], near[0])
                total = term if total is None else total + term
        return total

    def apply(source, target, finish, gain):
        def xz_part(y, carry):
            column = source[pl.ds(ring, count_x), ring + y]
            flat = column.reshape(count_x * each, nz)
            high = flat.astype(jnp.bfloat16)
            low = (flat - high.astype(jnp.float32)).astype(jnp.bfloat16)
            both = jnp.dot(
                jnp.concatenate([high, low], axis=1), z_matrix, preferred_element_type=jnp.float32
            )
            along_z = (both[:, :nz] + both[:, nz:]).reshape(column.shape)
            cells = [column[x] for x in range(count_x)]
            for x in range(count_x):
                partial[x, y] = along_z[x] + diagonal[x, y] * cells[x] + along(cells, x)
            return carry

        lax.fori_loop(0, count_y, xz_part, 0, unroll=6)

        def y_part(x, carry):
            cells = [source[ring + x, ring + y] for y in range(count_y)]
            for y in range(count_y):
                total = partial[x, y] + along(cells, y)
                target[ring + x, ring + y] = finish(total, target, ring + x, ring + y)
            return carry

        lax.fori_loop(0, count_x, y_part, 0, unroll=4)

        def place_of(g, a):
            return (
                ring + numbers[g, 2 * atoms, a].astype(jnp.int32),
                ring + numbers[g, 2 * atoms + 1, a].astype(jnp.int32),
            )

        def gather_part(g):
            for a in range(atoms):
                at_x, at_y = place_of(g, a)
                totals = [None] * projs
                for t in range(tiles):
                    tile = source[at_x + offsets_x[t], at_y + offsets_y[t]]
                    for p in range(projs):
                        term = tile * shared_row(g, (a * tiles + t) * projs + p)
                        totals[p] = term if t == 0 else totals[p] + term
                for p in range(projs):
                    energy = numbers[g, a, p] + numbers[g, atoms + a, p] * (1.0 / remainder_gain)
                    coeffs[g, a * projs + p] = jnp.broadcast_to(
                        jnp.sum(totals[p], axis=-1, keepdims=True)
                        * (energy * (gain / projector_gain / projector_gain)),
                        (each, nz),
                    )

        over_slabs(gather_part, 4)

        def scatter_part(g):
            for a in range(atoms):
                at_x, at_y = place_of(g, a)
                factor = [coeffs[g, a * projs + p] for p in range(projs)]
                for t in range(tiles):
                    row = (a * tiles + t) * projs
                    spread = factor[0] * shared_row(g, row)
                    for p in range(1, projs):
                        spread = spread + factor[p] * shared_row(g, row + p)
                    to_x = at_x + offsets_x[t]
                    to_y = at_y + offsets_y[t]
                    target[to_x, to_y] = target[to_x, to_y] + spread

        over_slabs(scatter_part, 2)

    for copy in copies:
        copy.wait()
    apply(first, second, lambda total, target, x, y: total, scale)

    for x in (0, ring + count_x):
        second[x] = jnp.zeros(second.shape[1:], jnp.float32)
    for y in (0, ring + count_y):
        second[:, y] = jnp.zeros((second.shape[0],) + second.shape[2:], jnp.float32)

    apply(second, first, lambda total, target, x, y: 2.0 * total - target[x, y], 2.0 * scale)

    portion = rounded_ref.shape[-1] // nz

    parts = slab_cells // portion
    leaving = []
    for part in range(parts):

        def round_slab(g):
            place, x0, y0 = corner(g)
            for within in range(portion):
                i, j = divmod(part * portion + within, cells_y)
                rounded_ref[part * group + place, :, pl.ds(within * nz, nz)] = first[
                    ring + x0 + i, ring + y0 + j
                ].astype(jnp.bfloat16)

        over_slabs(round_slab, 1)
        shares = pl.ds(part * group, group)
        leaving.append(
            pltpu.make_async_copy(rounded_ref.at[shares], rounded_out.at[shares], sent.at[part])
        )
        leaving[-1].start()
    for copy in leaving:
        copy.wait()


def scale_kernel(slabs_y, cells_x, cells_y, by_swaps, values_ref, field_ref):
    group, rows, nz = field_ref.shape
    each = values_ref.shape[2]
    ring = 1
    count_x, count_y = values_ref.shape[0] - 2 * ring, values_ref.shape[1] - 2 * ring
    me = lax.axis_index("sx") * slabs_y + lax.axis_index("sy") if by_swaps else 0

    def largest_of(x, largest):
        row = jnp.abs(values_ref[ring + x, pl.ds(ring, count_y)])
        return jnp.maximum(largest, jnp.max(row, axis=0))

    largest = lax.fori_loop(0, count_x, largest_of, jnp.zeros((each, nz), jnp.float32), unroll=2)
    level, gain = level_of(jnp.max(largest))
    level_rows = jnp.full((8, nz), level, jnp.float32)

    def give_slab(g, carry):
        place = jnp.bitwise_xor(me, g) if by_swaps else g
        x0 = (place // slabs_y) * cells_x
        y0 = (place % slabs_y) * cells_y
        field_ref[g, pl.ds(rows - 8, 8), :] = level_rows
        for i in range(cells_x):
            for j in range(cells_y):
                field_ref[g, pl.ds((i * cells_y + j) * each, each), :] = (
                    values_ref[ring + x0 + i, ring + y0 + j] * gain
                )
        return carry

    lax.fori_loop(0, group, give_slab, 0)


def entry(block, place):
    picked = jnp.where(place, block, 0.0)
    return jnp.sum(jnp.sum(picked, axis=0, keepdims=True), axis=1, keepdims=True)


def band_corner(shape, band):
    row = lax.broadcasted_iota(jnp.int32, shape, 0)
    column = lax.broadcasted_iota(jnp.int32, shape, 1)
    return (
        (row == 1) & (column == band * shape[0]),
        (row == 0) & (column == band * shape[0] + 1),
    )


def gram_kernel(matrix_ref, out_ref, sums_ref):
    bands, rows, columns = out_ref.shape
    matrix = matrix_ref[...]
    sums = lax.dot_general(
        matrix, matrix, (((1,), (1,)), ((), ())), preferred_element_type=jnp.float32
    )
    level, gain = level_of(jnp.max(jnp.abs(sums)))
    sums_ref[...] = sums * gain
    me = lax.axis_index("band")
    for k in range(bands):
        band = jnp.bitwise_xor(me, k)
        spare, _ = band_corner((rows, columns), band)
        block = sums_ref[pl.ds(pl.multiple_of(band * rows, rows), rows), :]
        out_ref[k] = jnp.where(spare, level, block)


def rows_kernel(cells, own_ref, *refs):
    out_ref = refs[-1]
    spare, twin = band_corner(out_ref.shape, lax.axis_index("band"))
    total = None
    for block in [own_ref[0]] + [ref[...] for ref in refs[:-1]]:
        block = block * shrink_of(entry(block, spare))
        total = block if total is None else total + block
    out_ref[...] = jnp.where(spare, entry(total, twin), total) / cells


def unpack_kernel(each, slabs_y, places, *refs):
    pieces = refs[:-3]
    filtered_hbm, filtered_ref, chunk_sems = refs[-3:]
    slab_cells, _, nz = filtered_ref.shape
    chunks = chunk_sems.shape[0]
    chunk = slab_cells // chunks
    me = lax.axis_index("sx") * slabs_y + lax.axis_index("sy") if len(pieces) > 1 else 0
    copies = []
    for c in range(chunks):
        for which, entry, other in places:
            piece = pieces[which]
            shrink = shrink_of(piece[entry, pl.ds(slab_cells * each, 1), :])
            if len(pieces) > 1:
                rows = pl.ds(pl.multiple_of(jnp.bitwise_xor(me, other) * each, each), each)
            else:
                rows = pl.ds(other * each, each)
            for cell in range(c * chunk, (c + 1) * chunk):
                filtered_ref[cell, rows, :] = piece[entry, pl.ds(cell * each, each), :] * shrink
        part = pl.ds(c * chunk, chunk)
        copies.append(
            pltpu.make_async_copy(filtered_ref.at[part], filtered_hbm.at[part], chunk_sems.at[c])
        )
        copies[-1].start()
    for copy in copies:
        copy.wait()


def swap(block, value):
    group = lax.axis_size(plane)
    return lax.ppermute(block, plane, [(i, i ^ value) for i in range(group)])


def local(orbitals, potential, projectors, energies, centers):
    band_orbitals, cells_x, cells_y, nz = orbitals.shape
    bands = lax.axis_size("band")
    slabs_x = lax.axis_size("sx")
    slabs_y = lax.axis_size("sy")
    group = slabs_x * slabs_y
    each = band_orbitals // group
    total_orbitals = bands * band_orbitals
    slab_cells = cells_x * cells_y
    grid = (slabs_x * cells_x, slabs_y * cells_y)
    atoms, projs, tiles, _ = projectors.shape

    near = slabs_y
    far = [v for v in range(1, group) if not v & near]
    by_swaps = group <= 8 and each % 8 == 0 and slabs_x > 1
    by_swaps = by_swaps and group & (group - 1) == 0 and bands & (bands - 1) == 0

    number_rows = 2 * atoms + 2
    rows = atoms * projs * tiles + slab_cells + number_rows
    rows += -rows % 8
    piece_rows = slab_cells * each
    chunks = (orbitals * orbital_gain).astype(jnp.float16)
    chunks = chunks.transpose(1, 2, 0, 3).reshape(slab_cells, group, each, nz)
    chunks = chunks.transpose(1, 0, 2, 3).reshape(group, piece_rows, nz)
    shared = pl.pallas_call(
        share_kernel,
        in_specs=[hbm, vmem, vmem, vmem, vmem],
        out_specs=vmem,
        out_shape=jax.ShapeDtypeStruct((rows, nz), jnp.float32),
        compiler_params=params,
    )(chunks[0, :8].astype(jnp.float32), energies, centers.T, projectors.transpose(0, 2, 1, 3), potential)
    narrow = shared.astype(jnp.float16)
    if by_swaps:
        me = lax.axis_index(plane)

        def chunk_for(value):
            return lax.dynamic_index_in_dim(chunks, me ^ value, 0, keepdims=False)

        came = [swap(jnp.concatenate([chunk_for(v), narrow, chunk_for(v ^ near)]), v) for v in far]
        mine = jnp.concatenate([narrow, chunk_for(near)])
        passed = {0: mine, **{v: block[piece_rows:] for v, block in zip(far, came)}}
        operands = [chunk_for(0)[None], narrow[None]] + [block[None] for block in came]
        slabs = {0: ((0, 0, 0), (1, 0, 0))}
        for i, v in enumerate(far):
            slabs[v] = ((2 + i, 0, 0), (2 + i, 0, piece_rows))
        for part in ([0], far[-1:], far[:-1]):
            if part:
                for i, v in enumerate(part):
                    slabs[v ^ near] = ((len(operands), i, rows), (len(operands), i, 0))
                operands.append(swap(jnp.stack([passed[v] for v in part]), near))
        operands = [block.astype(jnp.float32) for block in operands]
        operands[1] = shared[None]
    else:
        sent = jnp.concatenate([chunks, jnp.broadcast_to(narrow[None], (group, rows, nz))], axis=1)
        operands = [lax.all_to_all(sent, plane, 0, 0).astype(jnp.float32)]
        slabs = None

    portion = slab_cells // bands
    ringed = (grid[0] + 2, grid[1] + 2, each, nz)
    shares = bands * group
    rounded_shape = (shares, each, portion * nz)
    values, rounded = pl.pallas_call(
        functools.partial(filter_kernel, slabs_y, cells_x, cells_y, each, atoms, projs, slabs),
        in_specs=[vmem] * len(operands),
        out_specs=[vmem, hbm],
        out_shape=[
            jax.ShapeDtypeStruct(ringed, jnp.float32),
            jax.ShapeDtypeStruct(rounded_shape, jnp.bfloat16),
        ],
        scratch_shapes=[
            pltpu.VMEM(ringed, jnp.float32),
            pltpu.VMEM(grid + (each, nz), jnp.float32),
            pltpu.VMEM(grid + (1, nz), jnp.float32),
            pltpu.VMEM((group, atoms * projs, each, nz), jnp.float32),
            pltpu.SMEM((group, number_rows, nz), jnp.float32),
            pltpu.VMEM(rounded_shape, jnp.bfloat16),
            pltpu.SemaphoreType.DMA((group,)),
            pltpu.SemaphoreType.DMA((bands,)),
        ],
        compiler_params=params,
        cost_estimate=pl.CostEstimate(
            flops=2 * 2 * 40 * grid[0] * grid[1] * each * nz,
            bytes_accessed=8 * grid[0] * grid[1] * each * nz,
            transcendentals=0,
        ),
    )(*operands)

    matrix = lax.all_to_all(rounded, every, 0, 0)
    matrix = matrix.reshape(total_orbitals, portion * nz)
    field = pl.pallas_call(
        functools.partial(scale_kernel, slabs_y, cells_x, cells_y, by_swaps),
        in_specs=[vmem],
        out_specs=vmem,
        out_shape=jax.ShapeDtypeStruct((group, piece_rows + 8, nz), jnp.float32),
        compiler_params=params,
    )(values)
    narrow = field.astype(jnp.float16)
    if by_swaps:
        came = [swap(jnp.stack([narrow[v], narrow[v | near]]), v) for v in far]
        others, matrix = lax.optimization_barrier((came[1:], matrix))
        came = came[:1] + others
        came.append(swap(jnp.stack([narrow[near]] + [block[1] for block in came]), near))
        pieces = [field] + [block.astype(jnp.float32) for block in came]
        places = [(0, 0, 0), (len(pieces) - 1, 0, near)]
        for i, v in enumerate(far):
            places += [(i + 1, 0, v), (len(pieces) - 1, i + 1, v | near)]
    else:
        pieces = [lax.all_to_all(narrow, plane, 0, 0).astype(jnp.float32)]
        places = [(0, g, g) for g in range(group)]

    def unpack(pieces):
        return pl.pallas_call(
            functools.partial(unpack_kernel, each, slabs_y, places),
            in_specs=[vmem] * len(pieces),
            out_specs=hbm,
            out_shape=jax.ShapeDtypeStruct((slab_cells, band_orbitals, nz), jnp.float32),
            scratch_shapes=[
                pltpu.VMEM((slab_cells, band_orbitals, nz), jnp.float32),
                pltpu.SemaphoreType.DMA((cells_x,)),
            ],
            compiler_params=params,
        )(*pieces)

    cells = grid[0] * grid[1] * nz
    if by_swaps:
        sums = pl.pallas_call(
            gram_kernel,
            in_specs=[vmem],
            out_specs=vmem,
            out_shape=jax.ShapeDtypeStruct((bands, band_orbitals, total_orbitals), jnp.float32),
            scratch_shapes=[pltpu.VMEM((total_orbitals, total_orbitals), jnp.float32)],
            compiler_params=params,
        )(matrix)
        parts = [
            lax.ppermute(
                sums[k].astype(jnp.float16), "band", [(i, i ^ k) for i in range(bands)]
            ).astype(jnp.float32)
            for k in range(1, bands)
        ]
        parts, pieces = lax.optimization_barrier((parts, pieces))
        gram = pl.pallas_call(
            functools.partial(rows_kernel, cells),
            in_specs=[vmem] * bands,
            out_specs=vmem,
            out_shape=jax.ShapeDtypeStruct((band_orbitals, total_orbitals), jnp.float32),
            compiler_params=params,
        )(sums, *parts)
        terms = {v: swap(gram, v) for v in far}
        terms[0] = gram
        bit = 1
        while len(terms) > 1:
            if any(v ^ bit in terms for v in terms):
                terms = {v: terms[v] + terms[v ^ bit] for v in terms if not v & bit}
            bit *= 2
        gram, filtered = lax.optimization_barrier((terms[0], unpack(pieces)))
        gram = gram + swap(gram, near)
    else:
        sums = lax.dot_general(
            matrix, matrix, (((1,), (1,)), ((), ())), preferred_element_type=jnp.float32
        )
        parts = lax.all_to_all(sums.reshape(shares, each, total_orbitals), every, 0, 0)
        rows = jnp.sum(parts, axis=0) / cells
        gram = lax.all_to_all(jnp.broadcast_to(rows[None], (group,) + rows.shape), plane, 0, 0)
        gram = gram.reshape(band_orbitals, total_orbitals)
        filtered = unpack(pieces)

    filtered = filtered.reshape(cells_x, cells_y, band_orbitals, nz).transpose(2, 0, 1, 3)
    return (filtered, gram)


def solution(mesh):
    in_specs = (
        P("band", "sx", "sy", None),
        P("sx", "sy", None),
        P(("sx", "sy"), None, None, None),
        P(("sx", "sy"), None),
        P(("sx", "sy"), None),
    )
    out_specs = (P("band", "sx", "sy", None), P("band", None))
    return jax.shard_map(local, mesh=mesh, in_specs=in_specs, out_specs=out_specs, check_vma=False)
```

```python
import functools

import jax
import jax.numpy as jnp
from jax import lax
from jax.experimental import pallas as pl
from jax.experimental.pallas import tpu as pltpu
from jax.sharding import PartitionSpec as P

stencil_weights = (
    -5369.0 / 1800.0,
    12.0 / 7.0,
    -15.0 / 56.0,
    10.0 / 189.0,
    -1.0 / 112.0,
    2.0 / 1925.0,
    -1.0 / 16632.0,
)
filter_center = 6.5
filter_half = 6.0
offsets_x = (0, -1, 1, 0, 0)
offsets_y = (0, 0, 0, -1, 1)
reach = 6
plane = ("sx", "sy")
every = ("band", "sx", "sy")

orbital_gain = 2.0**12
projector_gain = 2.0**17
potential_gain = 2.0**13
remainder_gain = 2.0**10
top = 15
middle = 8
levels = 17

vmem = pl.BlockSpec(memory_space=pltpu.VMEM)
hbm = pl.BlockSpec(memory_space=pl.ANY)
params = pltpu.CompilerParams(vmem_limit_bytes=24 * 1024 * 1024)


def level_of(largest):
    level = jnp.float32(0.0)
    scale = jnp.float32(2.0 ** (top + 8 * middle))
    for j in range(levels):
        above = largest >= jnp.float32(2.0 ** (8 * (j - middle)))
        level = jnp.where(above, jnp.float32(j + 1), level)
        scale = jnp.where(above, jnp.float32(2.0 ** (top - 8 * (j + 1 - middle))), scale)
    return level, scale


def shrink_of(level):
    shrink = jnp.full(level.shape, 2.0 ** (-top - 8 * middle), jnp.float32)
    for j in range(levels):
        shrink = jnp.where(level > j, jnp.float32(2.0 ** (8 * (j + 1 - middle) - top)), shrink)
    return shrink


def share_kernel(_, energies_ref, centers_ref, projectors_ref, potential_ref, out_ref):
    rows, nz = out_ref.shape
    atoms, tiles, projs = projectors_ref.shape[:3]

    row = 0
    for a in range(atoms):
        for t in range(tiles):
            out_ref[pl.ds(row, projs), :] = projectors_ref[a, t] * projector_gain
            row += projs
    for i in range(potential_ref.shape[0]):
        count = potential_ref.shape[1]
        out_ref[pl.ds(row, count), :] = potential_ref[i] * potential_gain
        row += count
    out_ref[pl.ds(row, rows - row), :] = jnp.zeros((rows - row, nz), jnp.float32)
    energies = energies_ref[...]
    high = energies.astype(jnp.bfloat16).astype(jnp.float32)
    out_ref[pl.ds(row, atoms), :projs] = high
    out_ref[pl.ds(row + atoms, atoms), :projs] = (energies - high) * remainder_gain
    out_ref[pl.ds(row + 2 * atoms, 2), :atoms] = centers_ref[...].astype(jnp.float32)


def filter_kernel(slabs_y, cells_x, cells_y, each, atoms, projs, slabs, *refs):
    inputs, (first, rounded_out) = refs[:-10], refs[-10:-8]
    second, partial, diagonal, coeffs, numbers, rounded_ref, arrived, sent = refs[-8:]
    group, number_rows, _ = numbers.shape
    nz = first.shape[-1]
    count_x, count_y = diagonal.shape[0], diagonal.shape[1]
    tiles = len(offsets_x)
    slab_cells = cells_x * cells_y
    pot_row = atoms * projs * tiles
    number_row = pot_row + slab_cells
    scale = 1.0 / filter_half
    factors = [-0.5 * scale * w for w in stencil_weights]
    ring = 1
    me = 0 if slabs is None else lax.axis_index("sx") * slabs_y + lax.axis_index("sy")

    def rows_of(g, shared, row, count):
        if slabs is None:
            return inputs[0].at[g, pl.ds(row + (slab_cells * each if shared else 0), count), :]
        which, at, start = slabs[g][1 if shared else 0]
        return inputs[which].at[at, pl.ds(start + row, count), :]

    def shared_row(g, row):
        return rows_of(g, True, row, 1)[...]

    def over_slabs(body, unroll):
        if slabs is None:
            lax.fori_loop(0, group, lambda g, carry: body(g) or carry, 0, unroll=min(group, unroll))
        else:
            for g in range(group):
                body(g)

    def corner(g):
        place = g if slabs is None else jnp.bitwise_xor(me, g)
        return place, (place // slabs_y) * cells_x, (place % slabs_y) * cells_y

    if slabs is None:
        copies = [
            pltpu.make_async_copy(
                inputs[0].at[:, pl.ds(slab_cells * each + number_row, number_rows), :],
                numbers,
                arrived.at[0],
            )
        ]
    else:
        copies = [
            pltpu.make_async_copy(
                rows_of(g, True, number_row, number_rows), numbers.at[g], arrived.at[g]
            )
            for g in range(group)
        ]
    for copy in copies:
        copy.start()

    for field in (first, second):
        for x in (0, ring + count_x):
            field[x] = jnp.zeros(field.shape[1:], jnp.float32)
        for y in (0, ring + count_y):
            field[:, y] = jnp.zeros((field.shape[0],) + field.shape[2:], jnp.float32)

    def take_slab(g):
        _, x0, y0 = corner(g)
        for i in range(cells_x):
            for j in range(cells_y):
                cell = i * cells_y + j
                first[ring + x0 + i, ring + y0 + j] = rows_of(g, False, cell * each, each)[...] * (
                    1.0 / orbital_gain
                )
                diagonal[x0 + i, y0 + j] = shared_row(g, pot_row + cell) * (
                    scale / potential_gain
                ) + (3.0 * factors[0] - filter_center * scale)

    over_slabs(take_slab, 1)

    distance = jnp.abs(
        lax.broadcasted_iota(jnp.int32, (nz, nz), 0) - lax.broadcasted_iota(jnp.int32, (nz, nz), 1)
    )
    along_z = jnp.zeros((nz, nz), jnp.float32)
    for step in range(1, reach + 1):
        along_z = jnp.where(distance == step, factors[step], along_z)
    z_high = along_z.astype(jnp.bfloat16)
    z_low = (along_z - z_high.astype(jnp.float32)).astype(jnp.bfloat16)
    z_matrix = jnp.concatenate(
        [
            jnp.concatenate([z_high, z_low], axis=1),
            jnp.concatenate([z_high, jnp.zeros_like(z_high)], axis=1),
        ],
        axis=0,
    )

    def along(cells, at):
        total = None
        for step in range(1, reach + 1):
            near = [cells[n] for n in (at - step, at + step) if 0 <= n < len(cells)]
            if near:
                term = factors[step] * sum(near[1:], near[0])
                total = term if total is None else total + term
        return total

    def apply(source, target, finish, gain):
        def xz_part(y, carry):
            column = source[pl.ds(ring, count_x), ring + y]
            flat = column.reshape(count_x * each, nz)
            high = flat.astype(jnp.bfloat16)
            low = (flat - high.astype(jnp.float32)).astype(jnp.bfloat16)
            both = jnp.dot(
                jnp.concatenate([high, low], axis=1), z_matrix, preferred_element_type=jnp.float32
            )
            along_z = (both[:, :nz] + both[:, nz:]).reshape(column.shape)
            cells = [column[x] for x in range(count_x)]
            for x in range(count_x):
                partial[x, y] = along_z[x] + diagonal[x, y] * cells[x] + along(cells, x)
            return carry

        lax.fori_loop(0, count_y, xz_part, 0, unroll=4)

        def y_part(x, carry):
            cells = [source[ring + x, ring + y] for y in range(count_y)]
            for y in range(count_y):
                total = partial[x, y] + along(cells, y)
                target[ring + x, ring + y] = finish(total, target, ring + x, ring + y)
            return carry

        lax.fori_loop(0, count_x, y_part, 0, unroll=2)

        def place_of(g, a):
            return (
                ring + numbers[g, 2 * atoms, a].astype(jnp.int32),
                ring + numbers[g, 2 * atoms + 1, a].astype(jnp.int32),
            )

        def gather_part(g):
            for a in range(atoms):
                at_x, at_y = place_of(g, a)
                totals = [None] * projs
                for t in range(tiles):
                    tile = source[at_x + offsets_x[t], at_y + offsets_y[t]]
                    for p in range(projs):
                        term = tile * shared_row(g, (a * tiles + t) * projs + p)
                        totals[p] = term if t == 0 else totals[p] + term
                for p in range(projs):
                    energy = numbers[g, a, p] + numbers[g, atoms + a, p] * (1.0 / remainder_gain)
                    coeffs[g, a * projs + p] = jnp.broadcast_to(
                        jnp.sum(totals[p], axis=-1, keepdims=True)
                        * (energy * (gain / projector_gain / projector_gain)),
                        (each, nz),
                    )

        over_slabs(gather_part, 4)

        def scatter_part(g):
            for a in range(atoms):
                at_x, at_y = place_of(g, a)
                factor = [coeffs[g, a * projs + p] for p in range(projs)]
                for t in range(tiles):
                    row = (a * tiles + t) * projs
                    spread = factor[0] * shared_row(g, row)
                    for p in range(1, projs):
                        spread = spread + factor[p] * shared_row(g, row + p)
                    to_x = at_x + offsets_x[t]
                    to_y = at_y + offsets_y[t]
                    target[to_x, to_y] = target[to_x, to_y] + spread

        over_slabs(scatter_part, 2)

    for copy in copies:
        copy.wait()
    apply(first, second, lambda total, target, x, y: total, scale)

    for x in (0, ring + count_x):
        second[x] = jnp.zeros(second.shape[1:], jnp.float32)
    for y in (0, ring + count_y):
        second[:, y] = jnp.zeros((second.shape[0],) + second.shape[2:], jnp.float32)

    apply(second, first, lambda total, target, x, y: 2.0 * total - target[x, y], 2.0 * scale)

    portion = rounded_ref.shape[-1] // nz

    parts = slab_cells // portion
    leaving = []
    for part in range(parts):

        def round_slab(g):
            place, x0, y0 = corner(g)
            for within in range(portion):
                i, j = divmod(part * portion + within, cells_y)
                rounded_ref[part * group + place, :, pl.ds(within * nz, nz)] = first[
                    ring + x0 + i, ring + y0 + j
                ].astype(jnp.bfloat16)

        over_slabs(round_slab, 1)
        shares = pl.ds(part * group, group)
        leaving.append(
            pltpu.make_async_copy(rounded_ref.at[shares], rounded_out.at[shares], sent.at[part])
        )
        leaving[-1].start()
    for copy in leaving:
        copy.wait()


def scale_kernel(slabs_y, cells_x, cells_y, by_swaps, values_ref, field_ref):
    group, rows, nz = field_ref.shape
    each = values_ref.shape[2]
    ring = 1
    count_x, count_y = values_ref.shape[0] - 2 * ring, values_ref.shape[1] - 2 * ring
    me = lax.axis_index("sx") * slabs_y + lax.axis_index("sy") if by_swaps else 0

    def largest_of(x, largest):
        row = jnp.abs(values_ref[ring + x, pl.ds(ring, count_y)])
        return jnp.maximum(largest, jnp.max(row, axis=0))

    largest = lax.fori_loop(0, count_x, largest_of, jnp.zeros((each, nz), jnp.float32), unroll=2)
    level, gain = level_of(jnp.max(largest))
    level_rows = jnp.full((8, nz), level, jnp.float32)

    def give_slab(g, carry):
        place = jnp.bitwise_xor(me, g) if by_swaps else g
        x0 = (place // slabs_y) * cells_x
        y0 = (place % slabs_y) * cells_y
        field_ref[g, pl.ds(rows - 8, 8), :] = level_rows
        for i in range(cells_x):
            for j in range(cells_y):
                field_ref[g, pl.ds((i * cells_y + j) * each, each), :] = (
                    values_ref[ring + x0 + i, ring + y0 + j] * gain
                )
        return carry

    lax.fori_loop(0, group, give_slab, 0)


def entry(block, place):
    picked = jnp.where(place, block, 0.0)
    return jnp.sum(jnp.sum(picked, axis=0, keepdims=True), axis=1, keepdims=True)


def band_corner(shape, band):
    row = lax.broadcasted_iota(jnp.int32, shape, 0)
    column = lax.broadcasted_iota(jnp.int32, shape, 1)
    return (
        (row == 1) & (column == band * shape[0]),
        (row == 0) & (column == band * shape[0] + 1),
    )


def gram_kernel(matrix_ref, out_ref, sums_ref):
    bands, rows, columns = out_ref.shape
    matrix = matrix_ref[...]
    sums = lax.dot_general(
        matrix, matrix, (((1,), (1,)), ((), ())), preferred_element_type=jnp.float32
    )
    level, gain = level_of(jnp.max(jnp.abs(sums)))
    sums_ref[...] = sums * gain
    me = lax.axis_index("band")
    for k in range(bands):
        band = jnp.bitwise_xor(me, k)
        spare, _ = band_corner((rows, columns), band)
        block = sums_ref[pl.ds(pl.multiple_of(band * rows, rows), rows), :]
        out_ref[k] = jnp.where(spare, level, block)


def rows_kernel(cells, own_ref, *refs):
    out_ref = refs[-1]
    spare, twin = band_corner(out_ref.shape, lax.axis_index("band"))
    total = None
    for block in [own_ref[0]] + [ref[...] for ref in refs[:-1]]:
        block = block * shrink_of(entry(block, spare))
        total = block if total is None else total + block
    out_ref[...] = jnp.where(spare, entry(total, twin), total) / cells


def unpack_kernel(each, slabs_y, places, *refs):
    pieces = refs[:-3]
    filtered_hbm, filtered_ref, chunk_sems = refs[-3:]
    slab_cells, _, nz = filtered_ref.shape
    chunks = chunk_sems.shape[0]
    chunk = slab_cells // chunks
    me = lax.axis_index("sx") * slabs_y + lax.axis_index("sy") if len(pieces) > 1 else 0
    copies = []
    for c in range(chunks):
        for which, entry, other in places:
            piece = pieces[which]
            shrink = shrink_of(piece[entry, pl.ds(slab_cells * each, 1), :])
            if len(pieces) > 1:
                rows = pl.ds(pl.multiple_of(jnp.bitwise_xor(me, other) * each, each), each)
            else:
                rows = pl.ds(other * each, each)
            for cell in range(c * chunk, (c + 1) * chunk):
                filtered_ref[cell, rows, :] = piece[entry, pl.ds(cell * each, each), :] * shrink
        part = pl.ds(c * chunk, chunk)
        copies.append(
            pltpu.make_async_copy(filtered_ref.at[part], filtered_hbm.at[part], chunk_sems.at[c])
        )
        copies[-1].start()
    for copy in copies:
        copy.wait()


def swap(block, value):
    group = lax.axis_size(plane)
    return lax.ppermute(block, plane, [(i, i ^ value) for i in range(group)])


def local(orbitals, potential, projectors, energies, centers):
    band_orbitals, cells_x, cells_y, nz = orbitals.shape
    bands = lax.axis_size("band")
    slabs_x = lax.axis_size("sx")
    slabs_y = lax.axis_size("sy")
    group = slabs_x * slabs_y
    each = band_orbitals // group
    total_orbitals = bands * band_orbitals
    slab_cells = cells_x * cells_y
    grid = (slabs_x * cells_x, slabs_y * cells_y)
    atoms, projs, tiles, _ = projectors.shape

    near = slabs_y
    far = [v for v in range(1, group) if not v & near]
    by_swaps = group <= 8 and each % 8 == 0 and slabs_x > 1
    by_swaps = by_swaps and group & (group - 1) == 0 and bands & (bands - 1) == 0

    number_rows = 2 * atoms + 2
    rows = atoms * projs * tiles + slab_cells + number_rows
    rows += -rows % 8
    piece_rows = slab_cells * each
    chunks = (orbitals * orbital_gain).astype(jnp.float16)
    chunks = chunks.transpose(1, 2, 0, 3).reshape(slab_cells, group, each, nz)
    chunks = chunks.transpose(1, 0, 2, 3).reshape(group, piece_rows, nz)
    shared = pl.pallas_call(
        share_kernel,
        in_specs=[hbm, vmem, vmem, vmem, vmem],
        out_specs=vmem,
        out_shape=jax.ShapeDtypeStruct((rows, nz), jnp.float32),
        compiler_params=params,
    )(chunks[0, :8].astype(jnp.float32), energies, centers.T, projectors.transpose(0, 2, 1, 3), potential)
    narrow = shared.astype(jnp.float16)
    if by_swaps:
        me = lax.axis_index(plane)

        def chunk_for(value):
            return lax.dynamic_index_in_dim(chunks, me ^ value, 0, keepdims=False)

        came = [swap(jnp.concatenate([chunk_for(v), narrow, chunk_for(v ^ near)]), v) for v in far]
        mine = jnp.concatenate([narrow, chunk_for(near)])
        passed = {0: mine, **{v: block[piece_rows:] for v, block in zip(far, came)}}
        operands = [chunk_for(0)[None], narrow[None]] + [block[None] for block in came]
        slabs = {0: ((0, 0, 0), (1, 0, 0))}
        for i, v in enumerate(far):
            slabs[v] = ((2 + i, 0, 0), (2 + i, 0, piece_rows))
        for part in ([0], far[-1:], far[:-1]):
            if part:
                for i, v in enumerate(part):
                    slabs[v ^ near] = ((len(operands), i, rows), (len(operands), i, 0))
                operands.append(swap(jnp.stack([passed[v] for v in part]), near))
        operands = [block.astype(jnp.float32) for block in operands]
        operands[1] = shared[None]
    else:
        sent = jnp.concatenate([chunks, jnp.broadcast_to(narrow[None], (group, rows, nz))], axis=1)
        operands = [lax.all_to_all(sent, plane, 0, 0).astype(jnp.float32)]
        slabs = None

    portion = slab_cells // bands
    ringed = (grid[0] + 2, grid[1] + 2, each, nz)
    shares = bands * group
    rounded_shape = (shares, each, portion * nz)
    values, rounded = pl.pallas_call(
        functools.partial(filter_kernel, slabs_y, cells_x, cells_y, each, atoms, projs, slabs),
        in_specs=[vmem] * len(operands),
        out_specs=[vmem, hbm],
        out_shape=[
            jax.ShapeDtypeStruct(ringed, jnp.float32),
            jax.ShapeDtypeStruct(rounded_shape, jnp.bfloat16),
        ],
        scratch_shapes=[
            pltpu.VMEM(ringed, jnp.float32),
            pltpu.VMEM(grid + (each, nz), jnp.float32),
            pltpu.VMEM(grid + (1, nz), jnp.float32),
            pltpu.VMEM((group, atoms * projs, each, nz), jnp.float32),
            pltpu.SMEM((group, number_rows, nz), jnp.float32),
            pltpu.VMEM(rounded_shape, jnp.bfloat16),
            pltpu.SemaphoreType.DMA((group,)),
            pltpu.SemaphoreType.DMA((bands,)),
        ],
        compiler_params=params,
        cost_estimate=pl.CostEstimate(
            flops=2 * 2 * 40 * grid[0] * grid[1] * each * nz,
            bytes_accessed=8 * grid[0] * grid[1] * each * nz,
            transcendentals=0,
        ),
    )(*operands)

    matrix = lax.all_to_all(rounded, every, 0, 0)
    matrix = matrix.reshape(total_orbitals, portion * nz)
    field = pl.pallas_call(
        functools.partial(scale_kernel, slabs_y, cells_x, cells_y, by_swaps),
        in_specs=[vmem],
        out_specs=vmem,
        out_shape=jax.ShapeDtypeStruct((group, piece_rows + 8, nz), jnp.float32),
        compiler_params=params,
    )(values)
    narrow = field.astype(jnp.float16)
    if by_swaps:
        came = [swap(jnp.stack([narrow[v], narrow[v | near]]), v) for v in far]
        others, matrix = lax.optimization_barrier((came[1:], matrix))
    else:
        pieces = [lax.all_to_all(narrow, plane, 0, 0).astype(jnp.float32)]
        places = [(0, g, g) for g in range(group)]

    def unpack(pieces, places):
        return pl.pallas_call(
            functools.partial(unpack_kernel, each, slabs_y, places),
            in_specs=[vmem] * len(pieces),
            out_specs=hbm,
            out_shape=jax.ShapeDtypeStruct((slab_cells, band_orbitals, nz), jnp.float32),
            scratch_shapes=[
                pltpu.VMEM((slab_cells, band_orbitals, nz), jnp.float32),
                pltpu.SemaphoreType.DMA((cells_x,)),
            ],
            compiler_params=params,
        )(*pieces)

    cells = grid[0] * grid[1] * nz
    if by_swaps:
        sums = pl.pallas_call(
            gram_kernel,
            in_specs=[vmem],
            out_specs=vmem,
            out_shape=jax.ShapeDtypeStruct((bands, band_orbitals, total_orbitals), jnp.float32),
            scratch_shapes=[pltpu.VMEM((total_orbitals, total_orbitals), jnp.float32)],
            compiler_params=params,
        )(matrix)
        parts = [
            lax.ppermute(
                sums[k].astype(jnp.float16), "band", [(i, i ^ k) for i in range(bands)]
            ).astype(jnp.float32)
            for k in range(1, bands)
        ]
        gram = pl.pallas_call(
            functools.partial(rows_kernel, cells),
            in_specs=[vmem] * bands,
            out_specs=vmem,
            out_shape=jax.ShapeDtypeStruct((band_orbitals, total_orbitals), jnp.float32),
            compiler_params=params,
        )(sums, *parts)
        beside, gram = lax.optimization_barrier((came[0], gram))
        came = [beside] + others
        came.append(swap(jnp.stack([narrow[near]] + [block[1] for block in came]), near))
        pieces = [field] + [block.astype(jnp.float32) for block in came]
        places = [(0, 0, 0), (len(pieces) - 1, 0, near)]
        for i, v in enumerate(far):
            places += [(i + 1, 0, v), (len(pieces) - 1, i + 1, v | near)]
        terms = {v: swap(gram, v) for v in far}
        terms[0] = gram
        bit = 1
        while len(terms) > 1:
            if any(v ^ bit in terms for v in terms):
                terms = {v: terms[v] + terms[v ^ bit] for v in terms if not v & bit}
            bit *= 2
        gram = terms[0]
        other, filtered = lax.optimization_barrier((swap(gram, near), unpack(pieces, places)))
        gram = gram + other
    else:
        sums = lax.dot_general(
            matrix, matrix, (((1,), (1,)), ((), ())), preferred_element_type=jnp.float32
        )
        parts = lax.all_to_all(sums.reshape(shares, each, total_orbitals), every, 0, 0)
        rows = jnp.sum(parts, axis=0) / cells
        gram = lax.all_to_all(jnp.broadcast_to(rows[None], (group,) + rows.shape), plane, 0, 0)
        gram = gram.reshape(band_orbitals, total_orbitals)
        filtered = unpack(pieces, places)

    filtered = filtered.reshape(cells_x, cells_y, band_orbitals, nz).transpose(2, 0, 1, 3)
    return (filtered, gram)


def solution(mesh):
    in_specs = (
        P("band", "sx", "sy", None),
        P("sx", "sy", None),
        P(("sx", "sy"), None, None, None),
        P(("sx", "sy"), None),
        P(("sx", "sy"), None),
    )
    out_specs = (P("band", "sx", "sy", None), P("band", None))
    return jax.shard_map(local, mesh=mesh, in_specs=in_specs, out_specs=out_specs, check_vma=False)
```

```python
import functools

import jax
import jax.numpy as jnp
from jax import lax
from jax.experimental import pallas as pl
from jax.experimental.pallas import tpu as pltpu
from jax.sharding import PartitionSpec as P

stencil_weights = (
    -5369.0 / 1800.0,
    12.0 / 7.0,
    -15.0 / 56.0,
    10.0 / 189.0,
    -1.0 / 112.0,
    2.0 / 1925.0,
    -1.0 / 16632.0,
)
filter_center = 6.5
filter_half = 6.0
offsets_x = (0, -1, 1, 0, 0)
offsets_y = (0, 0, 0, -1, 1)
reach = 6
plane = ("sx", "sy")
every = ("band", "sx", "sy")

orbital_gain = 2.0**12
projector_gain = 2.0**17
potential_gain = 2.0**13
remainder_gain = 2.0**10
top = 15
middle = 8
levels = 17

vmem = pl.BlockSpec(memory_space=pltpu.VMEM)
hbm = pl.BlockSpec(memory_space=pl.ANY)
params = pltpu.CompilerParams(vmem_limit_bytes=24 * 1024 * 1024)


def level_of(largest):
    level = jnp.float32(0.0)
    scale = jnp.float32(2.0 ** (top + 8 * middle))
    for j in range(levels):
        above = largest >= jnp.float32(2.0 ** (8 * (j - middle)))
        level = jnp.where(above, jnp.float32(j + 1), level)
        scale = jnp.where(above, jnp.float32(2.0 ** (top - 8 * (j + 1 - middle))), scale)
    return level, scale


def shrink_of(level):
    shrink = jnp.full(level.shape, 2.0 ** (-top - 8 * middle), jnp.float32)
    for j in range(levels):
        shrink = jnp.where(level > j, jnp.float32(2.0 ** (8 * (j + 1 - middle) - top)), shrink)
    return shrink


def share_kernel(_, energies_ref, centers_ref, projectors_ref, potential_ref, out_ref):
    rows, nz = out_ref.shape
    atoms, tiles, projs = projectors_ref.shape[:3]

    row = 0
    for a in range(atoms):
        for t in range(tiles):
            out_ref[pl.ds(row, projs), :] = projectors_ref[a, t] * projector_gain
            row += projs
    for i in range(potential_ref.shape[0]):
        count = potential_ref.shape[1]
        out_ref[pl.ds(row, count), :] = potential_ref[i] * potential_gain
        row += count
    out_ref[pl.ds(row, rows - row), :] = jnp.zeros((rows - row, nz), jnp.float32)
    energies = energies_ref[...]
    high = energies.astype(jnp.bfloat16).astype(jnp.float32)
    out_ref[pl.ds(row, atoms), :projs] = high
    out_ref[pl.ds(row + atoms, atoms), :projs] = (energies - high) * remainder_gain
    out_ref[pl.ds(row + 2 * atoms, 2), :atoms] = centers_ref[...].astype(jnp.float32)


def filter_kernel(slabs_y, cells_x, cells_y, each, atoms, projs, slabs, *refs):
    inputs, (first, rounded_out) = refs[:-10], refs[-10:-8]
    second, partial, diagonal, coeffs, numbers, rounded_ref, arrived, sent = refs[-8:]
    group, number_rows, _ = numbers.shape
    nz = first.shape[-1]
    count_x, count_y = diagonal.shape[0], diagonal.shape[1]
    tiles = len(offsets_x)
    slab_cells = cells_x * cells_y
    pot_row = atoms * projs * tiles
    number_row = pot_row + slab_cells
    scale = 1.0 / filter_half
    factors = [-0.5 * scale * w for w in stencil_weights]
    ring = 1
    me = 0 if slabs is None else lax.axis_index("sx") * slabs_y + lax.axis_index("sy")

    def rows_of(g, shared, row, count):
        if slabs is None:
            return inputs[0].at[g, pl.ds(row + (slab_cells * each if shared else 0), count), :]
        which, at, start = slabs[g][1 if shared else 0]
        return inputs[which].at[at, pl.ds(start + row, count), :]

    def shared_row(g, row):
        return rows_of(g, True, row, 1)[...]

    def over_slabs(body, unroll):
        if slabs is None:
            lax.fori_loop(0, group, lambda g, carry: body(g) or carry, 0, unroll=min(group, unroll))
        else:
            for g in range(group):
                body(g)

    def corner(g):
        place = g if slabs is None else jnp.bitwise_xor(me, g)
        return place, (place // slabs_y) * cells_x, (place % slabs_y) * cells_y

    if slabs is None:
        copies = [
            pltpu.make_async_copy(
                inputs[0].at[:, pl.ds(slab_cells * each + number_row, number_rows), :],
                numbers,
                arrived.at[0],
            )
        ]
    else:
        copies = [
            pltpu.make_async_copy(
                rows_of(g, True, number_row, number_rows), numbers.at[g], arrived.at[g]
            )
            for g in range(group)
        ]
    for copy in copies:
        copy.start()

    for field in (first, second):
        for x in (0, ring + count_x):
            field[x] = jnp.zeros(field.shape[1:], jnp.float32)
        for y in (0, ring + count_y):
            field[:, y] = jnp.zeros((field.shape[0],) + field.shape[2:], jnp.float32)

    def take_slab(g):
        _, x0, y0 = corner(g)
        for i in range(cells_x):
            for j in range(cells_y):
                cell = i * cells_y + j
                first[ring + x0 + i, ring + y0 + j] = rows_of(g, False, cell * each, each)[...] * (
                    1.0 / orbital_gain
                )
                diagonal[x0 + i, y0 + j] = shared_row(g, pot_row + cell) * (
                    scale / potential_gain
                ) + (3.0 * factors[0] - filter_center * scale)

    over_slabs(take_slab, 1)

    distance = jnp.abs(
        lax.broadcasted_iota(jnp.int32, (nz, nz), 0) - lax.broadcasted_iota(jnp.int32, (nz, nz), 1)
    )
    along_z = jnp.zeros((nz, nz), jnp.float32)
    for step in range(1, reach + 1):
        along_z = jnp.where(distance == step, factors[step], along_z)
    z_high = along_z.astype(jnp.bfloat16)
    z_low = (along_z - z_high.astype(jnp.float32)).astype(jnp.bfloat16)
    z_matrix = jnp.concatenate(
        [
            jnp.concatenate([z_high, z_low], axis=1),
            jnp.concatenate([z_high, jnp.zeros_like(z_high)], axis=1),
        ],
        axis=0,
    )

    def along(cells, at):
        total = None
        for step in range(1, reach + 1):
            near = [cells[n] for n in (at - step, at + step) if 0 <= n < len(cells)]
            if near:
                term = factors[step] * sum(near[1:], near[0])
                total = term if total is None else total + term
        return total

    def apply(source, target, finish, gain):
        def xz_part(y, carry):
            column = source[pl.ds(ring, count_x), ring + y]
            flat = column.reshape(count_x * each, nz)
            high = flat.astype(jnp.bfloat16)
            low = (flat - high.astype(jnp.float32)).astype(jnp.bfloat16)
            both = jnp.dot(
                jnp.concatenate([high, low], axis=1), z_matrix, preferred_element_type=jnp.float32
            )
            along_z = (both[:, :nz] + both[:, nz:]).reshape(column.shape)
            cells = [column[x] for x in range(count_x)]
            for x in range(count_x):
                partial[x, y] = along_z[x] + diagonal[x, y] * cells[x] + along(cells, x)
            return carry

        lax.fori_loop(0, count_y, xz_part, 0, unroll=6)

        def y_part(x, carry):
            cells = [source[ring + x, ring + y] for y in range(count_y)]
            for y in range(count_y):
                total = partial[x, y] + along(cells, y)
                target[ring + x, ring + y] = finish(total, target, ring + x, ring + y)
            return carry

        lax.fori_loop(0, count_x, y_part, 0, unroll=4)

        def place_of(g, a):
            return (
                ring + numbers[g, 2 * atoms, a].astype(jnp.int32),
                ring + numbers[g, 2 * atoms + 1, a].astype(jnp.int32),
            )

        def gather_part(g):
            for a in range(atoms):
                at_x, at_y = place_of(g, a)
                totals = [None] * projs
                for t in range(tiles):
                    tile = source[at_x + offsets_x[t], at_y + offsets_y[t]]
                    for p in range(projs):
                        term = tile * shared_row(g, (a * tiles + t) * projs + p)
                        totals[p] = term if t == 0 else totals[p] + term
                for p in range(projs):
                    energy = numbers[g, a, p] + numbers[g, atoms + a, p] * (1.0 / remainder_gain)
                    coeffs[g, a * projs + p] = jnp.broadcast_to(
                        jnp.sum(totals[p], axis=-1, keepdims=True)
                        * (energy * (gain / projector_gain / projector_gain)),
                        (each, nz),
                    )

        over_slabs(gather_part, 4)

        def scatter_part(g):
            for a in range(atoms):
                at_x, at_y = place_of(g, a)
                factor = [coeffs[g, a * projs + p] for p in range(projs)]
                for t in range(tiles):
                    row = (a * tiles + t) * projs
                    spread = factor[0] * shared_row(g, row)
                    for p in range(1, projs):
                        spread = spread + factor[p] * shared_row(g, row + p)
                    to_x = at_x + offsets_x[t]
                    to_y = at_y + offsets_y[t]
                    target[to_x, to_y] = target[to_x, to_y] + spread

        over_slabs(scatter_part, 2)

    for copy in copies:
        copy.wait()
    apply(first, second, lambda total, target, x, y: total, scale)

    for x in (0, ring + count_x):
        second[x] = jnp.zeros(second.shape[1:], jnp.float32)
    for y in (0, ring + count_y):
        second[:, y] = jnp.zeros((second.shape[0],) + second.shape[2:], jnp.float32)

    apply(second, first, lambda total, target, x, y: 2.0 * total - target[x, y], 2.0 * scale)

    portion = rounded_ref.shape[-1] // nz

    parts = slab_cells // portion
    leaving = []
    for part in range(parts):

        def round_slab(g):
            place, x0, y0 = corner(g)
            for within in range(portion):
                i, j = divmod(part * portion + within, cells_y)
                rounded_ref[part * group + place, :, pl.ds(within * nz, nz)] = first[
                    ring + x0 + i, ring + y0 + j
                ].astype(jnp.bfloat16)

        over_slabs(round_slab, 1)
        shares = pl.ds(part * group, group)
        leaving.append(
            pltpu.make_async_copy(rounded_ref.at[shares], rounded_out.at[shares], sent.at[part])
        )
        leaving[-1].start()
    for copy in leaving:
        copy.wait()


def scale_kernel(slabs_y, cells_x, cells_y, by_swaps, values_ref, field_ref):
    group, rows, nz = field_ref.shape
    each = values_ref.shape[2]
    ring = 1
    count_x, count_y = values_ref.shape[0] - 2 * ring, values_ref.shape[1] - 2 * ring
    me = lax.axis_index("sx") * slabs_y + lax.axis_index("sy") if by_swaps else 0

    def largest_of(x, largest):
        row = jnp.abs(values_ref[ring + x, pl.ds(ring, count_y)])
        return jnp.maximum(largest, jnp.max(row, axis=0))

    largest = lax.fori_loop(0, count_x, largest_of, jnp.zeros((each, nz), jnp.float32), unroll=2)
    level, gain = level_of(jnp.max(largest))
    level_rows = jnp.full((8, nz), level, jnp.float32)

    def give_slab(g, carry):
        place = jnp.bitwise_xor(me, g) if by_swaps else g
        x0 = (place // slabs_y) * cells_x
        y0 = (place % slabs_y) * cells_y
        field_ref[g, pl.ds(rows - 8, 8), :] = level_rows
        for i in range(cells_x):
            for j in range(cells_y):
                field_ref[g, pl.ds((i * cells_y + j) * each, each), :] = (
                    values_ref[ring + x0 + i, ring + y0 + j] * gain
                )
        return carry

    lax.fori_loop(0, group, give_slab, 0)


def entry(block, place):
    picked = jnp.where(place, block, 0.0)
    return jnp.sum(jnp.sum(picked, axis=0, keepdims=True), axis=1, keepdims=True)


def band_corner(shape, band):
    row = lax.broadcasted_iota(jnp.int32, shape, 0)
    column = lax.broadcasted_iota(jnp.int32, shape, 1)
    return (
        (row == 1) & (column == band * shape[0]),
        (row == 0) & (column == band * shape[0] + 1),
    )


def gram_kernel(matrix_ref, out_ref, sums_ref):
    bands, rows, columns = out_ref.shape
    matrix = matrix_ref[...]
    sums = lax.dot_general(
        matrix, matrix, (((1,), (1,)), ((), ())), preferred_element_type=jnp.float32
    )
    level, gain = level_of(jnp.max(jnp.abs(sums)))
    sums_ref[...] = sums * gain
    me = lax.axis_index("band")
    for k in range(bands):
        band = jnp.bitwise_xor(me, k)
        spare, _ = band_corner((rows, columns), band)
        block = sums_ref[pl.ds(pl.multiple_of(band * rows, rows), rows), :]
        out_ref[k] = jnp.where(spare, level, block)


def rows_kernel(cells, own_ref, *refs):
    out_ref = refs[-1]
    spare, twin = band_corner(out_ref.shape, lax.axis_index("band"))
    total = None
    for block in [own_ref[0]] + [ref[...] for ref in refs[:-1]]:
        block = block * shrink_of(entry(block, spare))
        total = block if total is None else total + block
    out_ref[...] = jnp.where(spare, entry(total, twin), total) / cells


def unpack_kernel(each, slabs_y, places, *refs):
    pieces = refs[:-3]
    filtered_hbm, filtered_ref, chunk_sems = refs[-3:]
    slab_cells, _, nz = filtered_ref.shape
    chunks = chunk_sems.shape[0]
    chunk = slab_cells // chunks
    me = lax.axis_index("sx") * slabs_y + lax.axis_index("sy") if len(pieces) > 1 else 0
    copies = []
    for c in range(chunks):
        for which, entry, other in places:
            piece = pieces[which]
            shrink = shrink_of(piece[entry, pl.ds(slab_cells * each, 1), :])
            if len(pieces) > 1:
                rows = pl.ds(pl.multiple_of(jnp.bitwise_xor(me, other) * each, each), each)
            else:
                rows = pl.ds(other * each, each)
            for cell in range(c * chunk, (c + 1) * chunk):
                filtered_ref[cell, rows, :] = piece[entry, pl.ds(cell * each, each), :] * shrink
        part = pl.ds(c * chunk, chunk)
        copies.append(
            pltpu.make_async_copy(filtered_ref.at[part], filtered_hbm.at[part], chunk_sems.at[c])
        )
        copies[-1].start()
    for copy in copies:
        copy.wait()


def swap(block, value):
    group = lax.axis_size(plane)
    return lax.ppermute(block, plane, [(i, i ^ value) for i in range(group)])


def local(orbitals, potential, projectors, energies, centers):
    band_orbitals, cells_x, cells_y, nz = orbitals.shape
    bands = lax.axis_size("band")
    slabs_x = lax.axis_size("sx")
    slabs_y = lax.axis_size("sy")
    group = slabs_x * slabs_y
    each = band_orbitals // group
    total_orbitals = bands * band_orbitals
    slab_cells = cells_x * cells_y
    grid = (slabs_x * cells_x, slabs_y * cells_y)
    atoms, projs, tiles, _ = projectors.shape

    near = slabs_y
    far = [v for v in range(1, group) if not v & near]
    by_swaps = group <= 8 and each % 8 == 0 and slabs_x > 1
    by_swaps = by_swaps and group & (group - 1) == 0 and bands & (bands - 1) == 0

    number_rows = 2 * atoms + 2
    rows = atoms * projs * tiles + slab_cells + number_rows
    rows += -rows % 8
    piece_rows = slab_cells * each
    chunks = (orbitals * orbital_gain).astype(jnp.float16)
    chunks = chunks.transpose(1, 2, 0, 3).reshape(slab_cells, group, each, nz)
    chunks = chunks.transpose(1, 0, 2, 3).reshape(group, piece_rows, nz)
    shared = pl.pallas_call(
        share_kernel,
        in_specs=[hbm, vmem, vmem, vmem, vmem],
        out_specs=vmem,
        out_shape=jax.ShapeDtypeStruct((rows, nz), jnp.float32),
        compiler_params=params,
    )(chunks[0, :8].astype(jnp.float32), energies, centers.T, projectors.transpose(0, 2, 1, 3), potential)
    narrow = shared.astype(jnp.float16)
    if by_swaps:
        me = lax.axis_index(plane)

        def chunk_for(value):
            return lax.dynamic_index_in_dim(chunks, me ^ value, 0, keepdims=False)

        came = [swap(jnp.concatenate([chunk_for(v), narrow, chunk_for(v ^ near)]), v) for v in far]
        mine = jnp.concatenate([narrow, chunk_for(near)])
        passed = {0: mine, **{v: block[piece_rows:] for v, block in zip(far, came)}}
        operands = [chunk_for(0)[None], narrow[None]] + [block[None] for block in came]
        slabs = {0: ((0, 0, 0), (1, 0, 0))}
        for i, v in enumerate(far):
            slabs[v] = ((2 + i, 0, 0), (2 + i, 0, piece_rows))
        for part in ([0], far[-1:], far[:-1]):
            if part:
                for i, v in enumerate(part):
                    slabs[v ^ near] = ((len(operands), i, rows), (len(operands), i, 0))
                operands.append(swap(jnp.stack([passed[v] for v in part]), near))
        operands = [block.astype(jnp.float32) for block in operands]
        operands[1] = shared[None]
    else:
        sent = jnp.concatenate([chunks, jnp.broadcast_to(narrow[None], (group, rows, nz))], axis=1)
        operands = [lax.all_to_all(sent, plane, 0, 0).astype(jnp.float32)]
        slabs = None

    portion = slab_cells // bands
    ringed = (grid[0] + 2, grid[1] + 2, each, nz)
    shares = bands * group
    rounded_shape = (shares, each, portion * nz)
    values, rounded = pl.pallas_call(
        functools.partial(filter_kernel, slabs_y, cells_x, cells_y, each, atoms, projs, slabs),
        in_specs=[vmem] * len(operands),
        out_specs=[vmem, hbm],
        out_shape=[
            jax.ShapeDtypeStruct(ringed, jnp.float32),
            jax.ShapeDtypeStruct(rounded_shape, jnp.bfloat16),
        ],
        scratch_shapes=[
            pltpu.VMEM(ringed, jnp.float32),
            pltpu.VMEM(grid + (each, nz), jnp.float32),
            pltpu.VMEM(grid + (1, nz), jnp.float32),
            pltpu.VMEM((group, atoms * projs, each, nz), jnp.float32),
            pltpu.SMEM((group, number_rows, nz), jnp.float32),
            pltpu.VMEM(rounded_shape, jnp.bfloat16),
            pltpu.SemaphoreType.DMA((group,)),
            pltpu.SemaphoreType.DMA((bands,)),
        ],
        compiler_params=params,
        cost_estimate=pl.CostEstimate(
            flops=2 * 2 * 40 * grid[0] * grid[1] * each * nz,
            bytes_accessed=8 * grid[0] * grid[1] * each * nz,
            transcendentals=0,
        ),
    )(*operands)

    matrix = lax.all_to_all(rounded, every, 0, 0)
    matrix = matrix.reshape(total_orbitals, portion * nz)
    field = pl.pallas_call(
        functools.partial(scale_kernel, slabs_y, cells_x, cells_y, by_swaps),
        in_specs=[vmem],
        out_specs=vmem,
        out_shape=jax.ShapeDtypeStruct((group, piece_rows + 8, nz), jnp.float32),
        compiler_params=params,
    )(values)
    narrow = field.astype(jnp.float16)
    if by_swaps:
        came = {v: swap(jnp.stack([narrow[v], narrow[v | near]]), v) for v in far}
        along_x = [v for v in far if v % slabs_y == 0]
        along_y = [v for v in far if v % slabs_y > 0]
        tied, matrix = lax.optimization_barrier(([came[v] for v in along_x], matrix))
    else:
        pieces = [lax.all_to_all(narrow, plane, 0, 0).astype(jnp.float32)]
        places = [(0, g, g) for g in range(group)]

    def unpack(pieces, places):
        return pl.pallas_call(
            functools.partial(unpack_kernel, each, slabs_y, places),
            in_specs=[vmem] * len(pieces),
            out_specs=hbm,
            out_shape=jax.ShapeDtypeStruct((slab_cells, band_orbitals, nz), jnp.float32),
            scratch_shapes=[
                pltpu.VMEM((slab_cells, band_orbitals, nz), jnp.float32),
                pltpu.SemaphoreType.DMA((cells_x,)),
            ],
            compiler_params=params,
        )(*pieces)

    cells = grid[0] * grid[1] * nz
    if by_swaps:
        sums = pl.pallas_call(
            gram_kernel,
            in_specs=[vmem],
            out_specs=vmem,
            out_shape=jax.ShapeDtypeStruct((bands, band_orbitals, total_orbitals), jnp.float32),
            scratch_shapes=[pltpu.VMEM((total_orbitals, total_orbitals), jnp.float32)],
            compiler_params=params,
        )(matrix)
        parts = [
            lax.ppermute(
                sums[k].astype(jnp.float16), "band", [(i, i ^ k) for i in range(bands)]
            ).astype(jnp.float32)
            for k in range(1, bands)
        ]
        gram = pl.pallas_call(
            functools.partial(rows_kernel, cells),
            in_specs=[vmem] * bands,
            out_specs=vmem,
            out_shape=jax.ShapeDtypeStruct((band_orbitals, total_orbitals), jnp.float32),
            compiler_params=params,
        )(sums, *parts)
        free, gram = lax.optimization_barrier(([came[v] for v in along_y], gram))
        came = dict(zip(along_x + along_y, tied + free))
        came = [came[v] for v in far]
        came.append(swap(jnp.stack([narrow[near]] + [block[1] for block in came]), near))
        pieces = [field] + [block.astype(jnp.float32) for block in came]
        places = [(0, 0, 0), (len(pieces) - 1, 0, near)]
        for i, v in enumerate(far):
            places += [(i + 1, 0, v), (len(pieces) - 1, i + 1, v | near)]
        terms = {v: swap(gram, v) for v in far}
        terms[0] = gram
        bit = 1
        while len(terms) > 1:
            if any(v ^ bit in terms for v in terms):
                terms = {v: terms[v] + terms[v ^ bit] for v in terms if not v & bit}
            bit *= 2
        gram = terms[0]
        other, filtered = lax.optimization_barrier((swap(gram, near), unpack(pieces, places)))
        gram = gram + other
    else:
        sums = lax.dot_general(
            matrix, matrix, (((1,), (1,)), ((), ())), preferred_element_type=jnp.float32
        )
        parts = lax.all_to_all(sums.reshape(shares, each, total_orbitals), every, 0, 0)
        rows = jnp.sum(parts, axis=0) / cells
        gram = lax.all_to_all(jnp.broadcast_to(rows[None], (group,) + rows.shape), plane, 0, 0)
        gram = gram.reshape(band_orbitals, total_orbitals)
        filtered = unpack(pieces, places)

    filtered = filtered.reshape(cells_x, cells_y, band_orbitals, nz).transpose(2, 0, 1, 3)
    return (filtered, gram)


def solution(mesh):
    in_specs = (
        P("band", "sx", "sy", None),
        P("sx", "sy", None),
        P(("sx", "sy"), None, None, None),
        P(("sx", "sy"), None),
        P(("sx", "sy"), None),
    )
    out_specs = (P("band", "sx", "sy", None), P("band", None))
    return jax.shard_map(local, mesh=mesh, in_specs=in_specs, out_specs=out_specs, check_vma=False)
```

```python
import functools

import jax
import jax.numpy as jnp
from jax import lax
from jax.experimental import pallas as pl
from jax.experimental.pallas import tpu as pltpu
from jax.sharding import PartitionSpec as P

stencil_weights = (
    -5369.0 / 1800.0,
    12.0 / 7.0,
    -15.0 / 56.0,
    10.0 / 189.0,
    -1.0 / 112.0,
    2.0 / 1925.0,
    -1.0 / 16632.0,
)
filter_center = 6.5
filter_half = 6.0
offsets_x = (0, -1, 1, 0, 0)
offsets_y = (0, 0, 0, -1, 1)
reach = 6
plane = ("sx", "sy")
every = ("band", "sx", "sy")

orbital_gain = 2.0**12
projector_gain = 2.0**17
potential_gain = 2.0**13
remainder_gain = 2.0**10
top = 15
middle = 8
levels = 17

vmem = pl.BlockSpec(memory_space=pltpu.VMEM)
hbm = pl.BlockSpec(memory_space=pl.ANY)
params = pltpu.CompilerParams(vmem_limit_bytes=24 * 1024 * 1024)


def level_of(largest):
    level = jnp.float32(0.0)
    scale = jnp.float32(2.0 ** (top + 8 * middle))
    for j in range(levels):
        above = largest >= jnp.float32(2.0 ** (8 * (j - middle)))
        level = jnp.where(above, jnp.float32(j + 1), level)
        scale = jnp.where(above, jnp.float32(2.0 ** (top - 8 * (j + 1 - middle))), scale)
    return level, scale


def shrink_of(level):
    shrink = jnp.full(level.shape, 2.0 ** (-top - 8 * middle), jnp.float32)
    for j in range(levels):
        shrink = jnp.where(level > j, jnp.float32(2.0 ** (8 * (j + 1 - middle) - top)), shrink)
    return shrink


def share_kernel(_, energies_ref, centers_ref, projectors_ref, potential_ref, out_ref):
    rows, nz = out_ref.shape
    atoms, tiles, projs = projectors_ref.shape[:3]

    row = 0
    for a in range(atoms):
        for t in range(tiles):
            out_ref[pl.ds(row, projs), :] = projectors_ref[a, t] * projector_gain
            row += projs
    for i in range(potential_ref.shape[0]):
        count = potential_ref.shape[1]
        out_ref[pl.ds(row, count), :] = potential_ref[i] * potential_gain
        row += count
    out_ref[pl.ds(row, rows - row), :] = jnp.zeros((rows - row, nz), jnp.float32)
    energies = energies_ref[...]
    high = energies.astype(jnp.bfloat16).astype(jnp.float32)
    out_ref[pl.ds(row, atoms), :projs] = high
    out_ref[pl.ds(row + atoms, atoms), :projs] = (energies - high) * remainder_gain
    out_ref[pl.ds(row + 2 * atoms, 2), :atoms] = centers_ref[...].astype(jnp.float32)


def filter_kernel(slabs_y, cells_x, cells_y, each, atoms, projs, slabs, *refs):
    inputs, (first, rounded_out) = refs[:-10], refs[-10:-8]
    second, partial, diagonal, coeffs, numbers, rounded_ref, arrived, sent = refs[-8:]
    group, number_rows, _ = numbers.shape
    nz = first.shape[-1]
    count_x, count_y = diagonal.shape[0], diagonal.shape[1]
    tiles = len(offsets_x)
    slab_cells = cells_x * cells_y
    pot_row = atoms * projs * tiles
    number_row = pot_row + slab_cells
    scale = 1.0 / filter_half
    factors = [-0.5 * scale * w for w in stencil_weights]
    ring = 1
    me = 0 if slabs is None else lax.axis_index("sx") * slabs_y + lax.axis_index("sy")

    def rows_of(g, shared, row, count):
        if slabs is None:
            return inputs[0].at[g, pl.ds(row + (slab_cells * each if shared else 0), count), :]
        which, at, start = slabs[g][1 if shared else 0]
        return inputs[which].at[at, pl.ds(start + row, count), :]

    def shared_row(g, row):
        return rows_of(g, True, row, 1)[...]

    def over_slabs(body, unroll):
        if slabs is None:
            lax.fori_loop(0, group, lambda g, carry: body(g) or carry, 0, unroll=min(group, unroll))
        else:
            for g in range(group):
                body(g)

    def corner(g):
        place = g if slabs is None else jnp.bitwise_xor(me, g)
        return place, (place // slabs_y) * cells_x, (place % slabs_y) * cells_y

    if slabs is None:
        copies = [
            pltpu.make_async_copy(
                inputs[0].at[:, pl.ds(slab_cells * each + number_row, number_rows), :],
                numbers,
                arrived.at[0],
            )
        ]
    else:
        copies = [
            pltpu.make_async_copy(
                rows_of(g, True, number_row, number_rows), numbers.at[g], arrived.at[g]
            )
            for g in range(group)
        ]
    for copy in copies:
        copy.start()

    for field in (first, second):
        for x in (0, ring + count_x):
            field[x] = jnp.zeros(field.shape[1:], jnp.float32)
        for y in (0, ring + count_y):
            field[:, y] = jnp.zeros((field.shape[0],) + field.shape[2:], jnp.float32)

    def take_slab(g):
        _, x0, y0 = corner(g)
        for i in range(cells_x):
            for j in range(cells_y):
                cell = i * cells_y + j
                first[ring + x0 + i, ring + y0 + j] = rows_of(g, False, cell * each, each)[...] * (
                    1.0 / orbital_gain
                )
                diagonal[x0 + i, y0 + j] = shared_row(g, pot_row + cell) * (
                    scale / potential_gain
                ) + (3.0 * factors[0] - filter_center * scale)

    over_slabs(take_slab, 1)

    distance = jnp.abs(
        lax.broadcasted_iota(jnp.int32, (nz, nz), 0) - lax.broadcasted_iota(jnp.int32, (nz, nz), 1)
    )
    along_z = jnp.zeros((nz, nz), jnp.float32)
    for step in range(1, reach + 1):
        along_z = jnp.where(distance == step, factors[step], along_z)
    z_high = along_z.astype(jnp.bfloat16)
    z_low = (along_z - z_high.astype(jnp.float32)).astype(jnp.bfloat16)
    z_matrix = jnp.concatenate(
        [
            jnp.concatenate([z_high, z_low], axis=1),
            jnp.concatenate([z_high, jnp.zeros_like(z_high)], axis=1),
        ],
        axis=0,
    )

    def along(cells, at):
        total = None
        for step in range(1, reach + 1):
            near = [cells[n] for n in (at - step, at + step) if 0 <= n < len(cells)]
            if near:
                term = factors[step] * sum(near[1:], near[0])
                total = term if total is None else total + term
        return total

    def apply(source, target, finish, gain):
        def xz_part(y, carry):
            column = source[pl.ds(ring, count_x), ring + y]
            flat = column.reshape(count_x * each, nz)
            high = flat.astype(jnp.bfloat16)
            low = (flat - high.astype(jnp.float32)).astype(jnp.bfloat16)
            both = jnp.dot(
                jnp.concatenate([high, low], axis=1), z_matrix, preferred_element_type=jnp.float32
            )
            along_z = (both[:, :nz] + both[:, nz:]).reshape(column.shape)
            cells = [column[x] for x in range(count_x)]
            for x in range(count_x):
                partial[x, y] = along_z[x] + diagonal[x, y] * cells[x] + along(cells, x)
            return carry

        lax.fori_loop(0, count_y, xz_part, 0, unroll=6)

        def y_part(x, carry):
            cells = [source[ring + x, ring + y] for y in range(count_y)]
            for y in range(count_y):
                total = partial[x, y] + along(cells, y)
                target[ring + x, ring + y] = finish(total, target, ring + x, ring + y)
            return carry

        lax.fori_loop(0, count_x, y_part, 0, unroll=4)

        def place_of(g, a):
            return (
                ring + numbers[g, 2 * atoms, a].astype(jnp.int32),
                ring + numbers[g, 2 * atoms + 1, a].astype(jnp.int32),
            )

        def gather_part(g):
            for a in range(atoms):
                at_x, at_y = place_of(g, a)
                totals = [None] * projs
                for t in range(tiles):
                    tile = source[at_x + offsets_x[t], at_y + offsets_y[t]]
                    for p in range(projs):
                        term = tile * shared_row(g, (a * tiles + t) * projs + p)
                        totals[p] = term if t == 0 else totals[p] + term
                for p in range(projs):
                    energy = numbers[g, a, p] + numbers[g, atoms + a, p] * (1.0 / remainder_gain)
                    coeffs[g, a * projs + p] = jnp.broadcast_to(
                        jnp.sum(totals[p], axis=-1, keepdims=True)
                        * (energy * (gain / projector_gain / projector_gain)),
                        (each, nz),
                    )

        over_slabs(gather_part, 4)

        def scatter_part(g):
            for a in range(atoms):
                at_x, at_y = place_of(g, a)
                factor = [coeffs[g, a * projs + p] for p in range(projs)]
                for t in range(tiles):
                    row = (a * tiles + t) * projs
                    spread = factor[0] * shared_row(g, row)
                    for p in range(1, projs):
                        spread = spread + factor[p] * shared_row(g, row + p)
                    to_x = at_x + offsets_x[t]
                    to_y = at_y + offsets_y[t]
                    target[to_x, to_y] = target[to_x, to_y] + spread

        over_slabs(scatter_part, 2)

    for copy in copies:
        copy.wait()
    apply(first, second, lambda total, target, x, y: total, scale)

    for x in (0, ring + count_x):
        second[x] = jnp.zeros(second.shape[1:], jnp.float32)
    for y in (0, ring + count_y):
        second[:, y] = jnp.zeros((second.shape[0],) + second.shape[2:], jnp.float32)

    apply(second, first, lambda total, target, x, y: 2.0 * total - target[x, y], 2.0 * scale)

    portion = rounded_ref.shape[-1] // nz

    parts = slab_cells // portion
    leaving = []
    for part in range(parts):

        def round_slab(g):
            place, x0, y0 = corner(g)
            for within in range(portion):
                i, j = divmod(part * portion + within, cells_y)
                rounded_ref[part * group + place, :, pl.ds(within * nz, nz)] = first[
                    ring + x0 + i, ring + y0 + j
                ].astype(jnp.bfloat16)

        over_slabs(round_slab, 1)
        shares = pl.ds(part * group, group)
        leaving.append(
            pltpu.make_async_copy(rounded_ref.at[shares], rounded_out.at[shares], sent.at[part])
        )
        leaving[-1].start()
    for copy in leaving:
        copy.wait()


def scale_kernel(slabs_y, cells_x, cells_y, by_swaps, values_ref, field_ref):
    group, rows, nz = field_ref.shape
    each = values_ref.shape[2]
    ring = 1
    count_x, count_y = values_ref.shape[0] - 2 * ring, values_ref.shape[1] - 2 * ring
    me = lax.axis_index("sx") * slabs_y + lax.axis_index("sy") if by_swaps else 0

    def largest_of(x, largest):
        row = jnp.abs(values_ref[ring + x, pl.ds(ring, count_y)])
        return jnp.maximum(largest, jnp.max(row, axis=0))

    largest = lax.fori_loop(0, count_x, largest_of, jnp.zeros((each, nz), jnp.float32), unroll=2)
    level, gain = level_of(jnp.max(largest))
    level_rows = jnp.full((8, nz), level, jnp.float32)

    def give_slab(g, carry):
        place = jnp.bitwise_xor(me, g) if by_swaps else g
        x0 = (place // slabs_y) * cells_x
        y0 = (place % slabs_y) * cells_y
        field_ref[g, pl.ds(rows - 8, 8), :] = level_rows
        for i in range(cells_x):
            for j in range(cells_y):
                field_ref[g, pl.ds((i * cells_y + j) * each, each), :] = (
                    values_ref[ring + x0 + i, ring + y0 + j] * gain
                )
        return carry

    lax.fori_loop(0, group, give_slab, 0)


def entry(block, place):
    picked = jnp.where(place, block, 0.0)
    return jnp.sum(jnp.sum(picked, axis=0, keepdims=True), axis=1, keepdims=True)


def band_corner(shape, band):
    row = lax.broadcasted_iota(jnp.int32, shape, 0)
    column = lax.broadcasted_iota(jnp.int32, shape, 1)
    return (
        (row == 1) & (column == band * shape[0]),
        (row == 0) & (column == band * shape[0] + 1),
    )


def gram_kernel(matrix_ref, out_ref, sums_ref):
    bands, rows, columns = out_ref.shape
    matrix = matrix_ref[...]
    sums = lax.dot_general(
        matrix, matrix, (((1,), (1,)), ((), ())), preferred_element_type=jnp.float32
    )
    level, gain = level_of(jnp.max(jnp.abs(sums)))
    sums_ref[...] = sums * gain
    me = lax.axis_index("band")
    for k in range(bands):
        band = jnp.bitwise_xor(me, k)
        spare, _ = band_corner((rows, columns), band)
        block = sums_ref[pl.ds(pl.multiple_of(band * rows, rows), rows), :]
        out_ref[k] = jnp.where(spare, level, block)


def rows_kernel(cells, own_ref, *refs):
    out_ref = refs[-1]
    spare, twin = band_corner(out_ref.shape, lax.axis_index("band"))
    total = None
    for block in [own_ref[0]] + [ref[...] for ref in refs[:-1]]:
        block = block * shrink_of(entry(block, spare))
        total = block if total is None else total + block
    out_ref[...] = jnp.where(spare, entry(total, twin), total) / cells


def unpack_kernel(each, slabs_y, places, *refs):
    pieces = refs[:-3]
    filtered_hbm, filtered_ref, chunk_sems = refs[-3:]
    slab_cells, _, nz = filtered_ref.shape
    chunks = chunk_sems.shape[0]
    chunk = slab_cells // chunks
    me = lax.axis_index("sx") * slabs_y + lax.axis_index("sy") if len(pieces) > 1 else 0
    copies = []
    for c in range(chunks):
        for which, entry, other in places:
            piece = pieces[which]
            shrink = shrink_of(piece[entry, pl.ds(slab_cells * each, 1), :])
            if len(pieces) > 1:
                rows = pl.ds(pl.multiple_of(jnp.bitwise_xor(me, other) * each, each), each)
            else:
                rows = pl.ds(other * each, each)
            for cell in range(c * chunk, (c + 1) * chunk):
                filtered_ref[cell, rows, :] = piece[entry, pl.ds(cell * each, each), :] * shrink
        part = pl.ds(c * chunk, chunk)
        copies.append(
            pltpu.make_async_copy(filtered_ref.at[part], filtered_hbm.at[part], chunk_sems.at[c])
        )
        copies[-1].start()
    for copy in copies:
        copy.wait()


def swap(block, value):
    group = lax.axis_size(plane)
    return lax.ppermute(block, plane, [(i, i ^ value) for i in range(group)])


def local(orbitals, potential, projectors, energies, centers):
    band_orbitals, cells_x, cells_y, nz = orbitals.shape
    bands = lax.axis_size("band")
    slabs_x = lax.axis_size("sx")
    slabs_y = lax.axis_size("sy")
    group = slabs_x * slabs_y
    each = band_orbitals // group
    total_orbitals = bands * band_orbitals
    slab_cells = cells_x * cells_y
    grid = (slabs_x * cells_x, slabs_y * cells_y)
    atoms, projs, tiles, _ = projectors.shape

    near = slabs_y
    far = [v for v in range(1, group) if not v & near]
    by_swaps = group <= 8 and each % 8 == 0 and slabs_x > 1
    by_swaps = by_swaps and group & (group - 1) == 0 and bands & (bands - 1) == 0

    number_rows = 2 * atoms + 2
    rows = atoms * projs * tiles + slab_cells + number_rows
    rows += -rows % 8
    piece_rows = slab_cells * each
    chunks = (orbitals * orbital_gain).astype(jnp.float16)
    chunks = chunks.transpose(1, 2, 0, 3).reshape(slab_cells, group, each, nz)
    chunks = chunks.transpose(1, 0, 2, 3).reshape(group, piece_rows, nz)
    shared = pl.pallas_call(
        share_kernel,
        in_specs=[hbm, vmem, vmem, vmem, vmem],
        out_specs=vmem,
        out_shape=jax.ShapeDtypeStruct((rows, nz), jnp.float32),
        compiler_params=params,
    )(chunks[0, :8].astype(jnp.float32), energies, centers.T, projectors.transpose(0, 2, 1, 3), potential)
    narrow = shared.astype(jnp.float16)
    if by_swaps:
        me = lax.axis_index(plane)

        def chunk_for(value):
            return lax.dynamic_index_in_dim(chunks, me ^ value, 0, keepdims=False)

        came = [swap(jnp.concatenate([chunk_for(v), narrow, chunk_for(v ^ near)]), v) for v in far]
        mine = jnp.concatenate([narrow, chunk_for(near)])
        passed = {0: mine, **{v: block[piece_rows:] for v, block in zip(far, came)}}
        operands = [chunk_for(0)[None], narrow[None]] + [block[None] for block in came]
        slabs = {0: ((0, 0, 0), (1, 0, 0))}
        for i, v in enumerate(far):
            slabs[v] = ((2 + i, 0, 0), (2 + i, 0, piece_rows))
        for part in ([0], far[-1:], far[:-1]):
            if part:
                for i, v in enumerate(part):
                    slabs[v ^ near] = ((len(operands), i, rows), (len(operands), i, 0))
                operands.append(swap(jnp.stack([passed[v] for v in part]), near))
        operands = [block.astype(jnp.float32) for block in operands]
        operands[1] = shared[None]
    else:
        sent = jnp.concatenate([chunks, jnp.broadcast_to(narrow[None], (group, rows, nz))], axis=1)
        operands = [lax.all_to_all(sent, plane, 0, 0).astype(jnp.float32)]
        slabs = None

    portion = slab_cells // bands
    ringed = (grid[0] + 2, grid[1] + 2, each, nz)
    shares = bands * group
    rounded_shape = (shares, each, portion * nz)
    values, rounded = pl.pallas_call(
        functools.partial(filter_kernel, slabs_y, cells_x, cells_y, each, atoms, projs, slabs),
        in_specs=[vmem] * len(operands),
        out_specs=[vmem, hbm],
        out_shape=[
            jax.ShapeDtypeStruct(ringed, jnp.float32),
            jax.ShapeDtypeStruct(rounded_shape, jnp.bfloat16),
        ],
        scratch_shapes=[
            pltpu.VMEM(ringed, jnp.float32),
            pltpu.VMEM(grid + (each, nz), jnp.float32),
            pltpu.VMEM(grid + (1, nz), jnp.float32),
            pltpu.VMEM((group, atoms * projs, each, nz), jnp.float32),
            pltpu.SMEM((group, number_rows, nz), jnp.float32),
            pltpu.VMEM(rounded_shape, jnp.bfloat16),
            pltpu.SemaphoreType.DMA((group,)),
            pltpu.SemaphoreType.DMA((bands,)),
        ],
        compiler_params=params,
        cost_estimate=pl.CostEstimate(
            flops=2 * 2 * 40 * grid[0] * grid[1] * each * nz,
            bytes_accessed=8 * grid[0] * grid[1] * each * nz,
            transcendentals=0,
        ),
    )(*operands)

    matrix = lax.all_to_all(rounded, every, 0, 0)
    matrix = matrix.reshape(total_orbitals, portion * nz)
    field = pl.pallas_call(
        functools.partial(scale_kernel, slabs_y, cells_x, cells_y, by_swaps),
        in_specs=[vmem],
        out_specs=vmem,
        out_shape=jax.ShapeDtypeStruct((group, piece_rows + 8, nz), jnp.float32),
        compiler_params=params,
    )(values)
    narrow = field.astype(jnp.float16)
    if by_swaps:
        came = {v: swap(jnp.stack([narrow[v], narrow[v | near]]), v) for v in far}
        along_x = [v for v in far if v % slabs_y == 0]
        along_y = [v for v in far if v % slabs_y > 0]
        tied, matrix = lax.optimization_barrier(([came[v] for v in along_x], matrix))
    else:
        pieces = [lax.all_to_all(narrow, plane, 0, 0).astype(jnp.float32)]
        places = [(0, g, g) for g in range(group)]

    def unpack(pieces, places):
        return pl.pallas_call(
            functools.partial(unpack_kernel, each, slabs_y, places),
            in_specs=[vmem] * len(pieces),
            out_specs=hbm,
            out_shape=jax.ShapeDtypeStruct((slab_cells, band_orbitals, nz), jnp.float32),
            scratch_shapes=[
                pltpu.VMEM((slab_cells, band_orbitals, nz), jnp.float32),
                pltpu.SemaphoreType.DMA((cells_x,)),
            ],
            compiler_params=params,
        )(*pieces)

    cells = grid[0] * grid[1] * nz
    if by_swaps:
        sums = pl.pallas_call(
            gram_kernel,
            in_specs=[vmem],
            out_specs=vmem,
            out_shape=jax.ShapeDtypeStruct((bands, band_orbitals, total_orbitals), jnp.float32),
            scratch_shapes=[pltpu.VMEM((total_orbitals, total_orbitals), jnp.float32)],
            compiler_params=params,
        )(matrix)
        parts = [
            lax.ppermute(
                sums[k].astype(jnp.float16), "band", [(i, i ^ k) for i in range(bands)]
            ).astype(jnp.float32)
            for k in range(bands - 1, 0, -1)
        ]
        gram = pl.pallas_call(
            functools.partial(rows_kernel, cells),
            in_specs=[vmem] * bands,
            out_specs=vmem,
            out_shape=jax.ShapeDtypeStruct((band_orbitals, total_orbitals), jnp.float32),
            compiler_params=params,
        )(sums, *parts)
        free, gram = lax.optimization_barrier(([came[v] for v in along_y], gram))
        came = dict(zip(along_x + along_y, tied + free))
        came = [came[v] for v in far]
        came.append(swap(jnp.stack([narrow[near]] + [block[1] for block in came]), near))
        pieces = [field] + [block.astype(jnp.float32) for block in came]
        places = [(0, 0, 0), (len(pieces) - 1, 0, near)]
        for i, v in enumerate(far):
            places += [(i + 1, 0, v), (len(pieces) - 1, i + 1, v | near)]
        terms = {v: swap(gram, v) for v in far}
        terms[0] = gram
        bit = 1
        while len(terms) > 1:
            if any(v ^ bit in terms for v in terms):
                terms = {v: terms[v] + terms[v ^ bit] for v in terms if not v & bit}
            bit *= 2
        gram = terms[0]
        other, filtered = lax.optimization_barrier((swap(gram, near), unpack(pieces, places)))
        gram = gram + other
    else:
        sums = lax.dot_general(
            matrix, matrix, (((1,), (1,)), ((), ())), preferred_element_type=jnp.float32
        )
        parts = lax.all_to_all(sums.reshape(shares, each, total_orbitals), every, 0, 0)
        rows = jnp.sum(parts, axis=0) / cells
        gram = lax.all_to_all(jnp.broadcast_to(rows[None], (group,) + rows.shape), plane, 0, 0)
        gram = gram.reshape(band_orbitals, total_orbitals)
        filtered = unpack(pieces, places)

    filtered = filtered.reshape(cells_x, cells_y, band_orbitals, nz).transpose(2, 0, 1, 3)
    return (filtered, gram)


def solution(mesh):
    in_specs = (
        P("band", "sx", "sy", None),
        P("sx", "sy", None),
        P(("sx", "sy"), None, None, None),
        P(("sx", "sy"), None),
        P(("sx", "sy"), None),
    )
    out_specs = (P("band", "sx", "sy", None), P("band", None))
    return jax.shard_map(local, mesh=mesh, in_specs=in_specs, out_specs=out_specs, check_vma=False)
```

```python
import functools

import jax
import jax.numpy as jnp
from jax import lax
from jax.experimental import pallas as pl
from jax.experimental.pallas import tpu as pltpu
from jax.sharding import PartitionSpec as P

stencil_weights = (
    -5369.0 / 1800.0,
    12.0 / 7.0,
    -15.0 / 56.0,
    10.0 / 189.0,
    -1.0 / 112.0,
    2.0 / 1925.0,
    -1.0 / 16632.0,
)
filter_center = 6.5
filter_half = 6.0
offsets_x = (0, -1, 1, 0, 0)
offsets_y = (0, 0, 0, -1, 1)
reach = 6
plane = ("sx", "sy")
every = ("band", "sx", "sy")

orbital_gain = 2.0**12
projector_gain = 2.0**17
potential_gain = 2.0**13
remainder_gain = 2.0**10
top = 15
middle = 8
levels = 17

vmem = pl.BlockSpec(memory_space=pltpu.VMEM)
hbm = pl.BlockSpec(memory_space=pl.ANY)
params = pltpu.CompilerParams(vmem_limit_bytes=24 * 1024 * 1024)


def level_of(largest):
    level = jnp.float32(0.0)
    scale = jnp.float32(2.0 ** (top + 8 * middle))
    for j in range(levels):
        above = largest >= jnp.float32(2.0 ** (8 * (j - middle)))
        level = jnp.where(above, jnp.float32(j + 1), level)
        scale = jnp.where(above, jnp.float32(2.0 ** (top - 8 * (j + 1 - middle))), scale)
    return level, scale


def shrink_of(level):
    shrink = jnp.full(level.shape, 2.0 ** (-top - 8 * middle), jnp.float32)
    for j in range(levels):
        shrink = jnp.where(level > j, jnp.float32(2.0 ** (8 * (j + 1 - middle) - top)), shrink)
    return shrink


def share_kernel(_, energies_ref, centers_ref, projectors_ref, potential_ref, out_ref):
    rows, nz = out_ref.shape
    atoms, tiles, projs = projectors_ref.shape[:3]

    row = 0
    for a in range(atoms):
        for t in range(tiles):
            out_ref[pl.ds(row, projs), :] = projectors_ref[a, t] * projector_gain
            row += projs
    for i in range(potential_ref.shape[0]):
        count = potential_ref.shape[1]
        out_ref[pl.ds(row, count), :] = potential_ref[i] * potential_gain
        row += count
    out_ref[pl.ds(row, rows - row), :] = jnp.zeros((rows - row, nz), jnp.float32)
    energies = energies_ref[...]
    high = energies.astype(jnp.bfloat16).astype(jnp.float32)
    out_ref[pl.ds(row, atoms), :projs] = high
    out_ref[pl.ds(row + atoms, atoms), :projs] = (energies - high) * remainder_gain
    out_ref[pl.ds(row + 2 * atoms, 2), :atoms] = centers_ref[...].astype(jnp.float32)


def filter_kernel(slabs_y, cells_x, cells_y, each, atoms, projs, slabs, *refs):
    inputs, (first, rounded_out) = refs[:-10], refs[-10:-8]
    second, partial, diagonal, coeffs, numbers, rounded_ref, arrived, sent = refs[-8:]
    group, number_rows, _ = numbers.shape
    nz = first.shape[-1]
    count_x, count_y = diagonal.shape[0], diagonal.shape[1]
    tiles = len(offsets_x)
    slab_cells = cells_x * cells_y
    pot_row = atoms * projs * tiles
    number_row = pot_row + slab_cells
    scale = 1.0 / filter_half
    factors = [-0.5 * scale * w for w in stencil_weights]
    ring = 1
    me = 0 if slabs is None else lax.axis_index("sx") * slabs_y + lax.axis_index("sy")

    def rows_of(g, shared, row, count):
        if slabs is None:
            return inputs[0].at[g, pl.ds(row + (slab_cells * each if shared else 0), count), :]
        which, at, start = slabs[g][1 if shared else 0]
        return inputs[which].at[at, pl.ds(start + row, count), :]

    def shared_row(g, row):
        return rows_of(g, True, row, 1)[...]

    def over_slabs(body, unroll):
        if slabs is None:
            lax.fori_loop(0, group, lambda g, carry: body(g) or carry, 0, unroll=min(group, unroll))
        else:
            for g in range(group):
                body(g)

    def corner(g):
        place = g if slabs is None else jnp.bitwise_xor(me, g)
        return place, (place // slabs_y) * cells_x, (place % slabs_y) * cells_y

    if slabs is None:
        copies = [
            pltpu.make_async_copy(
                inputs[0].at[:, pl.ds(slab_cells * each + number_row, number_rows), :],
                numbers,
                arrived.at[0],
            )
        ]
    else:
        copies = [
            pltpu.make_async_copy(
                rows_of(g, True, number_row, number_rows), numbers.at[g], arrived.at[g]
            )
            for g in range(group)
        ]
    for copy in copies:
        copy.start()

    for field in (first, second):
        for x in (0, ring + count_x):
            field[x] = jnp.zeros(field.shape[1:], jnp.float32)
        for y in (0, ring + count_y):
            field[:, y] = jnp.zeros((field.shape[0],) + field.shape[2:], jnp.float32)

    def take_slab(g):
        _, x0, y0 = corner(g)
        for i in range(cells_x):
            for j in range(cells_y):
                cell = i * cells_y + j
                first[ring + x0 + i, ring + y0 + j] = rows_of(g, False, cell * each, each)[...] * (
                    1.0 / orbital_gain
                )
                diagonal[x0 + i, y0 + j] = shared_row(g, pot_row + cell) * (
                    scale / potential_gain
                ) + (3.0 * factors[0] - filter_center * scale)

    over_slabs(take_slab, 1)

    distance = jnp.abs(
        lax.broadcasted_iota(jnp.int32, (nz, nz), 0) - lax.broadcasted_iota(jnp.int32, (nz, nz), 1)
    )
    along_z = jnp.zeros((nz, nz), jnp.float32)
    for step in range(1, reach + 1):
        along_z = jnp.where(distance == step, factors[step], along_z)
    z_high = along_z.astype(jnp.bfloat16)
    z_low = (along_z - z_high.astype(jnp.float32)).astype(jnp.bfloat16)
    z_matrix = jnp.concatenate(
        [
            jnp.concatenate([z_high, z_low], axis=1),
            jnp.concatenate([z_high, jnp.zeros_like(z_high)], axis=1),
        ],
        axis=0,
    )

    def along(cells, at):
        total = None
        for step in range(1, reach + 1):
            near = [cells[n] for n in (at - step, at + step) if 0 <= n < len(cells)]
            if near:
                term = factors[step] * sum(near[1:], near[0])
                total = term if total is None else total + term
        return total

    def apply(source, target, finish, gain):
        def xz_part(y, carry):
            column = source[pl.ds(ring, count_x), ring + y]
            flat = column.reshape(count_x * each, nz)
            high = flat.astype(jnp.bfloat16)
            low = (flat - high.astype(jnp.float32)).astype(jnp.bfloat16)
            both = jnp.dot(
                jnp.concatenate([high, low], axis=1), z_matrix, preferred_element_type=jnp.float32
            )
            along_z = (both[:, :nz] + both[:, nz:]).reshape(column.shape)
            cells = [column[x] for x in range(count_x)]
            for x in range(count_x):
                partial[x, y] = along_z[x] + diagonal[x, y] * cells[x] + along(cells, x)
            return carry

        lax.fori_loop(0, count_y, xz_part, 0, unroll=6)

        def y_part(x, carry):
            cells = [source[ring + x, ring + y] for y in range(count_y)]
            for y in range(count_y):
                total = partial[x, y] + along(cells, y)
                target[ring + x, ring + y] = finish(total, target, ring + x, ring + y)
            return carry

        lax.fori_loop(0, count_x, y_part, 0, unroll=4)

        def place_of(g, a):
            return (
                ring + numbers[g, 2 * atoms, a].astype(jnp.int32),
                ring + numbers[g, 2 * atoms + 1, a].astype(jnp.int32),
            )

        def gather_part(g):
            for a in range(atoms):
                at_x, at_y = place_of(g, a)
                totals = [None] * projs
                for t in range(tiles):
                    tile = source[at_x + offsets_x[t], at_y + offsets_y[t]]
                    for p in range(projs):
                        term = tile * shared_row(g, (a * tiles + t) * projs + p)
                        totals[p] = term if t == 0 else totals[p] + term
                for p in range(projs):
                    energy = numbers[g, a, p] + numbers[g, atoms + a, p] * (1.0 / remainder_gain)
                    coeffs[g, a * projs + p] = jnp.broadcast_to(
                        jnp.sum(totals[p], axis=-1, keepdims=True)
                        * (energy * (gain / projector_gain / projector_gain)),
                        (each, nz),
                    )

        over_slabs(gather_part, 4)

        def scatter_part(g):
            for a in range(atoms):
                at_x, at_y = place_of(g, a)
                factor = [coeffs[g, a * projs + p] for p in range(projs)]
                for t in range(tiles):
                    row = (a * tiles + t) * projs
                    spread = factor[0] * shared_row(g, row)
                    for p in range(1, projs):
                        spread = spread + factor[p] * shared_row(g, row + p)
                    to_x = at_x + offsets_x[t]
                    to_y = at_y + offsets_y[t]
                    target[to_x, to_y] = target[to_x, to_y] + spread

        over_slabs(scatter_part, 2)

    for copy in copies:
        copy.wait()
    apply(first, second, lambda total, target, x, y: total, scale)

    for x in (0, ring + count_x):
        second[x] = jnp.zeros(second.shape[1:], jnp.float32)
    for y in (0, ring + count_y):
        second[:, y] = jnp.zeros((second.shape[0],) + second.shape[2:], jnp.float32)

    apply(second, first, lambda total, target, x, y: 2.0 * total - target[x, y], 2.0 * scale)

    portion = rounded_ref.shape[-1] // nz

    parts = slab_cells // portion
    leaving = []
    for part in range(parts):

        def round_slab(g):
            place, x0, y0 = corner(g)
            for within in range(portion):
                i, j = divmod(part * portion + within, cells_y)
                rounded_ref[part * group + place, :, pl.ds(within * nz, nz)] = first[
                    ring + x0 + i, ring + y0 + j
                ].astype(jnp.bfloat16)

        over_slabs(round_slab, 1)
        shares = pl.ds(part * group, group)
        leaving.append(
            pltpu.make_async_copy(rounded_ref.at[shares], rounded_out.at[shares], sent.at[part])
        )
        leaving[-1].start()
    for copy in leaving:
        copy.wait()


def scale_kernel(slabs_y, cells_x, cells_y, by_swaps, values_ref, field_ref):
    group, rows, nz = field_ref.shape
    each = values_ref.shape[2]
    ring = 1
    count_x, count_y = values_ref.shape[0] - 2 * ring, values_ref.shape[1] - 2 * ring
    me = lax.axis_index("sx") * slabs_y + lax.axis_index("sy") if by_swaps else 0

    def largest_of(x, largest):
        row = jnp.abs(values_ref[ring + x, pl.ds(ring, count_y)])
        return jnp.maximum(largest, jnp.max(row, axis=0))

    largest = lax.fori_loop(0, count_x, largest_of, jnp.zeros((each, nz), jnp.float32), unroll=2)
    level, gain = level_of(jnp.max(largest))
    level_rows = jnp.full((8, nz), level, jnp.float32)

    def give_slab(g, carry):
        place = jnp.bitwise_xor(me, g) if by_swaps else g
        x0 = (place // slabs_y) * cells_x
        y0 = (place % slabs_y) * cells_y
        field_ref[g, pl.ds(rows - 8, 8), :] = level_rows
        for i in range(cells_x):
            for j in range(cells_y):
                field_ref[g, pl.ds((i * cells_y + j) * each, each), :] = (
                    values_ref[ring + x0 + i, ring + y0 + j] * gain
                )
        return carry

    lax.fori_loop(0, group, give_slab, 0)


def entry(block, place):
    picked = jnp.where(place, block, 0.0)
    return jnp.sum(jnp.sum(picked, axis=0, keepdims=True), axis=1, keepdims=True)


def band_corner(shape, band):
    row = lax.broadcasted_iota(jnp.int32, shape, 0)
    column = lax.broadcasted_iota(jnp.int32, shape, 1)
    return (
        (row == 1) & (column == band * shape[0]),
        (row == 0) & (column == band * shape[0] + 1),
    )


def gram_kernel(matrix_ref, out_ref, sums_ref):
    bands, rows, columns = out_ref.shape
    matrix = matrix_ref[...]
    sums = lax.dot_general(
        matrix, matrix, (((1,), (1,)), ((), ())), preferred_element_type=jnp.float32
    )
    level, gain = level_of(jnp.max(jnp.abs(sums)))
    sums_ref[...] = sums * gain
    me = lax.axis_index("band")
    for k in range(bands):
        band = jnp.bitwise_xor(me, k)
        spare, _ = band_corner((rows, columns), band)
        block = sums_ref[pl.ds(pl.multiple_of(band * rows, rows), rows), :]
        out_ref[k] = jnp.where(spare, level, block)


def rows_kernel(cells, own_ref, *refs):
    out_ref = refs[-1]
    spare, twin = band_corner(out_ref.shape, lax.axis_index("band"))
    total = None
    for block in [own_ref[0]] + [ref[...] for ref in refs[:-1]]:
        block = block * shrink_of(entry(block, spare))
        total = block if total is None else total + block
    out_ref[...] = jnp.where(spare, entry(total, twin), total) / cells


def unpack_kernel(each, slabs_y, places, *refs):
    pieces = refs[:-3]
    filtered_hbm, filtered_ref, chunk_sems = refs[-3:]
    slab_cells, _, nz = filtered_ref.shape
    chunks = chunk_sems.shape[0]
    chunk = slab_cells // chunks
    me = lax.axis_index("sx") * slabs_y + lax.axis_index("sy") if len(pieces) > 1 else 0
    copies = []
    for c in range(chunks):
        for which, entry, other in places:
            piece = pieces[which]
            shrink = shrink_of(piece[entry, pl.ds(slab_cells * each, 1), :])
            if len(pieces) > 1:
                rows = pl.ds(pl.multiple_of(jnp.bitwise_xor(me, other) * each, each), each)
            else:
                rows = pl.ds(other * each, each)
            for cell in range(c * chunk, (c + 1) * chunk):
                filtered_ref[cell, rows, :] = piece[entry, pl.ds(cell * each, each), :] * shrink
        part = pl.ds(c * chunk, chunk)
        copies.append(
            pltpu.make_async_copy(filtered_ref.at[part], filtered_hbm.at[part], chunk_sems.at[c])
        )
        copies[-1].start()
    for copy in copies:
        copy.wait()


def swap(block, value):
    group = lax.axis_size(plane)
    return lax.ppermute(block, plane, [(i, i ^ value) for i in range(group)])


def local(orbitals, potential, projectors, energies, centers):
    band_orbitals, cells_x, cells_y, nz = orbitals.shape
    bands = lax.axis_size("band")
    slabs_x = lax.axis_size("sx")
    slabs_y = lax.axis_size("sy")
    group = slabs_x * slabs_y
    each = band_orbitals // group
    total_orbitals = bands * band_orbitals
    slab_cells = cells_x * cells_y
    grid = (slabs_x * cells_x, slabs_y * cells_y)
    atoms, projs, tiles, _ = projectors.shape

    near = slabs_y
    far = [v for v in range(1, group) if not v & near]
    by_swaps = group <= 8 and each % 8 == 0 and slabs_x > 1
    by_swaps = by_swaps and group & (group - 1) == 0 and bands & (bands - 1) == 0

    number_rows = 2 * atoms + 2
    rows = atoms * projs * tiles + slab_cells + number_rows
    rows += -rows % 8
    piece_rows = slab_cells * each
    chunks = (orbitals * orbital_gain).astype(jnp.float16)
    chunks = chunks.transpose(1, 2, 0, 3).reshape(slab_cells, group, each, nz)
    chunks = chunks.transpose(1, 0, 2, 3).reshape(group, piece_rows, nz)
    shared = pl.pallas_call(
        share_kernel,
        in_specs=[hbm, vmem, vmem, vmem, vmem],
        out_specs=vmem,
        out_shape=jax.ShapeDtypeStruct((rows, nz), jnp.float32),
        compiler_params=params,
    )(chunks[0, :8].astype(jnp.float32), energies, centers.T, projectors.transpose(0, 2, 1, 3), potential)
    narrow = shared.astype(jnp.float16)
    if by_swaps:
        me = lax.axis_index(plane)

        def chunk_for(value):
            return lax.dynamic_index_in_dim(chunks, me ^ value, 0, keepdims=False)

        came = [swap(jnp.concatenate([chunk_for(v), narrow, chunk_for(v ^ near)]), v) for v in far]
        mine = jnp.concatenate([narrow, chunk_for(near)])
        passed = {0: mine, **{v: block[piece_rows:] for v, block in zip(far, came)}}
        operands = [chunk_for(0)[None], narrow[None]] + [block[None] for block in came]
        slabs = {0: ((0, 0, 0), (1, 0, 0))}
        for i, v in enumerate(far):
            slabs[v] = ((2 + i, 0, 0), (2 + i, 0, piece_rows))
        for part in ([0], far[-1:], far[:-1]):
            if part:
                for i, v in enumerate(part):
                    slabs[v ^ near] = ((len(operands), i, rows), (len(operands), i, 0))
                operands.append(swap(jnp.stack([passed[v] for v in part]), near))
        operands = [block.astype(jnp.float32) for block in operands]
        operands[1] = shared[None]
    else:
        sent = jnp.concatenate([chunks, jnp.broadcast_to(narrow[None], (group, rows, nz))], axis=1)
        operands = [lax.all_to_all(sent, plane, 0, 0).astype(jnp.float32)]
        slabs = None

    portion = slab_cells // bands
    ringed = (grid[0] + 2, grid[1] + 2, each, nz)
    shares = bands * group
    rounded_shape = (shares, each, portion * nz)
    values, rounded = pl.pallas_call(
        functools.partial(filter_kernel, slabs_y, cells_x, cells_y, each, atoms, projs, slabs),
        in_specs=[vmem] * len(operands),
        out_specs=[vmem, hbm],
        out_shape=[
            jax.ShapeDtypeStruct(ringed, jnp.float32),
            jax.ShapeDtypeStruct(rounded_shape, jnp.bfloat16),
        ],
        scratch_shapes=[
            pltpu.VMEM(ringed, jnp.float32),
            pltpu.VMEM(grid + (each, nz), jnp.float32),
            pltpu.VMEM(grid + (1, nz), jnp.float32),
            pltpu.VMEM((group, atoms * projs, each, nz), jnp.float32),
            pltpu.SMEM((group, number_rows, nz), jnp.float32),
            pltpu.VMEM(rounded_shape, jnp.bfloat16),
            pltpu.SemaphoreType.DMA((group,)),
            pltpu.SemaphoreType.DMA((bands,)),
        ],
        compiler_params=params,
        cost_estimate=pl.CostEstimate(
            flops=2 * 2 * 40 * grid[0] * grid[1] * each * nz,
            bytes_accessed=8 * grid[0] * grid[1] * each * nz,
            transcendentals=0,
        ),
    )(*operands)

    matrix = lax.all_to_all(rounded, every, 0, 0)
    matrix = matrix.reshape(total_orbitals, portion * nz)
    field = pl.pallas_call(
        functools.partial(scale_kernel, slabs_y, cells_x, cells_y, by_swaps),
        in_specs=[vmem],
        out_specs=vmem,
        out_shape=jax.ShapeDtypeStruct((group, piece_rows + 8, nz), jnp.float32),
        compiler_params=params,
    )(values)
    narrow = field.astype(jnp.float16)
    if by_swaps:
        along_x = [v for v in far if v % slabs_y == 0]
        along_y = [v for v in far if v % slabs_y > 0]
        came = {v: swap(jnp.stack([narrow[v], narrow[v | near]]), v) for v in along_x}
        came, narrow = lax.optimization_barrier((came, narrow))
        came |= {v: swap(jnp.stack([narrow[v], narrow[v | near]]), v) for v in along_y}
        tied, matrix = lax.optimization_barrier(([came[v] for v in along_x], matrix))
    else:
        pieces = [lax.all_to_all(narrow, plane, 0, 0).astype(jnp.float32)]
        places = [(0, g, g) for g in range(group)]

    def unpack(pieces, places):
        return pl.pallas_call(
            functools.partial(unpack_kernel, each, slabs_y, places),
            in_specs=[vmem] * len(pieces),
            out_specs=hbm,
            out_shape=jax.ShapeDtypeStruct((slab_cells, band_orbitals, nz), jnp.float32),
            scratch_shapes=[
                pltpu.VMEM((slab_cells, band_orbitals, nz), jnp.float32),
                pltpu.SemaphoreType.DMA((cells_x,)),
            ],
            compiler_params=params,
        )(*pieces)

    cells = grid[0] * grid[1] * nz
    if by_swaps:
        sums = pl.pallas_call(
            gram_kernel,
            in_specs=[vmem],
            out_specs=vmem,
            out_shape=jax.ShapeDtypeStruct((bands, band_orbitals, total_orbitals), jnp.float32),
            scratch_shapes=[pltpu.VMEM((total_orbitals, total_orbitals), jnp.float32)],
            compiler_params=params,
        )(matrix)
        parts = [
            lax.ppermute(
                sums[k].astype(jnp.float16), "band", [(i, i ^ k) for i in range(bands)]
            ).astype(jnp.float32)
            for k in range(1, bands)
        ]
        gram = pl.pallas_call(
            functools.partial(rows_kernel, cells),
            in_specs=[vmem] * bands,
            out_specs=vmem,
            out_shape=jax.ShapeDtypeStruct((band_orbitals, total_orbitals), jnp.float32),
            compiler_params=params,
        )(sums, *parts)
        free, gram = lax.optimization_barrier(([came[v] for v in along_y], gram))
        came = dict(zip(along_x + along_y, tied + free))
        came = [came[v] for v in far]
        came.append(swap(jnp.stack([narrow[near]] + [block[1] for block in came]), near))
        pieces = [field] + [block.astype(jnp.float32) for block in came]
        places = [(0, 0, 0), (len(pieces) - 1, 0, near)]
        for i, v in enumerate(far):
            places += [(i + 1, 0, v), (len(pieces) - 1, i + 1, v | near)]
        terms = {v: swap(gram, v) for v in far}
        terms[0] = gram
        bit = 1
        while len(terms) > 1:
            if any(v ^ bit in terms for v in terms):
                terms = {v: terms[v] + terms[v ^ bit] for v in terms if not v & bit}
            bit *= 2
        gram = terms[0]
        other, filtered = lax.optimization_barrier((swap(gram, near), unpack(pieces, places)))
        gram = gram + other
    else:
        sums = lax.dot_general(
            matrix, matrix, (((1,), (1,)), ((), ())), preferred_element_type=jnp.float32
        )
        parts = lax.all_to_all(sums.reshape(shares, each, total_orbitals), every, 0, 0)
        rows = jnp.sum(parts, axis=0) / cells
        gram = lax.all_to_all(jnp.broadcast_to(rows[None], (group,) + rows.shape), plane, 0, 0)
        gram = gram.reshape(band_orbitals, total_orbitals)
        filtered = unpack(pieces, places)

    filtered = filtered.reshape(cells_x, cells_y, band_orbitals, nz).transpose(2, 0, 1, 3)
    return (filtered, gram)


def solution(mesh):
    in_specs = (
        P("band", "sx", "sy", None),
        P("sx", "sy", None),
        P(("sx", "sy"), None, None, None),
        P(("sx", "sy"), None),
        P(("sx", "sy"), None),
    )
    out_specs = (P("band", "sx", "sy", None), P("band", None))
    return jax.shard_map(local, mesh=mesh, in_specs=in_specs, out_specs=out_specs, check_vma=False)
```
